32 devices in a mesh: batch: 8 (over z, x), blk: 4 (over y, core).
Axes of the slice: x: 2, y: 2, z: 4, core: 2. Of those that a mesh axis runs over, the one named last changes fastest.
Arguments:
- tokens: bfloat16 [16, 2048, 768], P('batch', 'blk'), may hold values from -6 to 6
- proj_weight: bfloat16 [768, 2304], P('batch', 'blk'), may hold values from -0.3125 to 0.3125
- out_weight: bfloat16 [768, 768], P('batch', 'blk'), may hold values from -0.875 to 0.875
- up_weight: bfloat16 [768, 3072], P('batch', 'blk'), may hold values from -0.21875 to 0.21875
- down_weight: bfloat16 [3072, 768], P('batch', 'blk'), may hold values from -0.109375 to 0.109375
- gain_one: bfloat16 [768], P('blk'), may hold values from 0.25 to 1.75
- bias_one: bfloat16 [768], P('blk'), may hold values from -3 to 3
- gain_two: bfloat16 [768], P('blk'), may hold values from 0.25 to 1.75
- bias_two: bfloat16 [768], P('blk'), may hold values from -3 to 3
- segments: int32 [16, 2048], P('batch', 'blk'), may hold values from 0 to 4, as said below
- present: int32 [16, 2048], P('batch', 'blk'), may hold values from 0 to 1, as said below
- cotangent: bfloat16 [16, 2048, 768], P('batch', 'blk'), may hold values from -6 to 6
Outputs:
- output: bfloat16 [16, 2048, 768], P('batch', 'blk')
- token_grad: bfloat16 [16, 2048, 768], P('batch', 'blk')
- proj_grad: float32 [768, 2304], P('batch', 'blk')
- out_grad: float32 [768, 768], P('batch', 'blk')
- up_grad: float32 [768, 3072], P('batch', 'blk')
- down_grad: float32 [3072, 768], P('batch', 'blk')
- gain_one_grad: float32 [768], P('blk')
- bias_one_grad: float32 [768], P('blk')
- gain_two_grad: float32 [768], P('blk')
- bias_two_grad: float32 [768], P('blk')
The draws below stay inside these ranges and needn't reach their ends.
Inputs may be any that keep to these rules, and one draw needn't show every extreme that they name: `segments`: in every row the numbers never fall and the last token has 4; the tokens numbered 2 begin within the first half of 512 tokens of the row and end within its last half of 512 tokens. `present`: each row is 1 on a leading run and 0 on the rest, which lies inside clip 4 and holds fewer than a quarter of 512 tokens.
All inputs are finite; a program needn't handle non-finite values.
Results may differ from the reference program's by a relative error of at most 0.02.
Values may be sent and summed in bfloat16 or wider, within the bound.
A program may use at most 192 MiB of HBM per device.

```python
import math
import jax
import jax.numpy as jnp
from jax import lax

D = 768
HEADS = 12
HEAD_DIM = 64
FF = 3072
SEQ_LEN = 2048
BLK_TOK = 512
ROWS = 16


def clip_bounds(key):
    keys = jax.random.split(key, 5)
    shape = (ROWS, 1)
    head_end = jax.random.randint(keys[0], shape, max(1, BLK_TOK // 4), BLK_TOK // 2 + 1)
    first_cut = jax.random.randint(keys[1], shape, 0, head_end + 1)
    tail_length = jax.random.randint(keys[2], shape, max(2, BLK_TOK // 4), BLK_TOK // 2 + 1)
    tail_start = SEQ_LEN - tail_length
    tail_cut = tail_start + jax.random.randint(keys[3], shape, 1, tail_length // 2 + 1)
    padding = jax.random.randint(keys[4], shape, 0, (SEQ_LEN - tail_cut) // 2 + 1)
    return (first_cut, head_end, tail_start, tail_cut, SEQ_LEN - padding)


def draw_segments(key, part):
    first_cut, head_end, tail_start, tail_cut, pad_start = clip_bounds(key)
    positions = jnp.arange(SEQ_LEN, dtype=jnp.int32)[None, :]
    total = (positions >= first_cut).astype(jnp.int32) + (positions >= head_end).astype(jnp.int32)
    total = total + (positions >= tail_start).astype(jnp.int32) + (positions >= tail_cut).astype(jnp.int32)
    return total


def draw_present(key, part):
    first_cut, head_end, tail_start, tail_cut, pad_start = clip_bounds(key)
    positions = jnp.arange(SEQ_LEN, dtype=jnp.int32)[None, :]
    return (positions < pad_start).astype(jnp.int32)


def levels(own_key, extent, cuts, low, high):
    level, own = 1.0, jax.random.fold_in(own_key, 6)
    for position, blocks in cuts:
        heights = jnp.exp(jax.random.uniform(jax.random.fold_in(own, position), (blocks,), jnp.float32, low / len(cuts), high / len(cuts)))
        level = level * jnp.repeat(heights, extent[position] // blocks).reshape([-1 if axis == position else 1 for axis in range(len(extent))])
    return level


def gaussian(stream_key, extent, scale, limit, cuts=(), kind=jnp.bfloat16):
    drawn = jax.random.normal(stream_key, extent, jnp.float32) * scale
    if len(cuts) > 0:
        drawn = levels(stream_key, extent, cuts, -0.22, 0.18) * drawn
    return jnp.clip(drawn, min=-limit, max=limit).astype(kind)


def setup_inputs(seed: int = 0) -> dict:
    key_of = jax.random.split(jax.random.key(seed), 13)
    tokens = gaussian(key_of[0], (ROWS, SEQ_LEN, D), 1.0, 6.0, ((0, 8), (1, 4)))
    proj_weight = gaussian(key_of[1], (D, 3 * D), (D // 2) ** -0.5, 0.3125, ((0, 8), (1, 4)))
    out_weight = gaussian(key_of[2], (D, D), (D // 16) ** -0.5, 0.875, ((0, 8), (1, 4)))
    up_weight = gaussian(key_of[3], (D, FF), D ** -0.5, 0.21875, ((0, 8), (1, 4)))
    down_weight = gaussian(key_of[4], (FF, D), FF ** -0.5, 0.109375, ((0, 8), (1, 4)))
    gain_one = jnp.clip(1.0 + 0.15 * jax.random.normal(key_of[5], (D,), jnp.float32), 0.25, 1.75).astype(jnp.bfloat16)
    bias_one = gaussian(key_of[6], (D,), 0.5, 3.0, ((0, 4),))
    gain_two = jnp.clip(1.0 + 0.15 * jax.random.normal(key_of[7], (D,), jnp.float32), 0.25, 1.75).astype(jnp.bfloat16)
    bias_two = gaussian(key_of[8], (D,), 0.5, 3.0, ((0, 4),))
    segments = draw_segments(jax.random.fold_in(key_of[12], 71), 0)
    present = draw_present(jax.random.fold_in(key_of[12], 71), 0)
    cotangent = gaussian(key_of[11], (ROWS, SEQ_LEN, D), 1.0, 6.0, ((0, 8), (1, 4)))
    return dict(tokens=tokens, proj_weight=proj_weight, out_weight=out_weight, up_weight=up_weight, down_weight=down_weight, gain_one=gain_one, bias_one=bias_one, gain_two=gain_two, bias_two=bias_two, segments=segments, present=present, cotangent=cotangent)


epsilon = 1e-05
masked_score = -1e+30
highest = lax.Precision.HIGHEST

@jax.custom_vjp
def low(v):
    return lax.optimization_barrier(v.astype(jnp.bfloat16)).astype(jnp.float32)

@jax.custom_vjp
def low_back(v):
    return v

def low_keep(v):
    return (low(v), None)

def low_pass(kept, grad):
    return (grad,)

def back_keep(v):
    return (v, None)

def back_low(kept, grad):
    return (low(grad),)
low.defvjp(low_keep, low_pass)
low_back.defvjp(back_keep, back_low)

def layer_norm(values, gain, shift):
    average = lax.optimization_barrier(jnp.mean(values, axis=-1, keepdims=True))
    centered = values - average
    variance = lax.optimization_barrier(jnp.mean(centered * centered, axis=-1, keepdims=True))
    return centered * lax.rsqrt(variance + epsilon) * gain + shift

def row_attention(inputs):
    queries, keys, values, tags = inputs
    block = math.gcd(SEQ_LEN, 512)
    positions = jnp.arange(SEQ_LEN, dtype=jnp.int32)
    scale = HEAD_DIM ** (-0.5)

    def one_block(index):
        start = (index * block).astype(jnp.int32)
        query_block = lax.dynamic_slice_in_dim(queries, start, block, 0)
        query_tags = lax.dynamic_slice_in_dim(tags, start, block, 0)
        query_pos = start + jnp.arange(block, dtype=jnp.int32)
        scores = low_back(jnp.einsum('qhd,khd->hqk', query_block, keys, precision=highest) * scale)
        visible = jnp.logical_and(positions[None, :] <= query_pos[:, None], tags[None, :] == query_tags[:, None])
        scores = jnp.where(visible[None], scores, masked_score)
        largest = lax.optimization_barrier(jnp.max(scores, axis=-1, keepdims=True))
        raised = jnp.exp(scores - largest)
        weights = low(raised / lax.optimization_barrier(jnp.sum(raised, axis=-1, keepdims=True)))
        return jnp.einsum('hqk,khd->qhd', weights, values, precision=highest)
    pieces = lax.map(jax.checkpoint(one_block), jnp.arange(SEQ_LEN // block, dtype=jnp.int32))
    return pieces.reshape(SEQ_LEN, HEADS, HEAD_DIM)

def forward(tokens, proj_weight, out_weight, up_weight, down_weight, gain_one, bias_one, gain_two, bias_two, tags):
    width = tokens.shape[-1]
    normed = low(layer_norm(tokens, gain_one, bias_one))
    projected = low_back(low(jnp.dot(normed, proj_weight, precision=highest)))
    split = projected.reshape(ROWS, SEQ_LEN, 3, HEADS, HEAD_DIM)
    attended = lax.map(row_attention, (split[:, :, 0], split[:, :, 1], split[:, :, 2], tags))
    attended = low_back(low(attended.reshape(ROWS, SEQ_LEN, width)))
    middle = tokens + low_back(jnp.dot(attended, out_weight, precision=highest))
    normed_two = low(layer_norm(middle, gain_two, bias_two))
    hidden = low_back(jnp.dot(normed_two, up_weight, precision=highest))
    activated = low(jax.nn.gelu(hidden, approximate=True))
    return middle + jnp.dot(activated, down_weight, precision=highest)

def reference(tokens, proj_weight, out_weight, up_weight, down_weight, gain_one, bias_one, gain_two, bias_two, segments, present, cotangent):
    positions = jnp.arange(SEQ_LEN, dtype=jnp.int32)
    tags = jnp.where(present == 1, segments, -1 - positions[None, :]).astype(jnp.int32)
    params = (tokens, proj_weight, out_weight, up_weight, down_weight, gain_one, bias_one, gain_two, bias_two)
    params = tuple((item.astype(jnp.float32) for item in params))

    def layer(*values):
        return forward(*values, tags)
    result, pullback = jax.vjp(layer, *params)
    grads = pullback(cotangent.astype(jnp.float32))
    return (result.astype(jnp.bfloat16), grads[0].astype(jnp.bfloat16), grads[1], grads[2], grads[3], grads[4], grads[5], grads[6], grads[7], grads[8])
```

```python
import functools

import jax
import jax.numpy as jnp
from jax import lax
from jax.experimental import pallas as pl
from jax.experimental.pallas import tpu as pltpu
from jax.sharding import PartitionSpec as P

HEADS = 12
HEAD_DIM = 64
CORES = 2
LANE_X = 2
MESH = pl.DeviceIdType.MESH
LOG2E = 1.4426950408889634
epsilon = 1e-05
masked = -1e30
bf16 = jnp.bfloat16
f32 = jnp.float32


def dot(left, right, left_dim, right_dim):
    return lax.dot_general(
        left, right, (((left_dim,), (right_dim,)), ((), ())), preferred_element_type=f32
    )


class Place:
    def __init__(self, sizes):
        self.batch, self.blk = sizes
        self.Z, self.X = self.batch // LANE_X, LANE_X
        self.Y, self.C = self.blk // CORES, CORES

    def here(self):
        b, d = lax.axis_index("batch"), lax.axis_index("blk")
        return b // self.X, b % self.X, d // self.C, d % self.C

    def device(self, z, x, p, c):
        return (z * self.X + x, p * self.C + c)


def split_rows(count):
    return 16 * ((count // 2) // 16)


class Sends:
    def __init__(self, send_sem, recv_sem):
        self.send_sem, self.recv_sem, self.count = send_sem, recv_sem, 0

    def start(self, src, dst, device):
        copy = pltpu.make_async_remote_copy(
            src_ref=src,
            dst_ref=dst,
            send_sem=self.send_sem.at[self.count],
            recv_sem=self.recv_sem.at[self.count],
            device_id=device,
            device_id_type=MESH,
        )
        self.count += 1
        copy.start()
        return copy


def greet(place, partners):
    barrier = pltpu.get_barrier_semaphore()
    for partner in partners:
        pl.semaphore_signal(barrier, inc=1, device_id=partner, device_id_type=MESH)
    pl.semaphore_wait(barrier, len(partners))


def partners_of(place):
    z, x, p, c = place.here()
    found = [place.device((z + k) % place.Z, x, p, c) for k in range(1, place.Z)]
    found += [place.device(z, 1 - x, p, c)]
    found += [place.device(z, x, (p + k) % place.Y, c) for k in range(1, place.Y)]
    found += [place.device(z, x, p, 1 - c)]
    return found


def gather_kernel(place, matrices, *refs):
    n = len(matrices)
    mats, (tok, cot, tag, vec) = refs[:n], refs[n : n + 4]
    outs, (tok_g, cot_g, tag_g, vec_g) = refs[n + 4 : 2 * n + 4], refs[2 * n + 4 : 2 * n + 8]
    send_sem, recv_sem, local_sem = refs[2 * n + 8 :]
    z, x, p, c = place.here()
    Z, X, Y = place.Z, place.X, place.Y
    greet(place, partners_of(place))
    sends = Sends(send_sem, recv_sem)
    started = []

    def go(src, dst, device):
        copy = sends.start(src, dst, device)
        started.append(copy)
        return copy

    local = []

    def keep(src, dst):
        copy = pltpu.make_async_copy(src, dst, local_sem.at[len(local)])
        copy.start()
        local.append(copy)
        return copy

    row_copies, cot_copies = [], []
    for k in range(1, Y):
        to = (p + k) % Y
        device = place.device(z, x, to, c)
        row_copies.append(go(tok.at[to], tok_g.at[p, c], device))
        row_copies.append(go(tag.at[to], tag_g.at[p, c], device))
        row_copies.append(go(vec, vec_g.at[p, c], device))
    own = [
        keep(tok.at[p], tok_g.at[p, c]),
        keep(tag.at[p], tag_g.at[p, c]),
        keep(vec, vec_g.at[p, c]),
        keep(cot.at[p], cot_g.at[p]),
    ]
    first = []
    for m in range(n):
        place_here = outs[m].at[p, c, z, x]
        keep(mats[m], place_here)
        first.append(
            [
                go(mats[m], place_here, place.device((z + k) % Z, x, p, c))
                for k in range(1, Z)
            ]
        )
    for k in range(1, Y):
        to = (p + k) % Y
        cot_copies.append(go(cot.at[to], cot_g.at[p], place.device(z, x, to, c)))
    for copy in local:
        copy.wait()
    second = []
    for m in range(n):
        for copy in first[m]:
            copy.wait_recv()
        h = split_rows(mats[m].shape[0])
        r = mats[m].shape[0]
        low = outs[m].at[p, c, :, x, 0:h]
        high = outs[m].at[p, c, :, x, h:r]
        second.append(
            (
                [go(low, low, place.device(z, 1 - x, p, c))],
                [go(high, high, place.device(z, x, (p + k) % Y, c)) for k in range(1, Y)],
            )
        )
    third = []
    for m in range(n):
        h = split_rows(mats[m].shape[0])
        r = mats[m].shape[0]
        for copy in second[m][0]:
            copy.wait_recv()
        low = outs[m].at[p, c, :, :, 0:h]
        a = [go(low, low, place.device(z, x, (p + k) % Y, c)) for k in range(1, Y)]
        for copy in second[m][1]:
            copy.wait_recv()
        high = outs[m].at[:, c, :, x, h:r]
        b = [go(high, high, place.device(z, 1 - x, p, c))]
        third.append(a + b)
    for copy in row_copies:
        copy.wait_recv()
    sibling = place.device(z, x, p, 1 - c)
    last = []
    for ref in (tok_g, tag_g, vec_g):
        last.append(go(ref.at[:, c], ref.at[:, c], sibling))
    for m in range(n):
        for copy in third[m]:
            copy.wait_recv()
        last.append(go(outs[m].at[:, c], outs[m].at[:, c], sibling))
    for copy in last + cot_copies:
        copy.wait_recv()
    for copy in started:
        copy.wait_send()


def gather_all(place, mats, tok, cot, tag, vec):
    n = len(mats)
    Z, X, Y, C = place.Z, place.X, place.Y, place.C
    out = [jax.ShapeDtypeStruct((Y, C, Z, X) + m.shape, m.dtype) for m in mats]
    out += [
        jax.ShapeDtypeStruct((Y, C) + tok.shape[1:], tok.dtype),
        jax.ShapeDtypeStruct((Y,) + cot.shape[1:], cot.dtype),
        jax.ShapeDtypeStruct((Y, C) + tag.shape[1:], tag.dtype),
        jax.ShapeDtypeStruct((Y, C) + vec.shape, vec.dtype),
    ]
    copies = 4 * (Y - 1) + n * ((Z - 1) + 1 + (Y - 1) + (Y - 1) + 1) + 3 + n
    anywhere = pl.BlockSpec(memory_space=pl.ANY)
    return pl.pallas_call(
        functools.partial(gather_kernel, place, tuple(m.shape for m in mats)),
        out_shape=out,
        in_specs=[anywhere] * (n + 4),
        out_specs=[anywhere] * (n + 4),
        scratch_shapes=[
            pltpu.SemaphoreType.DMA((copies,)),
            pltpu.SemaphoreType.DMA((copies,)),
            pltpu.SemaphoreType.DMA((n + 4,)),
        ],
        compiler_params=pltpu.CompilerParams(collective_id=0, has_side_effects=True),
        name="gather_all",
    )(*mats, tok, cot, tag, vec)


def swap_kernel(place, src, dst, send_sem, recv_sem):
    z, x, p, c = place.here()
    sibling = place.device(z, x, p, 1 - c)
    greet(place, [sibling])
    copy = pltpu.make_async_remote_copy(
        src_ref=src.at[1 - c],
        dst_ref=dst,
        send_sem=send_sem,
        recv_sem=recv_sem,
        device_id=sibling,
        device_id_type=MESH,
    )
    copy.start()
    copy.wait()


def swap(place, value, number):
    anywhere = pl.BlockSpec(memory_space=pl.ANY)
    return pl.pallas_call(
        functools.partial(swap_kernel, place),
        out_shape=jax.ShapeDtypeStruct(value.shape[1:], value.dtype),
        in_specs=[anywhere],
        out_specs=anywhere,
        scratch_shapes=[pltpu.SemaphoreType.DMA, pltpu.SemaphoreType.DMA],
        compiler_params=pltpu.CompilerParams(collective_id=number, has_side_effects=True),
        name=f"swap_{number}",
    )(value)


def head_masked(value, h, axis):
    index = lax.broadcasted_iota(jnp.int32, value.shape, axis)
    return jnp.where((index // HEAD_DIM) == h, value, jnp.zeros_like(value))


def attention_forward_kernel(BQ, start_ref, q_ref, k_ref, v_ref, o_ref, oT_ref, lt_ref, qT, vT):
    L = q_ref.shape[0]
    nq = L // BQ
    scale = HEAD_DIM ** (-0.5) * LOG2E
    qT[...] = q_ref[...].T
    vT[...] = v_ref[...].T
    for qi in range(nq):
        qs = slice(qi * BQ, (qi + 1) * BQ)
        begin = start_ref[:, qs]
        d0 = qi * BQ
        if qi == nq - 1:
            cuts = [(0, d0, 1)] if d0 else []
        elif d0 > 256:
            cuts = [(0, 256, 1), (256, d0, 0)]
        else:
            cuts = [(0, d0, 1)] if d0 else []
        cuts.append((d0, d0 + BQ, 2))
        for h in range(2):
            query = head_masked(qT[:, qs], h, 0)
            parts = []
            for a, b, mode in cuts:
                s = dot(k_ref[a:b, :], query, 1, 0) * scale
                if mode:
                    key_pos = lax.broadcasted_iota(jnp.int32, (b - a, BQ), 0) + a
                    visible = key_pos >= begin
                    if mode == 2:
                        query_pos = lax.broadcasted_iota(jnp.int32, (b - a, BQ), 1) + d0
                        visible = jnp.logical_and(visible, key_pos <= query_pos)
                    s = jnp.where(visible, s, masked)
                parts.append(s)
            top = functools.reduce(
                jnp.maximum, [jnp.max(s, axis=0, keepdims=True) for s in parts]
            )
            total, accum = 0.0, 0.0
            for (a, b, mode), s in zip(cuts, parts):
                e = jnp.exp2(s - top)
                total = total + jnp.sum(e, axis=0, keepdims=True)
                accum = accum + dot(
                    vT[h * HEAD_DIM : (h + 1) * HEAD_DIM, a:b], e.astype(bf16), 1, 0
                )
            oT_ref[h * HEAD_DIM : (h + 1) * HEAD_DIM, qs] = accum / total
            lt_ref[0, h : h + 1, qs] = top + jnp.log2(total)
        o_ref[qs, :] = oT_ref[:, qs].astype(bf16).T


def attention_forward(projected, begin):
    L = projected.shape[0]
    pairs = projected.shape[1] // 3 // 128
    return pl.pallas_call(
        functools.partial(attention_forward_kernel, 512),
        grid=(pairs,),
        in_specs=[
            pl.BlockSpec((1, L), lambda i: (0, 0)),
            pl.BlockSpec((L, 128), lambda i: (0, i)),
            pl.BlockSpec((L, 128), lambda i: (0, pairs + i)),
            pl.BlockSpec((L, 128), lambda i: (0, 2 * pairs + i)),
        ],
        out_specs=[
            pl.BlockSpec((L, 128), lambda i: (0, i)),
            pl.BlockSpec((128, L), lambda i: (i, 0)),
            pl.BlockSpec((1, 2, L), lambda i: (i, 0, 0)),
        ],
        out_shape=[
            jax.ShapeDtypeStruct((L, pairs * 128), bf16),
            jax.ShapeDtypeStruct((pairs * 128, L), f32),
            jax.ShapeDtypeStruct((pairs, 2, L), f32),
        ],
        scratch_shapes=[pltpu.VMEM((128, L), bf16), pltpu.VMEM((128, L), bf16)],
        compiler_params=pltpu.CompilerParams(vmem_limit_bytes=50 << 20),
        name="attention_forward",
    )(begin, projected, projected, projected)


def attention_backward_kernel(
    BQ, start_ref, q_ref, k_ref, v_ref, do_ref, oT_ref, lt_ref,
    dq_ref, dk_ref, dv_ref, qT, kT, doT, dk, dv, dqT,
):
    L = q_ref.shape[0]
    nq = L // BQ
    scale = HEAD_DIM ** (-0.5) * LOG2E
    qT[...] = q_ref[...].T
    kT[...] = k_ref[...].T
    doT[...] = do_ref[...].T
    dk[...] = jnp.zeros_like(dk)
    dv[...] = jnp.zeros_like(dv)

    def tile(h, qi, kj, query, grad, deltas, dq, mode):
        qs = pl.ds(pl.multiple_of(qi * BQ, BQ), BQ)
        ks = pl.ds(pl.multiple_of(kj * BQ, BQ), BQ)
        s = dot(k_ref[ks, :], query, 1, 0) * scale
        prob = jnp.exp2(s - lt_ref[0, h : h + 1, qs])
        if mode:
            key_pos = lax.broadcasted_iota(jnp.int32, (BQ, BQ), 0)
            visible = key_pos >= (start_ref[:, qs] - kj * BQ)
            if mode == 2:
                query_pos = lax.broadcasted_iota(jnp.int32, (BQ, BQ), 1)
                visible = jnp.logical_and(visible, key_pos <= query_pos)
            prob = jnp.where(visible, prob, 0.0)
        dp = dot(v_ref[ks, :], grad, 1, 0)
        ds = (prob * (dp - deltas)).astype(bf16)
        dv[ks, :] += dot(prob.astype(bf16), head_masked(do_ref[qs, :], h, 1), 1, 0)
        dk[ks, :] += dot(ds, head_masked(q_ref[qs, :], h, 1), 1, 0)
        return dq + dot(kT[h * HEAD_DIM : (h + 1) * HEAD_DIM, ks], ds, 1, 0)

    def one_query(i, nothing):
        qi = nq - 1 - i
        qs = pl.ds(pl.multiple_of(qi * BQ, BQ), BQ)
        for h in range(2):
            rows = slice(h * HEAD_DIM, (h + 1) * HEAD_DIM)
            deltas = jnp.sum(
                doT[rows, qs].astype(f32) * oT_ref[rows, qs], axis=0, keepdims=True
            )
            query, grad = head_masked(qT[:, qs], h, 0), head_masked(doT[:, qs], h, 0)
            step = functools.partial(tile, h, qi)

            def run(kj, dq, mode):
                return tile(h, qi, kj, query, grad, deltas, dq, mode)

            dq = run(qi, jnp.zeros((HEAD_DIM, BQ), f32), 2)

            def last(dq):
                return lax.fori_loop(0, qi, lambda kj, d: run(kj, d, 1), dq)

            def others(dq):
                dq = lax.cond(qi > 0, lambda d: run(0, d, 1), lambda d: d, dq)
                return lax.fori_loop(1, qi, lambda kj, d: run(kj, d, 0), dq)

            dq = lax.cond(qi == nq - 1, last, others, dq)
            dqT[rows, qs] = dq
        return nothing

    lax.fori_loop(0, nq, one_query, 0)
    scale_back = HEAD_DIM ** (-0.5)
    dq_ref[...] = (dqT[...] * scale_back).astype(bf16).T
    dk_ref[...] = (dk[...] * scale_back).astype(bf16)
    dv_ref[...] = dv[...].astype(bf16)


def attention_backward(projected, grads, oT, lt, begin):
    L = projected.shape[0]
    pairs = projected.shape[1] // 3 // 128
    wide = pl.BlockSpec((L, 128), lambda i: (0, i))
    return pl.pallas_call(
        functools.partial(attention_backward_kernel, 512),
        grid=(pairs,),
        in_specs=[
            pl.BlockSpec((1, L), lambda i: (0, 0)),
            wide,
            pl.BlockSpec((L, 128), lambda i: (0, pairs + i)),
            pl.BlockSpec((L, 128), lambda i: (0, 2 * pairs + i)),
            wide,
            pl.BlockSpec((128, L), lambda i: (i, 0)),
            pl.BlockSpec((1, 2, L), lambda i: (i, 0, 0)),
        ],
        out_specs=[wide] * 3,
        out_shape=[jax.ShapeDtypeStruct((L, pairs * 128), bf16)] * 3,
        scratch_shapes=[pltpu.VMEM((128, L), bf16)] * 3
        + [pltpu.VMEM((L, 128), f32)] * 2
        + [pltpu.VMEM((128, L), f32)],
        compiler_params=pltpu.CompilerParams(vmem_limit_bytes=50 << 20),
        name="attention_backward",
    )(begin, projected, projected, projected, grads, oT, lt)


def reduce_kernel(place, n, *refs):
    parts, (vec, out_in, tg_in) = refs[:n], refs[n : n + 3]
    sums, (vec_out, out_out, tg_out) = refs[n + 3 : 2 * n + 3], refs[2 * n + 3 : 2 * n + 6]
    scratch = refs[2 * n + 6 :]
    per = 7
    stage = [scratch[per * m : per * (m + 1)] for m in range(n)]
    vec_core, vec_y, vec_x, vec_z, vec_acc = scratch[per * n : per * n + 5]
    send_sem, recv_sem, local_sem = scratch[per * n + 5 :]
    z, x, p, c = place.here()
    Z, X, Y = place.Z, place.X, place.Y
    greet(place, partners_of(place))
    sends = Sends(send_sem, recv_sem)
    started = []
    sibling = place.device(z, x, p, 1 - c)
    beside = place.device(z, 1 - x, p, c)

    def go(src, dst, device):
        copy = sends.start(src, dst, device)
        started.append(copy)
        return copy

    def add(target, sources, count):
        def one(i, nothing):
            total = sources[0](i).astype(f32)
            for source in sources[1:]:
                total = total + source(i).astype(f32)
            target(i, total)
            return nothing

        lax.fori_loop(0, count, one, 0)

    core = [go(parts[m].at[:, 1 - c], stage[m][0], sibling) for m in range(n)]
    vec_copy = go(vec.at[:, 1 - c], vec_core, sibling)
    home = []
    for k in range(1, Y):
        to = (p + k) % Y
        device = place.device(z, x, to, c)
        home.append(go(tg_in.at[to], tg_out.at[p], device))
        home.append(go(out_in.at[to], out_out.at[p], device))
    kept = [
        pltpu.make_async_copy(tg_in.at[p], tg_out.at[p], local_sem.at[0]),
        pltpu.make_async_copy(out_in.at[p], out_out.at[p], local_sem.at[1]),
    ]
    for copy in kept:
        copy.start()
    second = []
    for m in range(n):
        recv0, acc, xa, yb, ya, xb, zz = stage[m]
        rows = acc.shape[3]
        h = split_rows(rows)
        core[m].wait_recv()

        def read_part(i):
            return parts[m][i // (Z * X), c, (i // X) % Z, i % X]

        def read_recv(i):
            return recv0[i // (Z * X), (i // X) % Z, i % X]

        def write_acc(i, value):
            acc[i // (Z * X), (i // X) % Z, i % X] = value.astype(bf16)

        add(write_acc, [read_part, read_recv], Y * Z * X)
        second.append(
            (
                go(acc.at[:, :, 1 - x, 0:h], xa, beside),
                [
                    go(
                        acc.at[(p + k) % Y, :, :, h:rows],
                        yb.at[k - 1],
                        place.device(z, x, (p + k) % Y, c),
                    )
                    for k in range(1, Y)
                ],
            )
        )
    vec_copy.wait_recv()
    vec_acc[...] = vec[:, c] + vec_core[...]
    vec_copies = [
        go(vec_acc.at[(p + k) % Y], vec_y.at[k - 1], place.device(z, x, (p + k) % Y, c))
        for k in range(1, Y)
    ]
    third = []
    for m in range(n):
        recv0, acc, xa, yb, ya, xb, zz = stage[m]
        rows = acc.shape[3]
        h = split_rows(rows)
        second[m][0].wait_recv()

        def write_a(i, value):
            acc[i // Z, i % Z, x, 0:h] = value.astype(bf16)

        add(
            write_a,
            [lambda i: acc[i // Z, i % Z, x, 0:h], lambda i: xa[i // Z, i % Z]],
            Y * Z,
        )
        a = [
            go(acc.at[(p + k) % Y, :, x, 0:h], ya.at[k - 1], place.device(z, x, (p + k) % Y, c))
            for k in range(1, Y)
        ]
        for copy in second[m][1]:
            copy.wait_recv()

        def write_b(i, value):
            acc[p, i // X, i % X, h:rows] = value.astype(bf16)

        add(
            write_b,
            [lambda i: acc[p, i // X, i % X, h:rows]]
            + [lambda i, k=k: yb[k, i // X, i % X] for k in range(Y - 1)],
            Z * X,
        )
        b = go(acc.at[p, :, 1 - x, h:rows], xb, beside)
        third.append((a, b))
    for copy in vec_copies:
        copy.wait_recv()
    vec_acc[p] = vec_acc[p] + sum(vec_y[k] for k in range(Y - 1))
    vec_next = go(vec_acc.at[p], vec_x, beside)
    fourth = []
    for m in range(n):
        recv0, acc, xa, yb, ya, xb, zz = stage[m]
        rows = acc.shape[3]
        h = split_rows(rows)
        for copy in third[m][0]:
            copy.wait_recv()

        def write_a2(i, value):
            acc[p, i, x, 0:h] = value.astype(bf16)

        add(
            write_a2,
            [lambda i: acc[p, i, x, 0:h]] + [lambda i, k=k: ya[k, i] for k in range(Y - 1)],
            Z,
        )
        third[m][1].wait_recv()

        def write_b2(i, value):
            acc[p, i, x, h:rows] = value.astype(bf16)

        add(write_b2, [lambda i: acc[p, i, x, h:rows], lambda i: xb[i]], Z)
        fourth.append(
            [
                go(acc.at[p, (z + k) % Z, x], zz.at[k - 1], place.device((z + k) % Z, x, p, c))
                for k in range(1, Z)
            ]
        )
    vec_next.wait_recv()
    vec_next.wait_send()
    vec_acc[p] = vec_acc[p] + vec_x[...]
    vec_last = [
        go(vec_acc.at[p], vec_z.at[k - 1], place.device((z + k) % Z, x, p, c))
        for k in range(1, Z)
    ]
    for m in range(n):
        recv0, acc, xa, yb, ya, xb, zz = stage[m]
        for copy in fourth[m]:
            copy.wait_recv()
        total = acc[p, z, x].astype(f32)
        for k in range(Z - 1):
            total = total + zz[k].astype(f32)
        sums[m][...] = total
    for copy in vec_last:
        copy.wait_recv()
    total = vec_acc[p]
    for k in range(Z - 1):
        total = total + vec_z[k]
    vec_out[...] = total
    for copy in home:
        copy.wait_recv()
    for copy in kept:
        copy.wait()
    for copy in started:
        if copy is not vec_next:
            copy.wait_send()


def reduce_all(place, parts, vec, out_in, tg_in):
    n = len(parts)
    Z, X, Y, C = place.Z, place.X, place.Y, place.C
    inside = pl.BlockSpec(memory_space=pltpu.VMEM)
    anywhere = pl.BlockSpec(memory_space=pl.ANY)
    scratch = []
    for part in parts:
        r, w = part.shape[4:]
        h = split_rows(r)
        scratch += [
            pltpu.VMEM((Y, Z, X, r, w), bf16),
            pltpu.VMEM((Y, Z, X, r, w), bf16),
            pltpu.VMEM((Y, Z, h, w), bf16),
            pltpu.VMEM((Y - 1, Z, X, r - h, w), bf16),
            pltpu.VMEM((Y - 1, Z, h, w), bf16),
            pltpu.VMEM((Z, r - h, w), bf16),
            pltpu.VMEM((Z - 1, r, w), bf16),
        ]
    vs = vec.shape[2:]
    scratch += [
        pltpu.VMEM((Y,) + vs, f32),
        pltpu.VMEM((Y - 1,) + vs, f32),
        pltpu.VMEM(vs, f32),
        pltpu.VMEM((Z - 1,) + vs, f32),
        pltpu.VMEM((Y,) + vs, f32),
    ]
    copies = n * (1 + 1 + (Y - 1) + (Y - 1) + 1 + (Z - 1)) + 1 + (Y - 1) + 1 + (Z - 1) + 2 * (Y - 1)
    scratch += [
        pltpu.SemaphoreType.DMA((copies,)),
        pltpu.SemaphoreType.DMA((copies,)),
        pltpu.SemaphoreType.DMA((2,)),
    ]
    out_shape = [jax.ShapeDtypeStruct(part.shape[4:], f32) for part in parts]
    out_shape += [
        jax.ShapeDtypeStruct(vs, f32),
        jax.ShapeDtypeStruct(out_in.shape, out_in.dtype),
        jax.ShapeDtypeStruct(tg_in.shape, tg_in.dtype),
    ]
    return pl.pallas_call(
        functools.partial(reduce_kernel, place, n),
        out_shape=out_shape,
        in_specs=[inside] * (n + 1) + [anywhere] * 2,
        out_specs=[inside] * (n + 1) + [anywhere] * 2,
        scratch_shapes=scratch,
        compiler_params=pltpu.CompilerParams(
            collective_id=1, has_side_effects=True, vmem_limit_bytes=60 << 20
        ),
        name="reduce_all",
    )(*parts, vec, out_in, tg_in)


def normed(values):
    average = jnp.mean(values, axis=-1, keepdims=True)
    centered = values - average
    variance = jnp.mean(centered * centered, axis=-1, keepdims=True)
    factor = lax.rsqrt(variance + epsilon)
    return centered * factor, factor


def norm_back(grad, gain, unit, factor):
    e = grad * gain
    return factor * (
        e - jnp.mean(e, axis=-1, keepdims=True) - unit * jnp.mean(e * unit, axis=-1, keepdims=True)
    )


def gelu_tanh(values):
    return jax.nn.gelu(values, approximate=True)


def joined(gathered, axis):
    Y, C, Z, X, r, w = gathered.shape
    if axis == 0:
        return gathered.reshape(Y * C, Z * X * r, w).transpose(1, 0, 2).reshape(Z * X * r, -1)
    return gathered.reshape(Y * C, Z * X, r, w).transpose(0, 2, 1, 3).reshape(Y * C * r, -1)


def parted(whole, place, axis):
    Y, C, Z, X = place.Y, place.C, place.Z, place.X
    rows, columns = whole.shape
    if axis == 0:
        value = whole.reshape(Z * X, rows // (Z * X), Y * C, columns // (Y * C))
        value = value.transpose(2, 0, 1, 3)
    else:
        value = whole.reshape(Y * C, rows // (Y * C), Z * X, columns // (Z * X))
        value = value.transpose(0, 2, 1, 3)
    return value.reshape((Y, C, Z, X) + value.shape[2:])


def chosen(pair, c):
    return jnp.where(c == 0, pair[0], pair[1])


def body(
    place,
    tokens,
    proj_weight,
    out_weight,
    up_weight,
    down_weight,
    gain_one,
    bias_one,
    gain_two,
    bias_two,
    segments,
    present,
    cotangent,
):
    rows, block, width = tokens.shape
    Y, C = place.Y, place.C
    length = place.blk * block
    index = lax.axis_index("blk")
    c = index % C
    half = width // C
    query_pos = index * block + jnp.arange(block, dtype=jnp.int32)
    local_tags = jnp.where(present == 1, segments, -1 - query_pos[None, :])
    tag_in = jnp.broadcast_to(local_tags[:, None, :], (rows, 8, block))
    vec_in = jnp.stack([gain_one, bias_one, gain_two, bias_two])
    vec_in = jnp.pad(vec_in, ((0, 12), (0, 0)))
    proj_g, out_g, up_g, down_g, tok_g, cot_g, tag_g, vec_g = gather_all(
        place,
        [proj_weight, out_weight, up_weight, down_weight.T],
        tokens,
        cotangent,
        tag_in,
        vec_in,
    )
    proj_full, out_full, up_full = joined(proj_g, 0), joined(out_g, 0), joined(up_g, 0)
    down_full_t = joined(down_g, 1)
    gain_a, bias_a, gain_b, bias_b = (
        vec_g.reshape(place.blk, 16, -1)[:, :4].transpose(1, 0, 2).reshape(4, width).astype(f32)
    )
    proj_own = lax.dynamic_index_in_dim(
        proj_full.reshape(width, 3, C, half), c, 2, keepdims=False
    ).reshape(width, 3 * half)
    row_tags = tag_g[:, :, 0].reshape(length)
    row_pos = jnp.arange(length, dtype=jnp.int32)
    begin = sum(
        jnp.where(row_tags > s, jnp.sum((row_tags == s).astype(jnp.int32)), 0) for s in range(4)
    )
    begin = jnp.where(row_tags < 0, row_pos, begin)[None]
    inputs = tok_g.reshape(length, width).astype(f32)
    unit, factor = normed(inputs)
    normed_low = (unit * gain_a + bias_a).astype(bf16)
    projected = dot(normed_low, proj_own, 1, 0).astype(bf16)
    attended, attended_t, log_total = attention_forward(projected, begin)
    by_core = attended.reshape(Y, C, block, half).transpose(1, 0, 2, 3)
    other = swap(place, by_core, 2).reshape(Y * block, half)
    mine = lax.dynamic_index_in_dim(by_core, c, 0, keepdims=False).reshape(Y * block, half)
    attended_low = jnp.concatenate(
        [chosen((mine, other), c), chosen((other, mine), c)], axis=1
    )
    inputs_mine = (
        lax.dynamic_index_in_dim(tok_g, c, 1, keepdims=False)
        .reshape(Y * block, width)
        .astype(f32)
    )
    middle = inputs_mine + dot(attended_low, out_full, 1, 0)
    unit_two, factor_two = normed(middle)
    normed_two_low = (unit_two * gain_b + bias_b).astype(bf16)
    hidden = dot(normed_two_low, up_full, 1, 0)
    activated_low = gelu_tanh(hidden).astype(bf16)
    output = (middle + dot(activated_low, down_full_t, 1, 1)).astype(bf16)
    grad_out = cot_g.reshape(Y * block, width)
    down_grad_t = dot(grad_out, activated_low, 0, 0).astype(bf16)
    grad_act = dot(grad_out, down_full_t, 1, 0)
    unused_value, gelu_back = jax.vjp(gelu_tanh, hidden)
    grad_hidden = gelu_back(grad_act)[0].astype(bf16)
    up_grad = dot(normed_two_low, grad_hidden, 0, 0).astype(bf16)
    grad_normed_two = dot(grad_hidden, up_full, 1, 1)
    gain_two_grad = jnp.sum(grad_normed_two * unit_two, axis=0)
    bias_two_grad = jnp.sum(grad_normed_two, axis=0)
    grad_middle = grad_out.astype(f32) + norm_back(grad_normed_two, gain_b, unit_two, factor_two)
    grad_middle_low = grad_middle.astype(bf16)
    out_grad = dot(attended_low, grad_middle_low, 0, 0).astype(bf16)
    grad_attended = dot(grad_middle_low, out_full, 1, 1).astype(bf16)
    grad_by_core = grad_attended.reshape(Y, block, C, half).transpose(2, 0, 1, 3)
    grad_other = swap(place, grad_by_core, 3)
    grad_mine = lax.dynamic_index_in_dim(grad_by_core, c, 0, keepdims=False)
    grad_heads = jnp.stack(
        [chosen((grad_mine, grad_other), c), chosen((grad_other, grad_mine), c)], axis=1
    ).reshape(length, half)
    dq, dk, dv = attention_backward(projected, grad_heads, attended_t, log_total, begin)
    projected_grad = jnp.concatenate([dq, dk, dv], axis=1)
    proj_grad_own = dot(normed_low, projected_grad, 0, 0).astype(bf16)
    spread = jnp.zeros((width, 3, C, half), bf16)
    proj_grad = lax.dynamic_update_slice(
        spread, proj_grad_own.reshape(width, 3, 1, half), (0, 0, c, 0)
    ).reshape(width, 3 * width)
    g_part = dot(projected_grad, proj_own, 1, 1)
    g_by_core = g_part.astype(bf16).reshape(Y, C, block, width).transpose(1, 0, 2, 3)
    g_other = swap(place, g_by_core, 4).reshape(Y * block, width)
    g_mine = lax.dynamic_index_in_dim(
        g_part.reshape(Y, C, block, width), c, 1, keepdims=False
    ).reshape(Y * block, width)
    grad_normed = g_mine + g_other.astype(f32)
    unit_mine, factor_mine = normed(inputs_mine)
    gain_one_grad = jnp.sum(grad_normed * unit_mine, axis=0)
    bias_one_grad = jnp.sum(grad_normed, axis=0)
    token_grad = (
        grad_middle + norm_back(grad_normed, gain_a, unit_mine, factor_mine)
    ).astype(bf16)
    vec = jnp.stack([gain_one_grad, bias_one_grad, gain_two_grad, bias_two_grad])
    vec = jnp.pad(vec, ((0, 4), (0, 0)))
    vec = vec.reshape(8, Y, C, width // place.blk).transpose(1, 2, 0, 3)
    proj_sum, out_sum, up_sum, down_sum, vec_sum, output, token_grad = reduce_all(
        place,
        [
            parted(proj_grad, place, 0),
            parted(out_grad, place, 0),
            parted(up_grad, place, 0),
            parted(down_grad_t, place, 1),
        ],
        vec,
        output.reshape(Y, block, width),
        token_grad.reshape(Y, block, width),
    )
    return (
        output,
        token_grad,
        proj_sum,
        out_sum,
        up_sum,
        down_sum.T,
        vec_sum[0],
        vec_sum[1],
        vec_sum[2],
        vec_sum[3],
    )


def solution(mesh):
    place = Place((mesh.shape["batch"], mesh.shape["blk"]))
    weight, vector = P("batch", "blk"), P("blk")
    row = P("batch", "blk", None)
    in_specs = (row,) + (weight,) * 4 + (vector,) * 4 + (weight,) * 2 + (row,)
    out_specs = (row, row) + (weight,) * 4 + (vector,) * 4
    return jax.shard_map(
        functools.partial(body, place),
        mesh=mesh,
        in_specs=in_specs,
        out_specs=out_specs,
        check_vma=False,
    )
```

```python
import functools

import jax
import jax.numpy as jnp
from jax import lax
from jax.experimental import pallas as pl
from jax.experimental.pallas import tpu as pltpu
from jax.sharding import PartitionSpec as P

HEADS = 12
HEAD_DIM = 64
CORES = 2
LANE_X = 2
MESH = pl.DeviceIdType.MESH
LOG2E = 1.4426950408889634
epsilon = 1e-05
masked = -1e30
bf16 = jnp.bfloat16
f32 = jnp.float32


def dot(left, right, left_dim, right_dim):
    return lax.dot_general(
        left, right, (((left_dim,), (right_dim,)), ((), ())), preferred_element_type=f32
    )


class Place:
    def __init__(self, sizes):
        self.batch, self.blk = sizes
        self.Z, self.X = self.batch // LANE_X, LANE_X
        self.Y, self.C = self.blk // CORES, CORES

    def here(self):
        b, d = lax.axis_index("batch"), lax.axis_index("blk")
        return b // self.X, b % self.X, d // self.C, d % self.C

    def device(self, z, x, p, c):
        return (z * self.X + x, p * self.C + c)


def split_rows(count):
    return 16 * ((count // 2) // 16)


class Sends:
    def __init__(self, send_sem, recv_sem):
        self.send_sem, self.recv_sem, self.count = send_sem, recv_sem, 0

    def start(self, src, dst, device):
        copy = pltpu.make_async_remote_copy(
            src_ref=src,
            dst_ref=dst,
            send_sem=self.send_sem.at[self.count],
            recv_sem=self.recv_sem.at[self.count],
            device_id=device,
            device_id_type=MESH,
        )
        self.count += 1
        copy.start()
        return copy


def greet(place, partners):
    barrier = pltpu.get_barrier_semaphore()
    for partner in partners:
        pl.semaphore_signal(barrier, inc=1, device_id=partner, device_id_type=MESH)
    pl.semaphore_wait(barrier, len(partners))


def partners_of(place):
    z, x, p, c = place.here()
    found = [place.device((z + k) % place.Z, x, p, c) for k in range(1, place.Z)]
    found += [place.device(z, 1 - x, p, c)]
    found += [place.device(z, x, (p + k) % place.Y, c) for k in range(1, place.Y)]
    found += [place.device(z, x, p, 1 - c)]
    return found


def gather_kernel(place, matrices, *refs):
    n = len(matrices)
    mats, (tok, cot, tag, vec) = refs[:n], refs[n : n + 4]
    outs, (tok_g, cot_g, tag_g, vec_g) = refs[n + 4 : 2 * n + 4], refs[2 * n + 4 : 2 * n + 8]
    send_sem, recv_sem, local_sem = refs[2 * n + 8 :]
    z, x, p, c = place.here()
    Z, X, Y = place.Z, place.X, place.Y
    greet(place, partners_of(place))
    sends = Sends(send_sem, recv_sem)
    started = []

    def go(src, dst, device):
        copy = sends.start(src, dst, device)
        started.append(copy)
        return copy

    local = []

    def keep(src, dst):
        copy = pltpu.make_async_copy(src, dst, local_sem.at[len(local)])
        copy.start()
        local.append(copy)
        return copy

    row_copies, cot_copies = [], []
    for k in range(1, Y):
        to = (p + k) % Y
        device = place.device(z, x, to, c)
        row_copies.append(go(tok.at[to], tok_g.at[p, c], device))
        row_copies.append(go(tag.at[to], tag_g.at[p, c], device))
        row_copies.append(go(vec, vec_g.at[p, c], device))
    own = [
        keep(tok.at[p], tok_g.at[p, c]),
        keep(tag.at[p], tag_g.at[p, c]),
        keep(vec, vec_g.at[p, c]),
        keep(cot.at[p], cot_g.at[p]),
    ]
    first = []
    for m in range(n):
        place_here = outs[m].at[p, c, z, x]
        keep(mats[m], place_here)
        first.append(
            [
                go(mats[m], place_here, place.device((z + k) % Z, x, p, c))
                for k in range(1, Z)
            ]
        )
    for k in range(1, Y):
        to = (p + k) % Y
        cot_copies.append(go(cot.at[to], cot_g.at[p], place.device(z, x, to, c)))
    for copy in local:
        copy.wait()
    second = []
    for m in range(n):
        for copy in first[m]:
            copy.wait_recv()
        h = split_rows(mats[m].shape[0])
        r = mats[m].shape[0]
        low = outs[m].at[p, c, :, x, 0:h]
        high = outs[m].at[p, c, :, x, h:r]
        second.append(
            (
                [go(low, low, place.device(z, 1 - x, p, c))],
                [go(high, high, place.device(z, x, (p + k) % Y, c)) for k in range(1, Y)],
            )
        )
    third = []
    for m in range(n):
        h = split_rows(mats[m].shape[0])
        r = mats[m].shape[0]
        for copy in second[m][0]:
            copy.wait_recv()
        low = outs[m].at[p, c, :, :, 0:h]
        a = [go(low, low, place.device(z, x, (p + k) % Y, c)) for k in range(1, Y)]
        for copy in second[m][1]:
            copy.wait_recv()
        high = outs[m].at[:, c, :, x, h:r]
        b = [go(high, high, place.device(z, 1 - x, p, c))]
        third.append(a + b)
    for copy in row_copies:
        copy.wait_recv()
    sibling = place.device(z, x, p, 1 - c)
    last = []
    for ref in (tok_g, tag_g, vec_g):
        last.append(go(ref.at[:, c], ref.at[:, c], sibling))
    for m in range(n):
        for copy in third[m]:
            copy.wait_recv()
        last.append(go(outs[m].at[:, c], outs[m].at[:, c], sibling))
    for copy in last + cot_copies:
        copy.wait_recv()
    for copy in started:
        copy.wait_send()


def gather_all(place, mats, tok, cot, tag, vec):
    n = len(mats)
    Z, X, Y, C = place.Z, place.X, place.Y, place.C
    out = [jax.ShapeDtypeStruct((Y, C, Z, X) + m.shape, m.dtype) for m in mats]
    out += [
        jax.ShapeDtypeStruct((Y, C) + tok.shape[1:], tok.dtype),
        jax.ShapeDtypeStruct((Y,) + cot.shape[1:], cot.dtype),
        jax.ShapeDtypeStruct((Y, C) + tag.shape[1:], tag.dtype),
        jax.ShapeDtypeStruct((Y, C) + vec.shape, vec.dtype),
    ]
    copies = 4 * (Y - 1) + n * ((Z - 1) + 1 + (Y - 1) + (Y - 1) + 1) + 3 + n
    anywhere = pl.BlockSpec(memory_space=pl.ANY)
    return pl.pallas_call(
        functools.partial(gather_kernel, place, tuple(m.shape for m in mats)),
        out_shape=out,
        in_specs=[anywhere] * (n + 4),
        out_specs=[anywhere] * (n + 4),
        scratch_shapes=[
            pltpu.SemaphoreType.DMA((copies,)),
            pltpu.SemaphoreType.DMA((copies,)),
            pltpu.SemaphoreType.DMA((n + 4,)),
        ],
        compiler_params=pltpu.CompilerParams(collective_id=0, has_side_effects=True),
        name="gather_all",
    )(*mats, tok, cot, tag, vec)


def swap_kernel(place, src, dst, send_sem, recv_sem):
    z, x, p, c = place.here()
    sibling = place.device(z, x, p, 1 - c)
    greet(place, [sibling])
    copy = pltpu.make_async_remote_copy(
        src_ref=src.at[1 - c],
        dst_ref=dst,
        send_sem=send_sem,
        recv_sem=recv_sem,
        device_id=sibling,
        device_id_type=MESH,
    )
    copy.start()
    copy.wait()


def swap(place, value, number):
    anywhere = pl.BlockSpec(memory_space=pl.ANY)
    return pl.pallas_call(
        functools.partial(swap_kernel, place),
        out_shape=jax.ShapeDtypeStruct(value.shape[1:], value.dtype),
        in_specs=[anywhere],
        out_specs=anywhere,
        scratch_shapes=[pltpu.SemaphoreType.DMA, pltpu.SemaphoreType.DMA],
        compiler_params=pltpu.CompilerParams(collective_id=number, has_side_effects=True),
        name=f"swap_{number}",
    )(value)


def head_masked(value, h, axis):
    index = lax.broadcasted_iota(jnp.int32, value.shape, axis)
    return jnp.where((index // HEAD_DIM) == h, value, jnp.zeros_like(value))


def attention_forward_kernel(BQ, start_ref, q_ref, k_ref, v_ref, o_ref, oT_ref, lt_ref, qT, vT):
    L = q_ref.shape[0]
    nq = L // BQ
    scale = HEAD_DIM ** (-0.5) * LOG2E
    qT[...] = q_ref[...].T
    vT[...] = v_ref[...].T
    for qi in range(nq):
        qs = slice(qi * BQ, (qi + 1) * BQ)
        begin = start_ref[:, qs]
        d0 = qi * BQ
        if qi == nq - 1:
            cuts = [(0, d0, 1)] if d0 else []
        elif d0 > 256:
            cuts = [(0, 256, 1), (256, d0, 0)]
        else:
            cuts = [(0, d0, 1)] if d0 else []
        cuts.append((d0, d0 + BQ, 2))
        for h in range(2):
            query = head_masked(qT[:, qs], h, 0)
            parts = []
            for a, b, mode in cuts:
                s = dot(k_ref[a:b, :], query, 1, 0) * scale
                if mode:
                    key_pos = lax.broadcasted_iota(jnp.int32, (b - a, BQ), 0) + a
                    visible = key_pos >= begin
                    if mode == 2:
                        query_pos = lax.broadcasted_iota(jnp.int32, (b - a, BQ), 1) + d0
                        visible = jnp.logical_and(visible, key_pos <= query_pos)
                    s = jnp.where(visible, s, masked)
                parts.append(s)
            top = functools.reduce(
                jnp.maximum, [jnp.max(s, axis=0, keepdims=True) for s in parts]
            )
            total, accum = 0.0, 0.0
            for (a, b, mode), s in zip(cuts, parts):
                e = jnp.exp2(s - top)
                total = total + jnp.sum(e, axis=0, keepdims=True)
                accum = accum + dot(
                    vT[h * HEAD_DIM : (h + 1) * HEAD_DIM, a:b], e.astype(bf16), 1, 0
                )
            oT_ref[h * HEAD_DIM : (h + 1) * HEAD_DIM, qs] = accum / total
            lt_ref[0, h : h + 1, qs] = top + jnp.log2(total)
        o_ref[qs, :] = oT_ref[:, qs].astype(bf16).T


def attention_forward(projected, begin):
    L = projected.shape[0]
    pairs = projected.shape[1] // 3 // 128
    return pl.pallas_call(
        functools.partial(attention_forward_kernel, 512),
        grid=(pairs,),
        in_specs=[
            pl.BlockSpec((1, L), lambda i: (0, 0)),
            pl.BlockSpec((L, 128), lambda i: (0, i)),
            pl.BlockSpec((L, 128), lambda i: (0, pairs + i)),
            pl.BlockSpec((L, 128), lambda i: (0, 2 * pairs + i)),
        ],
        out_specs=[
            pl.BlockSpec((L, 128), lambda i: (0, i)),
            pl.BlockSpec((128, L), lambda i: (i, 0)),
            pl.BlockSpec((1, 2, L), lambda i: (i, 0, 0)),
        ],
        out_shape=[
            jax.ShapeDtypeStruct((L, pairs * 128), bf16),
            jax.ShapeDtypeStruct((pairs * 128, L), f32),
            jax.ShapeDtypeStruct((pairs, 2, L), f32),
        ],
        scratch_shapes=[pltpu.VMEM((128, L), bf16), pltpu.VMEM((128, L), bf16)],
        compiler_params=pltpu.CompilerParams(vmem_limit_bytes=50 << 20),
        name="attention_forward",
    )(begin, projected, projected, projected)


class Wire:
    def __init__(self, send_sem, recv_sem):
        self.send_sem, self.recv_sem, self.names = send_sem, recv_sem, {}

    def copy(self, name, src, dst, device):
        i = self.names.setdefault(name, len(self.names))
        return pltpu.make_async_remote_copy(
            src_ref=src,
            dst_ref=dst,
            send_sem=self.send_sem.at[i],
            recv_sem=self.recv_sem.at[i],
            device_id=device,
            device_id_type=MESH,
        )


def start_all(copies):
    for copy in copies:
        copy.start()


def arrive_all(copies):
    for copy in copies:
        copy.wait_recv()


def leave_all(copies):
    for copy in copies:
        copy.wait_send()


def first_rows(rows, sixths):
    return min(rows - 16, 16 * ((rows * sixths // 6) // 16)) if rows > 16 else 0


class Summing:
    def __init__(self, place, wire, name, spots, acc, xa, yb, ya, xb, zz):
        self.place, self.wire, self.name, self.spots = place, wire, name, spots
        self.acc, self.xa, self.yb, self.ya, self.xb, self.zz = acc, xa, yb, ya, xb, zz
        self.rows = acc.shape[3]
        self.h = xa.shape[2]

    def one(self):
        z, x, p, c = self.spots
        place, h, r = self.place, self.h, self.rows
        side = place.device(z, 1 - x, p, c)
        found = [
            self.wire.copy((self.name, "xa"), self.acc.at[:, :, 1 - x, 0:h], self.xa, side)
        ]
        for k in range(1, place.Y):
            to = (p + k) % place.Y
            found.append(
                self.wire.copy(
                    (self.name, "yb", k),
                    self.acc.at[to, :, :, h:r],
                    self.yb.at[k - 1],
                    place.device(z, x, to, c),
                )
            )
        return found

    def two(self):
        z, x, p, c = self.spots
        place, h, r = self.place, self.h, self.rows
        found = []
        for k in range(1, place.Y):
            to = (p + k) % place.Y
            found.append(
                self.wire.copy(
                    (self.name, "ya", k),
                    self.acc.at[to, :, x, 0:h],
                    self.ya.at[k - 1],
                    place.device(z, x, to, c),
                )
            )
        side = place.device(z, 1 - x, p, c)
        found.append(
            self.wire.copy((self.name, "xb"), self.acc.at[p, :, 1 - x, h:r], self.xb, side)
        )
        return found

    def three(self):
        z, x, p, c = self.spots
        place = self.place
        found = []
        for k in range(1, place.Z):
            to = (z + k) % place.Z
            found.append(
                self.wire.copy(
                    (self.name, "z", k),
                    self.acc.at[p, to, x],
                    self.zz.at[k - 1],
                    place.device(to, x, p, c),
                )
            )
        return found

    def add_one(self):
        z, x, p, c = self.spots
        place, h, r, acc = self.place, self.h, self.rows, self.acc
        ones = self.one()
        ones[0].wait_recv()

        def low(i, nothing):
            a, b = i // place.Z, i % place.Z
            total = acc[a, b, x, 0:h].astype(f32) + self.xa[a, b].astype(f32)
            acc[a, b, x, 0:h] = total.astype(bf16)
            return nothing

        lax.fori_loop(0, place.Y * place.Z, low, 0)
        twos = self.two()
        start_all(twos[:-1])
        arrive_all(ones[1:])

        def high(i, nothing):
            a, b = i // place.X, i % place.X
            total = acc[p, a, b, h:r].astype(f32)
            for k in range(place.Y - 1):
                total = total + self.yb[k, a, b].astype(f32)
            acc[p, a, b, h:r] = total.astype(bf16)
            return nothing

        lax.fori_loop(0, place.Z * place.X, high, 0)
        twos[-1].start()

    def add_two(self):
        z, x, p, c = self.spots
        place, h, r, acc = self.place, self.h, self.rows, self.acc
        arrive_all(self.two())

        def both(i, nothing):
            total = acc[p, i, x, 0:h].astype(f32)
            for k in range(place.Y - 1):
                total = total + self.ya[k, i].astype(f32)
            acc[p, i, x, 0:h] = total.astype(bf16)
            total = acc[p, i, x, h:r].astype(f32) + self.xb[i].astype(f32)
            acc[p, i, x, h:r] = total.astype(bf16)
            return nothing

        lax.fori_loop(0, place.Z, both, 0)
        start_all(self.three())

    def finish(self, target):
        z, x, p, c = self.spots
        arrive_all(self.three())
        total = self.acc[p, z, x].astype(f32)
        for k in range(self.place.Z - 1):
            total = total + self.zz[k].astype(f32)
        target[...] = total

    def leave(self):
        leave_all(self.one())
        leave_all(self.two())
        leave_all(self.three())


def backward_kernel(place, n, BQ, *refs):
    (begin, proj, ga, oT_in, lt, normedT, w_in, tok, gm, out_in, vec, vec_two) = refs[:12]
    parts = refs[12 : 12 + n]
    outs = refs[12 + n :]
    sums, (vec_out, out_home, tg_home) = outs[: n + 1], outs[n + 1 : n + 4]
    landing = outs[n + 4 : 2 * n + 4]
    rest = outs[2 * n + 4 :]
    (
        pv, do, oT, wv, kT, dk, dv, nT, pacc, p_recv,
        keep, g_send, g_recv, tok_v, gm_v, grads, v0, v1, v2, v3, vc, vy, vx, vz,
    ) = rest[:24]
    buffers = rest[24 : 24 + 6 * (n + 1)]
    send_sem, recv_sem, local_sem = rest[24 + 6 * (n + 1) :]
    tg_v = g_recv
    spots = place.here()
    z, x, p, c = spots
    Z, X, Y, C = place.Z, place.X, place.Y, place.C
    L, W3 = pv.shape
    H = W3 // 3
    D = wv.shape[0]
    T = L // (Y * C)
    pairs = H // 128
    nq = L // BQ
    scale = HEAD_DIM ** (-0.5) * LOG2E
    scale_back = HEAD_DIM ** (-0.5)
    wire = Wire(send_sem, recv_sem)
    sibling = place.device(z, x, p, 1 - c)
    beside = place.device(z, 1 - x, p, c)
    adds = [
        Summing(place, wire, m, spots, *buffers[6 * m : 6 * m + 6]) for m in range(n + 1)
    ]

    def local(i, src, dst):
        return pltpu.make_async_copy(src, dst, local_sem.at[i])

    def lane(offset, size):
        return pl.ds(pl.multiple_of(offset, 128), size)

    def line(offset, size):
        return pl.ds(pl.multiple_of(offset, 16), size)

    def grad_swap():
        return [
            wire.copy(
                ("ga", q),
                ga.at[q * T : (q + 1) * T, lane((1 - c) * H, H)],
                do.at[line((2 * q + c) * T, T), :],
                sibling,
            )
            for q in range(Y)
        ]

    def core_sends(m):
        return [wire.copy(("core", m), parts[m].at[:, 1 - c], landing[m], sibling)]

    def out_sends():
        found = []
        for k in range(1, Y):
            to = (p + k) % Y
            found.append(
                wire.copy(
                    ("out", k), out_in.at[line(to * T, T)], out_home.at[p], place.device(z, x, to, c)
                )
            )
        return found

    greet(place, partners_of(place))
    start_all(grad_swap())
    own = [
        local(q, ga.at[q * T : (q + 1) * T, lane(c * H, H)], do.at[line((2 * q + c) * T, T), :])
        for q in range(Y)
    ]
    def out_fetch(qi):
        return local(Y + 1, oT_in.at[:, lane(qi * BQ, BQ)], oT)

    loads = [local(Y, proj, pv), local(Y + 2, w_in, wv)]
    out_fetch(nq - 1).start()
    out_own = local(Y + 3, out_in.at[line(p * T, T)], out_home.at[p])
    acc_own = [
        local(Y + 4 + m, parts[m].at[:, c], adds[m + 1].acc) for m in range(n)
    ]
    start_all(own + loads)
    for m in range(n):
        start_all(core_sends(m))
    start_all(out_sends())
    start_all(acc_own + [out_own])
    row_sem = Y + 4 + n

    def core_add(m):
        arrive_all(core_sends(m))
        acc_own[m].wait()
        acc, other = adds[m + 1].acc, landing[m]

        def one(i, nothing):
            a, b, d = i // (Z * X), (i // X) % Z, i % X
            total = acc[a, b, d].astype(f32) + other[a, b, d].astype(f32)
            acc[a, b, d] = total.astype(bf16)
            return nothing

        lax.fori_loop(0, Y * Z * X, one, 0)
        start_all(adds[m + 1].one())

    for copy in loads:
        copy.wait()
    kT[...] = pv[:, H : 2 * H].T
    dk[...] = jnp.zeros_like(dk)
    dv[...] = jnp.zeros_like(dv)
    pacc[...] = jnp.zeros_like(pacc)
    grads[...] = jnp.zeros_like(grads)
    for copy in own:
        copy.wait()
    arrive_all(grad_swap())

    U = BQ // T
    gain = vec[0:1, :]

    def sub_blocks(qi):
        found = []
        for u in range(U):
            block = qi * U + u
            found.append((u, block // C, block % C))
        return found

    reserved = send_sem.shape[0] - 3 * Y

    def g_wire(q):
        return pltpu.make_async_remote_copy(
            src_ref=g_send.at[q],
            dst_ref=g_recv.at[q],
            send_sem=send_sem.at[reserved + q],
            recv_sem=recv_sem.at[reserved + q],
            device_id=sibling,
            device_id_type=MESH,
        )

    def home_from(k):
        q = (p + k) % Y
        return pltpu.make_async_remote_copy(
            src_ref=tg_v.at[p],
            dst_ref=tg_home.at[q],
            send_sem=send_sem.at[reserved + Y + q],
            recv_sem=recv_sem.at[reserved + 2 * Y + q],
            device_id=place.device(z, x, q, c),
            device_id_type=MESH,
        )

    def home_to(q):
        return pltpu.make_async_remote_copy(
            src_ref=tg_v.at[q],
            dst_ref=tg_home.at[p],
            send_sem=send_sem.at[reserved + Y + q],
            recv_sem=recv_sem.at[reserved + 2 * Y + p],
            device_id=place.device(z, x, q, c),
            device_id_type=MESH,
        )

    def block_done(qi):
        qs = line(qi * BQ, BQ)
        fetch = local(row_sem, normedT.at[:, lane(qi * BQ, BQ)], nT)
        fetch.start()
        pv[qs, H : 2 * H] = (dk[qs, :] * scale_back).astype(bf16)
        pv[qs, 2 * H :] = dv[qs, :].astype(bf16)
        g = dot(pv[qs, :], wv[...], 1, 1)
        for u, q, owner in sub_blocks(qi):
            rows = slice(u * T, (u + 1) * T)

            @pl.when(owner == c)
            def _():
                keep[u // C] = g[rows, :]

            @pl.when(owner != c)
            def _():
                g_send[q] = g[rows, :].astype(bf16)
                g_wire(q).start()

        fetch.wait()
        pacc[...] += dot(nT[...], pv[qs, :], 1, 0)

    def token_rows(qi):
        for u, q, owner in sub_blocks(qi):

            @pl.when(owner == c)
            def _():
                a = local(row_sem, tok.at[line(q * T, T)], tok_v)
                b = local(row_sem + 1, gm.at[line(q * T, T)], gm_v)
                a.start()
                b.start()
                g_wire(q).wait_recv()
                grad = keep[u // C] + g_recv[q].astype(f32)
                a.wait()
                unit, factor = normed(tok_v[...].astype(f32))
                grads[0:1, :] += jnp.sum(grad * unit, axis=0, keepdims=True)
                grads[1:2, :] += jnp.sum(grad, axis=0, keepdims=True)
                b.wait()
                tg_v[q] = (gm_v[...] + norm_back(grad, gain, unit, factor)).astype(bf16)

                @pl.when(q == p)
                def _():
                    local(row_sem + 2, tg_v.at[q], tg_home.at[p]).start()

                @pl.when(q != p)
                def _():
                    home_to(q).start()

    def step(s, nothing):
        qi = nq - 1 - s // pairs
        pair = s % pairs
        qs = line(qi * BQ, BQ)
        ql = lane(qi * BQ, BQ)
        cols = lane(pair * 128, 128)
        k_cols, v_cols = lane(H + pair * 128, 128), lane(2 * H + pair * 128, 128)
        q_val, do_val = pv[qs, cols], do[qs, cols]
        qT_val, doT_val = q_val.T, do_val.T
        heads = []

        @pl.when(pair == 0)
        def _():
            out_fetch(qi).wait()

        for h in range(2):
            rows = slice(h * HEAD_DIM, (h + 1) * HEAD_DIM)
            head_rows = pl.ds(pl.multiple_of(pair * 128 + h * HEAD_DIM, HEAD_DIM), HEAD_DIM)
            delta = jnp.sum(
                doT_val[rows, :].astype(f32) * oT[head_rows, :], axis=0, keepdims=True
            )
            heads.append(
                (
                    head_masked(qT_val, h, 0),
                    head_masked(doT_val, h, 0),
                    head_masked(q_val, h, 1),
                    head_masked(do_val, h, 1),
                    delta,
                    lt[pair, h : h + 1, ql],
                    head_rows,
                )
            )

        @pl.when(jnp.logical_and(pair == pairs - 1, qi > 0))
        def _():
            out_fetch(qi - 1).start()

        def tile(kj, dqs, mode):
            ks = line(kj * BQ, BQ)
            kl = lane(kj * BQ, BQ)
            if mode:
                key_pos = lax.broadcasted_iota(jnp.int32, (BQ, BQ), 0)
                visible = key_pos >= (begin[:, ql] - kj * BQ)
                if mode == 2:
                    query_pos = lax.broadcasted_iota(jnp.int32, (BQ, BQ), 1)
                    visible = jnp.logical_and(visible, key_pos <= query_pos)
            more_dv, more_dk, found = 0.0, 0.0, []
            for h in range(2):
                query, grad, q_nat, do_nat, delta, log_total, head_rows = heads[h]
                sc = dot(pv[ks, k_cols], query, 1, 0) * scale
                prob = jnp.exp2(sc - log_total)
                if mode:
                    prob = jnp.where(visible, prob, 0.0)
                dp = dot(pv[ks, v_cols], grad, 1, 0)
                ds = (prob * (dp - delta)).astype(bf16)
                more_dv = more_dv + dot(prob.astype(bf16), do_nat, 1, 0)
                more_dk = more_dk + dot(ds, q_nat, 1, 0)
                found.append(dqs[h] + dot(kT[head_rows, kl], ds, 1, 0))
            dv[ks, cols] += more_dv
            dk[ks, cols] += more_dk
            return tuple(found)

        zero = jnp.zeros((HEAD_DIM, BQ), f32)
        dqs = tile(qi, (zero, zero), 2)

        def last(d):
            return lax.fori_loop(0, qi, lambda kj, e: tile(kj, e, 1), d)

        def others(d):
            d = lax.cond(qi > 0, lambda e: tile(0, e, 1), lambda e: e, d)
            return lax.fori_loop(1, qi, lambda kj, e: tile(kj, e, 0), d)

        dqs = lax.cond(qi == nq - 1, last, others, dqs)
        dq = jnp.concatenate(dqs, axis=0) * scale_back
        pv[qs, cols] = dq.astype(bf16).T

        def at(number, *events):
            @pl.when(s == number)
            def _():
                for event in events:
                    event()

        @pl.when(pair == pairs - 1)
        def _():
            block_done(qi)

        @pl.when(jnp.logical_and(pair == 0, qi < nq - 1))
        def _():
            token_rows(qi + 1)

        def do_it(f, *args):
            return lambda: f(*args)

        out_m, up_m, down_m = 0, 1, 2
        at(0, do_it(core_add, down_m))
        at(1, do_it(core_add, out_m))
        at(3, adds[up_m + 1].add_one)
        at(7, adds[up_m + 1].add_two)
        at(8, adds[down_m + 1].add_one)
        at(9, adds[out_m + 1].add_one)
        return nothing

    core_add(1)
    lax.fori_loop(0, nq * pairs, step, 0)
    p_send = pv.at[0:D, :]
    p_send[...] = pacc[...].astype(bf16)
    p_swap = wire.copy("p", p_send, p_recv, sibling)
    p_swap.start()
    adds[3].add_two()
    token_rows(0)
    p_swap.wait_recv()
    acc = adds[0].acc
    r, w = acc.shape[3:]
    for mine in range(C):

        @pl.when(c == mine)
        def _():
            for q in range(Y):
                low_col = w * (C * q + mine)
                for third in range(3):
                    for half in range(C):
                        base = third * D + half * H
                        a, b = max(base, low_col), min(base + H, low_col + w)
                        if a >= b:
                            continue
                        source = p_send if half == mine else p_recv
                        off = third * H - base
                        for i in range(Z * X):
                            acc[q, i // X, i % X, :, a - low_col : b - low_col] = source[
                                i * r : (i + 1) * r, a + off : b + off
                            ]

    start_all(adds[0].one())
    grads[2:4, :] = vec_two[...]
    v0[0:4, :] = grads[0:4, 0:H]
    v0[4:8, :] = grads[0:4, H:]
    v_core = wire.copy("vc", v0, vc, sibling)
    v_core.start()
    adds[1].add_two()
    v_core.wait_recv()
    v1[...] = v0[...] + vc[...]
    v_y = [
        wire.copy(("vy", k), v1, vy.at[k - 1], place.device(z, x, (p + k) % Y, c))
        for k in range(1, Y)
    ]
    start_all(v_y)
    adds[2].finish(sums[2])
    adds[0].add_one()
    arrive_all(v_y)
    total = v1[...]
    for k in range(Y - 1):
        total = total + vy[k]
    v2[...] = total
    v_x = wire.copy("vx", v2, vx, beside)
    v_x.start()
    adds[3].finish(sums[3])
    adds[0].add_two()
    v_x.wait_recv()
    v3[...] = v2[...] + vx[...]
    v_z = [
        wire.copy(("vz", k), v3, vz.at[k - 1], place.device((z + k) % Z, x, p, c))
        for k in range(1, Z)
    ]
    start_all(v_z)
    adds[1].finish(sums[1])
    adds[0].finish(sums[0])
    arrive_all(v_z)
    total = v3[...]
    for k in range(Z - 1):
        total = total + vz[k]
    vec_out[...] = total
    for k in range(1, Y):
        home_from(k).wait_recv()
        home_to((p + k) % Y).wait_send()
    local(row_sem + 2, tg_v.at[p], tg_home.at[p]).wait()
    out_own.wait()
    arrive_all(out_sends())
    leave_all(out_sends())
    leave_all(grad_swap())
    for q in range(Y):
        g_wire(q).wait_send()
    for m in range(n):
        leave_all(core_sends(m))
    p_swap.wait_send()
    v_core.wait_send()
    leave_all(v_y)
    v_x.wait_send()
    leave_all(v_z)
    for summing in adds:
        summing.leave()


def backward(place, parts, proj_shape, begin, proj, ga, oT, lt, normedT, w_own, tok, gm, out, vec, vec_two):
    n = len(parts)
    Z, X, Y, C = place.Z, place.X, place.Y, place.C
    L, W3 = proj.shape
    H = W3 // 3
    D = w_own.shape[0]
    T = L // (Y * C)
    BQ = 512
    inside = pl.BlockSpec(memory_space=pltpu.VMEM)
    anywhere = pl.BlockSpec(memory_space=pl.ANY)
    shapes = [proj_shape] + [part.shape[4:] for part in parts]
    sixths = [3, 4, 5, 5]
    out_shape = [jax.ShapeDtypeStruct(shape, f32) for shape in shapes]
    out_shape += [
        jax.ShapeDtypeStruct((8, H), f32),
        jax.ShapeDtypeStruct((Y, T, D), bf16),
        jax.ShapeDtypeStruct((Y, T, D), bf16),
    ]
    scratch = [pltpu.VMEM((Y, Z, X) + shape, bf16) for shape in shapes[1:]]
    scratch += [
        pltpu.VMEM((L, W3), bf16),
        pltpu.VMEM((L, H), bf16),
        pltpu.VMEM((H, BQ), f32),
        pltpu.VMEM((D, W3), bf16),
        pltpu.VMEM((H, L), bf16),
        pltpu.VMEM((L, H), f32),
        pltpu.VMEM((L, H), f32),
        pltpu.VMEM((D, BQ), bf16),
        pltpu.VMEM((D, W3), f32),
        pltpu.VMEM((D, W3), bf16),
        pltpu.VMEM((max(1, BQ // T // C), T, D), f32),
        pltpu.VMEM((Y, T, D), bf16),
        pltpu.VMEM((Y, T, D), bf16),
        pltpu.VMEM((T, D), bf16),
        pltpu.VMEM((T, D), f32),
    ]
    scratch += [pltpu.VMEM((8, D), f32)] + [pltpu.VMEM((8, H), f32)] * 5
    scratch += [
        pltpu.VMEM((Y - 1, 8, H), f32),
        pltpu.VMEM((8, H), f32),
        pltpu.VMEM((Z - 1, 8, H), f32),
    ]
    for shape, part in zip(shapes, sixths):
        r, w = shape
        h = first_rows(r, part)
        scratch += [
            pltpu.VMEM((Y, Z, X, r, w), bf16),
            pltpu.VMEM((Y, Z, h, w), bf16),
            pltpu.VMEM((Y - 1, Z, X, r - h, w), bf16),
            pltpu.VMEM((Y - 1, Z, h, w), bf16),
            pltpu.VMEM((Z, r - h, w), bf16),
            pltpu.VMEM((Z - 1, r, w), bf16),
        ]
    each = 1 + (Y - 1) + (Y - 1) + 1 + (Z - 1)
    copies = Y + n + (Y - 1) + (n + 1) * each + 2 + (Y - 1) + 1 + (Z - 1) + 3 * Y
    scratch += [
        pltpu.SemaphoreType.DMA((copies,)),
        pltpu.SemaphoreType.DMA((copies,)),
        pltpu.SemaphoreType.DMA((Y + 4 + n + 3,)),
    ]
    return pl.pallas_call(
        functools.partial(backward_kernel, place, n, BQ),
        out_shape=out_shape,
        in_specs=[inside] + [anywhere] * 3 + [inside] + [anywhere] * 5 + [inside] * 2 + [anywhere] * n,
        out_specs=[inside] * (n + 2) + [anywhere] * 2,
        scratch_shapes=scratch,
        compiler_params=pltpu.CompilerParams(
            collective_id=1, has_side_effects=True, vmem_limit_bytes=63 << 20
        ),
        name="backward",
    )(begin, proj, ga, oT, lt, normedT, w_own, tok, gm, out, vec, vec_two, *parts)


def gelu_both(u):
    k = 0.7978845608028654
    square = u * u
    t = jnp.tanh(k * u * (1.0 + 0.044715 * square))
    half = 0.5 * (1.0 + t)
    slope = half + 0.5 * k * u * (1.0 - t * t) * (1.0 + 3 * 0.044715 * square)
    return u * half, slope


def dense_kernel(
    place, aligned, att, tok, cot, out_w, up_w, down_w, vec,
    output, gm_out, ga_out, up_p, down_p, out_p, vec_out,
    att_v, tok_v, cot_v, out_v, up_v, down_v, out_full, mid, n2, act, gh, n2T, cotT, g2,
    wide, stage, load_sem, store_sem,
):
    S, nb = place.blk, place.batch
    M, D = att_v.shape
    FF = up_v.shape[1]
    J = FF // D
    loads = []

    def load(src, dst):
        copy = pltpu.make_async_copy(src, dst, load_sem.at[len(loads)])
        copy.start()
        loads.append(copy)
        return copy

    first = [load(att, att_v), load(tok, tok_v), load(out_w, out_v)]
    first.append(load(cot, cot_v))
    if aligned:
        w = up_w.shape[2]
        weights = [load(up_w.at[d], up_v.at[:, d * w : (d + 1) * w]) for d in range(S)]
        r, w = down_w.shape[2:]
        for d in range(S):
            for b in range(nb):
                weights.append(
                    load(
                        down_w.at[d, b],
                        down_v.at[d * r : (d + 1) * r, b * w : (b + 1) * w],
                    )
                )
    else:
        weights = [load(up_w, up_v), load(down_w, down_v)]
    for copy in first:
        copy.wait()
    w = out_v.shape[2]
    for d in range(S):
        out_full[:, d * w : (d + 1) * w] = out_v[d]
    gain, shift = vec[2:3, :], vec[3:4, :]
    T = M // 2
    for t in range(2):
        ts = slice(t * T, (t + 1) * T)
        middle = tok_v[ts, :].astype(f32) + dot(att_v[ts, :], out_full[...], 1, 0)
        unit, factor = normed(middle)
        mid[ts, :] = middle
        n2[ts, :] = (unit * gain + shift).astype(bf16)
    for copy in weights:
        copy.wait()
    n2T[...] = n2[...].T
    cotT[...] = cot_v[...].T
    gain_sum = jnp.zeros((1, D), f32)
    shift_sum = jnp.zeros((1, D), f32)
    stores = [None, None]
    for t in range(2):
        ts = slice(t * T, (t + 1) * T)

        def chunk(j, nothing):
            js = pl.ds(pl.multiple_of(j * D, D), D)
            h = dot(n2[ts, :], up_v[:, js], 1, 0)
            g = dot(cot_v[ts, :], down_v[:, js], 1, 0)
            a, slope = gelu_both(h)
            a = a.astype(bf16)
            b = (g * slope).astype(bf16)
            act[ts, js] = a
            gh[ts, js] = b
            more_out = dot(a, down_v[:, js], 1, 1)
            more_g2 = dot(b, up_v[:, js], 1, 1)
            mid[ts, :] += more_out

            @pl.when(j == 0)
            def _():
                g2[...] = more_g2

            @pl.when(j > 0)
            def _():
                g2[...] += more_g2

            return nothing

        middle = mid[ts, :]
        unit, factor = normed(middle)
        lax.fori_loop(0, J, chunk, 0)
        middle_unit, middle_factor = unit, factor
        wide[...] = middle_unit
        if stores[0] is not None:
            for copy in stores:
                copy.wait()
        stage[0, 0:T, :] = mid[ts, :].astype(bf16)
        copy = pltpu.make_async_copy(stage.at[0, 0:T], output.at[ts], store_sem.at[0])
        copy.start()
        stores[0] = copy
        grad = g2[...]
        n = wide[...]
        gain_sum = gain_sum + jnp.sum(grad * n, axis=0, keepdims=True)
        shift_sum = shift_sum + jnp.sum(grad, axis=0, keepdims=True)
        gm = cot_v[ts, :].astype(f32) + norm_back(grad, gain, n, middle_factor)
        mid[ts, :] = gm
        low = gm.astype(bf16)
        n2[ts, :] = low
        stage[1, 0:T, :] = dot(low, out_full[...], 1, 1).astype(bf16)
        copy = pltpu.make_async_copy(stage.at[1, 0:T], ga_out.at[ts], store_sem.at[1])
        copy.start()
        stores[1] = copy
    for copy in stores:
        copy.wait()
    save = pltpu.make_async_copy(mid, gm_out, store_sem.at[2])
    save.start()
    vec_out[0:1, :] = gain_sum
    vec_out[1:2, :] = shift_sum
    pending = [[], []]
    turn = 0

    def put(value, pieces):
        nonlocal turn
        slot = turn % 2
        turn += 1
        for copy in pending[slot]:
            copy.wait()
        stage[slot, 0 : value.shape[0], :] = value
        pending[slot] = []
        for i, (rows, columns, dst) in enumerate(pieces):
            copy = pltpu.make_async_copy(
                stage.at[slot, rows, columns], dst, store_sem.at[3 + slot * 64 + i]
            )
            copy.start()
            pending[slot].append(copy)

    every = slice(0, D)
    for j in range(J):
        js = slice(j * D, (j + 1) * D)
        value = dot(n2T[...], gh[:, js], 1, 0).astype(bf16)
        if aligned:
            w = up_p.shape[2]
            pieces = [
                (every, slice(i * w, (i + 1) * w), up_p.at[j * D // w + i]) for i in range(D // w)
            ]
        else:
            pieces = [(every, every, up_p.at[:, js])]
        put(value, pieces)
        value = dot(cotT[...], act[:, js], 1, 0).astype(bf16)
        if aligned:
            r, w = down_p.shape[2:]
            pieces = [
                (
                    slice(d * r, (d + 1) * r),
                    slice(i * w, (i + 1) * w),
                    down_p.at[d, j * D // w + i],
                )
                for d in range(S)
                for i in range(D // w)
            ]
        else:
            pieces = [(every, every, down_p.at[:, js])]
        put(value, pieces)
    value = dot(att_v[...], n2[...], 0, 0).astype(bf16)
    for copy in pending[turn % 2]:
        copy.wait()
    pending[turn % 2] = []
    stage[turn % 2, 0:D, :] = value
    w = out_v.shape[2]
    for d in range(S):
        out_v[d] = stage[turn % 2, 0:D, d * w : (d + 1) * w]
    copy = pltpu.make_async_copy(out_v, out_p, store_sem.at[3])
    for group in pending:
        for other in group:
            other.wait()
    copy.start()
    copy.wait()
    save.wait()


def dense(place, att, tok, cot, out_g, up_g, down_g, vec):
    M, D = att.shape
    S, nb = place.blk, place.batch
    aligned = up_g.shape[-1] % 128 == 0 and down_g.shape[-1] % 128 == 0
    out_w = out_g.reshape(S, D, -1)
    FF = S * up_g.shape[-1]
    if aligned:
        up_w = up_g.reshape(S, D, -1)
        down_w = down_g.reshape((S, nb) + down_g.shape[-2:])
    else:
        up_w, down_w = joined(up_g, 0), joined(down_g, 1)
    anywhere = pl.BlockSpec(memory_space=pl.ANY)
    inside = pl.BlockSpec(memory_space=pltpu.VMEM)
    loads = 8 + S + S * nb
    results = pl.pallas_call(
        functools.partial(dense_kernel, place, aligned),
        out_shape=[
            jax.ShapeDtypeStruct((M, D), bf16),
            jax.ShapeDtypeStruct((M, D), f32),
            jax.ShapeDtypeStruct((M, D), bf16),
            jax.ShapeDtypeStruct(up_w.shape, bf16),
            jax.ShapeDtypeStruct(down_w.shape, bf16),
            jax.ShapeDtypeStruct(out_w.shape, bf16),
            jax.ShapeDtypeStruct((2, D), f32),
        ],
        in_specs=[anywhere] * 6 + [inside],
        out_specs=[anywhere] * 6 + [inside],
        scratch_shapes=[
            pltpu.VMEM((M, D), bf16),
            pltpu.VMEM((M, D), bf16),
            pltpu.VMEM((M, D), bf16),
            pltpu.VMEM(out_w.shape, bf16),
            pltpu.VMEM((D, FF), bf16),
            pltpu.VMEM((D, FF), bf16),
            pltpu.VMEM((D, D), bf16),
            pltpu.VMEM((M, D), f32),
            pltpu.VMEM((M, D), bf16),
            pltpu.VMEM((M, FF), bf16),
            pltpu.VMEM((M, FF), bf16),
            pltpu.VMEM((D, M), bf16),
            pltpu.VMEM((D, M), bf16),
            pltpu.VMEM((M // 2, D), f32),
            pltpu.VMEM((M // 2, D), f32),
            pltpu.VMEM((2, max(D, M // 2), D), bf16),
            pltpu.SemaphoreType.DMA((loads,)),
            pltpu.SemaphoreType.DMA((3 + 128,)),
        ],
        compiler_params=pltpu.CompilerParams(vmem_limit_bytes=62 << 20),
        name="dense",
    )(att, tok, cot, out_w, up_w, down_w, vec)
    output, gm, ga, up_p, down_p, out_p, vec_grads = results
    out_p = out_p.reshape(out_g.shape)
    if aligned:
        up_p, down_p = up_p.reshape(up_g.shape), down_p.reshape(down_g.shape)
    else:
        up_p, down_p = parted(up_p, place, 0), parted(down_p, place, 1)
    return output, gm, ga, up_p, down_p, out_p, vec_grads


def normed(values):
    average = jnp.mean(values, axis=-1, keepdims=True)
    centered = values - average
    variance = jnp.mean(centered * centered, axis=-1, keepdims=True)
    factor = lax.rsqrt(variance + epsilon)
    return centered * factor, factor


def norm_back(grad, gain, unit, factor):
    e = grad * gain
    return factor * (
        e - jnp.mean(e, axis=-1, keepdims=True) - unit * jnp.mean(e * unit, axis=-1, keepdims=True)
    )


def joined(gathered, axis):
    Y, C, Z, X, r, w = gathered.shape
    if axis == 0:
        return gathered.reshape(Y * C, Z * X * r, w).transpose(1, 0, 2).reshape(Z * X * r, -1)
    return gathered.reshape(Y * C, Z * X, r, w).transpose(0, 2, 1, 3).reshape(Y * C * r, -1)


def parted(whole, place, axis):
    Y, C, Z, X = place.Y, place.C, place.Z, place.X
    rows, columns = whole.shape
    if axis == 0:
        value = whole.reshape(Z * X, rows // (Z * X), Y * C, columns // (Y * C))
        value = value.transpose(2, 0, 1, 3)
    else:
        value = whole.reshape(Y * C, rows // (Y * C), Z * X, columns // (Z * X))
        value = value.transpose(0, 2, 1, 3)
    return value.reshape((Y, C, Z, X) + value.shape[2:])


def chosen(pair, c):
    return jnp.where(c == 0, pair[0], pair[1])


def body(
    place,
    tokens,
    proj_weight,
    out_weight,
    up_weight,
    down_weight,
    gain_one,
    bias_one,
    gain_two,
    bias_two,
    segments,
    present,
    cotangent,
):
    rows, block, width = tokens.shape
    Y, C = place.Y, place.C
    length = place.blk * block
    index = lax.axis_index("blk")
    c = index % C
    half = width // C
    query_pos = index * block + jnp.arange(block, dtype=jnp.int32)
    local_tags = jnp.where(present == 1, segments, -1 - query_pos[None, :])
    tag_in = jnp.broadcast_to(local_tags[:, None, :], (rows, 8, block))
    vec_in = jnp.stack([gain_one, bias_one, gain_two, bias_two])
    vec_in = jnp.pad(vec_in, ((0, 12), (0, 0)))
    proj_g, out_g, up_g, down_g, tok_g, cot_g, tag_g, vec_g = gather_all(
        place,
        [proj_weight, out_weight, up_weight, down_weight.T],
        tokens,
        cotangent,
        tag_in,
        vec_in,
    )
    proj_full = joined(proj_g, 0)
    vec = vec_g.reshape(place.blk, 16, -1)[:, :8].transpose(1, 0, 2).reshape(8, width).astype(f32)
    gain_a, bias_a = vec[0], vec[1]
    proj_own = lax.dynamic_index_in_dim(
        proj_full.reshape(width, 3, C, half), c, 2, keepdims=False
    ).reshape(width, 3 * half)
    row_tags = tag_g[:, :, 0].reshape(length)
    row_pos = jnp.arange(length, dtype=jnp.int32)
    begin = sum(
        jnp.where(row_tags > s, jnp.sum((row_tags == s).astype(jnp.int32)), 0) for s in range(4)
    )
    begin = jnp.where(row_tags < 0, row_pos, begin)[None]
    inputs = tok_g.reshape(length, width).astype(f32)
    unit, factor = normed(inputs)
    normed_low = (unit * gain_a + bias_a).astype(bf16)
    projected = dot(normed_low, proj_own, 1, 0).astype(bf16)
    attended, attended_t, log_total = attention_forward(projected, begin)
    by_core = attended.reshape(Y, C, block, half).transpose(1, 0, 2, 3)
    other = swap(place, by_core, 2).reshape(Y * block, half)
    mine = lax.dynamic_index_in_dim(by_core, c, 0, keepdims=False).reshape(Y * block, half)
    attended_low = jnp.concatenate(
        [chosen((mine, other), c), chosen((other, mine), c)], axis=1
    )
    inputs_mine = (
        lax.dynamic_index_in_dim(tok_g, c, 1, keepdims=False)
        .reshape(Y * block, width)
        .astype(f32)
    )
    output, grad_middle, grad_attended, up_p, down_p, out_p, vec_two = dense(
        place,
        attended_low,
        lax.dynamic_index_in_dim(tok_g, c, 1, keepdims=False).reshape(Y * block, width),
        cot_g.reshape(Y * block, width),
        out_g,
        up_g,
        down_g,
        vec,
    )
    inputs_mine = lax.dynamic_index_in_dim(tok_g, c, 1, keepdims=False)
    proj_sum, out_sum, up_sum, down_sum, vec_sum, output, token_grad = backward(
        place,
        [out_p, up_p, down_p],
        proj_weight.shape,
        begin,
        projected,
        grad_attended,
        attended_t,
        log_total,
        normed_low.T,
        proj_own,
        inputs_mine.reshape(Y * block, width),
        grad_middle,
        output,
        vec,
        vec_two,
    )
    share = width // place.blk
    vec_sum = jnp.concatenate([vec_sum[:4], vec_sum[4:]], axis=1)
    vec_sum = lax.dynamic_slice(vec_sum, (0, index * share), (4, share))
    return (
        output,
        token_grad,
        proj_sum,
        out_sum,
        up_sum,
        down_sum.T,
        vec_sum[0],
        vec_sum[1],
        vec_sum[2],
        vec_sum[3],
    )


def solution(mesh):
    place = Place((mesh.shape["batch"], mesh.shape["blk"]))
    weight, vector = P("batch", "blk"), P("blk")
    row = P("batch", "blk", None)
    in_specs = (row,) + (weight,) * 4 + (vector,) * 4 + (weight,) * 2 + (row,)
    out_specs = (row, row) + (weight,) * 4 + (vector,) * 4
    return jax.shard_map(
        functools.partial(body, place),
        mesh=mesh,
        in_specs=in_specs,
        out_specs=out_specs,
        check_vma=False,
    )
```

```python
import functools

import jax
import jax.numpy as jnp
from jax import lax
from jax.experimental import pallas as pl
from jax.experimental.pallas import tpu as pltpu
from jax.sharding import PartitionSpec as P

HEADS = 12
HEAD_DIM = 64
CORES = 2
LANE_X = 2
MESH = pl.DeviceIdType.MESH
LOG2E = 1.4426950408889634
epsilon = 1e-05
masked = -1e30
bf16 = jnp.bfloat16
f32 = jnp.float32


def dot(left, right, left_dim, right_dim):
    return lax.dot_general(
        left, right, (((left_dim,), (right_dim,)), ((), ())), preferred_element_type=f32
    )


class Place:
    def __init__(self, sizes):
        self.batch, self.blk = sizes
        self.Z, self.X = self.batch // LANE_X, LANE_X
        self.Y, self.C = self.blk // CORES, CORES

    def here(self):
        b, d = lax.axis_index("batch"), lax.axis_index("blk")
        return b // self.X, b % self.X, d // self.C, d % self.C

    def device(self, z, x, p, c):
        return (z * self.X + x, p * self.C + c)


class Wire:
    def __init__(self, send_sem, recv_sem):
        self.send_sem, self.recv_sem, self.names = send_sem, recv_sem, {}

    def copy(self, name, src, dst, device):
        i = self.names.setdefault(name, len(self.names))
        return pltpu.make_async_remote_copy(
            src_ref=src,
            dst_ref=dst,
            send_sem=self.send_sem.at[i],
            recv_sem=self.recv_sem.at[i],
            device_id=device,
            device_id_type=MESH,
        )


def start_all(copies):
    for copy in copies:
        copy.start()


def arrive_all(copies):
    for copy in copies:
        copy.wait_recv()


def leave_all(copies):
    for copy in copies:
        copy.wait_send()


def first_rows(rows, sixths):
    return min(rows - 16, 16 * ((rows * sixths // 6) // 16)) if rows > 16 else 0


def greet(place, partners):
    barrier = pltpu.get_barrier_semaphore()
    for partner in partners:
        pl.semaphore_signal(barrier, inc=1, device_id=partner, device_id_type=MESH)
    pl.semaphore_wait(barrier, len(partners))


def partners_of(place):
    z, x, p, c = place.here()
    found = [place.device((z + k) % place.Z, x, p, c) for k in range(1, place.Z)]
    found += [place.device(z, 1 - x, p, c)]
    found += [place.device(z, x, (p + k) % place.Y, c) for k in range(1, place.Y)]
    found += [place.device(z, x, p, 1 - c)]
    return found


def head_masked(value, h, axis):
    index = lax.broadcasted_iota(jnp.int32, value.shape, axis)
    return jnp.where((index // HEAD_DIM) == h, value, jnp.zeros_like(value))


class Spreading:
    def __init__(self, place, wire, name, spots, shard, whole, sixths):
        self.place, self.wire, self.name, self.spots = place, wire, name, spots
        self.shard, self.whole = shard, whole
        self.rows = shard.shape[0]
        self.h = first_rows(self.rows, sixths)

    def zero(self):
        z, x, p, c = self.spots
        place = self.place
        found = []
        for k in range(1, place.Z):
            found.append(
                self.wire.copy(
                    (self.name, "z", k),
                    self.shard,
                    self.whole.at[p, c, z, x],
                    place.device((z + k) % place.Z, x, p, c),
                )
            )
        return found

    def one(self):
        z, x, p, c = self.spots
        place, h, r = self.place, self.h, self.rows
        low = self.whole.at[p, c, :, x, 0:h]
        found = [self.wire.copy((self.name, "xa"), low, low, place.device(z, 1 - x, p, c))]
        high = self.whole.at[p, c, :, x, h:r]
        for k in range(1, place.Y):
            found.append(
                self.wire.copy(
                    (self.name, "yb", k), high, high, place.device(z, x, (p + k) % place.Y, c)
                )
            )
        return found

    def two(self):
        z, x, p, c = self.spots
        place, h, r = self.place, self.h, self.rows
        low = self.whole.at[p, c, :, :, 0:h]
        found = [
            self.wire.copy(
                (self.name, "ya", k), low, low, place.device(z, x, (p + k) % place.Y, c)
            )
            for k in range(1, place.Y)
        ]
        high = self.whole.at[:, c, :, x, h:r]
        found.append(
            self.wire.copy((self.name, "xb"), high, high, place.device(z, 1 - x, p, c))
        )
        return found

    def three(self):
        z, x, p, c = self.spots
        plane = self.whole.at[:, c]
        return [self.wire.copy((self.name, "core"), plane, plane, self.place.device(z, x, p, 1 - c))]

    def go_one(self):
        arrive_all(self.zero())
        start_all(self.one())

    def go_two(self):
        arrive_all(self.one())
        start_all(self.two())

    def go_three(self):
        arrive_all(self.two())
        start_all(self.three())

    def leave(self):
        for copies in (self.zero(), self.one(), self.two(), self.three()):
            leave_all(copies)


def forward_kernel(place, n, BQ, *refs):
    shards, (tok, cot, tag, vec_in) = refs[: n + 1], refs[n + 1 : n + 5]
    outs = refs[n + 5 :]
    wholes = outs[:n]
    (tok_out, cot_out, vec_out, begin, proj_out, w_out, normedT_out, att_out, oT_out, lt) = outs[
        n : n + 10
    ]
    (
        proj_v, tok_v, tag_v, vec_v, n_v, nT, wv, pv, vT, att, oT,
        send_sem, recv_sem, local_sem,
    ) = outs[n + 10 :]
    spots = place.here()
    z, x, p, c = spots
    Z, X, Y, C = place.Z, place.X, place.Y, place.C
    D, W3 = wv.shape
    H = W3 // 3
    L = pv.shape[0]
    T = L // (Y * C)
    U = BQ // T
    pairs = H // 128
    nq = L // BQ
    wire = Wire(send_sem, recv_sem)
    sibling = place.device(z, x, p, 1 - c)
    flows = [
        Spreading(place, wire, m, spots, shards[m], proj_v if m == 0 else wholes[m - 1], 3)
        for m in range(n + 1)
    ]

    def local(i, src, dst):
        return pltpu.make_async_copy(src, dst, local_sem.at[i])

    def lane(offset, size):
        return pl.ds(pl.multiple_of(offset, 128), size)

    def line(offset, size):
        return pl.ds(pl.multiple_of(offset, 16), size)

    row_parts = (("vec", vec_in, vec_v), ("tag", tag, tag_v), ("tok", tok, tok_v))

    def along_y(what, src, dst):
        found = []
        for k in range(1, Y):
            to = (p + k) % Y
            piece = src if what == "vec" else src.at[to]
            found.append(
                wire.copy((what, "y", k), piece, dst.at[p, c], place.device(z, x, to, c))
            )
        return found

    def to_sibling_own(what, src, dst):
        piece = src if what == "vec" else src.at[p]
        return wire.copy((what, "own"), piece, dst.at[p, c], sibling)

    def to_sibling(what, dst):
        found = []
        for k in range(1, Y):
            q = (p + k) % Y
            found.append(wire.copy((what, "pass", k), dst.at[q, c], dst.at[q, c], sibling))
        return found

    def cot_sends():
        return [
            wire.copy(
                ("cot", k), cot.at[(p + k) % Y], cot_out.at[p], place.device(z, x, (p + k) % Y, c)
            )
            for k in range(1, Y)
        ]

    greet(place, partners_of(place))
    for part in row_parts:
        start_all(along_y(*part))
    for part in row_parts:
        to_sibling_own(*part).start()
    for flow in flows:
        start_all(flow.zero())
    kept = [local(m, shards[m], flows[m].whole.at[p, c, z, x]) for m in range(n + 1)]
    kept += [
        local(n + 1, vec_in, vec_v.at[p, c]),
        local(n + 2, tag.at[p], tag_v.at[p, c]),
        local(n + 3, tok.at[p], tok_v.at[p, c]),
        local(n + 4, cot.at[p], cot_out.at[p]),
    ]
    start_all(kept)
    arrive_all(along_y(*row_parts[0]))
    start_all(to_sibling("vec", vec_v))
    for copy in kept[:-1]:
        copy.wait()
    flows[0].go_one()
    to_sibling_own(*row_parts[0]).wait_recv()
    arrive_all(to_sibling("vec", vec_v))
    share = vec_v.shape[3]
    for q in range(Y):
        for i in range(C):
            lo = (q * C + i) * share
            vec_out[:, lo : lo + share] = vec_v[q, i, 0:8, :].astype(f32)
    gain, shift = vec_out[0:1, :], vec_out[1:2, :]

    def norm_block(q, i):
        unit, factor = normed(tok_v[q, i].astype(f32))
        low = (unit * gain + shift).astype(bf16)
        rows = line((q * C + i) * T, T)
        n_v[rows, :] = low
        nT[:, lane((q * C + i) * T, T)] = low.T

    norm_block(p, c)
    to_sibling_own(*row_parts[2]).wait_recv()
    norm_block(p, 1 - c)
    arrive_all(flows[0].one()[:1])
    start_all(flows[0].two()[:-1])
    for what, src, dst in row_parts[1:]:
        arrive_all(along_y(what, src, dst))
        start_all(to_sibling(what, dst))
    for k in range(1, Y):
        norm_block((p + k) % Y, c)
    arrive_all(to_sibling("tok", tok_v))
    for k in range(1, Y):
        norm_block((p + k) % Y, 1 - c)
    arrive_all(flows[0].one()[1:])
    start_all(flows[0].two()[-1:])
    flows[1].go_one()
    flows[2].go_one()
    saves = [
        local(n + 5, nT, normedT_out),
        local(n + 6, tok_v.at[:, c], tok_out),
    ]
    start_all(saves)
    to_sibling_own(*row_parts[1]).wait_recv()
    arrive_all(to_sibling("tag", tag_v))
    tags = [tag_v[q, i, 0:1, :] for q in range(Y) for i in range(C)]
    counts = []
    for s in range(4):
        hits = sum((t == s).astype(f32) for t in tags)
        counts.append(jnp.sum(hits, axis=1, keepdims=True).astype(jnp.int32))
    for b, t in enumerate(tags):
        first = sum(jnp.where(t > s, counts[s], 0) for s in range(4))
        position = lax.broadcasted_iota(jnp.int32, (1, T), 1) + b * T
        begin[:, b * T : (b + 1) * T] = jnp.where(t < 0, position, first)
    flows[0].go_three()
    arrive_all(flows[0].three())
    r, w = proj_v.shape[4:]
    for mine in range(C):

        @pl.when(c == mine)
        def _():
            for third in range(3):
                base = third * D + mine * H
                for d in range(Y * C):
                    a, b = max(base, d * w), min(base + H, (d + 1) * w)
                    if a >= b:
                        continue
                    to = third * H + a - base
                    for i in range(Z * X):
                        wv[i * r : (i + 1) * r, to : to + b - a] = proj_v[
                            d // C, d % C, i // X, i % X, :, a - d * w : b - d * w
                        ]

    def project(i, nothing):
        rows = line(i * BQ, BQ)
        pv[rows, :] = dot(n_v[rows, :], wv[...], 1, 0).astype(bf16)
        return nothing

    lax.fori_loop(0, nq, project, 0)
    vT[...] = pv[:, 2 * H :].T
    saves += [local(n + 7, pv, proj_out), local(n + 8, wv, w_out)]
    start_all(saves[2:])
    flows[1].go_two()
    flows[2].go_two()
    scale = HEAD_DIM ** (-0.5) * LOG2E

    def block_copies(qi):
        found = []
        for u in range(U):
            b = qi * U + u
            q, owner = b // C, b % C
            src = att.at[b * T : (b + 1) * T, :]
            dst = att_out.at[q * T : (q + 1) * T, lane(c * H, H)]
            found.append(
                (owner, local(n + 9 + q, src, dst), wire.copy(("att", q), src, dst, sibling))
            )
        return found

    def event(pair, number, *events):
        @pl.when(pair == number)
        def _():
            for e in events:
                e()

    for qi in range(nq):
        qs = slice(qi * BQ, (qi + 1) * BQ)
        d0 = qi * BQ
        if qi == nq - 1:
            cuts = [(0, d0, 1)] if d0 else []
        elif d0 > 256:
            cuts = [(0, 256, 1), (256, d0, 0)]
        else:
            cuts = [(0, d0, 1)] if d0 else []
        cuts.append((d0, d0 + BQ, 2))

        def one_pair(pair, nothing):
            cols = lane(pair * 128, 128)
            k_cols = lane(H + pair * 128, 128)
            qT = pv[qs, cols].T
            found = []
            for h in range(2):
                query = head_masked(qT, h, 0)
                rows = pl.ds(pl.multiple_of(pair * 128 + h * HEAD_DIM, HEAD_DIM), HEAD_DIM)
                parts = []
                for a, b, mode in cuts:
                    s = dot(pv[a:b, k_cols], query, 1, 0) * scale
                    if mode:
                        key_pos = lax.broadcasted_iota(jnp.int32, (b - a, BQ), 0) + a
                        visible = key_pos >= begin[:, qs]
                        if mode == 2:
                            query_pos = lax.broadcasted_iota(jnp.int32, (b - a, BQ), 1) + d0
                            visible = jnp.logical_and(visible, key_pos <= query_pos)
                        s = jnp.where(visible, s, masked)
                    parts.append(s)
                top = functools.reduce(
                    jnp.maximum, [jnp.max(s, axis=0, keepdims=True) for s in parts]
                )
                total, accum = 0.0, 0.0
                for (a, b, mode), s in zip(cuts, parts):
                    e = jnp.exp2(s - top)
                    total = total + jnp.sum(e, axis=0, keepdims=True)
                    accum = accum + dot(vT[rows, a:b], e.astype(bf16), 1, 0)
                result = accum / total
                oT[rows, qs] = result
                found.append(result)
                lt[pair, h : h + 1, qs] = top + jnp.log2(total)
            att[qs, cols] = jnp.concatenate(found, axis=0).astype(bf16).T
            if qi == nq - 1:
                event(pair, 0, flows[3].go_two)
            return nothing

        lax.fori_loop(0, pairs, one_pair, 0)
        for owner, keep, send in block_copies(qi):

            @pl.when(owner == c)
            def _():
                keep.start()

            @pl.when(owner != c)
            def _():
                send.start()

        if qi == 0:
            flows[3].go_one()
            start_all(cot_sends())
        if qi == nq - 2:
            flows[1].go_three()
            flows[2].go_three()
    last = local(n + 9 + Y, oT, oT_out)
    last.start()
    flows[3].go_three()
    for flow in flows[1:]:
        arrive_all(flow.three())
    for qi in range(nq):
        for owner, keep, send in block_copies(qi):

            @pl.when(owner == c)
            def _():
                keep.wait()

            @pl.when(owner != c)
            def _():
                send.wait_send()

            @pl.when(owner == c)
            def _():
                send.wait_recv()

    arrive_all(cot_sends())
    leave_all(cot_sends())
    for what, src, dst in row_parts:
        leave_all(along_y(what, src, dst))
        to_sibling_own(what, src, dst).wait_send()
        leave_all(to_sibling(what, dst))
    for flow in flows:
        flow.leave()
    for copy in saves + [last, kept[-1]]:
        copy.wait()


def forward(place, shards, tok, cot, tag, vec_in):
    n = len(shards) - 1
    Z, X, Y, C = place.Z, place.X, place.Y, place.C
    R, T, D = tok.shape
    L = Y * C * T
    H = D // C
    W3 = 3 * H
    BQ = 512
    pairs = H // 128
    inside = pl.BlockSpec(memory_space=pltpu.VMEM)
    anywhere = pl.BlockSpec(memory_space=pl.ANY)
    out_shape = [jax.ShapeDtypeStruct((Y, C, Z, X) + m.shape, bf16) for m in shards[1:]]
    out_shape += [
        jax.ShapeDtypeStruct((Y, T, D), bf16),
        jax.ShapeDtypeStruct((Y, T, D), bf16),
        jax.ShapeDtypeStruct((8, D), f32),
        jax.ShapeDtypeStruct((1, L), jnp.int32),
        jax.ShapeDtypeStruct((L, W3), bf16),
        jax.ShapeDtypeStruct((D, W3), bf16),
        jax.ShapeDtypeStruct((D, L), bf16),
        jax.ShapeDtypeStruct((Y * T, D), bf16),
        jax.ShapeDtypeStruct((H, L), f32),
        jax.ShapeDtypeStruct((pairs, 2, L), f32),
    ]
    each = (Z - 1) + 2 * Y + 1
    copies = (n + 1) * each + 3 * (2 * (Y - 1) + 1) + (Y - 1) + Y
    scratch = [
        pltpu.VMEM((Y, C, Z, X) + shards[0].shape, bf16),
        pltpu.VMEM((Y, C, T, D), bf16),
        pltpu.VMEM((Y, C) + tag.shape[1:], jnp.int32),
        pltpu.VMEM((Y, C) + vec_in.shape, bf16),
        pltpu.VMEM((L, D), bf16),
        pltpu.VMEM((D, L), bf16),
        pltpu.VMEM((D, W3), bf16),
        pltpu.VMEM((L, W3), bf16),
        pltpu.VMEM((H, L), bf16),
        pltpu.VMEM((L, H), bf16),
        pltpu.VMEM((H, L), f32),
        pltpu.SemaphoreType.DMA((copies,)),
        pltpu.SemaphoreType.DMA((copies,)),
        pltpu.SemaphoreType.DMA((n + 10 + Y,)),
    ]
    return pl.pallas_call(
        functools.partial(forward_kernel, place, n, BQ),
        out_shape=out_shape,
        in_specs=[anywhere] * (n + 5),
        out_specs=[anywhere] * (n + 2) + [inside] * 2 + [anywhere] * 5 + [inside],
        scratch_shapes=scratch,
        compiler_params=pltpu.CompilerParams(
            collective_id=0, has_side_effects=True, vmem_limit_bytes=60 << 20
        ),
        name="forward",
    )(*shards, tok, cot, tag, vec_in)


class Summing:
    def __init__(self, place, wire, name, spots, acc, xa, yb, ya, xb, zz):
        self.place, self.wire, self.name, self.spots = place, wire, name, spots
        self.acc, self.xa, self.yb, self.ya, self.xb, self.zz = acc, xa, yb, ya, xb, zz
        self.rows = acc.shape[3]
        self.h = xa.shape[2]

    def one(self):
        z, x, p, c = self.spots
        place, h, r = self.place, self.h, self.rows
        side = place.device(z, 1 - x, p, c)
        found = [
            self.wire.copy((self.name, "xa"), self.acc.at[:, :, 1 - x, 0:h], self.xa, side)
        ]
        for k in range(1, place.Y):
            to = (p + k) % place.Y
            found.append(
                self.wire.copy(
                    (self.name, "yb", k),
                    self.acc.at[to, :, :, h:r],
                    self.yb.at[k - 1],
                    place.device(z, x, to, c),
                )
            )
        return found

    def two(self):
        z, x, p, c = self.spots
        place, h, r = self.place, self.h, self.rows
        found = []
        for k in range(1, place.Y):
            to = (p + k) % place.Y
            found.append(
                self.wire.copy(
                    (self.name, "ya", k),
                    self.acc.at[to, :, x, 0:h],
                    self.ya.at[k - 1],
                    place.device(z, x, to, c),
                )
            )
        side = place.device(z, 1 - x, p, c)
        found.append(
            self.wire.copy((self.name, "xb"), self.acc.at[p, :, 1 - x, h:r], self.xb, side)
        )
        return found

    def three(self):
        z, x, p, c = self.spots
        place = self.place
        found = []
        for k in range(1, place.Z):
            to = (z + k) % place.Z
            found.append(
                self.wire.copy(
                    (self.name, "z", k),
                    self.acc.at[p, to, x],
                    self.zz.at[k - 1],
                    place.device(to, x, p, c),
                )
            )
        return found

    def add_one(self):
        z, x, p, c = self.spots
        place, h, r, acc = self.place, self.h, self.rows, self.acc
        ones = self.one()
        ones[0].wait_recv()

        def low(i, nothing):
            a, b = i // place.Z, i % place.Z
            total = acc[a, b, x, 0:h].astype(f32) + self.xa[a, b].astype(f32)
            acc[a, b, x, 0:h] = total.astype(bf16)
            return nothing

        lax.fori_loop(0, place.Y * place.Z, low, 0)
        twos = self.two()
        start_all(twos[:-1])
        arrive_all(ones[1:])

        def high(i, nothing):
            a, b = i // place.X, i % place.X
            total = acc[p, a, b, h:r].astype(f32)
            for k in range(place.Y - 1):
                total = total + self.yb[k, a, b].astype(f32)
            acc[p, a, b, h:r] = total.astype(bf16)
            return nothing

        lax.fori_loop(0, place.Z * place.X, high, 0)
        twos[-1].start()

    def add_two(self):
        z, x, p, c = self.spots
        place, h, r, acc = self.place, self.h, self.rows, self.acc
        arrive_all(self.two())

        def both(i, nothing):
            total = acc[p, i, x, 0:h].astype(f32)
            for k in range(place.Y - 1):
                total = total + self.ya[k, i].astype(f32)
            acc[p, i, x, 0:h] = total.astype(bf16)
            total = acc[p, i, x, h:r].astype(f32) + self.xb[i].astype(f32)
            acc[p, i, x, h:r] = total.astype(bf16)
            return nothing

        lax.fori_loop(0, place.Z, both, 0)
        start_all(self.three())

    def finish(self, target):
        z, x, p, c = self.spots
        arrive_all(self.three())
        total = self.acc[p, z, x].astype(f32)
        for k in range(self.place.Z - 1):
            total = total + self.zz[k].astype(f32)
        target[...] = total

    def leave(self):
        leave_all(self.one())
        leave_all(self.two())
        leave_all(self.three())


def backward_kernel(place, n, BQ, *refs):
    (begin, proj, ga, oT_in, lt, normedT, w_in, tok, gm, out_in, vec, vec_two) = refs[:12]
    parts = refs[12 : 12 + n]
    outs = refs[12 + n :]
    sums, (vec_out, out_home, tg_home) = outs[: n + 1], outs[n + 1 : n + 4]
    landing = outs[n + 4 : 2 * n + 4]
    rest = outs[2 * n + 4 :]
    (
        pv, do, oT, wv, kT, dk, dv, nT, pacc, p_recv,
        keep, g_send, g_recv, tok_v, gm_v, grads, v0, v1, v2, v3, vc, vy, vx, vz,
    ) = rest[:24]
    buffers = rest[24 : 24 + 6 * (n + 1)]
    send_sem, recv_sem, local_sem = rest[24 + 6 * (n + 1) :]
    tg_v = g_recv
    spots = place.here()
    z, x, p, c = spots
    Z, X, Y, C = place.Z, place.X, place.Y, place.C
    L, W3 = pv.shape
    H = W3 // 3
    D = wv.shape[0]
    T = L // (Y * C)
    pairs = H // 128
    nq = L // BQ
    scale = HEAD_DIM ** (-0.5) * LOG2E
    scale_back = HEAD_DIM ** (-0.5)
    wire = Wire(send_sem, recv_sem)
    sibling = place.device(z, x, p, 1 - c)
    beside = place.device(z, 1 - x, p, c)
    adds = [
        Summing(place, wire, m, spots, *buffers[6 * m : 6 * m + 6]) for m in range(n + 1)
    ]

    def local(i, src, dst):
        return pltpu.make_async_copy(src, dst, local_sem.at[i])

    def lane(offset, size):
        return pl.ds(pl.multiple_of(offset, 128), size)

    def line(offset, size):
        return pl.ds(pl.multiple_of(offset, 16), size)

    def grad_swap():
        return [
            wire.copy(
                ("ga", q),
                ga.at[q * T : (q + 1) * T, lane((1 - c) * H, H)],
                do.at[line((2 * q + c) * T, T), :],
                sibling,
            )
            for q in range(Y)
        ]

    def core_sends(m):
        return [wire.copy(("core", m), parts[m].at[:, 1 - c], landing[m], sibling)]

    def out_sends():
        found = []
        for k in range(1, Y):
            to = (p + k) % Y
            found.append(
                wire.copy(
                    ("out", k), out_in.at[line(to * T, T)], out_home.at[p], place.device(z, x, to, c)
                )
            )
        return found

    greet(place, partners_of(place))
    start_all(grad_swap())
    own = [
        local(q, ga.at[q * T : (q + 1) * T, lane(c * H, H)], do.at[line((2 * q + c) * T, T), :])
        for q in range(Y)
    ]
    def out_fetch(qi):
        return local(Y + 1, oT_in.at[:, lane(qi * BQ, BQ)], oT)

    loads = [local(Y, proj, pv), local(Y + 2, w_in, wv)]
    out_fetch(nq - 1).start()
    out_own = local(Y + 3, out_in.at[line(p * T, T)], out_home.at[p])
    acc_own = [
        local(Y + 4 + m, parts[m].at[:, c], adds[m + 1].acc) for m in range(n)
    ]
    start_all(own + loads)
    for m in range(n):
        start_all(core_sends(m))
    start_all(out_sends())
    start_all(acc_own + [out_own])
    row_sem = Y + 4 + n

    def core_add(m):
        arrive_all(core_sends(m))
        acc_own[m].wait()
        acc, other = adds[m + 1].acc, landing[m]

        def one(i, nothing):
            a, b, d = i // (Z * X), (i // X) % Z, i % X
            total = acc[a, b, d].astype(f32) + other[a, b, d].astype(f32)
            acc[a, b, d] = total.astype(bf16)
            return nothing

        lax.fori_loop(0, Y * Z * X, one, 0)
        start_all(adds[m + 1].one())

    for copy in loads:
        copy.wait()
    kT[...] = pv[:, H : 2 * H].T
    dk[...] = jnp.zeros_like(dk)
    dv[...] = jnp.zeros_like(dv)
    pacc[...] = jnp.zeros_like(pacc)
    grads[...] = jnp.zeros_like(grads)
    for copy in own:
        copy.wait()
    arrive_all(grad_swap())

    U = BQ // T
    gain = vec[0:1, :]

    def sub_blocks(qi):
        found = []
        for u in range(U):
            block = qi * U + u
            found.append((u, block // C, block % C))
        return found

    reserved = send_sem.shape[0] - 3 * Y

    def g_wire(q):
        return pltpu.make_async_remote_copy(
            src_ref=g_send.at[q],
            dst_ref=g_recv.at[q],
            send_sem=send_sem.at[reserved + q],
            recv_sem=recv_sem.at[reserved + q],
            device_id=sibling,
            device_id_type=MESH,
        )

    def home_from(k):
        q = (p + k) % Y
        return pltpu.make_async_remote_copy(
            src_ref=tg_v.at[p],
            dst_ref=tg_home.at[q],
            send_sem=send_sem.at[reserved + Y + q],
            recv_sem=recv_sem.at[reserved + 2 * Y + q],
            device_id=place.device(z, x, q, c),
            device_id_type=MESH,
        )

    def home_to(q):
        return pltpu.make_async_remote_copy(
            src_ref=tg_v.at[q],
            dst_ref=tg_home.at[p],
            send_sem=send_sem.at[reserved + Y + q],
            recv_sem=recv_sem.at[reserved + 2 * Y + p],
            device_id=place.device(z, x, q, c),
            device_id_type=MESH,
        )

    def block_done(qi):
        qs = line(qi * BQ, BQ)
        fetch = local(row_sem, normedT.at[:, lane(qi * BQ, BQ)], nT)
        fetch.start()
        pv[qs, H : 2 * H] = (dk[qs, :] * scale_back).astype(bf16)
        pv[qs, 2 * H :] = dv[qs, :].astype(bf16)
        g = dot(pv[qs, :], wv[...], 1, 1)
        for u, q, owner in sub_blocks(qi):
            rows = slice(u * T, (u + 1) * T)

            @pl.when(owner == c)
            def _():
                keep[u // C] = g[rows, :]

            @pl.when(owner != c)
            def _():
                g_send[q] = g[rows, :].astype(bf16)
                g_wire(q).start()

        fetch.wait()
        pacc[...] += dot(nT[...], pv[qs, :], 1, 0)

    def token_rows(qi):
        for u, q, owner in sub_blocks(qi):

            @pl.when(owner == c)
            def _():
                a = local(row_sem, tok.at[line(q * T, T)], tok_v)
                b = local(row_sem + 1, gm.at[line(q * T, T)], gm_v)
                a.start()
                b.start()
                g_wire(q).wait_recv()
                grad = keep[u // C] + g_recv[q].astype(f32)
                a.wait()
                unit, factor = normed(tok_v[...].astype(f32))
                grads[0:1, :] += jnp.sum(grad * unit, axis=0, keepdims=True)
                grads[1:2, :] += jnp.sum(grad, axis=0, keepdims=True)
                b.wait()
                tg_v[q] = (gm_v[...] + norm_back(grad, gain, unit, factor)).astype(bf16)

                @pl.when(q == p)
                def _():
                    local(row_sem + 2, tg_v.at[q], tg_home.at[p]).start()

                @pl.when(q != p)
                def _():
                    home_to(q).start()

    def step(s, nothing):
        qi = nq - 1 - s // pairs
        pair = s % pairs
        qs = line(qi * BQ, BQ)
        ql = lane(qi * BQ, BQ)
        cols = lane(pair * 128, 128)
        k_cols, v_cols = lane(H + pair * 128, 128), lane(2 * H + pair * 128, 128)
        q_val, do_val = pv[qs, cols], do[qs, cols]
        qT_val, doT_val = q_val.T, do_val.T
        heads = []

        @pl.when(pair == 0)
        def _():
            out_fetch(qi).wait()

        for h in range(2):
            rows = slice(h * HEAD_DIM, (h + 1) * HEAD_DIM)
            head_rows = pl.ds(pl.multiple_of(pair * 128 + h * HEAD_DIM, HEAD_DIM), HEAD_DIM)
            delta = jnp.sum(
                doT_val[rows, :].astype(f32) * oT[head_rows, :], axis=0, keepdims=True
            )
            heads.append(
                (
                    head_masked(qT_val, h, 0),
                    head_masked(doT_val, h, 0),
                    head_masked(q_val, h, 1),
                    head_masked(do_val, h, 1),
                    delta,
                    lt[pair, h : h + 1, ql],
                    head_rows,
                )
            )

        @pl.when(jnp.logical_and(pair == pairs - 1, qi > 0))
        def _():
            out_fetch(qi - 1).start()

        def tile(kj, dqs, mode):
            ks = line(kj * BQ, BQ)
            kl = lane(kj * BQ, BQ)
            if mode:
                key_pos = lax.broadcasted_iota(jnp.int32, (BQ, BQ), 0)
                visible = key_pos >= (begin[:, ql] - kj * BQ)
                if mode == 2:
                    query_pos = lax.broadcasted_iota(jnp.int32, (BQ, BQ), 1)
                    visible = jnp.logical_and(visible, key_pos <= query_pos)
            more_dv, more_dk, found = 0.0, 0.0, []
            for h in range(2):
                query, grad, q_nat, do_nat, delta, log_total, head_rows = heads[h]
                sc = dot(pv[ks, k_cols], query, 1, 0) * scale
                prob = jnp.exp2(sc - log_total)
                if mode:
                    prob = jnp.where(visible, prob, 0.0)
                dp = dot(pv[ks, v_cols], grad, 1, 0)
                ds = (prob * (dp - delta)).astype(bf16)
                more_dv = more_dv + dot(prob.astype(bf16), do_nat, 1, 0)
                more_dk = more_dk + dot(ds, q_nat, 1, 0)
                found.append(dqs[h] + dot(kT[head_rows, kl], ds, 1, 0))
            dv[ks, cols] += more_dv
            dk[ks, cols] += more_dk
            return tuple(found)

        zero = jnp.zeros((HEAD_DIM, BQ), f32)
        dqs = tile(qi, (zero, zero), 2)

        def last(d):
            return lax.fori_loop(0, qi, lambda kj, e: tile(kj, e, 1), d)

        def others(d):
            d = lax.cond(qi > 0, lambda e: tile(0, e, 1), lambda e: e, d)
            return lax.fori_loop(1, qi, lambda kj, e: tile(kj, e, 0), d)

        dqs = lax.cond(qi == nq - 1, last, others, dqs)
        dq = jnp.concatenate(dqs, axis=0) * scale_back
        pv[qs, cols] = dq.astype(bf16).T

        def at(number, *events):
            @pl.when(s == number)
            def _():
                for event in events:
                    event()

        @pl.when(pair == pairs - 1)
        def _():
            block_done(qi)

        @pl.when(jnp.logical_and(pair == 0, qi < nq - 1))
        def _():
            token_rows(qi + 1)

        def do_it(f, *args):
            return lambda: f(*args)

        out_m, up_m, down_m = 0, 1, 2
        at(0, do_it(core_add, down_m))
        at(1, do_it(core_add, out_m))
        at(3, adds[up_m + 1].add_one)
        at(7, adds[up_m + 1].add_two)
        at(8, adds[down_m + 1].add_one)
        at(9, adds[out_m + 1].add_one)
        return nothing

    core_add(1)
    lax.fori_loop(0, nq * pairs, step, 0)
    p_send = pv.at[0:D, :]
    p_send[...] = pacc[...].astype(bf16)
    p_swap = wire.copy("p", p_send, p_recv, sibling)
    p_swap.start()
    adds[3].add_two()
    token_rows(0)
    p_swap.wait_recv()
    acc = adds[0].acc
    r, w = acc.shape[3:]
    for mine in range(C):

        @pl.when(c == mine)
        def _():
            for q in range(Y):
                low_col = w * (C * q + mine)
                for third in range(3):
                    for half in range(C):
                        base = third * D + half * H
                        a, b = max(base, low_col), min(base + H, low_col + w)
                        if a >= b:
                            continue
                        source = p_send if half == mine else p_recv
                        off = third * H - base
                        for i in range(Z * X):
                            acc[q, i // X, i % X, :, a - low_col : b - low_col] = source[
                                i * r : (i + 1) * r, a + off : b + off
                            ]

    start_all(adds[0].one())
    grads[2:4, :] = vec_two[...]
    v0[0:4, :] = grads[0:4, 0:H]
    v0[4:8, :] = grads[0:4, H:]
    v_core = wire.copy("vc", v0, vc, sibling)
    v_core.start()
    adds[1].add_two()
    v_core.wait_recv()
    v1[...] = v0[...] + vc[...]
    v_y = [
        wire.copy(("vy", k), v1, vy.at[k - 1], place.device(z, x, (p + k) % Y, c))
        for k in range(1, Y)
    ]
    start_all(v_y)
    adds[2].finish(sums[2])
    adds[0].add_one()
    arrive_all(v_y)
    total = v1[...]
    for k in range(Y - 1):
        total = total + vy[k]
    v2[...] = total
    v_x = wire.copy("vx", v2, vx, beside)
    v_x.start()
    adds[3].finish(sums[3])
    adds[0].add_two()
    v_x.wait_recv()
    v3[...] = v2[...] + vx[...]
    v_z = [
        wire.copy(("vz", k), v3, vz.at[k - 1], place.device((z + k) % Z, x, p, c))
        for k in range(1, Z)
    ]
    start_all(v_z)
    adds[1].finish(sums[1])
    adds[0].finish(sums[0])
    arrive_all(v_z)
    total = v3[...]
    for k in range(Z - 1):
        total = total + vz[k]
    vec_out[...] = total
    for k in range(1, Y):
        home_from(k).wait_recv()
        home_to((p + k) % Y).wait_send()
    local(row_sem + 2, tg_v.at[p], tg_home.at[p]).wait()
    out_own.wait()
    arrive_all(out_sends())
    leave_all(out_sends())
    leave_all(grad_swap())
    for q in range(Y):
        g_wire(q).wait_send()
    for m in range(n):
        leave_all(core_sends(m))
    p_swap.wait_send()
    v_core.wait_send()
    leave_all(v_y)
    v_x.wait_send()
    leave_all(v_z)
    for summing in adds:
        summing.leave()


def backward(place, parts, proj_shape, begin, proj, ga, oT, lt, normedT, w_own, tok, gm, out, vec, vec_two):
    n = len(parts)
    Z, X, Y, C = place.Z, place.X, place.Y, place.C
    L, W3 = proj.shape
    H = W3 // 3
    D = w_own.shape[0]
    T = L // (Y * C)
    BQ = 512
    inside = pl.BlockSpec(memory_space=pltpu.VMEM)
    anywhere = pl.BlockSpec(memory_space=pl.ANY)
    shapes = [proj_shape] + [part.shape[4:] for part in parts]
    sixths = [3, 4, 5, 5]
    out_shape = [jax.ShapeDtypeStruct(shape, f32) for shape in shapes]
    out_shape += [
        jax.ShapeDtypeStruct((8, H), f32),
        jax.ShapeDtypeStruct((Y, T, D), bf16),
        jax.ShapeDtypeStruct((Y, T, D), bf16),
    ]
    scratch = [pltpu.VMEM((Y, Z, X) + shape, bf16) for shape in shapes[1:]]
    scratch += [
        pltpu.VMEM((L, W3), bf16),
        pltpu.VMEM((L, H), bf16),
        pltpu.VMEM((H, BQ), f32),
        pltpu.VMEM((D, W3), bf16),
        pltpu.VMEM((H, L), bf16),
        pltpu.VMEM((L, H), f32),
        pltpu.VMEM((L, H), f32),
        pltpu.VMEM((D, BQ), bf16),
        pltpu.VMEM((D, W3), f32),
        pltpu.VMEM((D, W3), bf16),
        pltpu.VMEM((max(1, BQ // T // C), T, D), f32),
        pltpu.VMEM((Y, T, D), bf16),
        pltpu.VMEM((Y, T, D), bf16),
        pltpu.VMEM((T, D), bf16),
        pltpu.VMEM((T, D), f32),
    ]
    scratch += [pltpu.VMEM((8, D), f32)] + [pltpu.VMEM((8, H), f32)] * 5
    scratch += [
        pltpu.VMEM((Y - 1, 8, H), f32),
        pltpu.VMEM((8, H), f32),
        pltpu.VMEM((Z - 1, 8, H), f32),
    ]
    for shape, part in zip(shapes, sixths):
        r, w = shape
        h = first_rows(r, part)
        scratch += [
            pltpu.VMEM((Y, Z, X, r, w), bf16),
            pltpu.VMEM((Y, Z, h, w), bf16),
            pltpu.VMEM((Y - 1, Z, X, r - h, w), bf16),
            pltpu.VMEM((Y - 1, Z, h, w), bf16),
            pltpu.VMEM((Z, r - h, w), bf16),
            pltpu.VMEM((Z - 1, r, w), bf16),
        ]
    each = 1 + (Y - 1) + (Y - 1) + 1 + (Z - 1)
    copies = Y + n + (Y - 1) + (n + 1) * each + 2 + (Y - 1) + 1 + (Z - 1) + 3 * Y
    scratch += [
        pltpu.SemaphoreType.DMA((copies,)),
        pltpu.SemaphoreType.DMA((copies,)),
        pltpu.SemaphoreType.DMA((Y + 4 + n + 3,)),
    ]
    return pl.pallas_call(
        functools.partial(backward_kernel, place, n, BQ),
        out_shape=out_shape,
        in_specs=[inside] + [anywhere] * 3 + [inside] + [anywhere] * 5 + [inside] * 2 + [anywhere] * n,
        out_specs=[inside] * (n + 2) + [anywhere] * 2,
        scratch_shapes=scratch,
        compiler_params=pltpu.CompilerParams(
            collective_id=1, has_side_effects=True, vmem_limit_bytes=63 << 20
        ),
        name="backward",
    )(begin, proj, ga, oT, lt, normedT, w_own, tok, gm, out, vec, vec_two, *parts)


def gelu_both(u):
    k = 0.7978845608028654
    square = u * u
    t = jnp.tanh(k * u * (1.0 + 0.044715 * square))
    half = 0.5 * (1.0 + t)
    slope = half + 0.5 * k * u * (1.0 - t * t) * (1.0 + 3 * 0.044715 * square)
    return u * half, slope


def dense_kernel(
    place, aligned, att, tok, cot, out_w, up_w, down_w, vec,
    output, gm_out, ga_out, up_p, down_p, out_p, vec_out,
    att_v, tok_v, cot_v, out_v, up_v, down_v, out_full, mid, n2, act, gh, n2T, cotT, g2,
    wide, stage, load_sem, store_sem,
):
    S, nb = place.blk, place.batch
    M, D = att_v.shape
    FF = up_v.shape[1]
    J = FF // D
    loads = []

    def load(src, dst):
        copy = pltpu.make_async_copy(src, dst, load_sem.at[len(loads)])
        copy.start()
        loads.append(copy)
        return copy

    first = [load(att, att_v), load(tok, tok_v), load(out_w, out_v)]
    first.append(load(cot, cot_v))
    if aligned:
        w = up_w.shape[2]
        weights = [load(up_w.at[d], up_v.at[:, d * w : (d + 1) * w]) for d in range(S)]
        r, w = down_w.shape[2:]
        for d in range(S):
            for b in range(nb):
                weights.append(
                    load(
                        down_w.at[d, b],
                        down_v.at[d * r : (d + 1) * r, b * w : (b + 1) * w],
                    )
                )
    else:
        weights = [load(up_w, up_v), load(down_w, down_v)]
    for copy in first:
        copy.wait()
    w = out_v.shape[2]
    for d in range(S):
        out_full[:, d * w : (d + 1) * w] = out_v[d]
    gain, shift = vec[2:3, :], vec[3:4, :]
    T = M // 2
    for t in range(2):
        ts = slice(t * T, (t + 1) * T)
        middle = tok_v[ts, :].astype(f32) + dot(att_v[ts, :], out_full[...], 1, 0)
        unit, factor = normed(middle)
        mid[ts, :] = middle
        n2[ts, :] = (unit * gain + shift).astype(bf16)
    for copy in weights:
        copy.wait()
    n2T[...] = n2[...].T
    cotT[...] = cot_v[...].T
    gain_sum = jnp.zeros((1, D), f32)
    shift_sum = jnp.zeros((1, D), f32)
    stores = [None, None]
    for t in range(2):
        ts = slice(t * T, (t + 1) * T)

        def chunk(j, nothing):
            js = pl.ds(pl.multiple_of(j * D, D), D)
            h = dot(n2[ts, :], up_v[:, js], 1, 0)
            g = dot(cot_v[ts, :], down_v[:, js], 1, 0)
            a, slope = gelu_both(h)
            a = a.astype(bf16)
            b = (g * slope).astype(bf16)
            act[ts, js] = a
            gh[ts, js] = b
            more_out = dot(a, down_v[:, js], 1, 1)
            more_g2 = dot(b, up_v[:, js], 1, 1)
            mid[ts, :] += more_out

            @pl.when(j == 0)
            def _():
                g2[...] = more_g2

            @pl.when(j > 0)
            def _():
                g2[...] += more_g2

            return nothing

        middle = mid[ts, :]
        unit, factor = normed(middle)
        lax.fori_loop(0, J, chunk, 0)
        middle_unit, middle_factor = unit, factor
        wide[...] = middle_unit
        if stores[0] is not None:
            for copy in stores:
                copy.wait()
        stage[0, 0:T, :] = mid[ts, :].astype(bf16)
        copy = pltpu.make_async_copy(stage.at[0, 0:T], output.at[ts], store_sem.at[0])
        copy.start()
        stores[0] = copy
        grad = g2[...]
        n = wide[...]
        gain_sum = gain_sum + jnp.sum(grad * n, axis=0, keepdims=True)
        shift_sum = shift_sum + jnp.sum(grad, axis=0, keepdims=True)
        gm = cot_v[ts, :].astype(f32) + norm_back(grad, gain, n, middle_factor)
        mid[ts, :] = gm
        low = gm.astype(bf16)
        n2[ts, :] = low
        stage[1, 0:T, :] = dot(low, out_full[...], 1, 1).astype(bf16)
        copy = pltpu.make_async_copy(stage.at[1, 0:T], ga_out.at[ts], store_sem.at[1])
        copy.start()
        stores[1] = copy
    for copy in stores:
        copy.wait()
    save = pltpu.make_async_copy(mid, gm_out, store_sem.at[2])
    save.start()
    vec_out[0:1, :] = gain_sum
    vec_out[1:2, :] = shift_sum
    pending = [[], []]
    turn = 0

    def put(value, pieces):
        nonlocal turn
        slot = turn % 2
        turn += 1
        for copy in pending[slot]:
            copy.wait()
        stage[slot, 0 : value.shape[0], :] = value
        pending[slot] = []
        for i, (rows, columns, dst) in enumerate(pieces):
            copy = pltpu.make_async_copy(
                stage.at[slot, rows, columns], dst, store_sem.at[3 + slot * 64 + i]
            )
            copy.start()
            pending[slot].append(copy)

    every = slice(0, D)
    for j in range(J):
        js = slice(j * D, (j + 1) * D)
        value = dot(n2T[...], gh[:, js], 1, 0).astype(bf16)
        if aligned:
            w = up_p.shape[2]
            pieces = [
                (every, slice(i * w, (i + 1) * w), up_p.at[j * D // w + i]) for i in range(D // w)
            ]
        else:
            pieces = [(every, every, up_p.at[:, js])]
        put(value, pieces)
        value = dot(cotT[...], act[:, js], 1, 0).astype(bf16)
        if aligned:
            r, w = down_p.shape[2:]
            pieces = [
                (
                    slice(d * r, (d + 1) * r),
                    slice(i * w, (i + 1) * w),
                    down_p.at[d, j * D // w + i],
                )
                for d in range(S)
                for i in range(D // w)
            ]
        else:
            pieces = [(every, every, down_p.at[:, js])]
        put(value, pieces)
    value = dot(att_v[...], n2[...], 0, 0).astype(bf16)
    for copy in pending[turn % 2]:
        copy.wait()
    pending[turn % 2] = []
    stage[turn % 2, 0:D, :] = value
    w = out_v.shape[2]
    for d in range(S):
        out_v[d] = stage[turn % 2, 0:D, d * w : (d + 1) * w]
    copy = pltpu.make_async_copy(out_v, out_p, store_sem.at[3])
    for group in pending:
        for other in group:
            other.wait()
    copy.start()
    copy.wait()
    save.wait()


def dense(place, att, tok, cot, out_g, up_g, down_g, vec):
    M, D = att.shape
    S, nb = place.blk, place.batch
    aligned = up_g.shape[-1] % 128 == 0 and down_g.shape[-1] % 128 == 0
    out_w = out_g.reshape(S, D, -1)
    FF = S * up_g.shape[-1]
    if aligned:
        up_w = up_g.reshape(S, D, -1)
        down_w = down_g.reshape((S, nb) + down_g.shape[-2:])
    else:
        up_w, down_w = joined(up_g, 0), joined(down_g, 1)
    anywhere = pl.BlockSpec(memory_space=pl.ANY)
    inside = pl.BlockSpec(memory_space=pltpu.VMEM)
    loads = 8 + S + S * nb
    results = pl.pallas_call(
        functools.partial(dense_kernel, place, aligned),
        out_shape=[
            jax.ShapeDtypeStruct((M, D), bf16),
            jax.ShapeDtypeStruct((M, D), f32),
            jax.ShapeDtypeStruct((M, D), bf16),
            jax.ShapeDtypeStruct(up_w.shape, bf16),
            jax.ShapeDtypeStruct(down_w.shape, bf16),
            jax.ShapeDtypeStruct(out_w.shape, bf16),
            jax.ShapeDtypeStruct((2, D), f32),
        ],
        in_specs=[anywhere] * 6 + [inside],
        out_specs=[anywhere] * 6 + [inside],
        scratch_shapes=[
            pltpu.VMEM((M, D), bf16),
            pltpu.VMEM((M, D), bf16),
            pltpu.VMEM((M, D), bf16),
            pltpu.VMEM(out_w.shape, bf16),
            pltpu.VMEM((D, FF), bf16),
            pltpu.VMEM((D, FF), bf16),
            pltpu.VMEM((D, D), bf16),
            pltpu.VMEM((M, D), f32),
            pltpu.VMEM((M, D), bf16),
            pltpu.VMEM((M, FF), bf16),
            pltpu.VMEM((M, FF), bf16),
            pltpu.VMEM((D, M), bf16),
            pltpu.VMEM((D, M), bf16),
            pltpu.VMEM((M // 2, D), f32),
            pltpu.VMEM((M // 2, D), f32),
            pltpu.VMEM((2, max(D, M // 2), D), bf16),
            pltpu.SemaphoreType.DMA((loads,)),
            pltpu.SemaphoreType.DMA((3 + 128,)),
        ],
        compiler_params=pltpu.CompilerParams(vmem_limit_bytes=62 << 20),
        name="dense",
    )(att, tok, cot, out_w, up_w, down_w, vec)
    output, gm, ga, up_p, down_p, out_p, vec_grads = results
    out_p = out_p.reshape(out_g.shape)
    if aligned:
        up_p, down_p = up_p.reshape(up_g.shape), down_p.reshape(down_g.shape)
    else:
        up_p, down_p = parted(up_p, place, 0), parted(down_p, place, 1)
    return output, gm, ga, up_p, down_p, out_p, vec_grads


def normed(values):
    average = jnp.mean(values, axis=-1, keepdims=True)
    centered = values - average
    variance = jnp.mean(centered * centered, axis=-1, keepdims=True)
    factor = lax.rsqrt(variance + epsilon)
    return centered * factor, factor


def norm_back(grad, gain, unit, factor):
    e = grad * gain
    return factor * (
        e - jnp.mean(e, axis=-1, keepdims=True) - unit * jnp.mean(e * unit, axis=-1, keepdims=True)
    )


def joined(gathered, axis):
    Y, C, Z, X, r, w = gathered.shape
    if axis == 0:
        return gathered.reshape(Y * C, Z * X * r, w).transpose(1, 0, 2).reshape(Z * X * r, -1)
    return gathered.reshape(Y * C, Z * X, r, w).transpose(0, 2, 1, 3).reshape(Y * C * r, -1)


def parted(whole, place, axis):
    Y, C, Z, X = place.Y, place.C, place.Z, place.X
    rows, columns = whole.shape
    if axis == 0:
        value = whole.reshape(Z * X, rows // (Z * X), Y * C, columns // (Y * C))
        value = value.transpose(2, 0, 1, 3)
    else:
        value = whole.reshape(Y * C, rows // (Y * C), Z * X, columns // (Z * X))
        value = value.transpose(0, 2, 1, 3)
    return value.reshape((Y, C, Z, X) + value.shape[2:])


def body(
    place,
    tokens,
    proj_weight,
    out_weight,
    up_weight,
    down_weight,
    gain_one,
    bias_one,
    gain_two,
    bias_two,
    segments,
    present,
    cotangent,
):
    rows, block, width = tokens.shape
    Y = place.Y
    index = lax.axis_index("blk")
    query_pos = index * block + jnp.arange(block, dtype=jnp.int32)
    local_tags = jnp.where(present == 1, segments, -1 - query_pos[None, :])
    tag_in = jnp.broadcast_to(local_tags[:, None, :], (rows, 8, block))
    vec_in = jnp.stack([gain_one, bias_one, gain_two, bias_two])
    vec_in = jnp.pad(vec_in, ((0, 12), (0, 0)))
    (
        out_g, up_g, down_g, tok_mine, cot_mine, vec, begin, projected, proj_own, normed_t,
        attended_low, attended_t, log_total,
    ) = forward(
        place,
        [proj_weight, out_weight, up_weight, down_weight.T],
        tokens,
        cotangent,
        tag_in,
        vec_in,
    )
    tok_mine = tok_mine.reshape(Y * block, width)
    output, grad_middle, grad_attended, up_p, down_p, out_p, vec_two = dense(
        place,
        attended_low,
        tok_mine,
        cot_mine.reshape(Y * block, width),
        out_g,
        up_g,
        down_g,
        vec,
    )
    proj_sum, out_sum, up_sum, down_sum, vec_sum, output, token_grad = backward(
        place,
        [out_p, up_p, down_p],
        proj_weight.shape,
        begin,
        projected,
        grad_attended,
        attended_t,
        log_total,
        normed_t,
        proj_own,
        tok_mine,
        grad_middle,
        output,
        vec,
        vec_two,
    )
    share = width // place.blk
    vec_sum = jnp.concatenate([vec_sum[:4], vec_sum[4:]], axis=1)
    vec_sum = lax.dynamic_slice(vec_sum, (0, index * share), (4, share))
    return (
        output,
        token_grad,
        proj_sum,
        out_sum,
        up_sum,
        down_sum.T,
        vec_sum[0],
        vec_sum[1],
        vec_sum[2],
        vec_sum[3],
    )


def solution(mesh):
    place = Place((mesh.shape["batch"], mesh.shape["blk"]))
    weight, vector = P("batch", "blk"), P("blk")
    row = P("batch", "blk", None)
    in_specs = (row,) + (weight,) * 4 + (vector,) * 4 + (weight,) * 2 + (row,)
    out_specs = (row, row) + (weight,) * 4 + (vector,) * 4
    return jax.shard_map(
        functools.partial(body, place),
        mesh=mesh,
        in_specs=in_specs,
        out_specs=out_specs,
        check_vma=False,
    )
```

```python
import functools

import jax
import jax.numpy as jnp
from jax import lax
from jax.experimental import pallas as pl
from jax.experimental.pallas import tpu as pltpu
from jax.sharding import PartitionSpec as P

HEADS = 12
HEAD_DIM = 64
CORES = 2
LANE_X = 2
MESH = pl.DeviceIdType.MESH
LOG2E = 1.4426950408889634
epsilon = 1e-05
masked = -1e30
bf16 = jnp.bfloat16
f32 = jnp.float32


def dot(left, right, left_dim, right_dim):
    return lax.dot_general(
        left, right, (((left_dim,), (right_dim,)), ((), ())), preferred_element_type=f32
    )


class Place:
    def __init__(self, sizes):
        self.batch, self.blk = sizes
        self.Z, self.X = self.batch // LANE_X, LANE_X
        self.Y, self.C = self.blk // CORES, CORES

    def here(self):
        b, d = lax.axis_index("batch"), lax.axis_index("blk")
        return b // self.X, b % self.X, d // self.C, d % self.C

    def device(self, z, x, p, c):
        return (z * self.X + x, p * self.C + c)


class Wire:
    def __init__(self, send_sem, recv_sem):
        self.send_sem, self.recv_sem, self.names = send_sem, recv_sem, {}

    def copy(self, name, src, dst, device):
        i = self.names.setdefault(name, len(self.names))
        return pltpu.make_async_remote_copy(
            src_ref=src,
            dst_ref=dst,
            send_sem=self.send_sem.at[i],
            recv_sem=self.recv_sem.at[i],
            device_id=device,
            device_id_type=MESH,
        )


def start_all(copies):
    for copy in copies:
        copy.start()


def arrive_all(copies):
    for copy in copies:
        copy.wait_recv()


def leave_all(copies):
    for copy in copies:
        copy.wait_send()


def first_rows(rows, sixths):
    return min(rows - 16, 16 * ((rows * sixths // 6) // 16)) if rows > 16 else 0


def greet(place, partners):
    barrier = pltpu.get_barrier_semaphore()
    for partner in partners:
        pl.semaphore_signal(barrier, inc=1, device_id=partner, device_id_type=MESH)
    pl.semaphore_wait(barrier, len(partners))


def partners_of(place):
    z, x, p, c = place.here()
    found = [place.device((z + k) % place.Z, x, p, c) for k in range(1, place.Z)]
    found += [place.device(z, 1 - x, p, c)]
    found += [place.device(z, x, (p + k) % place.Y, c) for k in range(1, place.Y)]
    found += [place.device(z, x, p, 1 - c)]
    return found


def head_masked(value, h, axis):
    index = lax.broadcasted_iota(jnp.int32, value.shape, axis)
    return jnp.where((index // HEAD_DIM) == h, value, jnp.zeros_like(value))


class Spreading:
    def __init__(self, place, wire, name, spots, shard, whole, sixths):
        self.place, self.wire, self.name, self.spots = place, wire, name, spots
        self.shard, self.whole = shard, whole
        self.rows = shard.shape[0]
        self.h = first_rows(self.rows, sixths)

    def zero(self):
        z, x, p, c = self.spots
        place = self.place
        found = []
        for k in range(1, place.Z):
            found.append(
                self.wire.copy(
                    (self.name, "z", k),
                    self.shard,
                    self.whole.at[p, c, z, x],
                    place.device((z + k) % place.Z, x, p, c),
                )
            )
        return found

    def one(self):
        z, x, p, c = self.spots
        place, h, r = self.place, self.h, self.rows
        low = self.whole.at[p, c, :, x, 0:h]
        found = [self.wire.copy((self.name, "xa"), low, low, place.device(z, 1 - x, p, c))]
        high = self.whole.at[p, c, :, x, h:r]
        for k in range(1, place.Y):
            found.append(
                self.wire.copy(
                    (self.name, "yb", k), high, high, place.device(z, x, (p + k) % place.Y, c)
                )
            )
        return found

    def two(self):
        z, x, p, c = self.spots
        place, h, r = self.place, self.h, self.rows
        low = self.whole.at[p, c, :, :, 0:h]
        found = [
            self.wire.copy(
                (self.name, "ya", k), low, low, place.device(z, x, (p + k) % place.Y, c)
            )
            for k in range(1, place.Y)
        ]
        high = self.whole.at[:, c, :, x, h:r]
        found.append(
            self.wire.copy((self.name, "xb"), high, high, place.device(z, 1 - x, p, c))
        )
        return found

    def three(self):
        z, x, p, c = self.spots
        plane = self.whole.at[:, c]
        return [self.wire.copy((self.name, "core"), plane, plane, self.place.device(z, x, p, 1 - c))]

    def go_one(self):
        arrive_all(self.zero())
        start_all(self.one())

    def go_two_low(self):
        arrive_all(self.one()[:1])
        start_all(self.two()[:-1])

    def go_two_high(self):
        arrive_all(self.one()[1:])
        start_all(self.two()[-1:])

    def go_three(self):
        arrive_all(self.two())
        start_all(self.three())

    def leave(self):
        for copies in (self.zero(), self.one(), self.two(), self.three()):
            leave_all(copies)


FORWARD_PLAN = (
    "O1", "P1", "V", "N0", "K", "O2b", "P2a", "P2b", "U1", "N2", "P3", "O2a", "N3", "D1",
    "U2b", "W", "U2a", "O3", "J", "S00", "S01", "S02", "S10", "S11", "D2a", "S12", "D2b",
    "S20", "S21", "S22", "S30", "U3", "S31", "D3", "S32",
)


def forward_kernel(place, n, BQ, *refs):
    shards, (tok, segments, present, vec_in) = refs[: n + 1], refs[n + 1 : n + 5]
    outs = refs[n + 5 :]
    wholes = outs[:n]
    (tok_out, vec_out, begin, proj_out, w_out, normedT_out, att_out, oT_out, lt) = outs[
        n : n + 9
    ]
    (
        proj_v, tok_v, tag, tag_v, vec_v, n_v, nT, wv, pv, vT, att, oT,
        send_sem, recv_sem, local_sem,
    ) = outs[n + 9 :]
    spots = place.here()
    z, x, p, c = spots
    Z, X, Y, C = place.Z, place.X, place.Y, place.C
    D, W3 = wv.shape
    H = W3 // 3
    L = pv.shape[0]
    T = L // (Y * C)
    U = BQ // T
    pairs = H // 128
    nq = L // BQ
    wire = Wire(send_sem, recv_sem)
    sibling = place.device(z, x, p, 1 - c)
    flows = [
        Spreading(place, wire, m, spots, shards[m], proj_v if m == 0 else wholes[m - 1], 3)
        for m in range(n + 1)
    ]

    def local(i, src, dst):
        return pltpu.make_async_copy(src, dst, local_sem.at[i])

    def lane(offset, size):
        return pl.ds(pl.multiple_of(offset, 128), size)

    def line(offset, size):
        return pl.ds(pl.multiple_of(offset, 16), size)

    row_parts = (("vec", vec_in, vec_v), ("tag", tag, tag_v), ("tok", tok, tok_v))

    def along_y(what, src, dst):
        found = []
        for k in range(1, Y):
            to = (p + k) % Y
            piece = src if what == "vec" else src.at[to]
            found.append(
                wire.copy((what, "y", k), piece, dst.at[p, c], place.device(z, x, to, c))
            )
        return found

    def to_sibling_own(what, src, dst):
        piece = src if what == "vec" else src.at[p]
        return wire.copy((what, "own"), piece, dst.at[p, c], sibling)

    def to_sibling(what, dst):
        found = []
        for k in range(1, Y):
            q = (p + k) % Y
            found.append(wire.copy((what, "pass", k), dst.at[q, c], dst.at[q, c], sibling))
        return found

    position = lax.broadcasted_iota(jnp.int32, (Y, T), 1) + (p * C + c) * T
    tags = jnp.where(present[...] == 1, segments[...], -1 - position)
    for q in range(Y):
        tag[q] = jnp.broadcast_to(tags[q : q + 1, :], tag.shape[1:])
    greet(place, partners_of(place))
    for part in row_parts:
        start_all(along_y(*part))
    for part in row_parts:
        to_sibling_own(*part).start()
    for flow in flows:
        start_all(flow.zero())
    kept = [local(m, shards[m], flows[m].whole.at[p, c, z, x]) for m in range(n + 1)]
    kept += [
        local(n + 1, vec_in, vec_v.at[p, c]),
        local(n + 2, tag.at[p], tag_v.at[p, c]),
        local(n + 3, tok.at[p], tok_v.at[p, c]),
    ]
    start_all(kept)
    saves = [
        local(n + 5, nT, normedT_out),
        local(n + 6, tok_v.at[:, c], tok_out),
        local(n + 7, pv, proj_out),
        local(n + 8, wv, w_out),
    ]

    def norm_block(q, i):
        unit, factor = normed(tok_v[q, i].astype(f32))
        low = (unit * vec_out[0:1, :] + vec_out[1:2, :]).astype(bf16)
        rows = line((q * C + i) * T, T)
        n_v[rows, :] = low
        nT[:, lane((q * C + i) * T, T)] = low.T

    def begin_one(m):
        kept[m].wait()
        flows[m].go_one()

    def vector_pass():
        arrive_all(along_y(*row_parts[0]))
        start_all(to_sibling("vec", vec_v))

    def norm_near():
        for copy in kept[n + 1 :]:
            copy.wait()
        to_sibling_own(*row_parts[0]).wait_recv()
        arrive_all(to_sibling("vec", vec_v))
        share = vec_v.shape[3]
        for q in range(Y):
            for i in range(C):
                lo = (q * C + i) * share
                vec_out[:, lo : lo + share] = vec_v[q, i, 0:8, :].astype(f32)
        norm_block(p, c)
        to_sibling_own(*row_parts[2]).wait_recv()
        norm_block(p, 1 - c)

    def row_pass():
        for what, src, dst in row_parts[1:]:
            arrive_all(along_y(what, src, dst))
            start_all(to_sibling(what, dst))

    def norm_far():
        for k in range(1, Y):
            norm_block((p + k) % Y, c)

    def norm_last():
        arrive_all(to_sibling("tok", tok_v))
        for k in range(1, Y):
            norm_block((p + k) % Y, 1 - c)
        start_all(saves[:2])
        to_sibling_own(*row_parts[1]).wait_recv()
        arrive_all(to_sibling("tag", tag_v))
        tags = [tag_v[q, i, 0:1, :] for q in range(Y) for i in range(C)]
        counts = []
        for s in range(4):
            hits = sum((t == s).astype(f32) for t in tags)
            counts.append(jnp.sum(hits, axis=1, keepdims=True).astype(jnp.int32))
        for b, t in enumerate(tags):
            first = sum(jnp.where(t > s, counts[s], 0) for s in range(4))
            position = lax.broadcasted_iota(jnp.int32, (1, T), 1) + b * T
            begin[:, b * T : (b + 1) * T] = jnp.where(t < 0, position, first)

    def weight_columns():
        arrive_all(flows[0].three())
        r, w = proj_v.shape[4:]
        for mine in range(C):

            @pl.when(c == mine)
            def _():
                for third in range(3):
                    base = third * D + mine * H
                    for d in range(Y * C):
                        a, b = max(base, d * w), min(base + H, (d + 1) * w)
                        if a >= b:
                            continue
                        to = third * H + a - base
                        for i in range(Z * X):
                            wv[i * r : (i + 1) * r, to : to + b - a] = proj_v[
                                d // C, d % C, i // X, i % X, :, a - d * w : b - d * w
                            ]

    def project_all():
        def project(i, nothing):
            rows = line(i * BQ, BQ)
            pv[rows, :] = dot(n_v[rows, :], wv[...], 1, 0).astype(bf16)
            return nothing

        lax.fori_loop(0, nq, project, 0)
        vT[...] = pv[:, 2 * H :].T
        start_all(saves[2:])

    scale = HEAD_DIM ** (-0.5) * LOG2E

    def block_copies(qi):
        found = []
        for u in range(U):
            b = qi * U + u
            q, owner = b // C, b % C
            src = att.at[b * T : (b + 1) * T, :]
            dst = att_out.at[q * T : (q + 1) * T, lane(c * H, H)]
            found.append(
                (owner, local(n + 9 + q, src, dst), wire.copy(("att", q), src, dst, sibling))
            )
        return found

    acts = {
        "V": vector_pass,
        "N0": norm_near,
        "K": row_pass,
        "N2": norm_far,
        "N3": norm_last,
        "W": weight_columns,
        "J": project_all,
    }
    for m, name in enumerate("POUD"):
        acts[name + "1"] = functools.partial(begin_one, m)
        acts[name + "2a"] = flows[m].go_two_low
        acts[name + "2b"] = flows[m].go_two_high
        acts[name + "3"] = flows[m].go_three
    events, spot = {}, None
    for name in FORWARD_PLAN:
        if name[0] == "S":
            spot = (int(name[1]), int(name[2]))
        else:
            events.setdefault(spot, []).append(name)
    for name in events[None]:
        acts[name]()
    for qi in range(nq):
        qs = slice(qi * BQ, (qi + 1) * BQ)
        d0 = qi * BQ
        if qi == nq - 1:
            cuts = [(0, d0, 1)] if d0 else []
        elif d0 > 256:
            cuts = [(0, 256, 1), (256, d0, 0)]
        else:
            cuts = [(0, d0, 1)] if d0 else []
        cuts.append((d0, d0 + BQ, 2))

        def one_pair(pair, nothing):
            cols = lane(pair * 128, 128)
            k_cols = lane(H + pair * 128, 128)
            qT = pv[qs, cols].T
            found = []
            for h in range(2):
                query = head_masked(qT, h, 0)
                rows = pl.ds(pl.multiple_of(pair * 128 + h * HEAD_DIM, HEAD_DIM), HEAD_DIM)
                parts = []
                for a, b, mode in cuts:
                    s = dot(pv[a:b, k_cols], query, 1, 0) * scale
                    if mode:
                        key_pos = lax.broadcasted_iota(jnp.int32, (b - a, BQ), 0) + a
                        visible = key_pos >= begin[:, qs]
                        if mode == 2:
                            query_pos = lax.broadcasted_iota(jnp.int32, (b - a, BQ), 1) + d0
                            visible = jnp.logical_and(visible, key_pos <= query_pos)
                        s = jnp.where(visible, s, masked)
                    parts.append(s)
                top = functools.reduce(
                    jnp.maximum, [jnp.max(s, axis=0, keepdims=True) for s in parts]
                )
                total, accum = 0.0, 0.0
                for (a, b, mode), s in zip(cuts, parts):
                    e = jnp.exp2(s - top)
                    total = total + jnp.sum(e, axis=0, keepdims=True)
                    accum = accum + dot(vT[rows, a:b], e.astype(bf16), 1, 0)
                result = accum / total
                oT[rows, qs] = result
                found.append(result)
                lt[pair, h : h + 1, qs] = top + jnp.log2(total)
            att[qs, cols] = jnp.concatenate(found, axis=0).astype(bf16).T
            for number in range(pairs):
                if (qi, number) in events:

                    @pl.when(pair == number)
                    def _():
                        for name in events[qi, number]:
                            acts[name]()

            return nothing

        lax.fori_loop(0, pairs, one_pair, 0)
        for owner, keep, send in block_copies(qi):

            @pl.when(owner == c)
            def _():
                keep.start()

            @pl.when(owner != c)
            def _():
                send.start()

    last = local(n + 9 + Y, oT, oT_out)
    last.start()
    for flow in flows[1:]:
        arrive_all(flow.three())
    for qi in range(nq):
        for owner, keep, send in block_copies(qi):

            @pl.when(owner == c)
            def _():
                keep.wait()

            @pl.when(owner != c)
            def _():
                send.wait_send()

            @pl.when(owner == c)
            def _():
                send.wait_recv()

    for what, src, dst in row_parts:
        leave_all(along_y(what, src, dst))
        to_sibling_own(what, src, dst).wait_send()
        leave_all(to_sibling(what, dst))
    for flow in flows:
        flow.leave()
    for copy in saves + [last]:
        copy.wait()


def forward(place, shards, tok, segments, present, vec_in):
    n = len(shards) - 1
    Z, X, Y, C = place.Z, place.X, place.Y, place.C
    R, T, D = tok.shape
    L = Y * C * T
    H = D // C
    W3 = 3 * H
    BQ = 512
    pairs = H // 128
    inside = pl.BlockSpec(memory_space=pltpu.VMEM)
    anywhere = pl.BlockSpec(memory_space=pl.ANY)
    out_shape = [jax.ShapeDtypeStruct((Y, C, Z, X) + m.shape, bf16) for m in shards[1:]]
    out_shape += [
        jax.ShapeDtypeStruct((Y, T, D), bf16),
        jax.ShapeDtypeStruct((8, D), f32),
        jax.ShapeDtypeStruct((1, L), jnp.int32),
        jax.ShapeDtypeStruct((L, W3), bf16),
        jax.ShapeDtypeStruct((D, W3), bf16),
        jax.ShapeDtypeStruct((D, L), bf16),
        jax.ShapeDtypeStruct((Y * T, D), bf16),
        jax.ShapeDtypeStruct((H, L), f32),
        jax.ShapeDtypeStruct((pairs, 2, L), f32),
    ]
    each = (Z - 1) + 2 * Y + 1
    copies = (n + 1) * each + 3 * (2 * (Y - 1) + 1) + Y
    scratch = [
        pltpu.VMEM((Y, C, Z, X) + shards[0].shape, bf16),
        pltpu.VMEM((Y, C, T, D), bf16),
        pltpu.VMEM((Y, 8, T), jnp.int32),
        pltpu.VMEM((Y, C, 8, T), jnp.int32),
        pltpu.VMEM((Y, C) + vec_in.shape, bf16),
        pltpu.VMEM((L, D), bf16),
        pltpu.VMEM((D, L), bf16),
        pltpu.VMEM((D, W3), bf16),
        pltpu.VMEM((L, W3), bf16),
        pltpu.VMEM((H, L), bf16),
        pltpu.VMEM((L, H), bf16),
        pltpu.VMEM((H, L), f32),
        pltpu.SemaphoreType.DMA((copies,)),
        pltpu.SemaphoreType.DMA((copies,)),
        pltpu.SemaphoreType.DMA((n + 10 + Y,)),
    ]
    return pl.pallas_call(
        functools.partial(forward_kernel, place, n, BQ),
        out_shape=out_shape,
        in_specs=[inside] * (n + 1) + [anywhere] + [inside] * 3,
        out_specs=[anywhere] * (n + 1) + [inside] * 2 + [anywhere] * 5 + [inside],
        scratch_shapes=scratch,
        compiler_params=pltpu.CompilerParams(
            collective_id=0, has_side_effects=True, vmem_limit_bytes=60 << 20
        ),
        name="forward",
    )(*shards, tok, segments, present, vec_in)


class Summing:
    def __init__(self, place, wire, name, spots, acc, xa, yb, ya, xb, zz):
        self.place, self.wire, self.name, self.spots = place, wire, name, spots
        self.acc, self.xa, self.yb, self.ya, self.xb, self.zz = acc, xa, yb, ya, xb, zz
        self.rows = acc.shape[3]
        self.h = xa.shape[2]

    def one(self):
        z, x, p, c = self.spots
        place, h, r = self.place, self.h, self.rows
        side = place.device(z, 1 - x, p, c)
        found = [
            self.wire.copy((self.name, "xa"), self.acc.at[:, :, 1 - x, 0:h], self.xa, side)
        ]
        for k in range(1, place.Y):
            to = (p + k) % place.Y
            found.append(
                self.wire.copy(
                    (self.name, "yb", k),
                    self.acc.at[to, :, :, h:r],
                    self.yb.at[k - 1],
                    place.device(z, x, to, c),
                )
            )
        return found

    def two(self):
        z, x, p, c = self.spots
        place, h, r = self.place, self.h, self.rows
        found = []
        for k in range(1, place.Y):
            to = (p + k) % place.Y
            found.append(
                self.wire.copy(
                    (self.name, "ya", k),
                    self.acc.at[to, :, x, 0:h],
                    self.ya.at[k - 1],
                    place.device(z, x, to, c),
                )
            )
        side = place.device(z, 1 - x, p, c)
        found.append(
            self.wire.copy((self.name, "xb"), self.acc.at[p, :, 1 - x, h:r], self.xb, side)
        )
        return found

    def three(self):
        z, x, p, c = self.spots
        place = self.place
        found = []
        for k in range(1, place.Z):
            to = (z + k) % place.Z
            found.append(
                self.wire.copy(
                    (self.name, "z", k),
                    self.acc.at[p, to, x],
                    self.zz.at[k - 1],
                    place.device(to, x, p, c),
                )
            )
        return found

    def add_one(self):
        z, x, p, c = self.spots
        place, h, r, acc = self.place, self.h, self.rows, self.acc
        ones = self.one()
        ones[0].wait_recv()

        def low(i, nothing):
            a, b = i // place.Z, i % place.Z
            total = acc[a, b, x, 0:h].astype(f32) + self.xa[a, b].astype(f32)
            acc[a, b, x, 0:h] = total.astype(bf16)
            return nothing

        lax.fori_loop(0, place.Y * place.Z, low, 0)
        twos = self.two()
        start_all(twos[:-1])
        arrive_all(ones[1:])

        def high(i, nothing):
            a, b = i // place.X, i % place.X
            total = acc[p, a, b, h:r].astype(f32)
            for k in range(place.Y - 1):
                total = total + self.yb[k, a, b].astype(f32)
            acc[p, a, b, h:r] = total.astype(bf16)
            return nothing

        lax.fori_loop(0, place.Z * place.X, high, 0)
        twos[-1].start()

    def add_two(self):
        z, x, p, c = self.spots
        place, h, r, acc = self.place, self.h, self.rows, self.acc
        arrive_all(self.two())

        def both(i, nothing):
            total = acc[p, i, x, 0:h].astype(f32)
            for k in range(place.Y - 1):
                total = total + self.ya[k, i].astype(f32)
            acc[p, i, x, 0:h] = total.astype(bf16)
            total = acc[p, i, x, h:r].astype(f32) + self.xb[i].astype(f32)
            acc[p, i, x, h:r] = total.astype(bf16)
            return nothing

        lax.fori_loop(0, place.Z, both, 0)
        start_all(self.three())

    def finish(self, target):
        z, x, p, c = self.spots
        arrive_all(self.three())
        total = self.acc[p, z, x].astype(f32)
        for k in range(self.place.Z - 1):
            total = total + self.zz[k].astype(f32)
        target[...] = total

    def leave(self):
        leave_all(self.one())
        leave_all(self.two())
        leave_all(self.three())


class DepthSum:
    def __init__(self, place, wire, name, spots, acc, zr, xr, yr):
        self.place, self.wire, self.name, self.spots = place, wire, name, spots
        self.acc, self.zr, self.xr, self.yr = acc, zr, xr, yr

    def one(self):
        z, x, p, c = self.spots
        place = self.place
        return [
            self.wire.copy(
                (self.name, "z", k),
                self.acc.at[:, (z + k) % place.Z],
                self.zr.at[k - 1],
                place.device((z + k) % place.Z, x, p, c),
            )
            for k in range(1, place.Z)
        ]

    def two(self):
        z, x, p, c = self.spots
        side = self.place.device(z, 1 - x, p, c)
        return [self.wire.copy((self.name, "x"), self.acc.at[:, z, 1 - x], self.xr, side)]

    def three(self):
        z, x, p, c = self.spots
        place = self.place
        return [
            self.wire.copy(
                (self.name, "y", k),
                self.acc.at[(p + k) % place.Y, z, x],
                self.yr.at[k - 1],
                place.device(z, x, (p + k) % place.Y, c),
            )
            for k in range(1, place.Y)
        ]

    def add_one(self):
        z, x, p, c = self.spots
        place, acc = self.place, self.acc
        arrive_all(self.one())

        def add(i, nothing):
            a, b = i // place.X, i % place.X
            total = acc[a, z, b].astype(f32)
            for k in range(place.Z - 1):
                total = total + self.zr[k, a, b].astype(f32)
            acc[a, z, b] = total.astype(bf16)
            return nothing

        lax.fori_loop(0, place.Y * place.X, add, 0)
        start_all(self.two())

    def add_two(self):
        z, x, p, c = self.spots
        place, acc = self.place, self.acc
        arrive_all(self.two())

        def add(i, nothing):
            total = acc[i, z, x].astype(f32) + self.xr[i].astype(f32)
            acc[i, z, x] = total.astype(bf16)
            return nothing

        lax.fori_loop(0, place.Y, add, 0)
        start_all(self.three())

    def finish(self, target):
        z, x, p, c = self.spots
        arrive_all(self.three())
        total = self.acc[p, z, x].astype(f32)
        for k in range(self.place.Y - 1):
            total = total + self.yr[k].astype(f32)
        target[...] = total

    def leave(self):
        leave_all(self.one())
        leave_all(self.two())
        leave_all(self.three())


class ChunkSum:
    def __init__(self, place, wire, name, spots, acc, xr, zr, total, far):
        self.place, self.wire, self.name, self.spots = place, wire, name, spots
        self.acc, self.xr, self.zr, self.total, self.far = acc, xr, zr, total, far

    def along_x(self):
        z, x, p, c = self.spots
        side = self.place.device(z, 1 - x, p, c)
        return [self.wire.copy((self.name, "x"), self.acc.at[:, 1 - x], self.xr, side)]

    def along_z(self):
        z, x, p, c = self.spots
        place = self.place
        return [
            self.wire.copy(
                (self.name, "z", k),
                self.acc.at[(z + k) % place.Z, x],
                self.zr.at[k - 1],
                place.device((z + k) % place.Z, x, p, c),
            )
            for k in range(1, place.Z)
        ]

    def along_y(self):
        z, x, p, c = self.spots
        place = self.place
        return [
            self.wire.copy(
                (self.name, "y", k),
                self.total.at[0],
                self.total.at[k],
                place.device(z, x, (p + k) % place.Y, c),
            )
            for k in range(1, place.Y)
        ]

    def to_core(self):
        z, x, p, c = self.spots
        return [
            self.wire.copy(
                (self.name, "core"), self.total, self.far, self.place.device(z, x, p, 1 - c)
            )
        ]

    def go_z(self):
        z, x, p, c = self.spots
        arrive_all(self.along_x())

        def one(i, nothing):
            total = self.acc[i, x].astype(f32) + self.xr[i].astype(f32)
            self.acc[i, x] = total.astype(bf16)
            return nothing

        lax.fori_loop(0, self.place.Z, one, 0)
        start_all(self.along_z())

    def go_y(self):
        z, x, p, c = self.spots
        arrive_all(self.along_z())
        total = self.acc[z, x].astype(f32)
        for k in range(self.place.Z - 1):
            total = total + self.zr[k].astype(f32)
        self.total[0] = total.astype(bf16)
        start_all(self.along_y())

    def go_core(self):
        arrive_all(self.along_y())
        start_all(self.to_core())

    def result(self):
        arrive_all(self.to_core())
        return [
            sum(part[k].astype(f32) for k in range(self.place.Y)) for part in (self.total, self.far)
        ]

    def leave(self):
        for copies in (self.along_x(), self.along_z(), self.along_y(), self.to_core()):
            leave_all(copies)


BACKWARD_PLAN = (
    "U0", "S00", "S01", "O0", "S02", "S03", "U1", "C0x", "S10", "D0", "U2", "S11", "S12",
    "C0z", "S13", "C1x", "S20", "B3", "D1", "S21", "C1z", "B2", "S22", "S23", "D2", "T3",
    "C2x", "B1", "C0y", "O1", "UF", "T2", "B0", "C1y", "T1", "C0c", "T0", "C2z", "C1c",
    "Vc", "Vx", "C2y", "Vz", "O2", "C0r", "Vy", "C1r", "DF", "C2c", "OF", "Vr", "C2r",
)


def backward_kernel(place, n, BQ, *refs):
    (begin, proj, grad_in, oT_in, lt, normedT, w_in, tok, gm, vec, vec_two) = refs[:11]
    parts, others = refs[11 : 11 + n], refs[11 + n : 11 + 2 * n]
    outs = refs[11 + 2 * n :]
    sums, (vec_out, tg_home) = outs[: n + 1], outs[n + 1 : n + 3]
    landing = outs[n + 3 : 2 * n + 3]
    rest = outs[2 * n + 3 :]
    (
        pv, do, oT, wv, kT, dk, dv, nT,
        keep, g_send, g_recv, tok_v, gm_v, grads, v0, v1, v2, v3, vc, vy, vx, vz, whole,
    ) = rest[:23]
    buffers = rest[23 : 23 + 6 * n - 2]
    chunk_buffers = rest[23 + 6 * n - 2 : -3]
    send_sem, recv_sem, local_sem = rest[-3:]
    tg_v = g_recv
    spots = place.here()
    z, x, p, c = spots
    Z, X, Y, C = place.Z, place.X, place.Y, place.C
    L, W3 = pv.shape
    H = W3 // 3
    D = wv.shape[0]
    T = L // (Y * C)
    pairs = H // 128
    nq = L // BQ
    scale = HEAD_DIM ** (-0.5) * LOG2E
    scale_back = HEAD_DIM ** (-0.5)
    wire = Wire(send_sem, recv_sem)
    sibling = place.device(z, x, p, 1 - c)
    beside = place.device(z, 1 - x, p, c)
    adds = [DepthSum(place, wire, 0, spots, *buffers[:4])]
    adds += [
        Summing(place, wire, m, spots, *buffers[6 * m - 2 : 6 * m + 4]) for m in range(1, n)
    ]
    chunks = [
        ChunkSum(place, wire, ("chunk", i), spots, *chunk_buffers[5 * i : 5 * i + 5])
        for i in range(pairs)
    ]

    def local(i, src, dst):
        return pltpu.make_async_copy(src, dst, local_sem.at[i])

    def lane(offset, size):
        return pl.ds(pl.multiple_of(offset, 128), size)

    def line(offset, size):
        return pl.ds(pl.multiple_of(offset, 16), size)

    def out_fetch(pair):
        return local(2, oT_in.at[line(pair * 128, 128), :], oT)

    loads = [local(0, proj, pv), local(1, grad_in, do), local(3, w_in, wv)]
    late = local(4 + 2 * n, normedT, nT)
    halves = [
        (local(4 + m, parts[m], adds[m].acc), local(4 + n + m, others[m], landing[m]))
        for m in range(n)
    ]
    for m in (1, 2, 0):
        start_all(halves[m])
    start_all(loads + [late])
    out_fetch(0).start()
    greet(place, partners_of(place))
    row_sem = 5 + 2 * n

    def core_add(m):
        for copy in halves[m]:
            copy.wait()
        acc, other = adds[m].acc, landing[m]

        def one(i, nothing):
            a, b, d = i // (Z * X), (i // X) % Z, i % X
            total = acc[a, b, d].astype(f32) + other[a, b, d].astype(f32)
            acc[a, b, d] = total.astype(bf16)
            return nothing

        lax.fori_loop(0, Y * Z * X, one, 0)

    for copy in loads:
        copy.wait()
    kT[...] = pv[:, H : 2 * H].T
    grads[...] = jnp.zeros_like(grads)

    U = BQ // T
    gain = vec[0:1, :]

    def sub_blocks(qi):
        found = []
        for u in range(U):
            block = qi * U + u
            found.append((u, block // C, block % C))
        return found

    reserved = send_sem.shape[0] - 3 * Y

    def g_wire(q):
        return pltpu.make_async_remote_copy(
            src_ref=g_send.at[q],
            dst_ref=g_recv.at[q],
            send_sem=send_sem.at[reserved + q],
            recv_sem=recv_sem.at[reserved + q],
            device_id=sibling,
            device_id_type=MESH,
        )

    def home_from(k):
        q = (p + k) % Y
        return pltpu.make_async_remote_copy(
            src_ref=tg_v.at[p],
            dst_ref=tg_home.at[q],
            send_sem=send_sem.at[reserved + Y + q],
            recv_sem=recv_sem.at[reserved + 2 * Y + q],
            device_id=place.device(z, x, q, c),
            device_id_type=MESH,
        )

    def home_to(q):
        return pltpu.make_async_remote_copy(
            src_ref=tg_v.at[q],
            dst_ref=tg_home.at[p],
            send_sem=send_sem.at[reserved + Y + q],
            recv_sem=recv_sem.at[reserved + 2 * Y + p],
            device_id=place.device(z, x, q, c),
            device_id_type=MESH,
        )

    def block_done(qi):
        g = dot(pv[line(qi * BQ, BQ), :], wv[...], 1, 1)
        for u, q, owner in sub_blocks(qi):
            rows = slice(u * T, (u + 1) * T)

            @pl.when(owner == c)
            def _():
                keep[(qi % 2 * U + u) // C] = g[rows, :]

            @pl.when(owner != c)
            def _():
                g_send[q] = g[rows, :].astype(bf16)
                g_wire(q).start()

    def pair_done(i):
        wide = [pv[:, t * H + i * 128 : t * H + (i + 1) * 128] for t in range(3)]
        value = dot(nT[...], jnp.concatenate(wide, axis=1), 1, 0).astype(bf16)
        chunk = chunks[i]
        r = chunk.acc.shape[2]
        for b in range(Z * X):
            chunk.acc[b // X, b % X] = value[b * r : (b + 1) * r, :]
        start_all(chunk.along_x())

    def token_rows(qi):
        for u, q, owner in sub_blocks(qi):

            @pl.when(owner == c)
            def _():
                a = local(row_sem, tok.at[line(q * T, T)], tok_v)
                b = local(row_sem + 1, gm.at[line(q * T, T)], gm_v)
                a.start()
                b.start()
                g_wire(q).wait_recv()
                grad = keep[(qi % 2 * U + u) // C] + g_recv[q].astype(f32)
                a.wait()
                unit, factor = normed(tok_v[...].astype(f32))
                grads[0:1, :] += jnp.sum(grad * unit, axis=0, keepdims=True)
                grads[1:2, :] += jnp.sum(grad, axis=0, keepdims=True)
                b.wait()
                tg_v[q] = (gm_v[...] + norm_back(grad, gain, unit, factor)).astype(bf16)

                @pl.when(q == p)
                def _():
                    local(row_sem + 2, tg_v.at[q], tg_home.at[p]).start()

                @pl.when(q != p)
                def _():
                    home_to(q).start()

    def one_query(pair, qi):
        d0 = qi * BQ
        qs = slice(d0, d0 + BQ)
        cols = lane(pair * 128, 128)
        k_cols, v_cols = lane(H + pair * 128, 128), lane(2 * H + pair * 128, 128)
        q_val, do_val = pv[qs, cols], do[qs, cols]
        qT, doT = q_val.T, do_val.T
        part = BQ // 2
        cuts = []
        if d0 and qi < nq - 1:
            cuts = [(0, part, 1, 0), (part, min(BQ, d0), 0, 0)]
            cuts += [(a, a + BQ, 0, 0) for a in range(BQ, d0, BQ)]
        elif d0:
            cuts = [(a, a + BQ, 1, 0) for a in range(0, d0, BQ)]
        cuts += [(d0, d0 + part, 2, 0), (d0 + part, d0 + BQ, 2, part)]
        dqs = []
        for h in range(2):
            rows = slice(h * HEAD_DIM, (h + 1) * HEAD_DIM)
            kT_rows = pl.ds(pl.multiple_of(pair * 128 + h * HEAD_DIM, HEAD_DIM), HEAD_DIM)
            query, grad = head_masked(qT, h, 0), head_masked(doT, h, 0)
            q_nat, do_nat = head_masked(q_val, h, 1), head_masked(do_val, h, 1)
            delta = jnp.sum(doT[rows, :].astype(f32) * oT[rows, qs], axis=0, keepdims=True)
            log_total = lt[pair, h : h + 1, qs]
            dq = jnp.zeros((HEAD_DIM, BQ), f32)
            for a, b, mode, qa in cuts:
                sc = dot(pv[a:b, k_cols], query[:, qa:], 1, 0) * scale
                prob = jnp.exp2(sc - log_total[:, qa:])
                if mode:
                    shape = (b - a, BQ - qa)
                    key_pos = lax.broadcasted_iota(jnp.int32, shape, 0) + a
                    visible = key_pos >= begin[:, d0 + qa : d0 + BQ]
                    if mode == 2:
                        query_pos = lax.broadcasted_iota(jnp.int32, shape, 1) + d0 + qa
                        visible = jnp.logical_and(visible, key_pos <= query_pos)
                    prob = jnp.where(visible, prob, 0.0)
                dp = dot(pv[a:b, v_cols], grad[:, qa:], 1, 0)
                ds = (prob * (dp - delta[:, qa:])).astype(bf16)
                dv[a:b, :] += dot(prob.astype(bf16), do_nat[qa:], 1, 0)
                dk[a:b, :] += dot(ds, q_nat[qa:], 1, 0)
                more = dot(kT[kT_rows, a:b], ds, 1, 0)
                if qa:
                    more = jnp.concatenate([jnp.zeros((HEAD_DIM, qa), f32), more], axis=1)
                dq = dq + more
            dqs.append(dq)
        pv[qs, cols] = (jnp.concatenate(dqs, axis=0) * scale_back).astype(bf16).T
        pv[qs, k_cols] = (dk[qs, :] * scale_back).astype(bf16)
        pv[qs, v_cols] = dv[qs, :].astype(bf16)

    out_m, up_m, down_m = adds
    v_core = wire.copy("vc", v0, vc, sibling)
    v_x = wire.copy("vx", v1, vx, beside)
    v_z = [
        wire.copy(("vz", k), v2, vz.at[k - 1], place.device((z + k) % Z, x, p, c))
        for k in range(1, Z)
    ]
    v_y = [
        wire.copy(("vy", k), v3, vy.at[k - 1], place.device(z, x, (p + k) % Y, c))
        for k in range(1, Y)
    ]

    def vector_core():
        grads[2:4, :] = vec_two[...]
        v0[0:4, :] = grads[0:4, 0:H]
        v0[4:8, :] = grads[0:4, H:]
        v_core.start()

    def vector_x():
        v_core.wait_recv()
        v1[...] = v0[...] + vc[...]
        v_x.start()

    def vector_z():
        v_x.wait_recv()
        v2[...] = v1[...] + vx[...]
        start_all(v_z)

    def vector_y():
        arrive_all(v_z)
        v3[...] = v2[...] + sum(vz[k] for k in range(Z - 1))
        start_all(v_y)

    def vector_end():
        arrive_all(v_y)
        vec_out[...] = v3[...] + sum(vy[k] for k in range(Y - 1))

    def chunk_end(i):
        mine, far = chunks[i].result()
        for half in range(C):

            @pl.when(c == half)
            def _():
                for value, core in ((mine, half), (far, 1 - half)):
                    for t in range(3):
                        lo = t * D + core * H + i * 128
                        whole[:, lo : lo + 128] = value[:, t * 128 : (t + 1) * 128]

    def out_start():
        core_add(0)
        start_all(out_m.one())

    def up_start():
        core_add(1)
        start_all(up_m.one())

    def down_start():
        core_add(2)
        start_all(down_m.one())

    acts = {
        "U0": up_start,
        "U1": up_m.add_one,
        "U2": up_m.add_two,
        "UF": lambda: up_m.finish(sums[2]),
        "D0": down_start,
        "D1": down_m.add_one,
        "D2": down_m.add_two,
        "DF": lambda: down_m.finish(sums[3]),
        "O0": out_start,
        "O1": out_m.add_one,
        "O2": out_m.add_two,
        "OF": lambda: out_m.finish(sums[1]),
        "Vc": vector_core,
        "Vx": vector_x,
        "Vz": vector_z,
        "Vy": vector_y,
        "Vr": vector_end,
    }
    for i, chunk in enumerate(chunks):
        acts[f"C{i}x"] = functools.partial(pair_done, i)
        acts[f"C{i}z"] = chunk.go_z
        acts[f"C{i}y"] = chunk.go_y
        acts[f"C{i}c"] = chunk.go_core
        acts[f"C{i}r"] = functools.partial(chunk_end, i)
    for qi in range(nq):
        acts[f"B{qi}"] = functools.partial(block_done, qi)
        acts[f"T{qi}"] = functools.partial(token_rows, qi)
    events, spot = {}, None
    for name in BACKWARD_PLAN:
        if name[0] == "S":
            spot = (int(name[1]), int(name[2]))
        else:
            events.setdefault(spot, []).append(name)

    def one_pair(pair, nothing):
        out_fetch(pair).wait()
        dk[...] = jnp.zeros_like(dk)
        dv[...] = jnp.zeros_like(dv)
        for i in range(nq):
            one_query(pair, nq - 1 - i)
            if i == nq - 1:

                @pl.when(pair < pairs - 1)
                def _():
                    out_fetch(pair + 1).start()

            for number in range(pairs):
                if (number, i) in events and (number, i) != (pairs - 1, nq - 1):

                    @pl.when(pair == number)
                    def _():
                        for name in events[number, i]:
                            acts[name]()

        return nothing

    for name in events.get(None, ()):
        acts[name]()
    late.wait()
    lax.fori_loop(0, pairs, one_pair, 0)
    for name in events[pairs - 1, nq - 1]:
        acts[name]()
    w = sums[0].shape[1]
    for d in range(Y * C):

        @pl.when(p * C + c == d)
        def _():
            sums[0][...] = whole[:, d * w : (d + 1) * w]

    for k in range(1, Y):
        home_from(k).wait_recv()
        home_to((p + k) % Y).wait_send()
    local(row_sem + 2, tg_v.at[p], tg_home.at[p]).wait()
    for q in range(Y):
        g_wire(q).wait_send()
    v_core.wait_send()
    leave_all(v_y)
    v_x.wait_send()
    leave_all(v_z)
    for summing in adds + chunks:
        summing.leave()


def backward(place, parts, others, proj_shape, begin, proj, heads, oT, lt, normedT, w_own, tok, gm, vec, vec_two):
    n = len(parts)
    Z, X, Y, C = place.Z, place.X, place.Y, place.C
    L, W3 = proj.shape
    H = W3 // 3
    D = w_own.shape[0]
    T = L // (Y * C)
    BQ = 512
    inside = pl.BlockSpec(memory_space=pltpu.VMEM)
    anywhere = pl.BlockSpec(memory_space=pl.ANY)
    shapes = [proj_shape] + [part.shape[3:] for part in parts]
    sixths = [3, 3]
    out_shape = [jax.ShapeDtypeStruct(shape, f32) for shape in shapes]
    out_shape += [
        jax.ShapeDtypeStruct((8, H), f32),
        jax.ShapeDtypeStruct((Y, T, D), bf16),
    ]
    scratch = [pltpu.VMEM((Y, Z, X) + shape, bf16) for shape in shapes[1:]]
    scratch += [
        pltpu.VMEM((L, W3), bf16),
        pltpu.VMEM((L, H), bf16),
        pltpu.VMEM((128, L), f32),
        pltpu.VMEM((D, W3), bf16),
        pltpu.VMEM((H, L), bf16),
        pltpu.VMEM((L, 128), f32),
        pltpu.VMEM((L, 128), f32),
        pltpu.VMEM((D, L), bf16),
        pltpu.VMEM((max(1, 2 * (BQ // T) // C), T, D), f32),
        pltpu.VMEM((Y, T, D), bf16),
        pltpu.VMEM((Y, T, D), bf16),
        pltpu.VMEM((T, D), bf16),
        pltpu.VMEM((T, D), f32),
    ]
    scratch += [pltpu.VMEM((8, D), f32)] + [pltpu.VMEM((8, H), f32)] * 5
    scratch += [
        pltpu.VMEM((Y - 1, 8, H), f32),
        pltpu.VMEM((8, H), f32),
        pltpu.VMEM((Z - 1, 8, H), f32),
        pltpu.VMEM((proj_shape[0], 3 * D), f32),
    ]
    r, w = shapes[1]
    scratch += [
        pltpu.VMEM((Y, Z, X, r, w), bf16),
        pltpu.VMEM((Z - 1, Y, X, r, w), bf16),
        pltpu.VMEM((Y, r, w), bf16),
        pltpu.VMEM((Y - 1, r, w), bf16),
    ]
    for shape, part in zip(shapes[2:], sixths):
        r, w = shape
        h = first_rows(r, part)
        scratch += [
            pltpu.VMEM((Y, Z, X, r, w), bf16),
            pltpu.VMEM((Y, Z, h, w), bf16),
            pltpu.VMEM((Y - 1, Z, X, r - h, w), bf16),
            pltpu.VMEM((Y - 1, Z, h, w), bf16),
            pltpu.VMEM((Z, r - h, w), bf16),
            pltpu.VMEM((Z - 1, r, w), bf16),
        ]
    r = proj_shape[0]
    for pair in range(H // 128):
        scratch += [
            pltpu.VMEM((Z, X, r, 384), bf16),
            pltpu.VMEM((Z, r, 384), bf16),
            pltpu.VMEM((Z - 1, r, 384), bf16),
            pltpu.VMEM((Y, r, 384), bf16),
            pltpu.VMEM((Y, r, 384), bf16),
        ]
    each = 1 + (Y - 1) + (Y - 1) + 1 + (Z - 1)
    chunk_copies = 1 + (Z - 1) + (Y - 1) + 1
    copies = n * each + (H // 128) * chunk_copies + 2 + (Y - 1) + 1 + (Z - 1) + 3 * Y
    scratch += [
        pltpu.SemaphoreType.DMA((copies,)),
        pltpu.SemaphoreType.DMA((copies,)),
        pltpu.SemaphoreType.DMA((5 + 2 * n + 3,)),
    ]
    return pl.pallas_call(
        functools.partial(backward_kernel, place, n, BQ),
        out_shape=out_shape,
        in_specs=[inside] + [anywhere] * 3 + [inside] + [anywhere] * 4 + [inside] * 2 + [anywhere] * (2 * n),
        out_specs=[inside] * (n + 2) + [anywhere],
        scratch_shapes=scratch,
        compiler_params=pltpu.CompilerParams(
            collective_id=1, has_side_effects=True, vmem_limit_bytes=63 << 20
        ),
        name="backward",
    )(begin, proj, heads, oT, lt, normedT, w_own, tok, gm, vec, vec_two, *parts, *others)


def gelu_both(u):
    k = 0.7978845608028654
    square = u * u
    t = jnp.tanh(k * u * (1.0 + 0.044715 * square))
    half = 0.5 * (1.0 + t)
    slope = half + 0.5 * k * u * (1.0 - t * t) * (1.0 + 3 * 0.044715 * square)
    return u * half, slope


class Task:
    def __init__(self, copy, far):
        self.copy, self.far, self.left, self.here = copy, far, False, False
        copy.start()

    def gone(self):
        if not self.left:
            if self.far:
                self.copy.wait_send()
            else:
                self.copy.wait()
            self.left = True

    def came(self):
        if self.far and not self.here:
            self.copy.wait_recv()
            self.here = True


def dense_kernel(
    place, aligned, att, tok, cot, out_w, up_w, down_w, vec,
    home, gm_out, heads, up_own, down_own, out_own, up_other, down_other, out_other, vec_out,
    att_v, tok_v, cot_v, out_v, up_v, down_v, out_full, mid, n2, act, gh, n2T, cotT, oacc, g2,
    h_buf, g_buf, stage, up_cut, down_cut, load_sem, store_sem, send_sem, recv_sem,
):
    S, nb, Y, C = place.blk, place.batch, place.Y, place.C
    z, x, p, c = place.here()
    M, D = att_v.shape
    J = up_v.shape[1] // D
    T = M // Y
    H = D // C
    half = M // 2
    sibling = place.device(z, x, p, 1 - c)
    others = [place.device(z, x, (p + k) % Y, c) for k in range(1, Y)]
    wire = Wire(send_sem, recv_sem)
    loads, tasks = [], []

    def line(offset, size):
        return pl.ds(pl.multiple_of(offset, 16), size)

    def lane(offset, size):
        return pl.ds(pl.multiple_of(offset, 128), size)

    def load(src, dst):
        task = Task(pltpu.make_async_copy(src, dst, load_sem.at[len(loads)]), False)
        loads.append(task)
        return task

    def store(src, dst):
        count = sum(not task.far for task in tasks)
        tasks.append(Task(pltpu.make_async_copy(src, dst, store_sem.at[count]), False))
        return tasks[-1]

    def send(name, src, dst, device):
        tasks.append(Task(wire.copy(name, src, dst, device), True))
        return tasks[-1]

    first = [load(att, att_v), load(tok, tok_v), load(out_w, out_v)]
    first.append(load(cot.at[p], cot_v.at[line(p * T, T), :]))
    if aligned:
        w = up_w.shape[2]
        weights = [load(up_w.at[d], up_v.at[:, d * w : (d + 1) * w]) for d in range(S)]
        r, w = down_w.shape[2:]
        weights += [
            load(down_w.at[d, b], down_v.at[d * r : (d + 1) * r, b * w : (b + 1) * w])
            for d in range(S)
            for b in range(nb)
        ]
    else:
        weights = [load(up_w, up_v), load(down_w, down_v)]
    greet(place, others + [sibling])
    cots = []
    for k in range(1, Y):
        to = (p + k) % Y
        cots.append(send(("cot", k), cot.at[to], cot_v.at[line(p * T, T), :], others[k - 1]))
    for task in first:
        task.gone()
    w = out_v.shape[2]
    for d in range(S):
        out_full[:, d * w : (d + 1) * w] = out_v[d]
    gain, shift = vec[2:3, :], vec[3:4, :]
    near = (p * T) // half
    halves = [1 - near, near]
    rows_of = [line(t * half, half) for t in halves]
    for t in (0, 1):
        ts = rows_of[t]
        middle = tok_v[ts, :].astype(f32) + dot(att_v[ts, :], out_full[...], 1, 0)
        unit, factor = normed(middle)
        mid[ts, :] = middle
        low = (unit * gain + shift).astype(bf16)
        n2[ts, :] = low
        n2T[:, lane(halves[t] * half, half)] = low.T
    for task in weights:
        task.gone()
    w_up = up_own.shape[2]
    in_chunk = D // w_up
    chunks = []
    for s in range(J):
        if in_chunk == 1:
            chunks.append((s // C) * C + (1 - c if s % C == 0 else c))
        else:
            chunks.append(s)

    def cols(s):
        return lane(chunks[s] * D, D)

    busy = {}

    def staged(key, value, width, cut):
        for task in busy.get(key, []):
            task.gone()
        busy[key] = []
        if cut is not None:
            for i in range(value.shape[1] // width):
                cut[i] = value[:, i * width : (i + 1) * width]
            return lambda rows, i: cut.at[i, rows, :]
        stage[key] = value
        if value.shape[1] == width:
            return lambda rows, i: stage.at[key, rows, :]
        return lambda rows, i: stage.at[key, rows, i * width : (i + 1) * width]

    def up_gradient(s):
        value = dot(n2T[...], gh[:, cols(s)], 1, 0).astype(bf16)
        piece = staged(0, value, w_up, None if aligned else up_cut)
        every = slice(0, D)
        if in_chunk == 1:
            q = s // C
            if s % C == 0:
                busy[0].append(send(("up", s), piece(every, 0), up_other.at[q], sibling))
            else:
                busy[0].append(store(piece(every, 0), up_own.at[q]))
            return
        for i in range(in_chunk // C):
            q = s * in_chunk // C + i
            busy[0].append(store(piece(every, C * i + c), up_own.at[q]))
            busy[0].append(send(("up", q), piece(every, C * i + 1 - c), up_other.at[q], sibling))

    def down_gradient(s):
        value = dot(cotT[...], act[:, cols(s)], 1, 0).astype(bf16)
        r, w = down_own.shape[2:]
        piece = staged(1, value, w, None if aligned else down_cut)
        for q in range(Y):
            for i in range(D // w):
                b = chunks[s] * (D // w) + i
                busy[1].append(store(piece(line((C * q + c) * r, r), i), down_own.at[q, b]))
                busy[1].append(
                    send(
                        ("down", s, q, i),
                        piece(line((C * q + 1 - c) * r, r), i),
                        down_other.at[q, b],
                        sibling,
                    )
                )

    units = [(0, "f", s) for s in range(J)] + [(1, "fb", s) for s in range(J)]
    units += [(0, "b", s) for s in range(J)]

    def ahead(number):
        t, kind, s = units[number]
        slot = number % 2
        if "f" in kind:
            h_buf[slot] = dot(n2[rows_of[t], :], up_v[:, cols(s)], 1, 0)
        if "b" in kind:
            g_buf[slot] = dot(cot_v[rows_of[t], :], down_v[:, cols(s)], 1, 0)

    def output_rows(t):
        ts = rows_of[t]
        tok_v[ts, :] = (mid[ts, :] + oacc[...]).astype(bf16)
        for i in range(half // T):
            q = halves[t] * (half // T) + i
            if Y == 2 and t == 1:
                store(tok_v.at[ts, :], home.at[q])
            elif Y == 2:
                send("home", tok_v.at[ts, :], home.at[p], others[0])

    sums = [jnp.zeros((1, D), f32), jnp.zeros((1, D), f32)]

    def norm_rows(t):
        ts = rows_of[t]
        unit, factor = normed(mid[ts, :])
        grad = g2[...]
        sums[0] = sums[0] + jnp.sum(grad * unit, axis=0, keepdims=True)
        sums[1] = sums[1] + jnp.sum(grad, axis=0, keepdims=True)
        gm = cot_v[ts, :].astype(f32) + norm_back(grad, gain, unit, factor)
        mid[ts, :] = gm
        low = gm.astype(bf16)
        n2[ts, :] = low
        cot_v[ts, :] = dot(low, out_full[...], 1, 1).astype(bf16)
        store(mid.at[ts, :], gm_out.at[ts, :])
        for i in range(half // T):
            q = halves[t] * (half // T) + i
            rows = line(q * T, T)
            spot = line((C * q + c) * T, T)
            store(cot_v.at[rows, lane(c * H, H)], heads.at[spot, :])
            send(("ga", t, i), cot_v.at[rows, lane((1 - c) * H, H)], heads.at[spot, :], sibling)

    ahead(0)
    for number, (t, kind, s) in enumerate(units):
        ts, slot = rows_of[t], number % 2
        if number + 1 < len(units):
            if units[number + 1] == ((0, "b", 0) if Y == 2 else (1, "fb", 0)):
                for task in cots:
                    task.came()
            ahead(number + 1)
        if "f" in kind:
            a, slope = gelu_both(h_buf[slot])
            a = a.astype(bf16)
            act[ts, cols(s)] = a
            more = dot(a, down_v[:, cols(s)], 1, 1)
            if s == 0:
                oacc[...] = more
            else:
                oacc[...] += more
            if kind == "f":
                gh[ts, cols(s)] = slope.astype(bf16)
        else:
            slope = gh[ts, cols(s)].astype(f32)
        if "b" in kind:
            b = (g_buf[slot] * slope).astype(bf16)
            gh[ts, cols(s)] = b
            more = dot(b, up_v[:, cols(s)], 1, 1)
            if s == 0:
                g2[...] = more
            else:
                g2[...] += more
        if kind == "b":
            up_gradient(s)
            down_gradient(s)
        if s == J - 1:
            if kind == "f":
                output_rows(t)
            elif kind == "fb":
                output_rows(t)
                cotT[:, lane(halves[t] * half, half)] = cot_v[ts, :].T
                norm_rows(t)
                cotT[:, lane(halves[0] * half, half)] = cot_v[rows_of[0], :].T
            else:
                norm_rows(t)
    if Y > 2:
        store(tok_v.at[line(p * T, T), :], home.at[p])
        for k in range(1, Y):
            to = (p + k) % Y
            send(("home", k), tok_v.at[line(to * T, T), :], home.at[p], others[k - 1])
    vec_out[0:1, :] = sums[0]
    vec_out[1:2, :] = sums[1]
    value = dot(att_v[...], n2[...], 0, 0).astype(bf16)
    w = out_own.shape[2]
    for d in range(S):
        out_v[d] = value[:, d * w : (d + 1) * w]
    for q in range(Y):
        store(out_v.at[C * q + c], out_own.at[q])
        send(("out", q), out_v.at[C * q + 1 - c], out_other.at[q], sibling)
    for task in tasks:
        task.came()
    for task in tasks:
        task.gone()


def dense(place, att, tok, cot, out_g, up_g, down_g, vec):
    M, D = att.shape
    S, nb, Y, C = place.blk, place.batch, place.Y, place.C
    T = M // Y
    H = D // C
    aligned = up_g.shape[-1] % 128 == 0 and down_g.shape[-1] % 128 == 0
    out_w = out_g.reshape(S, D, -1)
    FF = S * up_g.shape[-1]
    if aligned:
        up_w = up_g.reshape(S, D, -1)
        down_w = down_g.reshape((S, nb) + down_g.shape[-2:])
    else:
        up_w, down_w = joined(up_g, 0), joined(down_g, 1)
    anywhere = pl.BlockSpec(memory_space=pl.ANY)
    inside = pl.BlockSpec(memory_space=pltpu.VMEM)
    pieces = [
        jax.ShapeDtypeStruct((Y, D, up_g.shape[-1]), bf16),
        jax.ShapeDtypeStruct((Y, nb) + down_g.shape[-2:], bf16),
        jax.ShapeDtypeStruct((Y, D, out_g.shape[-1]), bf16),
    ]
    none = (1, 16, 128)
    up_cut = none if aligned else (D // up_g.shape[-1], D, up_g.shape[-1])
    down_cut = none if aligned else (D // down_g.shape[-1], D, down_g.shape[-1])
    loads = 8 + S + S * nb
    J = FF // D
    down_count = J * Y * (D // down_g.shape[-1])
    copies = 2 * (Y - 1) + 2 * Y + S + down_count + 4 * Y + 8
    results = pl.pallas_call(
        functools.partial(dense_kernel, place, aligned),
        out_shape=[
            jax.ShapeDtypeStruct((Y, T, D), bf16),
            jax.ShapeDtypeStruct((M, D), f32),
            jax.ShapeDtypeStruct((S * T, H), bf16),
        ]
        + pieces
        + pieces
        + [jax.ShapeDtypeStruct((2, D), f32)],
        in_specs=[anywhere] * 6 + [inside],
        out_specs=[anywhere] * 9 + [inside],
        scratch_shapes=[
            pltpu.VMEM((M, D), bf16),
            pltpu.VMEM((M, D), bf16),
            pltpu.VMEM((M, D), bf16),
            pltpu.VMEM(out_w.shape, bf16),
            pltpu.VMEM((D, FF), bf16),
            pltpu.VMEM((D, FF), bf16),
            pltpu.VMEM((D, D), bf16),
            pltpu.VMEM((M, D), f32),
            pltpu.VMEM((M, D), bf16),
            pltpu.VMEM((M, FF), bf16),
            pltpu.VMEM((M, FF), bf16),
            pltpu.VMEM((D, M), bf16),
            pltpu.VMEM((D, M), bf16),
            pltpu.VMEM((M // 2, D), f32),
            pltpu.VMEM((M // 2, D), f32),
            pltpu.VMEM((2, M // 2, D), f32),
            pltpu.VMEM((2, M // 2, D), f32),
            pltpu.VMEM((2, D, D), bf16) if aligned else pltpu.VMEM((1, 16, 128), bf16),
            pltpu.VMEM(up_cut, bf16),
            pltpu.VMEM(down_cut, bf16),
            pltpu.SemaphoreType.DMA((loads,)),
            pltpu.SemaphoreType.DMA((copies,)),
            pltpu.SemaphoreType.DMA((copies,)),
            pltpu.SemaphoreType.DMA((copies,)),
        ],
        compiler_params=pltpu.CompilerParams(
            collective_id=2, has_side_effects=True, vmem_limit_bytes=62 << 20
        ),
        name="dense",
    )(att, tok, cot, out_w, up_w, down_w, vec)
    home, gm, heads = results[:3]
    shapes = [(Y,) + up_g.shape[2:], (Y,) + down_g.shape[2:], (Y,) + out_g.shape[2:]]
    own = [value.reshape(shape) for value, shape in zip(results[3:6], shapes)]
    other = [value.reshape(shape) for value, shape in zip(results[6:9], shapes)]
    return home, gm, heads, own, other, results[9]


def hand_over_kernel(place, n, *refs):
    given, vec, out, vec_out = refs[:n], refs[n], refs[n + 1 : 2 * n + 1], refs[2 * n + 1]
    whole, between, sem = refs[2 * n + 2], refs[2 * n + 3 : 3 * n + 3], refs[3 * n + 3]
    here = [pltpu.make_async_copy(given[i], between[i], sem.at[0, i]) for i in range(n)]
    away = [pltpu.make_async_copy(between[i], out[i], sem.at[1, i]) for i in range(n)]
    start_all(here)
    H = vec.shape[1]
    whole[0:4, 0:H] = vec[0:4, :]
    whole[0:4, H:] = vec[4:8, :]
    me = lax.axis_index("blk")
    w = vec_out.shape[1]
    for d in range(place.blk):

        @pl.when(me == d)
        def _():
            vec_out[...] = whole[0:4, d * w : (d + 1) * w]

    for i in range(n):
        here[i].wait()
        away[i].start()
    for copy in away:
        copy.wait()


def hand_over(place, given, vec):
    n = len(given)
    anywhere = pl.BlockSpec(memory_space=pl.ANY)
    inside = pl.BlockSpec(memory_space=pltpu.VMEM)
    H = vec.shape[1]
    return pl.pallas_call(
        functools.partial(hand_over_kernel, place, n),
        out_shape=[jax.ShapeDtypeStruct(v.shape, v.dtype) for v in given]
        + [jax.ShapeDtypeStruct((4, 2 * H // place.blk), f32)],
        in_specs=[anywhere] * n + [inside],
        out_specs=[anywhere] * n + [inside],
        scratch_shapes=[pltpu.VMEM((8, 2 * H), f32)]
        + [pltpu.VMEM(v.shape, v.dtype) for v in given]
        + [pltpu.SemaphoreType.DMA((2, n))],
        compiler_params=pltpu.CompilerParams(vmem_limit_bytes=62 << 20),
        name="hand_over",
    )(*given, vec)


def normed(values):
    average = jnp.mean(values, axis=-1, keepdims=True)
    centered = values - average
    variance = jnp.mean(centered * centered, axis=-1, keepdims=True)
    factor = lax.rsqrt(variance + epsilon)
    return centered * factor, factor


def norm_back(grad, gain, unit, factor):
    e = grad * gain
    return factor * (
        e - jnp.mean(e, axis=-1, keepdims=True) - unit * jnp.mean(e * unit, axis=-1, keepdims=True)
    )


def joined(gathered, axis):
    Y, C, Z, X, r, w = gathered.shape
    if axis == 0:
        return gathered.reshape(Y * C, Z * X * r, w).transpose(1, 0, 2).reshape(Z * X * r, -1)
    return gathered.reshape(Y * C, Z * X, r, w).transpose(0, 2, 1, 3).reshape(Y * C * r, -1)


def parted(whole, place, axis):
    Y, C, Z, X = place.Y, place.C, place.Z, place.X
    rows, columns = whole.shape
    if axis == 0:
        value = whole.reshape(Z * X, rows // (Z * X), Y * C, columns // (Y * C))
        value = value.transpose(2, 0, 1, 3)
    else:
        value = whole.reshape(Y * C, rows // (Y * C), Z * X, columns // (Z * X))
        value = value.transpose(0, 2, 1, 3)
    return value.reshape((Y, C, Z, X) + value.shape[2:])


def body(
    place,
    tokens,
    proj_weight,
    out_weight,
    up_weight,
    down_weight,
    gain_one,
    bias_one,
    gain_two,
    bias_two,
    segments,
    present,
    cotangent,
):
    rows, block, width = tokens.shape
    Y = place.Y
    row = lax.broadcasted_iota(jnp.int32, (16, width // place.blk), 0)
    vec_in = jnp.zeros(row.shape, bf16)
    for i, vector in enumerate((gain_one, bias_one, gain_two, bias_two)):
        vec_in = jnp.where(row == i, vector[None, :], vec_in)
    (
        out_g, up_g, down_g, tok_mine, vec, begin, projected, proj_own, normed_t,
        attended_low, attended_t, log_total,
    ) = forward(
        place,
        [proj_weight, out_weight, up_weight, down_weight.T],
        tokens,
        segments,
        present,
        vec_in,
    )
    tok_mine = tok_mine.reshape(Y * block, width)
    output, grad_middle, grad_heads, own, other, vec_two = dense(
        place, attended_low, tok_mine, cotangent, out_g, up_g, down_g, vec
    )
    order = (2, 0, 1)
    proj_sum, out_sum, up_sum, down_sum, vec_sum, token_grad = backward(
        place,
        [own[i] for i in order],
        [other[i] for i in order],
        proj_weight.shape,
        begin,
        projected,
        grad_heads,
        attended_t,
        log_total,
        normed_t,
        proj_own,
        tok_mine,
        grad_middle,
        vec,
        vec_two,
    )
    output, token_grad, proj_sum, out_sum, up_sum, down_sum, vectors = hand_over(
        place, (output, token_grad, proj_sum, out_sum, up_sum, down_sum), vec_sum
    )
    return (
        output,
        token_grad,
        proj_sum,
        out_sum,
        up_sum,
        down_sum.T,
        vectors[0],
        vectors[1],
        vectors[2],
        vectors[3],
    )


def solution(mesh):
    place = Place((mesh.shape["batch"], mesh.shape["blk"]))
    weight, vector = P("batch", "blk"), P("blk")
    row = P("batch", "blk", None)
    in_specs = (row,) + (weight,) * 4 + (vector,) * 4 + (weight,) * 2 + (row,)
    out_specs = (row, row) + (weight,) * 4 + (vector,) * 4
    return jax.shard_map(
        functools.partial(body, place),
        mesh=mesh,
        in_specs=in_specs,
        out_specs=out_specs,
        check_vma=False,
    )
```

```python
import functools

import jax
import jax.numpy as jnp
from jax import lax
from jax.experimental import pallas as pl
from jax.experimental.pallas import tpu as pltpu
from jax.sharding import PartitionSpec as P

HEADS = 12
HEAD_DIM = 64
CORES = 2
LANE_X = 2
MESH = pl.DeviceIdType.MESH
LOG2E = 1.4426950408889634
epsilon = 1e-05
masked = -1e30
bf16 = jnp.bfloat16
f32 = jnp.float32


def dot(left, right, left_dim, right_dim):
    return lax.dot_general(
        left, right, (((left_dim,), (right_dim,)), ((), ())), preferred_element_type=f32
    )


class Place:
    def __init__(self, sizes):
        self.batch, self.blk = sizes
        self.Z, self.X = self.batch // LANE_X, LANE_X
        self.Y, self.C = self.blk // CORES, CORES

    def here(self):
        b, d = lax.axis_index("batch"), lax.axis_index("blk")
        return b // self.X, b % self.X, d // self.C, d % self.C

    def device(self, z, x, p, c):
        return (z * self.X + x, p * self.C + c)

    def across_z(self):
        return [k for k in range(2, self.Z)] + [1]

    def mirror(self, z, k):
        for bit in range(self.Z.bit_length()):
            if k >> bit & 1:
                z = z + (1 << bit) - (2 << bit) * (z // (1 << bit) % 2)
        return z


class Wire:
    def __init__(self, send_sem, recv_sem):
        self.send_sem, self.recv_sem, self.names = send_sem, recv_sem, {}

    def copy(self, name, src, dst, device):
        i = self.names.setdefault(name, len(self.names))
        return pltpu.make_async_remote_copy(
            src_ref=src,
            dst_ref=dst,
            send_sem=self.send_sem.at[i],
            recv_sem=self.recv_sem.at[i],
            device_id=device,
            device_id_type=MESH,
        )


def start_all(copies):
    for copy in copies:
        copy.start()


def arrive_all(copies):
    for copy in copies:
        copy.wait_recv()


def leave_all(copies):
    for copy in copies:
        copy.wait_send()


def first_rows(rows, sixths):
    return min(rows - 16, 16 * ((rows * sixths // 6) // 16)) if rows > 16 else 0


def greet(place, partners):
    barrier = pltpu.get_barrier_semaphore()
    for partner in partners:
        pl.semaphore_signal(barrier, inc=1, device_id=partner, device_id_type=MESH)
    pl.semaphore_wait(barrier, len(partners))


def partners_of(place):
    z, x, p, c = place.here()
    found = [place.device(place.mirror(z, k), x, p, c) for k in place.across_z()]
    found += [place.device(z, 1 - x, p, c)]
    found += [place.device(z, x, (p + k) % place.Y, c) for k in range(1, place.Y)]
    found += [place.device(z, x, p, 1 - c)]
    return found


def head_masked(value, h, axis):
    index = lax.broadcasted_iota(jnp.int32, value.shape, axis)
    return jnp.where((index // HEAD_DIM) == h, value, jnp.zeros_like(value))


class Spreading:
    def __init__(self, place, wire, name, spots, shard, whole, deep, low):
        self.place, self.wire, self.name, self.spots = place, wire, name, spots
        self.shard, self.whole = shard, whole
        self.r = shard.shape[0]
        self.g = sixths(self.r, deep)
        self.h = self.g + sixths(self.r, low)

    def copy(self, what, src, dst, device):
        return self.wire.copy((self.name, what), src, dst, device)

    def sides(self):
        z, x, p, c = self.spots
        place = self.place
        along_y = [(k, place.device(z, x, (p + k) % place.Y, c)) for k in range(1, place.Y)]
        along_z = [(k, place.device(place.mirror(z, k), x, p, c)) for k in place.across_z()]
        return place.device(z, 1 - x, p, c), along_y, along_z

    def deep_one(self):
        z, x, p, c = self.spots
        src, dst = self.shard.at[0 : self.g], self.whole.at[p, c, z, x, 0 : self.g]
        return [self.copy(("dy", k), src, dst, side) for k, side in self.sides()[1]]

    def deep_two(self):
        z, x, p, c = self.spots
        part = self.whole.at[:, c, z, x, 0 : self.g]
        return [self.copy("dx", part, part, self.sides()[0])]

    def deep_three(self):
        z, x, p, c = self.spots
        part = self.whole.at[:, c, z, :, 0 : self.g]
        return [self.copy(("dz", k), part, part, side) for k, side in self.sides()[2]]

    def along_z(self, what, rows):
        z, x, p, c = self.spots
        src, dst = self.shard.at[rows], self.whole.at[p, c, z, x, rows]
        return [self.copy((what, k), src, dst, side) for k, side in self.sides()[2]]

    def low_zero(self):
        return self.along_z("za", slice(self.g, self.h))

    def high_zero(self):
        return self.along_z("zb", slice(self.h, self.r))

    def low_one(self):
        z, x, p, c = self.spots
        part = self.whole.at[p, c, :, x, self.g : self.h]
        return [self.copy("xa", part, part, self.sides()[0])]

    def high_one(self):
        z, x, p, c = self.spots
        part = self.whole.at[p, c, :, x, self.h : self.r]
        return [self.copy(("yb", k), part, part, side) for k, side in self.sides()[1]]

    def low_two(self):
        z, x, p, c = self.spots
        part = self.whole.at[p, c, :, :, self.g : self.h]
        return [self.copy(("ya", k), part, part, side) for k, side in self.sides()[1]]

    def high_two(self):
        z, x, p, c = self.spots
        part = self.whole.at[:, c, :, x, self.h : self.r]
        return [self.copy("xb", part, part, self.sides()[0])]

    def to_core(self, what, rows):
        z, x, p, c = self.spots
        part = self.whole.at[:, c, :, :, rows]
        return [self.copy(what, part, part, self.place.device(z, x, p, 1 - c))]

    def low_three(self):
        return self.to_core("ca", slice(self.g, self.h))

    def high_three(self):
        return self.to_core("cb", slice(self.h, self.r))

    def deep_four(self):
        return self.to_core("cd", slice(0, self.g))

    def chains(self):
        found = []
        if self.g:
            found.append([self.deep_one, self.deep_two, self.deep_three, self.deep_four])
        if self.g < self.h:
            found.append([self.low_zero, self.low_one, self.low_two, self.low_three])
        if self.h < self.r:
            found.append([self.high_zero, self.high_one, self.high_two, self.high_three])
        return found

    def begin(self):
        for chain in self.chains():
            start_all(chain[0]())

    def step(self, group, number):
        chain = (
            [self.deep_one, self.deep_two, self.deep_three, self.deep_four],
            [self.low_zero, self.low_one, self.low_two, self.low_three],
            [self.high_zero, self.high_one, self.high_two, self.high_three],
        )[group]
        arrive_all(chain[number - 1]())
        start_all(chain[number]())

    def arrive(self):
        for chain in self.chains():
            arrive_all(chain[3]())

    def leave(self):
        for chain in self.chains():
            for stage in chain:
                leave_all(stage())


FORWARD_PLAN = (
    "t1", "O1d", "V", "D1d", "O2d", "t2", "U1d", "N0", "P1a", "P1b", "t3", "P2b", "P2a",
    "U1b", "K", "U1a", "D1b", "P3b", "D1a", "P3a", "N2", "N3", "W", "U2b", "U2a", "D2d",
    "J", "S00", "S01", "D2b", "D2a", "S02", "S10", "O3d", "S11", "S12", "U2d", "S20",
    "S21", "S22", "U3a", "S30", "U3b", "D3b", "U3d", "S31", "D3a", "D3d", "S32",
)
ROW_PARTS = 4


def forward_kernel(place, n, BQ, *refs):
    shards, (tok, segments, present, vec_in) = refs[: n + 1], refs[n + 1 : n + 5]
    outs = refs[n + 5 :]
    wholes = outs[:n]
    (tok_out, vec_out, begin, proj_out, w_out, normedT_out, att_out, oT_out, lt) = outs[
        n : n + 9
    ]
    (
        proj_v, tok_v, tag, tag_v, vec_v, n_v, nT, wv, pv, vT, att, oT,
        send_sem, recv_sem, local_sem,
    ) = outs[n + 9 :]
    spots = place.here()
    z, x, p, c = spots
    Z, X, Y, C = place.Z, place.X, place.Y, place.C
    D, W3 = wv.shape
    H = W3 // 3
    L = pv.shape[0]
    T = L // (Y * C)
    U = BQ // T
    pairs = H // 128
    nq = L // BQ
    wire = Wire(send_sem, recv_sem)
    sibling = place.device(z, x, p, 1 - c)
    flows = [
        Spreading(place, wire, m, spots, shards[m], proj_v if m == 0 else wholes[m - 1], *way)
        for m, way in enumerate(((0, 3), (6, 0), (1, 3), (1, 3)))
    ]

    def local(i, src, dst):
        return pltpu.make_async_copy(src, dst, local_sem.at[i])

    def lane(offset, size):
        return pl.ds(pl.multiple_of(offset, 128), size)

    def line(offset, size):
        return pl.ds(pl.multiple_of(offset, 16), size)

    row_parts = (("vec", vec_in, vec_v), ("tag", tag, tag_v), ("tok", tok, tok_v))

    def along_y(what, src, dst):
        found = []
        for k in range(1, Y):
            to = (p + k) % Y
            device = place.device(z, x, to, c)
            if what == "tok":
                for i in range(ROW_PARTS):
                    rows = slice(i * T // ROW_PARTS, (i + 1) * T // ROW_PARTS)
                    found.append(
                        wire.copy(
                            (what, "y", k, i), src.at[to, rows], dst.at[p, c, rows], device
                        )
                    )
            else:
                piece = src if what == "vec" else src.at[to]
                found.append(wire.copy((what, "y", k), piece, dst.at[p, c], device))
        return found

    def send_tokens(i):
        start_all(along_y(*row_parts[2])[i::ROW_PARTS])

    def to_sibling_own(what, src, dst):
        piece = src if what == "vec" else src.at[p]
        return wire.copy((what, "own"), piece, dst.at[p, c], sibling)

    def to_sibling(what, dst):
        found = []
        for k in range(1, Y):
            q = (p + k) % Y
            found.append(wire.copy((what, "pass", k), dst.at[q, c], dst.at[q, c], sibling))
        return found

    position = lax.broadcasted_iota(jnp.int32, (Y, T), 1) + (p * C + c) * T
    tags = jnp.where(present[...] == 1, segments[...], -1 - position)
    for q in range(Y):
        tag[q] = jnp.broadcast_to(tags[q : q + 1, :], tag.shape[1:])
    greet(place, partners_of(place))
    start_all(along_y(*row_parts[0]))
    for part in row_parts:
        to_sibling_own(*part).start()
    for flow in flows:
        flow.begin()
    start_all(along_y(*row_parts[1]))
    send_tokens(0)
    kept = [local(m, shards[m], flows[m].whole.at[p, c, z, x]) for m in range(n + 1)]
    kept += [
        local(n + 1, vec_in, vec_v.at[p, c]),
        local(n + 2, tag.at[p], tag_v.at[p, c]),
        local(n + 3, tok.at[p], tok_v.at[p, c]),
    ]
    start_all(kept)
    saves = [
        local(n + 5, nT, normedT_out),
        local(n + 6, tok_v.at[:, c], tok_out),
        local(n + 7, pv, proj_out),
        local(n + 8, wv, w_out),
    ]

    def norm_block(q, i):
        unit, factor = normed(tok_v[q, i].astype(f32))
        low = (unit * vec_out[0:1, :] + vec_out[1:2, :]).astype(bf16)
        rows = line((q * C + i) * T, T)
        n_v[rows, :] = low
        nT[:, lane((q * C + i) * T, T)] = low.T

    waited = set()

    def own_shard(m):
        if m not in waited:
            kept[m].wait()
            waited.add(m)

    def advance(m, group, number):
        own_shard(m)
        flows[m].step(group, number)

    def vector_pass():
        arrive_all(along_y(*row_parts[0]))
        start_all(to_sibling("vec", vec_v))

    def norm_near():
        for copy in kept[n + 1 :]:
            copy.wait()
        to_sibling_own(*row_parts[0]).wait_recv()
        arrive_all(to_sibling("vec", vec_v))
        share = vec_v.shape[3]
        for q in range(Y):
            for i in range(C):
                lo = (q * C + i) * share
                vec_out[:, lo : lo + share] = vec_v[q, i, 0:8, :].astype(f32)
        norm_block(p, c)
        to_sibling_own(*row_parts[2]).wait_recv()
        norm_block(p, 1 - c)

    def row_pass():
        for what, src, dst in row_parts[1:]:
            arrive_all(along_y(what, src, dst))
            start_all(to_sibling(what, dst))

    def norm_far():
        for k in range(1, Y):
            norm_block((p + k) % Y, c)

    def norm_last():
        arrive_all(to_sibling("tok", tok_v))
        for k in range(1, Y):
            norm_block((p + k) % Y, 1 - c)
        start_all(saves[:2])
        to_sibling_own(*row_parts[1]).wait_recv()
        arrive_all(to_sibling("tag", tag_v))
        tags = [tag_v[q, i, 0:1, :] for q in range(Y) for i in range(C)]
        counts = []
        for s in range(4):
            hits = sum((t == s).astype(f32) for t in tags)
            counts.append(jnp.sum(hits, axis=1, keepdims=True).astype(jnp.int32))
        for b, t in enumerate(tags):
            first = sum(jnp.where(t > s, counts[s], 0) for s in range(4))
            position = lax.broadcasted_iota(jnp.int32, (1, T), 1) + b * T
            begin[:, b * T : (b + 1) * T] = jnp.where(t < 0, position, first)

    def weight_columns():
        flows[0].arrive()
        r, w = proj_v.shape[4:]
        for mine in range(C):

            @pl.when(c == mine)
            def _():
                for third in range(3):
                    base = third * D + mine * H
                    for d in range(Y * C):
                        a, b = max(base, d * w), min(base + H, (d + 1) * w)
                        if a >= b:
                            continue
                        to = third * H + a - base
                        for i in range(Z * X):
                            wv[i * r : (i + 1) * r, to : to + b - a] = proj_v[
                                d // C, d % C, i // X, i % X, :, a - d * w : b - d * w
                            ]

    def project_all():
        def project(i, nothing):
            rows = line(i * BQ, BQ)
            pv[rows, :] = dot(n_v[rows, :], wv[...], 1, 0).astype(bf16)
            return nothing

        lax.fori_loop(0, nq, project, 0)
        values = pv[:, 2 * H :].T
        for h in range(2 * pairs):
            vT[h, 0:HEAD_DIM, :] = values[h * HEAD_DIM : (h + 1) * HEAD_DIM, :]
            vT[h, HEAD_DIM:, :] = jnp.ones((16, L), bf16)
        start_all(saves[2:])

    scale = HEAD_DIM ** (-0.5) * LOG2E

    def block_copies(qi):
        found = []
        for u in range(U):
            b = qi * U + u
            q, owner = b // C, b % C
            src = att.at[b * T : (b + 1) * T, :]
            dst = att_out.at[q * T : (q + 1) * T, lane(c * H, H)]
            found.append(
                (owner, local(n + 9 + q, src, dst), wire.copy(("att", q), src, dst, sibling))
            )
        return found

    acts = {
        "V": vector_pass,
        "N0": norm_near,
        "K": row_pass,
        "N2": norm_far,
        "N3": norm_last,
        "W": weight_columns,
        "J": project_all,
    }
    for m, name in enumerate("POUD"):
        for group, letter in enumerate("dab"):
            for number in (1, 2, 3):
                acts[f"{name}{number}{letter}"] = functools.partial(advance, m, group, number)
    for i in range(1, ROW_PARTS):
        acts[f"t{i}"] = functools.partial(send_tokens, i)
    events, spot = {}, None
    for name in FORWARD_PLAN:
        if name[0] == "S":
            spot = (int(name[1]), int(name[2]))
        else:
            events.setdefault(spot, []).append(name)
    for name in events[None]:
        acts[name]()
    for qi in range(nq):
        qs = slice(qi * BQ, (qi + 1) * BQ)
        d0 = qi * BQ
        part = BQ // 2
        cuts = []
        if d0 and qi < nq - 1:
            cuts = [(0, part, 1, 0), (part, min(BQ, d0), 0, 0)]
            cuts += [(a, a + BQ, 0, 0) for a in range(BQ, d0, BQ)]
        elif d0:
            cuts = [(a, a + BQ, 1, 0) for a in range(0, d0, BQ)]
        cuts += [(d0, d0 + part, 2, 0), (d0 + part, d0 + BQ, 2, part)]

        def widened(value, qa, blank):
            if not qa:
                return value
            return jnp.concatenate([jnp.full((value.shape[0], qa), blank, f32), value], axis=1)

        def one_pair(pair, nothing):
            cols = lane(pair * 128, 128)
            k_cols = lane(H + pair * 128, 128)
            qT = pv[qs, cols].T
            found, scores = [], []
            for h in range(2):
                query = head_masked(qT, h, 0)
                parts = []
                for a, b, mode, qa in cuts:
                    s = dot(pv[a:b, k_cols], query[:, qa:], 1, 0)
                    if mode:
                        shape = (b - a, BQ - qa)
                        key_pos = lax.broadcasted_iota(jnp.int32, shape, 0) + a
                        visible = key_pos >= begin[:, d0 + qa : d0 + BQ]
                        if mode == 2:
                            query_pos = lax.broadcasted_iota(jnp.int32, shape, 1) + d0 + qa
                            visible = jnp.logical_and(visible, key_pos <= query_pos)
                        s = jnp.where(visible, s, masked)
                    parts.append(s)
                scores.append(parts)
            for h in range(2):
                tops = [
                    widened(jnp.max(s, axis=0, keepdims=True), cut[3], masked)
                    for cut, s in zip(cuts, scores[h])
                ]
                top = functools.reduce(jnp.maximum, tops) * scale
                accum = jnp.zeros((vT.shape[1], BQ), f32)
                for (a, b, mode, qa), s in zip(cuts, scores[h]):
                    e = jnp.exp2(s * scale - top[:, qa:]).astype(bf16)
                    accum = accum + widened(dot(vT[pair * 2 + h, :, a:b], e, 1, 0), qa, 0.0)
                total = accum[HEAD_DIM : HEAD_DIM + 1]
                result = accum[:HEAD_DIM] / total
                rows = pl.ds(pl.multiple_of(pair * 128 + h * HEAD_DIM, HEAD_DIM), HEAD_DIM)
                oT[rows, qs] = result
                found.append(result)
                lt[pair, h : h + 1, qs] = top + jnp.log2(total)
            att[qs, cols] = jnp.concatenate(found, axis=0).astype(bf16).T
            for number in range(pairs):
                if (qi, number) in events:

                    @pl.when(pair == number)
                    def _():
                        for name in events[qi, number]:
                            acts[name]()

            return nothing

        lax.fori_loop(0, pairs, one_pair, 0)
        save = local(n + 9 + Y + qi, oT.at[:, qs], oT_out.at[:, qs])
        save.start()
        saves.append(save)
        for owner, keep, send in block_copies(qi):

            @pl.when(owner == c)
            def _():
                keep.start()

            @pl.when(owner != c)
            def _():
                send.start()

    for flow in flows[1:]:
        flow.arrive()
    for qi in range(nq):
        for owner, keep, send in block_copies(qi):

            @pl.when(owner == c)
            def _():
                keep.wait()

            @pl.when(owner != c)
            def _():
                send.wait_send()

            @pl.when(owner == c)
            def _():
                send.wait_recv()

    for what, src, dst in row_parts:
        leave_all(along_y(what, src, dst))
        to_sibling_own(what, src, dst).wait_send()
        leave_all(to_sibling(what, dst))
    for flow in flows:
        flow.leave()
    for copy in saves:
        copy.wait()


def forward(place, shards, tok, segments, present, vec_in):
    n = len(shards) - 1
    Z, X, Y, C = place.Z, place.X, place.Y, place.C
    R, T, D = tok.shape
    L = Y * C * T
    H = D // C
    W3 = 3 * H
    BQ = 512
    pairs = H // 128
    inside = pl.BlockSpec(memory_space=pltpu.VMEM)
    anywhere = pl.BlockSpec(memory_space=pl.ANY)
    out_shape = [jax.ShapeDtypeStruct((Y, C, Z, X) + m.shape, bf16) for m in shards[1:]]
    out_shape += [
        jax.ShapeDtypeStruct((Y, T, D), bf16),
        jax.ShapeDtypeStruct((8, D), f32),
        jax.ShapeDtypeStruct((1, L), jnp.int32),
        jax.ShapeDtypeStruct((L, W3), bf16),
        jax.ShapeDtypeStruct((D, W3), bf16),
        jax.ShapeDtypeStruct((D, L), bf16),
        jax.ShapeDtypeStruct((Y * T, D), bf16),
        jax.ShapeDtypeStruct((H, L), f32),
        jax.ShapeDtypeStruct((pairs, 2, L), f32),
    ]
    each = 3 * (Z - 1) + 3 * (Y - 1) + 6
    copies = (n + 1) * each + 3 * (2 * (Y - 1) + 1) + ROW_PARTS * (Y - 1) + Y
    scratch = [
        pltpu.VMEM((Y, C, Z, X) + shards[0].shape, bf16),
        pltpu.VMEM((Y, C, T, D), bf16),
        pltpu.VMEM((Y, 8, T), jnp.int32),
        pltpu.VMEM((Y, C, 8, T), jnp.int32),
        pltpu.VMEM((Y, C) + vec_in.shape, bf16),
        pltpu.VMEM((L, D), bf16),
        pltpu.VMEM((D, L), bf16),
        pltpu.VMEM((D, W3), bf16),
        pltpu.VMEM((L, W3), bf16),
        pltpu.VMEM((H // HEAD_DIM, HEAD_DIM + 16, L), bf16),
        pltpu.VMEM((L, H), bf16),
        pltpu.VMEM((H, L), f32),
        pltpu.SemaphoreType.DMA((copies,)),
        pltpu.SemaphoreType.DMA((copies,)),
        pltpu.SemaphoreType.DMA((n + 9 + Y + L // BQ,)),
    ]
    return pl.pallas_call(
        functools.partial(forward_kernel, place, n, BQ),
        out_shape=out_shape,
        in_specs=[inside] * (n + 1) + [anywhere] + [inside] * 3,
        out_specs=[anywhere] * (n + 1) + [inside] * 2 + [anywhere] * 5 + [inside],
        scratch_shapes=scratch,
        compiler_params=pltpu.CompilerParams(
            collective_id=0, has_side_effects=True, vmem_limit_bytes=60 << 20
        ),
        name="forward",
    )(*shards, tok, segments, present, vec_in)


def sixths(rows, count):
    return rows if count == 6 else 0 if count == 0 else max(16, 16 * (rows * count // 96))


class Summing:
    def __init__(self, place, wire, name, spots, acc, xa, yb, ya, xb, zz):
        self.place, self.wire, self.name, self.spots = place, wire, name, spots
        self.acc, self.xa, self.yb, self.ya, self.xb, self.zz = acc, xa, yb, ya, xb, zz
        self.rows = acc.shape[3]
        self.h = xa.shape[2]

    def one(self):
        z, x, p, c = self.spots
        place, h, r = self.place, self.h, self.rows
        side = place.device(z, 1 - x, p, c)
        found = [
            self.wire.copy((self.name, "xa"), self.acc.at[:, :, 1 - x, 0:h], self.xa, side)
        ]
        for k in range(1, place.Y):
            to = (p + k) % place.Y
            found.append(
                self.wire.copy(
                    (self.name, "yb", k),
                    self.acc.at[to, :, :, h:r],
                    self.yb.at[k - 1],
                    place.device(z, x, to, c),
                )
            )
        return found

    def two(self):
        z, x, p, c = self.spots
        place, h, r = self.place, self.h, self.rows
        found = []
        for k in range(1, place.Y):
            to = (p + k) % place.Y
            found.append(
                self.wire.copy(
                    (self.name, "ya", k),
                    self.acc.at[to, :, x, 0:h],
                    self.ya.at[k - 1],
                    place.device(z, x, to, c),
                )
            )
        side = place.device(z, 1 - x, p, c)
        found.append(
            self.wire.copy((self.name, "xb"), self.acc.at[p, :, 1 - x, h:r], self.xb, side)
        )
        return found

    def three(self):
        z, x, p, c = self.spots
        place = self.place
        found = []
        for k in place.across_z():
            to = place.mirror(z, k)
            found.append(
                self.wire.copy(
                    (self.name, "z", k),
                    self.acc.at[p, to, x],
                    self.zz.at[k - 1],
                    place.device(to, x, p, c),
                )
            )
        return found

    def add_one(self):
        z, x, p, c = self.spots
        place, h, r, acc = self.place, self.h, self.rows, self.acc
        ones = self.one()
        ones[0].wait_recv()

        def low(i, nothing):
            a, b = i // place.Z, i % place.Z
            total = acc[a, b, x, 0:h].astype(f32) + self.xa[a, b].astype(f32)
            acc[a, b, x, 0:h] = total.astype(bf16)
            return nothing

        lax.fori_loop(0, place.Y * place.Z, low, 0)
        twos = self.two()
        start_all(twos[:-1])
        arrive_all(ones[1:])

        def high(i, nothing):
            a, b = i // place.X, i % place.X
            total = acc[p, a, b, h:r].astype(f32)
            for k in range(place.Y - 1):
                total = total + self.yb[k, a, b].astype(f32)
            acc[p, a, b, h:r] = total.astype(bf16)
            return nothing

        lax.fori_loop(0, place.Z * place.X, high, 0)
        twos[-1].start()

    def add_two(self):
        z, x, p, c = self.spots
        place, h, r, acc = self.place, self.h, self.rows, self.acc
        arrive_all(self.two())

        def both(i, nothing):
            total = acc[p, i, x, 0:h].astype(f32)
            for k in range(place.Y - 1):
                total = total + self.ya[k, i].astype(f32)
            acc[p, i, x, 0:h] = total.astype(bf16)
            total = acc[p, i, x, h:r].astype(f32) + self.xb[i].astype(f32)
            acc[p, i, x, h:r] = total.astype(bf16)
            return nothing

        lax.fori_loop(0, place.Z, both, 0)
        start_all(self.three())

    def finish(self, target):
        z, x, p, c = self.spots
        arrive_all(self.three())
        total = self.acc[p, z, x].astype(f32)
        for k in range(self.place.Z - 1):
            total = total + self.zz[k].astype(f32)
        target[...] = total

    def leave(self):
        leave_all(self.one())
        leave_all(self.two())
        leave_all(self.three())


class DepthSum:
    def __init__(self, place, wire, name, spots, acc, zr, xr, yr):
        self.place, self.wire, self.name, self.spots = place, wire, name, spots
        self.acc, self.zr, self.xr, self.yr = acc, zr, xr, yr

    def one(self):
        z, x, p, c = self.spots
        place = self.place
        return [
            self.wire.copy(
                (self.name, "z", k),
                self.acc.at[:, place.mirror(z, k)],
                self.zr.at[k - 1],
                place.device(place.mirror(z, k), x, p, c),
            )
            for k in place.across_z()
        ]

    def two(self):
        z, x, p, c = self.spots
        side = self.place.device(z, 1 - x, p, c)
        return [self.wire.copy((self.name, "x"), self.acc.at[:, z, 1 - x], self.xr, side)]

    def three(self):
        z, x, p, c = self.spots
        place = self.place
        return [
            self.wire.copy(
                (self.name, "y", k),
                self.acc.at[(p + k) % place.Y, z, x],
                self.yr.at[k - 1],
                place.device(z, x, (p + k) % place.Y, c),
            )
            for k in range(1, place.Y)
        ]

    def add_one(self):
        z, x, p, c = self.spots
        place, acc = self.place, self.acc
        arrive_all(self.one())

        def add(i, nothing):
            a, b = i // place.X, i % place.X
            total = acc[a, z, b].astype(f32)
            for k in range(place.Z - 1):
                total = total + self.zr[k, a, b].astype(f32)
            acc[a, z, b] = total.astype(bf16)
            return nothing

        lax.fori_loop(0, place.Y * place.X, add, 0)
        start_all(self.two())

    def add_two(self):
        z, x, p, c = self.spots
        place, acc = self.place, self.acc
        arrive_all(self.two())

        def add(i, nothing):
            total = acc[i, z, x].astype(f32) + self.xr[i].astype(f32)
            acc[i, z, x] = total.astype(bf16)
            return nothing

        lax.fori_loop(0, place.Y, add, 0)
        start_all(self.three())

    def finish(self, target):
        z, x, p, c = self.spots
        arrive_all(self.three())
        total = self.acc[p, z, x].astype(f32)
        for k in range(self.place.Y - 1):
            total = total + self.yr[k].astype(f32)
        target[...] = total

    def leave(self):
        leave_all(self.one())
        leave_all(self.two())
        leave_all(self.three())


class ChunkSum:
    def __init__(self, place, wire, name, spots, acc, xr, zr, total, far):
        self.place, self.wire, self.name, self.spots = place, wire, name, spots
        self.acc, self.xr, self.zr, self.total, self.far = acc, xr, zr, total, far

    def along_x(self):
        z, x, p, c = self.spots
        side = self.place.device(z, 1 - x, p, c)
        return [self.wire.copy((self.name, "x"), self.acc.at[:, 1 - x], self.xr, side)]

    def along_z(self):
        z, x, p, c = self.spots
        place = self.place
        return [
            self.wire.copy(
                (self.name, "z", k),
                self.acc.at[place.mirror(z, k), x],
                self.zr.at[k - 1],
                place.device(place.mirror(z, k), x, p, c),
            )
            for k in place.across_z()
        ]

    def along_y(self):
        z, x, p, c = self.spots
        place = self.place
        return [
            self.wire.copy(
                (self.name, "y", k),
                self.total.at[0],
                self.total.at[k],
                place.device(z, x, (p + k) % place.Y, c),
            )
            for k in range(1, place.Y)
        ]

    def to_core(self):
        z, x, p, c = self.spots
        return [
            self.wire.copy(
                (self.name, "core"), self.total, self.far, self.place.device(z, x, p, 1 - c)
            )
        ]

    def go_z(self):
        z, x, p, c = self.spots
        arrive_all(self.along_x())

        def one(i, nothing):
            total = self.acc[i, x].astype(f32) + self.xr[i].astype(f32)
            self.acc[i, x] = total.astype(bf16)
            return nothing

        lax.fori_loop(0, self.place.Z, one, 0)
        start_all(self.along_z())

    def go_y(self):
        z, x, p, c = self.spots
        arrive_all(self.along_z())
        total = self.acc[z, x].astype(f32)
        for k in range(self.place.Z - 1):
            total = total + self.zr[k].astype(f32)
        self.total[0] = total.astype(bf16)
        start_all(self.along_y())

    def go_core(self):
        arrive_all(self.along_y())
        start_all(self.to_core())

    def result(self):
        arrive_all(self.to_core())
        return [
            sum(part[k].astype(f32) for k in range(self.place.Y)) for part in (self.total, self.far)
        ]

    def leave(self):
        for copies in (self.along_x(), self.along_z(), self.along_y(), self.to_core()):
            leave_all(copies)


BACKWARD_PLAN = (
    "U0", "S00", "S01", "O0", "S02", "S03", "U1", "C0x", "S10", "D0", "U2", "S11", "S12",
    "C0z", "S13", "C1x", "S20", "B3", "D1", "S21", "C1z", "B2", "S22", "S23", "D2", "T3",
    "C2x", "B1", "C0y", "O1", "UF", "T2", "B0", "C1y", "T1", "C0c", "T0", "C2z", "C1c",
    "Vc", "Vx", "C2y", "Vz", "O2", "C0r", "Vy", "C1r", "DF", "C2c", "OF", "Vr", "C2r",
)


def backward_kernel(place, n, BQ, *refs):
    (begin, proj, grad_in, oT_in, lt, normedT, w_in, tok, gm, vec, vec_two) = refs[:11]
    parts, others = refs[11 : 11 + n], refs[11 + n : 11 + 2 * n]
    outs = refs[11 + 2 * n :]
    sums, (vec_out, tg_home) = outs[: n + 1], outs[n + 1 : n + 3]
    landing = outs[n + 3 : 2 * n + 3]
    rest = outs[2 * n + 3 :]
    (
        pv, do, oT, wv, kT, dk, dv, nT,
        keep, g_send, g_recv, tok_v, gm_v, grads, v0, v1, v2, v3, vc, vy, vx, vz, whole,
    ) = rest[:23]
    buffers = rest[23 : 23 + 6 * n - 2]
    chunk_buffers = rest[23 + 6 * n - 2 : -3]
    send_sem, recv_sem, local_sem = rest[-3:]
    tg_v = g_recv
    spots = place.here()
    z, x, p, c = spots
    Z, X, Y, C = place.Z, place.X, place.Y, place.C
    L, W3 = pv.shape
    H = W3 // 3
    D = wv.shape[0]
    T = L // (Y * C)
    pairs = H // 128
    nq = L // BQ
    scale = HEAD_DIM ** (-0.5) * LOG2E
    scale_back = HEAD_DIM ** (-0.5)
    wire = Wire(send_sem, recv_sem)
    sibling = place.device(z, x, p, 1 - c)
    beside = place.device(z, 1 - x, p, c)
    adds = [DepthSum(place, wire, 0, spots, *buffers[:4])]
    adds += [
        Summing(place, wire, m, spots, *buffers[6 * m - 2 : 6 * m + 4]) for m in range(1, n)
    ]
    chunks = [
        ChunkSum(place, wire, ("chunk", i), spots, *chunk_buffers[5 * i : 5 * i + 5])
        for i in range(pairs)
    ]

    def local(i, src, dst):
        return pltpu.make_async_copy(src, dst, local_sem.at[i])

    def lane(offset, size):
        return pl.ds(pl.multiple_of(offset, 128), size)

    def line(offset, size):
        return pl.ds(pl.multiple_of(offset, 16), size)

    def out_fetch(pair):
        return local(2, oT_in.at[line(pair * 128, 128), :], oT)

    loads = [local(0, proj, pv), local(1, grad_in, do)]
    columns = local(3, w_in, wv)
    late = local(4 + 2 * n, normedT, nT)
    halves = [
        (local(4 + m, parts[m], adds[m].acc), local(4 + n + m, others[m], landing[m]))
        for m in range(n)
    ]
    start_all(halves[1])
    start_all(loads)
    out_fetch(0).start()
    for m in (2, 0):
        start_all(halves[m])
    start_all([late, columns])
    greet(place, partners_of(place))
    row_sem = 5 + 2 * n

    def core_add(m):
        for copy in halves[m]:
            copy.wait()
        acc, other = adds[m].acc, landing[m]

        def one(i, nothing):
            a, b, d = i // (Z * X), (i // X) % Z, i % X
            total = acc[a, b, d].astype(f32) + other[a, b, d].astype(f32)
            acc[a, b, d] = total.astype(bf16)
            return nothing

        lax.fori_loop(0, Y * Z * X, one, 0)

    for copy in loads:
        copy.wait()
    kT[...] = pv[:, H : 2 * H].T
    grads[...] = jnp.zeros_like(grads)

    U = BQ // T
    gain = vec[0:1, :]

    def sub_blocks(qi):
        found = []
        for u in range(U):
            block = qi * U + u
            found.append((u, block // C, block % C))
        return found

    reserved = send_sem.shape[0] - 3 * Y

    def g_wire(q):
        return pltpu.make_async_remote_copy(
            src_ref=g_send.at[q],
            dst_ref=g_recv.at[q],
            send_sem=send_sem.at[reserved + q],
            recv_sem=recv_sem.at[reserved + q],
            device_id=sibling,
            device_id_type=MESH,
        )

    def home_from(k):
        q = (p + k) % Y
        return pltpu.make_async_remote_copy(
            src_ref=tg_v.at[p],
            dst_ref=tg_home.at[q],
            send_sem=send_sem.at[reserved + Y + q],
            recv_sem=recv_sem.at[reserved + 2 * Y + q],
            device_id=place.device(z, x, q, c),
            device_id_type=MESH,
        )

    def home_to(q):
        return pltpu.make_async_remote_copy(
            src_ref=tg_v.at[q],
            dst_ref=tg_home.at[p],
            send_sem=send_sem.at[reserved + Y + q],
            recv_sem=recv_sem.at[reserved + 2 * Y + p],
            device_id=place.device(z, x, q, c),
            device_id_type=MESH,
        )

    def block_done(qi):
        if qi == nq - 1:
            columns.wait()
        g = dot(pv[line(qi * BQ, BQ), :], wv[...], 1, 1)
        for u, q, owner in sub_blocks(qi):
            rows = slice(u * T, (u + 1) * T)

            @pl.when(owner == c)
            def _():
                keep[(qi % 2 * U + u) // C] = g[rows, :]

            @pl.when(owner != c)
            def _():
                g_send[q] = g[rows, :].astype(bf16)
                g_wire(q).start()

    def pair_done(i):
        if i == 0:
            late.wait()
        wide = [pv[:, t * H + i * 128 : t * H + (i + 1) * 128] for t in range(3)]
        value = dot(nT[...], jnp.concatenate(wide, axis=1), 1, 0).astype(bf16)
        chunk = chunks[i]
        r = chunk.acc.shape[2]
        for b in range(Z * X):
            chunk.acc[b // X, b % X] = value[b * r : (b + 1) * r, :]
        start_all(chunk.along_x())

    def token_rows(qi):
        for u, q, owner in sub_blocks(qi):

            @pl.when(owner == c)
            def _():
                a = local(row_sem, tok.at[line(q * T, T)], tok_v)
                b = local(row_sem + 1, gm.at[line(q * T, T)], gm_v)
                a.start()
                b.start()
                g_wire(q).wait_recv()
                grad = keep[(qi % 2 * U + u) // C] + g_recv[q].astype(f32)
                a.wait()
                unit, factor = normed(tok_v[...].astype(f32))
                grads[0:1, :] += jnp.sum(grad * unit, axis=0, keepdims=True)
                grads[1:2, :] += jnp.sum(grad, axis=0, keepdims=True)
                b.wait()
                tg_v[q] = (gm_v[...] + norm_back(grad, gain, unit, factor)).astype(bf16)

                @pl.when(q == p)
                def _():
                    local(row_sem + 2, tg_v.at[q], tg_home.at[p]).start()

                @pl.when(q != p)
                def _():
                    home_to(q).start()

    def one_query(pair, qi):
        d0 = qi * BQ
        qs = slice(d0, d0 + BQ)
        cols = lane(pair * 128, 128)
        k_cols, v_cols = lane(H + pair * 128, 128), lane(2 * H + pair * 128, 128)
        q_val, do_val = pv[qs, cols], do[qs, cols]
        qT, doT = q_val.T, do_val.T
        part = BQ // 2
        cuts = []
        if d0 and qi < nq - 1:
            cuts = [(0, part, 1, 0), (part, min(BQ, d0), 0, 0)]
            cuts += [(a, a + BQ, 0, 0) for a in range(BQ, d0, BQ)]
        elif d0:
            cuts = [(a, a + BQ, 1, 0) for a in range(0, d0, BQ)]
        cuts += [(d0, d0 + part, 2, 0), (d0 + part, d0 + BQ, 2, part)]
        dqs = []
        for h in range(2):
            rows = slice(h * HEAD_DIM, (h + 1) * HEAD_DIM)
            kT_rows = pl.ds(pl.multiple_of(pair * 128 + h * HEAD_DIM, HEAD_DIM), HEAD_DIM)
            query, grad = head_masked(qT, h, 0), head_masked(doT, h, 0)
            q_nat, do_nat = head_masked(q_val, h, 1), head_masked(do_val, h, 1)
            delta = jnp.sum(doT[rows, :].astype(f32) * oT[rows, qs], axis=0, keepdims=True)
            log_total = lt[pair, h : h + 1, qs]
            dq = jnp.zeros((HEAD_DIM, BQ), f32)
            for a, b, mode, qa in cuts:
                sc = dot(pv[a:b, k_cols], query[:, qa:], 1, 0) * scale
                prob = jnp.exp2(sc - log_total[:, qa:])
                if mode:
                    shape = (b - a, BQ - qa)
                    key_pos = lax.broadcasted_iota(jnp.int32, shape, 0) + a
                    visible = key_pos >= begin[:, d0 + qa : d0 + BQ]
                    if mode == 2:
                        query_pos = lax.broadcasted_iota(jnp.int32, shape, 1) + d0 + qa
                        visible = jnp.logical_and(visible, key_pos <= query_pos)
                    prob = jnp.where(visible, prob, 0.0)
                dp = dot(pv[a:b, v_cols], grad[:, qa:], 1, 0)
                ds = (prob * (dp - delta[:, qa:])).astype(bf16)
                dv[a:b, :] += dot(prob.astype(bf16), do_nat[qa:], 1, 0)
                dk[a:b, :] += dot(ds, q_nat[qa:], 1, 0)
                more = dot(kT[kT_rows, a:b], ds, 1, 0)
                if qa:
                    more = jnp.concatenate([jnp.zeros((HEAD_DIM, qa), f32), more], axis=1)
                dq = dq + more
            dqs.append(dq)
        pv[qs, cols] = (jnp.concatenate(dqs, axis=0) * scale_back).astype(bf16).T
        pv[qs, k_cols] = (dk[qs, :] * scale_back).astype(bf16)
        pv[qs, v_cols] = dv[qs, :].astype(bf16)

    out_m, up_m, down_m = adds
    v_core = wire.copy("vc", v0, vc, sibling)
    v_x = wire.copy("vx", v1, vx, beside)
    v_z = [
        wire.copy(("vz", k), v2, vz.at[k - 1], place.device(place.mirror(z, k), x, p, c))
        for k in place.across_z()
    ]
    v_y = [
        wire.copy(("vy", k), v3, vy.at[k - 1], place.device(z, x, (p + k) % Y, c))
        for k in range(1, Y)
    ]

    def vector_core():
        grads[2:4, :] = vec_two[...]
        v0[0:4, :] = grads[0:4, 0:H]
        v0[4:8, :] = grads[0:4, H:]
        v_core.start()

    def vector_x():
        v_core.wait_recv()
        v1[...] = v0[...] + vc[...]
        v_x.start()

    def vector_z():
        v_x.wait_recv()
        v2[...] = v1[...] + vx[...]
        start_all(v_z)

    def vector_y():
        arrive_all(v_z)
        v3[...] = v2[...] + sum(vz[k] for k in range(Z - 1))
        start_all(v_y)

    def vector_end():
        arrive_all(v_y)
        vec_out[...] = v3[...] + sum(vy[k] for k in range(Y - 1))

    def chunk_end(i):
        mine, far = chunks[i].result()
        for half in range(C):

            @pl.when(c == half)
            def _():
                for value, core in ((mine, half), (far, 1 - half)):
                    for t in range(3):
                        lo = t * D + core * H + i * 128
                        whole[:, lo : lo + 128] = value[:, t * 128 : (t + 1) * 128]

    def out_start():
        core_add(0)
        start_all(out_m.one())

    def up_start():
        core_add(1)
        start_all(up_m.one())

    def down_start():
        core_add(2)
        start_all(down_m.one())

    acts = {
        "U0": up_start,
        "U1": up_m.add_one,
        "U2": up_m.add_two,
        "UF": lambda: up_m.finish(sums[2]),
        "D0": down_start,
        "D1": down_m.add_one,
        "D2": down_m.add_two,
        "DF": lambda: down_m.finish(sums[3]),
        "O0": out_start,
        "O1": out_m.add_one,
        "O2": out_m.add_two,
        "OF": lambda: out_m.finish(sums[1]),
        "Vc": vector_core,
        "Vx": vector_x,
        "Vz": vector_z,
        "Vy": vector_y,
        "Vr": vector_end,
    }
    for i, chunk in enumerate(chunks):
        acts[f"C{i}x"] = functools.partial(pair_done, i)
        acts[f"C{i}z"] = chunk.go_z
        acts[f"C{i}y"] = chunk.go_y
        acts[f"C{i}c"] = chunk.go_core
        acts[f"C{i}r"] = functools.partial(chunk_end, i)
    for qi in range(nq):
        acts[f"B{qi}"] = functools.partial(block_done, qi)
        acts[f"T{qi}"] = functools.partial(token_rows, qi)
    events, spot = {}, None
    for name in BACKWARD_PLAN:
        if name[0] == "S":
            spot = (int(name[1]), int(name[2]))
        else:
            events.setdefault(spot, []).append(name)

    def one_pair(pair, nothing):
        out_fetch(pair).wait()
        dk[...] = jnp.zeros_like(dk)
        dv[...] = jnp.zeros_like(dv)
        for i in range(nq):
            one_query(pair, nq - 1 - i)
            if i == nq - 1:

                @pl.when(pair < pairs - 1)
                def _():
                    out_fetch(pair + 1).start()

            for number in range(pairs):
                if (number, i) in events and (number, i) != (pairs - 1, nq - 1):

                    @pl.when(pair == number)
                    def _():
                        for name in events[number, i]:
                            acts[name]()

        return nothing

    for name in events.get(None, ()):
        acts[name]()
    lax.fori_loop(0, pairs, one_pair, 0)
    for name in events[pairs - 1, nq - 1]:
        acts[name]()
    w = sums[0].shape[1]
    for d in range(Y * C):

        @pl.when(p * C + c == d)
        def _():
            sums[0][...] = whole[:, d * w : (d + 1) * w]

    for k in range(1, Y):
        home_from(k).wait_recv()
        home_to((p + k) % Y).wait_send()
    local(row_sem + 2, tg_v.at[p], tg_home.at[p]).wait()
    for q in range(Y):
        g_wire(q).wait_send()
    v_core.wait_send()
    leave_all(v_y)
    v_x.wait_send()
    leave_all(v_z)
    for summing in adds + chunks:
        summing.leave()


def backward(place, parts, others, proj_shape, begin, proj, heads, oT, lt, normedT, w_own, tok, gm, vec, vec_two):
    n = len(parts)
    Z, X, Y, C = place.Z, place.X, place.Y, place.C
    L, W3 = proj.shape
    H = W3 // 3
    D = w_own.shape[0]
    T = L // (Y * C)
    BQ = 512
    inside = pl.BlockSpec(memory_space=pltpu.VMEM)
    anywhere = pl.BlockSpec(memory_space=pl.ANY)
    shapes = [proj_shape] + [part.shape[3:] for part in parts]
    sixths = [3, 3]
    out_shape = [jax.ShapeDtypeStruct(shape, f32) for shape in shapes]
    out_shape += [
        jax.ShapeDtypeStruct((8, H), f32),
        jax.ShapeDtypeStruct((Y, T, D), bf16),
    ]
    scratch = [pltpu.VMEM((Y, Z, X) + shape, bf16) for shape in shapes[1:]]
    scratch += [
        pltpu.VMEM((L, W3), bf16),
        pltpu.VMEM((L, H), bf16),
        pltpu.VMEM((128, L), f32),
        pltpu.VMEM((D, W3), bf16),
        pltpu.VMEM((H, L), bf16),
        pltpu.VMEM((L, 128), f32),
        pltpu.VMEM((L, 128), f32),
        pltpu.VMEM((D, L), bf16),
        pltpu.VMEM((max(1, 2 * (BQ // T) // C), T, D), f32),
        pltpu.VMEM((Y, T, D), bf16),
        pltpu.VMEM((Y, T, D), bf16),
        pltpu.VMEM((T, D), bf16),
        pltpu.VMEM((T, D), f32),
    ]
    scratch += [pltpu.VMEM((8, D), f32)] + [pltpu.VMEM((8, H), f32)] * 5
    scratch += [
        pltpu.VMEM((Y - 1, 8, H), f32),
        pltpu.VMEM((8, H), f32),
        pltpu.VMEM((Z - 1, 8, H), f32),
        pltpu.VMEM((proj_shape[0], 3 * D), f32),
    ]
    r, w = shapes[1]
    scratch += [
        pltpu.VMEM((Y, Z, X, r, w), bf16),
        pltpu.VMEM((Z - 1, Y, X, r, w), bf16),
        pltpu.VMEM((Y, r, w), bf16),
        pltpu.VMEM((Y - 1, r, w), bf16),
    ]
    for shape, part in zip(shapes[2:], sixths):
        r, w = shape
        h = first_rows(r, part)
        scratch += [
            pltpu.VMEM((Y, Z, X, r, w), bf16),
            pltpu.VMEM((Y, Z, h, w), bf16),
            pltpu.VMEM((Y - 1, Z, X, r - h, w), bf16),
            pltpu.VMEM((Y - 1, Z, h, w), bf16),
            pltpu.VMEM((Z, r - h, w), bf16),
            pltpu.VMEM((Z - 1, r, w), bf16),
        ]
    r = proj_shape[0]
    for pair in range(H // 128):
        scratch += [
            pltpu.VMEM((Z, X, r, 384), bf16),
            pltpu.VMEM((Z, r, 384), bf16),
            pltpu.VMEM((Z - 1, r, 384), bf16),
            pltpu.VMEM((Y, r, 384), bf16),
            pltpu.VMEM((Y, r, 384), bf16),
        ]
    each = 1 + (Y - 1) + (Y - 1) + 1 + (Z - 1)
    chunk_copies = 1 + (Z - 1) + (Y - 1) + 1
    copies = n * each + (H // 128) * chunk_copies + 2 + (Y - 1) + 1 + (Z - 1) + 3 * Y
    scratch += [
        pltpu.SemaphoreType.DMA((copies,)),
        pltpu.SemaphoreType.DMA((copies,)),
        pltpu.SemaphoreType.DMA((5 + 2 * n + 3,)),
    ]
    return pl.pallas_call(
        functools.partial(backward_kernel, place, n, BQ),
        out_shape=out_shape,
        in_specs=[inside] + [anywhere] * 3 + [inside] + [anywhere] * 4 + [inside] * 2 + [anywhere] * (2 * n),
        out_specs=[inside] * (n + 2) + [anywhere],
        scratch_shapes=scratch,
        compiler_params=pltpu.CompilerParams(
            collective_id=1, has_side_effects=True, vmem_limit_bytes=63 << 20
        ),
        name="backward",
    )(begin, proj, heads, oT, lt, normedT, w_own, tok, gm, vec, vec_two, *parts, *others)


def gelu_both(u):
    k = 0.7978845608028654
    square = u * u
    t = jnp.tanh(k * u * (1.0 + 0.044715 * square))
    half = 0.5 * (1.0 + t)
    slope = half + 0.5 * k * u * (1.0 - t * t) * (1.0 + 3 * 0.044715 * square)
    return u * half, slope


class Task:
    def __init__(self, copy, far):
        self.copy, self.far, self.left, self.here = copy, far, False, False
        copy.start()

    def gone(self):
        if not self.left:
            if self.far:
                self.copy.wait_send()
            else:
                self.copy.wait()
            self.left = True

    def came(self):
        if self.far and not self.here:
            self.copy.wait_recv()
            self.here = True


def dense_kernel(
    place, aligned, att, tok, cot, out_w, up_w, down_w, vec,
    home, gm_out, heads, up_own, down_own, out_own, up_other, down_other, out_other, vec_out,
    att_v, tok_v, cot_v, out_v, up_v, down_v, out_full, mid, n2, act, gh, n2T, cotT, oacc, g2,
    h_buf, g_buf, stage, up_cut, down_cut, load_sem, store_sem, send_sem, recv_sem,
):
    S, nb, Y, C = place.blk, place.batch, place.Y, place.C
    z, x, p, c = place.here()
    M, D = att_v.shape
    J = up_v.shape[1] // D
    T = M // Y
    H = D // C
    half = M // 2
    sibling = place.device(z, x, p, 1 - c)
    others = [place.device(z, x, (p + k) % Y, c) for k in range(1, Y)]
    wire = Wire(send_sem, recv_sem)
    loads, tasks = [], []

    def line(offset, size):
        return pl.ds(pl.multiple_of(offset, 16), size)

    def lane(offset, size):
        return pl.ds(pl.multiple_of(offset, 128), size)

    def load(src, dst):
        task = Task(pltpu.make_async_copy(src, dst, load_sem.at[len(loads)]), False)
        loads.append(task)
        return task

    def store(src, dst):
        count = sum(not task.far for task in tasks)
        tasks.append(Task(pltpu.make_async_copy(src, dst, store_sem.at[count]), False))
        return tasks[-1]

    def send(name, src, dst, device):
        tasks.append(Task(wire.copy(name, src, dst, device), True))
        return tasks[-1]

    first = [load(att, att_v), load(tok, tok_v), load(out_w, out_v)]
    first.append(load(cot.at[p], cot_v.at[line(p * T, T), :]))
    if aligned:
        w = up_w.shape[2]
        weights = [load(up_w.at[d], up_v.at[:, d * w : (d + 1) * w]) for d in range(S)]
        r, w = down_w.shape[2:]
        weights += [
            load(down_w.at[d, b], down_v.at[d * r : (d + 1) * r, b * w : (b + 1) * w])
            for d in range(S)
            for b in range(nb)
        ]
    else:
        weights = [load(up_w, up_v), load(down_w, down_v)]
    greet(place, others + [sibling])
    cots = []
    for k in range(1, Y):
        to = (p + k) % Y
        cots.append(send(("cot", k), cot.at[to], cot_v.at[line(p * T, T), :], others[k - 1]))
    for task in first:
        task.gone()
    w = out_v.shape[2]
    for d in range(S):
        out_full[:, d * w : (d + 1) * w] = out_v[d]
    gain, shift = vec[2:3, :], vec[3:4, :]
    near = (p * T) // half
    halves = [1 - near, near]
    rows_of = [line(t * half, half) for t in halves]
    for t in (0, 1):
        ts = rows_of[t]
        middle = tok_v[ts, :].astype(f32) + dot(att_v[ts, :], out_full[...], 1, 0)
        unit, factor = normed(middle)
        mid[ts, :] = middle
        low = (unit * gain + shift).astype(bf16)
        n2[ts, :] = low
        n2T[:, lane(halves[t] * half, half)] = low.T
    for task in weights:
        task.gone()
    w_up = up_own.shape[2]
    in_chunk = D // w_up
    chunks = []
    for s in range(J):
        if in_chunk == 1:
            chunks.append((s // C) * C + (1 - c if s % C == 0 else c))
        else:
            chunks.append(s)

    def cols(s):
        return lane(chunks[s] * D, D)

    busy = {}

    def staged(key, value, width, cut):
        for task in busy.get(key, []):
            task.gone()
        busy[key] = []
        if cut is not None:
            for i in range(value.shape[1] // width):
                cut[i] = value[:, i * width : (i + 1) * width]
            return lambda rows, i: cut.at[i, rows, :]
        stage[key] = value
        if value.shape[1] == width:
            return lambda rows, i: stage.at[key, rows, :]
        return lambda rows, i: stage.at[key, rows, i * width : (i + 1) * width]

    def up_gradient(s):
        value = dot(n2T[...], gh[:, cols(s)], 1, 0).astype(bf16)
        piece = staged(0, value, w_up, None if aligned else up_cut)
        every = slice(0, D)
        if in_chunk == 1:
            q = s // C
            if s % C == 0:
                busy[0].append(send(("up", s), piece(every, 0), up_other.at[q], sibling))
            else:
                busy[0].append(store(piece(every, 0), up_own.at[q]))
            return
        for i in range(in_chunk // C):
            q = s * in_chunk // C + i
            busy[0].append(store(piece(every, C * i + c), up_own.at[q]))
            busy[0].append(send(("up", q), piece(every, C * i + 1 - c), up_other.at[q], sibling))

    def down_gradient(s):
        value = dot(cotT[...], act[:, cols(s)], 1, 0).astype(bf16)
        r, w = down_own.shape[2:]
        piece = staged(1, value, w, None if aligned else down_cut)
        for q in range(Y):
            for i in range(D // w):
                b = chunks[s] * (D // w) + i
                busy[1].append(store(piece(line((C * q + c) * r, r), i), down_own.at[q, b]))
                busy[1].append(
                    send(
                        ("down", s, q, i),
                        piece(line((C * q + 1 - c) * r, r), i),
                        down_other.at[q, b],
                        sibling,
                    )
                )

    units = [(0, "f", s) for s in range(J)] + [(1, "fb", s) for s in range(J)]
    units += [(0, "b", s) for s in range(J)]

    def ahead(number):
        t, kind, s = units[number]
        slot = number % 2
        if "f" in kind:
            h_buf[slot] = dot(n2[rows_of[t], :], up_v[:, cols(s)], 1, 0)
        if "b" in kind:
            g_buf[slot] = dot(cot_v[rows_of[t], :], down_v[:, cols(s)], 1, 0)

    def output_rows(t):
        ts = rows_of[t]
        tok_v[ts, :] = (mid[ts, :] + oacc[...]).astype(bf16)
        for i in range(half // T):
            q = halves[t] * (half // T) + i
            if Y == 2 and t == 1:
                store(tok_v.at[ts, :], home.at[q])
            elif Y == 2:
                send("home", tok_v.at[ts, :], home.at[p], others[0])

    sums = [jnp.zeros((1, D), f32), jnp.zeros((1, D), f32)]

    def norm_rows(t):
        ts = rows_of[t]
        unit, factor = normed(mid[ts, :])
        grad = g2[...]
        sums[0] = sums[0] + jnp.sum(grad * unit, axis=0, keepdims=True)
        sums[1] = sums[1] + jnp.sum(grad, axis=0, keepdims=True)
        gm = cot_v[ts, :].astype(f32) + norm_back(grad, gain, unit, factor)
        mid[ts, :] = gm
        low = gm.astype(bf16)
        n2[ts, :] = low
        cot_v[ts, :] = dot(low, out_full[...], 1, 1).astype(bf16)
        store(mid.at[ts, :], gm_out.at[ts, :])
        for i in range(half // T):
            q = halves[t] * (half // T) + i
            rows = line(q * T, T)
            spot = line((C * q + c) * T, T)
            store(cot_v.at[rows, lane(c * H, H)], heads.at[spot, :])
            send(("ga", t, i), cot_v.at[rows, lane((1 - c) * H, H)], heads.at[spot, :], sibling)

    ahead(0)
    for number, (t, kind, s) in enumerate(units):
        ts, slot = rows_of[t], number % 2
        if number + 1 < len(units):
            if units[number + 1] == ((0, "b", 0) if Y == 2 else (1, "fb", 0)):
                for task in cots:
                    task.came()
            ahead(number + 1)
        if "f" in kind:
            a, slope = gelu_both(h_buf[slot])
            a = a.astype(bf16)
            act[ts, cols(s)] = a
            more = dot(a, down_v[:, cols(s)], 1, 1)
            if s == 0:
                oacc[...] = more
            else:
                oacc[...] += more
            if kind == "f":
                gh[ts, cols(s)] = slope.astype(bf16)
        else:
            slope = gh[ts, cols(s)].astype(f32)
        if "b" in kind:
            b = (g_buf[slot] * slope).astype(bf16)
            gh[ts, cols(s)] = b
            more = dot(b, up_v[:, cols(s)], 1, 1)
            if s == 0:
                g2[...] = more
            else:
                g2[...] += more
        if kind == "b":
            up_gradient(s)
            down_gradient(s)
        if s == J - 1:
            if kind == "f":
                output_rows(t)
            elif kind == "fb":
                output_rows(t)
                cotT[:, lane(halves[t] * half, half)] = cot_v[ts, :].T
                norm_rows(t)
                cotT[:, lane(halves[0] * half, half)] = cot_v[rows_of[0], :].T
            else:
                norm_rows(t)
    if Y > 2:
        store(tok_v.at[line(p * T, T), :], home.at[p])
        for k in range(1, Y):
            to = (p + k) % Y
            send(("home", k), tok_v.at[line(to * T, T), :], home.at[p], others[k - 1])
    vec_out[0:1, :] = sums[0]
    vec_out[1:2, :] = sums[1]
    value = dot(att_v[...], n2[...], 0, 0).astype(bf16)
    w = out_own.shape[2]
    for d in range(S):
        out_v[d] = value[:, d * w : (d + 1) * w]
    for q in range(Y):
        store(out_v.at[C * q + c], out_own.at[q])
        send(("out", q), out_v.at[C * q + 1 - c], out_other.at[q], sibling)
    for task in tasks:
        task.came()
    for task in tasks:
        task.gone()


def dense(place, att, tok, cot, out_g, up_g, down_g, vec):
    M, D = att.shape
    S, nb, Y, C = place.blk, place.batch, place.Y, place.C
    T = M // Y
    H = D // C
    aligned = up_g.shape[-1] % 128 == 0 and down_g.shape[-1] % 128 == 0
    out_w = out_g.reshape(S, D, -1)
    FF = S * up_g.shape[-1]
    if aligned:
        up_w = up_g.reshape(S, D, -1)
        down_w = down_g.reshape((S, nb) + down_g.shape[-2:])
    else:
        up_w, down_w = joined(up_g, 0), joined(down_g, 1)
    anywhere = pl.BlockSpec(memory_space=pl.ANY)
    inside = pl.BlockSpec(memory_space=pltpu.VMEM)
    pieces = [
        jax.ShapeDtypeStruct((Y, D, up_g.shape[-1]), bf16),
        jax.ShapeDtypeStruct((Y, nb) + down_g.shape[-2:], bf16),
        jax.ShapeDtypeStruct((Y, D, out_g.shape[-1]), bf16),
    ]
    none = (1, 16, 128)
    up_cut = none if aligned else (D // up_g.shape[-1], D, up_g.shape[-1])
    down_cut = none if aligned else (D // down_g.shape[-1], D, down_g.shape[-1])
    loads = 8 + S + S * nb
    J = FF // D
    down_count = J * Y * (D // down_g.shape[-1])
    copies = 2 * (Y - 1) + 2 * Y + S + down_count + 4 * Y + 8
    results = pl.pallas_call(
        functools.partial(dense_kernel, place, aligned),
        out_shape=[
            jax.ShapeDtypeStruct((Y, T, D), bf16),
            jax.ShapeDtypeStruct((M, D), f32),
            jax.ShapeDtypeStruct((S * T, H), bf16),
        ]
        + pieces
        + pieces
        + [jax.ShapeDtypeStruct((2, D), f32)],
        in_specs=[anywhere] * 6 + [inside],
        out_specs=[anywhere] * 9 + [inside],
        scratch_shapes=[
            pltpu.VMEM((M, D), bf16),
            pltpu.VMEM((M, D), bf16),
            pltpu.VMEM((M, D), bf16),
            pltpu.VMEM(out_w.shape, bf16),
            pltpu.VMEM((D, FF), bf16),
            pltpu.VMEM((D, FF), bf16),
            pltpu.VMEM((D, D), bf16),
            pltpu.VMEM((M, D), f32),
            pltpu.VMEM((M, D), bf16),
            pltpu.VMEM((M, FF), bf16),
            pltpu.VMEM((M, FF), bf16),
            pltpu.VMEM((D, M), bf16),
            pltpu.VMEM((D, M), bf16),
            pltpu.VMEM((M // 2, D), f32),
            pltpu.VMEM((M // 2, D), f32),
            pltpu.VMEM((2, M // 2, D), f32),
            pltpu.VMEM((2, M // 2, D), f32),
            pltpu.VMEM((2, D, D), bf16) if aligned else pltpu.VMEM((1, 16, 128), bf16),
            pltpu.VMEM(up_cut, bf16),
            pltpu.VMEM(down_cut, bf16),
            pltpu.SemaphoreType.DMA((loads,)),
            pltpu.SemaphoreType.DMA((copies,)),
            pltpu.SemaphoreType.DMA((copies,)),
            pltpu.SemaphoreType.DMA((copies,)),
        ],
        compiler_params=pltpu.CompilerParams(
            collective_id=2, has_side_effects=True, vmem_limit_bytes=62 << 20
        ),
        name="dense",
    )(att, tok, cot, out_w, up_w, down_w, vec)
    home, gm, heads = results[:3]
    shapes = [(Y,) + up_g.shape[2:], (Y,) + down_g.shape[2:], (Y,) + out_g.shape[2:]]
    own = [value.reshape(shape) for value, shape in zip(results[3:6], shapes)]
    other = [value.reshape(shape) for value, shape in zip(results[6:9], shapes)]
    return home, gm, heads, own, other, results[9]


def hand_over_kernel(place, n, *refs):
    given, vec, out, vec_out = refs[:n], refs[n], refs[n + 1 : 2 * n + 1], refs[2 * n + 1]
    whole, between, sem = refs[2 * n + 2], refs[2 * n + 3 : 3 * n + 3], refs[3 * n + 3]
    here = [pltpu.make_async_copy(given[i], between[i], sem.at[0, i]) for i in range(n)]
    away = [pltpu.make_async_copy(between[i], out[i], sem.at[1, i]) for i in range(n)]
    start_all(here)
    H = vec.shape[1]
    whole[0:4, 0:H] = vec[0:4, :]
    whole[0:4, H:] = vec[4:8, :]
    me = lax.axis_index("blk")
    w = vec_out.shape[1]
    for d in range(place.blk):

        @pl.when(me == d)
        def _():
            vec_out[...] = whole[0:4, d * w : (d + 1) * w]

    for i in range(n):
        here[i].wait()
        away[i].start()
    for copy in away:
        copy.wait()


def hand_over(place, given, vec):
    n = len(given)
    anywhere = pl.BlockSpec(memory_space=pl.ANY)
    inside = pl.BlockSpec(memory_space=pltpu.VMEM)
    H = vec.shape[1]
    return pl.pallas_call(
        functools.partial(hand_over_kernel, place, n),
        out_shape=[jax.ShapeDtypeStruct(v.shape, v.dtype) for v in given]
        + [jax.ShapeDtypeStruct((4, 2 * H // place.blk), f32)],
        in_specs=[anywhere] * n + [inside],
        out_specs=[anywhere] * n + [inside],
        scratch_shapes=[pltpu.VMEM((8, 2 * H), f32)]
        + [pltpu.VMEM(v.shape, v.dtype) for v in given]
        + [pltpu.SemaphoreType.DMA((2, n))],
        compiler_params=pltpu.CompilerParams(vmem_limit_bytes=62 << 20),
        name="hand_over",
    )(*given, vec)


def normed(values):
    average = jnp.mean(values, axis=-1, keepdims=True)
    centered = values - average
    variance = jnp.mean(centered * centered, axis=-1, keepdims=True)
    factor = lax.rsqrt(variance + epsilon)
    return centered * factor, factor


def norm_back(grad, gain, unit, factor):
    e = grad * gain
    return factor * (
        e - jnp.mean(e, axis=-1, keepdims=True) - unit * jnp.mean(e * unit, axis=-1, keepdims=True)
    )


def joined(gathered, axis):
    Y, C, Z, X, r, w = gathered.shape
    if axis == 0:
        return gathered.reshape(Y * C, Z * X * r, w).transpose(1, 0, 2).reshape(Z * X * r, -1)
    return gathered.reshape(Y * C, Z * X, r, w).transpose(0, 2, 1, 3).reshape(Y * C * r, -1)


def parted(whole, place, axis):
    Y, C, Z, X = place.Y, place.C, place.Z, place.X
    rows, columns = whole.shape
    if axis == 0:
        value = whole.reshape(Z * X, rows // (Z * X), Y * C, columns // (Y * C))
        value = value.transpose(2, 0, 1, 3)
    else:
        value = whole.reshape(Y * C, rows // (Y * C), Z * X, columns // (Z * X))
        value = value.transpose(0, 2, 1, 3)
    return value.reshape((Y, C, Z, X) + value.shape[2:])


def body(
    place,
    tokens,
    proj_weight,
    out_weight,
    up_weight,
    down_weight,
    gain_one,
    bias_one,
    gain_two,
    bias_two,
    segments,
    present,
    cotangent,
):
    rows, block, width = tokens.shape
    Y = place.Y
    row = lax.broadcasted_iota(jnp.int32, (16, width // place.blk), 0)
    vec_in = jnp.zeros(row.shape, bf16)
    for i, vector in enumerate((gain_one, bias_one, gain_two, bias_two)):
        vec_in = jnp.where(row == i, vector[None, :], vec_in)
    (
        out_g, up_g, down_g, tok_mine, vec, begin, projected, proj_own, normed_t,
        attended_low, attended_t, log_total,
    ) = forward(
        place,
        [proj_weight, out_weight, up_weight, down_weight.T],
        tokens,
        segments,
        present,
        vec_in,
    )
    tok_mine = tok_mine.reshape(Y * block, width)
    output, grad_middle, grad_heads, own, other, vec_two = dense(
        place, attended_low, tok_mine, cotangent, out_g, up_g, down_g, vec
    )
    order = (2, 0, 1)
    proj_sum, out_sum, up_sum, down_sum, vec_sum, token_grad = backward(
        place,
        [own[i] for i in order],
        [other[i] for i in order],
        proj_weight.shape,
        begin,
        projected,
        grad_heads,
        attended_t,
        log_total,
        normed_t,
        proj_own,
        tok_mine,
        grad_middle,
        vec,
        vec_two,
    )
    output, token_grad, proj_sum, out_sum, up_sum, down_sum, vectors = hand_over(
        place, (output, token_grad, proj_sum, out_sum, up_sum, down_sum), vec_sum
    )
    return (
        output,
        token_grad,
        proj_sum,
        out_sum,
        up_sum,
        down_sum.T,
        vectors[0],
        vectors[1],
        vectors[2],
        vectors[3],
    )


def solution(mesh):
    place = Place((mesh.shape["batch"], mesh.shape["blk"]))
    weight, vector = P("batch", "blk"), P("blk")
    row = P("batch", "blk", None)
    in_specs = (row,) + (weight,) * 4 + (vector,) * 4 + (weight,) * 2 + (row,)
    out_specs = (row, row) + (weight,) * 4 + (vector,) * 4
    return jax.shard_map(
        functools.partial(body, place),
        mesh=mesh,
        in_specs=in_specs,
        out_specs=out_specs,
        check_vma=False,
    )
```

```python
import functools

import jax
import jax.numpy as jnp
from jax import lax
from jax.experimental import pallas as pl
from jax.experimental.pallas import tpu as pltpu
from jax.sharding import PartitionSpec as P

HEADS = 12
HEAD_DIM = 64
CORES = 2
LANE_X = 2
MESH = pl.DeviceIdType.MESH
LOG2E = 1.4426950408889634
epsilon = 1e-05
masked = -1e30
bf16 = jnp.bfloat16
f32 = jnp.float32


def dot(left, right, left_dim, right_dim):
    return lax.dot_general(
        left, right, (((left_dim,), (right_dim,)), ((), ())), preferred_element_type=f32
    )


class Place:
    def __init__(self, sizes):
        self.batch, self.blk = sizes
        self.Z, self.X = self.batch // LANE_X, LANE_X
        self.Y, self.C = self.blk // CORES, CORES

    def here(self):
        b, d = lax.axis_index("batch"), lax.axis_index("blk")
        return b // self.X, b % self.X, d // self.C, d % self.C

    def device(self, z, x, p, c):
        return (z * self.X + x, p * self.C + c)

    def across_z(self):
        return [k for k in range(2, self.Z)] + [1]

    def mirror(self, z, k):
        for bit in range(self.Z.bit_length()):
            if k >> bit & 1:
                z = z + (1 << bit) - (2 << bit) * (z // (1 << bit) % 2)
        return z


class Wire:
    def __init__(self, send_sem, recv_sem):
        self.send_sem, self.recv_sem, self.names = send_sem, recv_sem, {}

    def copy(self, name, src, dst, device):
        i = self.names.setdefault(name, len(self.names))
        return pltpu.make_async_remote_copy(
            src_ref=src,
            dst_ref=dst,
            send_sem=self.send_sem.at[i],
            recv_sem=self.recv_sem.at[i],
            device_id=device,
            device_id_type=MESH,
        )


def start_all(copies):
    for copy in copies:
        copy.start()


def arrive_all(copies):
    for copy in copies:
        copy.wait_recv()


def leave_all(copies):
    for copy in copies:
        copy.wait_send()


def first_rows(rows, sixths):
    return min(rows - 16, 16 * ((rows * sixths // 6) // 16)) if rows > 16 else 0


def greet(place, partners):
    barrier = pltpu.get_barrier_semaphore()
    for partner in partners:
        pl.semaphore_signal(barrier, inc=1, device_id=partner, device_id_type=MESH)
    pl.semaphore_wait(barrier, len(partners))


def partners_of(place):
    z, x, p, c = place.here()
    found = [place.device(place.mirror(z, k), x, p, c) for k in place.across_z()]
    found += [place.device(z, 1 - x, p, c)]
    found += [place.device(z, x, (p + k) % place.Y, c) for k in range(1, place.Y)]
    found += [place.device(z, x, p, 1 - c)]
    return found


def head_masked(value, h, axis):
    index = lax.broadcasted_iota(jnp.int32, value.shape, axis)
    return jnp.where((index // HEAD_DIM) == h, value, jnp.zeros_like(value))


class Spreading:
    def __init__(self, place, wire, name, spots, shard, whole, deep, low):
        self.place, self.wire, self.name, self.spots = place, wire, name, spots
        self.shard, self.whole = shard, whole
        self.r = shard.shape[0]
        self.g = sixths(self.r, deep)
        self.h = self.g + sixths(self.r, low)

    def copy(self, what, src, dst, device):
        return self.wire.copy((self.name, what), src, dst, device)

    def sides(self):
        z, x, p, c = self.spots
        place = self.place
        along_y = [(k, place.device(z, x, (p + k) % place.Y, c)) for k in range(1, place.Y)]
        along_z = [(k, place.device(place.mirror(z, k), x, p, c)) for k in place.across_z()]
        return place.device(z, 1 - x, p, c), along_y, along_z

    def deep_one(self):
        z, x, p, c = self.spots
        src, dst = self.shard.at[0 : self.g], self.whole.at[p, c, z, x, 0 : self.g]
        return [self.copy(("dy", k), src, dst, side) for k, side in self.sides()[1]]

    def deep_two(self):
        z, x, p, c = self.spots
        part = self.whole.at[:, c, z, x, 0 : self.g]
        return [self.copy("dx", part, part, self.sides()[0])]

    def deep_three(self):
        z, x, p, c = self.spots
        part = self.whole.at[:, c, z, :, 0 : self.g]
        return [self.copy(("dz", k), part, part, side) for k, side in self.sides()[2]]

    def along_z(self, what, rows):
        z, x, p, c = self.spots
        src, dst = self.shard.at[rows], self.whole.at[p, c, z, x, rows]
        return [self.copy((what, k), src, dst, side) for k, side in self.sides()[2]]

    def low_zero(self):
        return self.along_z("za", slice(self.g, self.h))

    def high_zero(self):
        return self.along_z("zb", slice(self.h, self.r))

    def low_one(self):
        z, x, p, c = self.spots
        part = self.whole.at[p, c, :, x, self.g : self.h]
        return [self.copy("xa", part, part, self.sides()[0])]

    def high_one(self):
        z, x, p, c = self.spots
        part = self.whole.at[p, c, :, x, self.h : self.r]
        return [self.copy(("yb", k), part, part, side) for k, side in self.sides()[1]]

    def low_two(self):
        z, x, p, c = self.spots
        part = self.whole.at[p, c, :, :, self.g : self.h]
        return [self.copy(("ya", k), part, part, side) for k, side in self.sides()[1]]

    def high_two(self):
        z, x, p, c = self.spots
        part = self.whole.at[:, c, :, x, self.h : self.r]
        return [self.copy("xb", part, part, self.sides()[0])]

    def to_core(self, what, rows):
        z, x, p, c = self.spots
        part = self.whole.at[:, c, :, :, rows]
        return [self.copy(what, part, part, self.place.device(z, x, p, 1 - c))]

    def low_three(self):
        return self.to_core("ca", slice(self.g, self.h))

    def high_three(self):
        return self.to_core("cb", slice(self.h, self.r))

    def deep_four(self):
        return self.to_core("cd", slice(0, self.g))

    def chains(self):
        found = []
        if self.g:
            found.append([self.deep_one, self.deep_two, self.deep_three, self.deep_four])
        if self.g < self.h:
            found.append([self.low_zero, self.low_one, self.low_two, self.low_three])
        if self.h < self.r:
            found.append([self.high_zero, self.high_one, self.high_two, self.high_three])
        return found

    def begin(self):
        for chain in self.chains():
            start_all(chain[0]())

    def step(self, group, number):
        chain = (
            [self.deep_one, self.deep_two, self.deep_three, self.deep_four],
            [self.low_zero, self.low_one, self.low_two, self.low_three],
            [self.high_zero, self.high_one, self.high_two, self.high_three],
        )[group]
        arrive_all(chain[number - 1]())
        start_all(chain[number]())

    def arrive(self):
        for chain in self.chains():
            arrive_all(chain[3]())

    def leave(self):
        for chain in self.chains():
            for stage in chain:
                leave_all(stage())


FORWARD_PLAN = (
    "t1", "O1d", "V", "D1d", "O2d", "t2", "U1d", "N0", "P1a", "P1b", "t3", "P2b", "P2a",
    "U1b", "K", "U1a", "D1b", "P3b", "D1a", "P3a", "N2", "N3", "W", "U2b", "U2a", "D2d",
    "J", "S00", "S01", "D2b", "D2a", "S02", "S10", "O3d", "S11", "S12", "U2d", "S20",
    "S21", "S22", "U3a", "S30", "U3b", "D3b", "U3d", "S31", "D3a", "D3d", "S32",
)
ROW_PARTS = 4


def forward_kernel(place, n, BQ, *refs):
    shards, (tok, segments, present, vec_in) = refs[: n + 1], refs[n + 1 : n + 5]
    outs = refs[n + 5 :]
    wholes = outs[:n]
    (tok_out, vec_out, begin, proj_out, w_out, normedT_out, att_out, oT_out, lt) = outs[
        n : n + 9
    ]
    (
        proj_v, tok_v, tag, tag_v, vec_v, n_v, nT, wv, pv, vT, att, oT,
        send_sem, recv_sem, local_sem,
    ) = outs[n + 9 :]
    spots = place.here()
    z, x, p, c = spots
    Z, X, Y, C = place.Z, place.X, place.Y, place.C
    D, W3 = wv.shape
    H = W3 // 3
    L = pv.shape[0]
    T = L // (Y * C)
    U = BQ // T
    pairs = H // 128
    nq = L // BQ
    wire = Wire(send_sem, recv_sem)
    sibling = place.device(z, x, p, 1 - c)
    flows = [
        Spreading(place, wire, m, spots, shards[m], proj_v if m == 0 else wholes[m - 1], *way)
        for m, way in enumerate(((0, 3), (6, 0), (1, 3), (1, 3)))
    ]

    def local(i, src, dst):
        return pltpu.make_async_copy(src, dst, local_sem.at[i])

    def lane(offset, size):
        return pl.ds(pl.multiple_of(offset, 128), size)

    def line(offset, size):
        return pl.ds(pl.multiple_of(offset, 16), size)

    row_parts = (("vec", vec_in, vec_v), ("tag", tag, tag_v), ("tok", tok, tok_v))

    def along_y(what, src, dst):
        found = []
        for k in range(1, Y):
            to = (p + k) % Y
            device = place.device(z, x, to, c)
            if what == "tok":
                for i in range(ROW_PARTS):
                    rows = slice(i * T // ROW_PARTS, (i + 1) * T // ROW_PARTS)
                    found.append(
                        wire.copy(
                            (what, "y", k, i), src.at[to, rows], dst.at[p, c, rows], device
                        )
                    )
            else:
                piece = src if what == "vec" else src.at[to]
                found.append(wire.copy((what, "y", k), piece, dst.at[p, c], device))
        return found

    def send_tokens(i):
        start_all(along_y(*row_parts[2])[i::ROW_PARTS])

    def to_sibling_own(what, src, dst):
        piece = src if what == "vec" else src.at[p]
        return wire.copy((what, "own"), piece, dst.at[p, c], sibling)

    def to_sibling(what, dst):
        found = []
        for k in range(1, Y):
            q = (p + k) % Y
            found.append(wire.copy((what, "pass", k), dst.at[q, c], dst.at[q, c], sibling))
        return found

    position = lax.broadcasted_iota(jnp.int32, (Y, T), 1) + (p * C + c) * T
    tags = jnp.where(present[...] == 1, segments[...], -1 - position)
    for q in range(Y):
        tag[q] = jnp.broadcast_to(tags[q : q + 1, :], tag.shape[1:])
    greet(place, partners_of(place))
    start_all(along_y(*row_parts[0]))
    for part in row_parts:
        to_sibling_own(*part).start()
    for flow in flows:
        flow.begin()
    start_all(along_y(*row_parts[1]))
    send_tokens(0)
    kept = [local(m, shards[m], flows[m].whole.at[p, c, z, x]) for m in range(n + 1)]
    kept += [
        local(n + 1, vec_in, vec_v.at[p, c]),
        local(n + 2, tag.at[p], tag_v.at[p, c]),
        local(n + 3, tok.at[p], tok_v.at[p, c]),
    ]
    start_all(kept)
    saves = [
        local(n + 5, nT, normedT_out),
        local(n + 6, tok_v.at[:, c], tok_out),
        local(n + 7, pv, proj_out),
        local(n + 8, wv, w_out),
    ]

    def norm_block(q, i):
        unit, factor = normed(tok_v[q, i].astype(f32))
        low = (unit * vec_out[0:1, :] + vec_out[1:2, :]).astype(bf16)
        rows = line((q * C + i) * T, T)
        n_v[rows, :] = low
        nT[:, lane((q * C + i) * T, T)] = low.T

    waited = set()

    def own_shard(m):
        if m not in waited:
            kept[m].wait()
            waited.add(m)

    def advance(m, group, number):
        own_shard(m)
        flows[m].step(group, number)

    def vector_pass():
        arrive_all(along_y(*row_parts[0]))
        start_all(to_sibling("vec", vec_v))

    def norm_near():
        for copy in kept[n + 1 :]:
            copy.wait()
        to_sibling_own(*row_parts[0]).wait_recv()
        arrive_all(to_sibling("vec", vec_v))
        share = vec_v.shape[3]
        for q in range(Y):
            for i in range(C):
                lo = (q * C + i) * share
                vec_out[:, lo : lo + share] = vec_v[q, i, 0:8, :].astype(f32)
        norm_block(p, c)
        to_sibling_own(*row_parts[2]).wait_recv()
        norm_block(p, 1 - c)

    def row_pass():
        for what, src, dst in row_parts[1:]:
            arrive_all(along_y(what, src, dst))
            start_all(to_sibling(what, dst))

    def norm_far():
        for k in range(1, Y):
            norm_block((p + k) % Y, c)

    def norm_last():
        arrive_all(to_sibling("tok", tok_v))
        for k in range(1, Y):
            norm_block((p + k) % Y, 1 - c)
        start_all(saves[:2])
        to_sibling_own(*row_parts[1]).wait_recv()
        arrive_all(to_sibling("tag", tag_v))
        tags = [tag_v[q, i, 0:1, :] for q in range(Y) for i in range(C)]
        counts = []
        for s in range(4):
            hits = sum((t == s).astype(f32) for t in tags)
            counts.append(jnp.sum(hits, axis=1, keepdims=True).astype(jnp.int32))
        for b, t in enumerate(tags):
            first = sum(jnp.where(t > s, counts[s], 0) for s in range(4))
            position = lax.broadcasted_iota(jnp.int32, (1, T), 1) + b * T
            begin[:, b * T : (b + 1) * T] = jnp.where(t < 0, position, first)

    def weight_columns():
        flows[0].arrive()
        r, w = proj_v.shape[4:]
        for mine in range(C):

            @pl.when(c == mine)
            def _():
                for third in range(3):
                    base = third * D + mine * H
                    for d in range(Y * C):
                        a, b = max(base, d * w), min(base + H, (d + 1) * w)
                        if a >= b:
                            continue
                        to = third * H + a - base
                        for i in range(Z * X):
                            wv[i * r : (i + 1) * r, to : to + b - a] = proj_v[
                                d // C, d % C, i // X, i % X, :, a - d * w : b - d * w
                            ]

    def project_all():
        def project(i, nothing):
            rows = line(i * BQ, BQ)
            pv[rows, :] = dot(n_v[rows, :], wv[...], 1, 0).astype(bf16)
            return nothing

        lax.fori_loop(0, nq, project, 0)
        values = pv[:, 2 * H :].T
        for h in range(2 * pairs):
            vT[h, 0:HEAD_DIM, :] = values[h * HEAD_DIM : (h + 1) * HEAD_DIM, :]
            vT[h, HEAD_DIM:, :] = jnp.ones((16, L), bf16)
        start_all(saves[2:])

    scale = HEAD_DIM ** (-0.5) * LOG2E

    def block_copies(qi):
        found = []
        for u in range(U):
            b = qi * U + u
            q, owner = b // C, b % C
            src = att.at[b * T : (b + 1) * T, :]
            dst = att_out.at[q * T : (q + 1) * T, lane(c * H, H)]
            found.append(
                (owner, local(n + 9 + q, src, dst), wire.copy(("att", q), src, dst, sibling))
            )
        return found

    acts = {
        "V": vector_pass,
        "N0": norm_near,
        "K": row_pass,
        "N2": norm_far,
        "N3": norm_last,
        "W": weight_columns,
        "J": project_all,
    }
    for m, name in enumerate("POUD"):
        for group, letter in enumerate("dab"):
            for number in (1, 2, 3):
                acts[f"{name}{number}{letter}"] = functools.partial(advance, m, group, number)
    for i in range(1, ROW_PARTS):
        acts[f"t{i}"] = functools.partial(send_tokens, i)
    events, spot = {}, None
    for name in FORWARD_PLAN:
        if name[0] == "S":
            spot = (int(name[1]), int(name[2]))
        else:
            events.setdefault(spot, []).append(name)
    for name in events[None]:
        acts[name]()
    for qi in range(nq):
        qs = slice(qi * BQ, (qi + 1) * BQ)
        d0 = qi * BQ
        part = BQ // 2
        cuts = []
        if d0 and qi < nq - 1:
            cuts = [(0, part, 1, 0), (part, min(BQ, d0), 0, 0)]
            cuts += [(a, a + BQ, 0, 0) for a in range(BQ, d0, BQ)]
        elif d0:
            cuts = [(a, a + BQ, 1, 0) for a in range(0, d0, BQ)]
        cuts += [(d0, d0 + part, 2, 0), (d0 + part, d0 + BQ, 2, part)]

        def widened(value, qa, blank):
            if not qa:
                return value
            return jnp.concatenate([jnp.full((value.shape[0], qa), blank, f32), value], axis=1)

        def one_pair(pair, nothing):
            cols = lane(pair * 128, 128)
            k_cols = lane(H + pair * 128, 128)
            qT = pv[qs, cols].T
            found, scores = [], []
            for h in range(2):
                query = head_masked(qT, h, 0)
                parts = []
                for a, b, mode, qa in cuts:
                    s = dot(pv[a:b, k_cols], query[:, qa:], 1, 0)
                    if mode:
                        shape = (b - a, BQ - qa)
                        key_pos = lax.broadcasted_iota(jnp.int32, shape, 0) + a
                        visible = key_pos >= begin[:, d0 + qa : d0 + BQ]
                        if mode == 2:
                            query_pos = lax.broadcasted_iota(jnp.int32, shape, 1) + d0 + qa
                            visible = jnp.logical_and(visible, key_pos <= query_pos)
                        s = jnp.where(visible, s, masked)
                    parts.append(s)
                scores.append(parts)
            for h in range(2):
                tops = [
                    widened(jnp.max(s, axis=0, keepdims=True), cut[3], masked)
                    for cut, s in zip(cuts, scores[h])
                ]
                top = functools.reduce(jnp.maximum, tops) * scale
                accum = jnp.zeros((vT.shape[1], BQ), f32)
                for (a, b, mode, qa), s in zip(cuts, scores[h]):
                    e = jnp.exp2(s * scale - top[:, qa:]).astype(bf16)
                    accum = accum + widened(dot(vT[pair * 2 + h, :, a:b], e, 1, 0), qa, 0.0)
                total = accum[HEAD_DIM : HEAD_DIM + 1]
                result = accum[:HEAD_DIM] / total
                rows = pl.ds(pl.multiple_of(pair * 128 + h * HEAD_DIM, HEAD_DIM), HEAD_DIM)
                oT[rows, qs] = result
                found.append(result)
                lt[pair, h : h + 1, qs] = top + jnp.log2(total)
            att[qs, cols] = jnp.concatenate(found, axis=0).astype(bf16).T
            for number in range(pairs):
                if (qi, number) in events:

                    @pl.when(pair == number)
                    def _():
                        for name in events[qi, number]:
                            acts[name]()

            return nothing

        lax.fori_loop(0, pairs, one_pair, 0)
        save = local(n + 9 + Y + qi, oT.at[:, qs], oT_out.at[:, qs])
        save.start()
        saves.append(save)
        for owner, keep, send in block_copies(qi):

            @pl.when(owner == c)
            def _():
                keep.start()

            @pl.when(owner != c)
            def _():
                send.start()

    for flow in flows[1:]:
        flow.arrive()
    for qi in range(nq):
        for owner, keep, send in block_copies(qi):

            @pl.when(owner == c)
            def _():
                keep.wait()

            @pl.when(owner != c)
            def _():
                send.wait_send()

            @pl.when(owner == c)
            def _():
                send.wait_recv()

    for what, src, dst in row_parts:
        leave_all(along_y(what, src, dst))
        to_sibling_own(what, src, dst).wait_send()
        leave_all(to_sibling(what, dst))
    for flow in flows:
        flow.leave()
    for copy in saves:
        copy.wait()


def forward(place, shards, tok, segments, present, vec_in):
    n = len(shards) - 1
    Z, X, Y, C = place.Z, place.X, place.Y, place.C
    R, T, D = tok.shape
    L = Y * C * T
    H = D // C
    W3 = 3 * H
    BQ = 512
    pairs = H // 128
    inside = pl.BlockSpec(memory_space=pltpu.VMEM)
    anywhere = pl.BlockSpec(memory_space=pl.ANY)
    out_shape = [jax.ShapeDtypeStruct((Y, C, Z, X) + m.shape, bf16) for m in shards[1:]]
    out_shape += [
        jax.ShapeDtypeStruct((Y, T, D), bf16),
        jax.ShapeDtypeStruct((8, D), f32),
        jax.ShapeDtypeStruct((1, L), jnp.int32),
        jax.ShapeDtypeStruct((L, W3), bf16),
        jax.ShapeDtypeStruct((D, W3), bf16),
        jax.ShapeDtypeStruct((D, L), bf16),
        jax.ShapeDtypeStruct((Y * T, D), bf16),
        jax.ShapeDtypeStruct((H, L), f32),
        jax.ShapeDtypeStruct((pairs, 2, L), f32),
    ]
    each = 3 * (Z - 1) + 3 * (Y - 1) + 6
    copies = (n + 1) * each + 3 * (2 * (Y - 1) + 1) + ROW_PARTS * (Y - 1) + Y
    scratch = [
        pltpu.VMEM((Y, C, Z, X) + shards[0].shape, bf16),
        pltpu.VMEM((Y, C, T, D), bf16),
        pltpu.VMEM((Y, 8, T), jnp.int32),
        pltpu.VMEM((Y, C, 8, T), jnp.int32),
        pltpu.VMEM((Y, C) + vec_in.shape, bf16),
        pltpu.VMEM((L, D), bf16),
        pltpu.VMEM((D, L), bf16),
        pltpu.VMEM((D, W3), bf16),
        pltpu.VMEM((L, W3), bf16),
        pltpu.VMEM((H // HEAD_DIM, HEAD_DIM + 16, L), bf16),
        pltpu.VMEM((L, H), bf16),
        pltpu.VMEM((H, L), f32),
        pltpu.SemaphoreType.DMA((copies,)),
        pltpu.SemaphoreType.DMA((copies,)),
        pltpu.SemaphoreType.DMA((n + 9 + Y + L // BQ,)),
    ]
    return pl.pallas_call(
        functools.partial(forward_kernel, place, n, BQ),
        out_shape=out_shape,
        in_specs=[inside] * (n + 1) + [anywhere] + [inside] * 3,
        out_specs=[anywhere] * (n + 1) + [inside] * 2 + [anywhere] * 5 + [inside],
        scratch_shapes=scratch,
        compiler_params=pltpu.CompilerParams(
            collective_id=0, has_side_effects=True, vmem_limit_bytes=60 << 20
        ),
        name="forward",
    )(*shards, tok, segments, present, vec_in)


def sixths(rows, count):
    return rows if count == 6 else 0 if count == 0 else max(16, 16 * (rows * count // 96))


class Summing:
    def __init__(self, place, wire, name, spots, acc, xa, yb, ya, xb, zz):
        self.place, self.wire, self.name, self.spots = place, wire, name, spots
        self.acc, self.xa, self.yb, self.ya, self.xb, self.zz = acc, xa, yb, ya, xb, zz
        self.rows = acc.shape[3]
        self.h = xa.shape[2]

    def one(self):
        z, x, p, c = self.spots
        place, h, r = self.place, self.h, self.rows
        side = place.device(z, 1 - x, p, c)
        found = [
            self.wire.copy((self.name, "xa"), self.acc.at[:, :, 1 - x, 0:h], self.xa, side)
        ]
        for k in range(1, place.Y):
            to = (p + k) % place.Y
            found.append(
                self.wire.copy(
                    (self.name, "yb", k),
                    self.acc.at[to, :, :, h:r],
                    self.yb.at[k - 1],
                    place.device(z, x, to, c),
                )
            )
        return found

    def two(self):
        z, x, p, c = self.spots
        place, h, r = self.place, self.h, self.rows
        found = []
        for k in range(1, place.Y):
            to = (p + k) % place.Y
            found.append(
                self.wire.copy(
                    (self.name, "ya", k),
                    self.acc.at[to, :, x, 0:h],
                    self.ya.at[k - 1],
                    place.device(z, x, to, c),
                )
            )
        side = place.device(z, 1 - x, p, c)
        found.append(
            self.wire.copy((self.name, "xb"), self.acc.at[p, :, 1 - x, h:r], self.xb, side)
        )
        return found

    def three(self):
        z, x, p, c = self.spots
        place = self.place
        found = []
        for k in place.across_z():
            to = place.mirror(z, k)
            found.append(
                self.wire.copy(
                    (self.name, "z", k),
                    self.acc.at[p, to, x],
                    self.zz.at[k - 1],
                    place.device(to, x, p, c),
                )
            )
        return found

    def add_one(self):
        z, x, p, c = self.spots
        place, h, r, acc = self.place, self.h, self.rows, self.acc
        ones = self.one()
        ones[0].wait_recv()

        def low(i, nothing):
            a, b = i // place.Z, i % place.Z
            total = acc[a, b, x, 0:h].astype(f32) + self.xa[a, b].astype(f32)
            acc[a, b, x, 0:h] = total.astype(bf16)
            return nothing

        lax.fori_loop(0, place.Y * place.Z, low, 0)
        twos = self.two()
        start_all(twos[:-1])
        arrive_all(ones[1:])

        def high(i, nothing):
            a, b = i // place.X, i % place.X
            total = acc[p, a, b, h:r].astype(f32)
            for k in range(place.Y - 1):
                total = total + self.yb[k, a, b].astype(f32)
            acc[p, a, b, h:r] = total.astype(bf16)
            return nothing

        lax.fori_loop(0, place.Z * place.X, high, 0)
        twos[-1].start()

    def add_two(self):
        z, x, p, c = self.spots
        place, h, r, acc = self.place, self.h, self.rows, self.acc
        arrive_all(self.two())

        def both(i, nothing):
            total = acc[p, i, x, 0:h].astype(f32)
            for k in range(place.Y - 1):
                total = total + self.ya[k, i].astype(f32)
            acc[p, i, x, 0:h] = total.astype(bf16)
            total = acc[p, i, x, h:r].astype(f32) + self.xb[i].astype(f32)
            acc[p, i, x, h:r] = total.astype(bf16)
            return nothing

        lax.fori_loop(0, place.Z, both, 0)
        start_all(self.three())

    def finish(self, target):
        z, x, p, c = self.spots
        arrive_all(self.three())
        total = self.acc[p, z, x].astype(f32)
        for k in range(self.place.Z - 1):
            total = total + self.zz[k].astype(f32)
        target[...] = total

    def leave(self):
        leave_all(self.one())
        leave_all(self.two())
        leave_all(self.three())


class DepthSum:
    def __init__(self, place, wire, name, spots, acc, zr, xr, yr):
        self.place, self.wire, self.name, self.spots = place, wire, name, spots
        self.acc, self.zr, self.xr, self.yr = acc, zr, xr, yr

    def one(self):
        z, x, p, c = self.spots
        place = self.place
        return [
            self.wire.copy(
                (self.name, "z", k),
                self.acc.at[:, place.mirror(z, k)],
                self.zr.at[k - 1],
                place.device(place.mirror(z, k), x, p, c),
            )
            for k in place.across_z()
        ]

    def two(self):
        z, x, p, c = self.spots
        side = self.place.device(z, 1 - x, p, c)
        return [self.wire.copy((self.name, "x"), self.acc.at[:, z, 1 - x], self.xr, side)]

    def three(self):
        z, x, p, c = self.spots
        place = self.place
        return [
            self.wire.copy(
                (self.name, "y", k),
                self.acc.at[(p + k) % place.Y, z, x],
                self.yr.at[k - 1],
                place.device(z, x, (p + k) % place.Y, c),
            )
            for k in range(1, place.Y)
        ]

    def add_one(self):
        z, x, p, c = self.spots
        place, acc = self.place, self.acc
        arrive_all(self.one())

        def add(i, nothing):
            a, b = i // place.X, i % place.X
            total = acc[a, z, b].astype(f32)
            for k in range(place.Z - 1):
                total = total + self.zr[k, a, b].astype(f32)
            acc[a, z, b] = total.astype(bf16)
            return nothing

        lax.fori_loop(0, place.Y * place.X, add, 0)
        start_all(self.two())

    def add_two(self):
        z, x, p, c = self.spots
        place, acc = self.place, self.acc
        arrive_all(self.two())

        def add(i, nothing):
            total = acc[i, z, x].astype(f32) + self.xr[i].astype(f32)
            acc[i, z, x] = total.astype(bf16)
            return nothing

        lax.fori_loop(0, place.Y, add, 0)
        start_all(self.three())

    def finish(self, target):
        z, x, p, c = self.spots
        arrive_all(self.three())
        total = self.acc[p, z, x].astype(f32)
        for k in range(self.place.Y - 1):
            total = total + self.yr[k].astype(f32)
        target[...] = total

    def leave(self):
        leave_all(self.one())
        leave_all(self.two())
        leave_all(self.three())


class ChunkSum:
    def __init__(self, place, wire, name, spots, acc, xr, zr, total, far):
        self.place, self.wire, self.name, self.spots = place, wire, name, spots
        self.acc, self.xr, self.zr, self.total, self.far = acc, xr, zr, total, far

    def along_x(self):
        z, x, p, c = self.spots
        side = self.place.device(z, 1 - x, p, c)
        return [self.wire.copy((self.name, "x"), self.acc.at[:, 1 - x], self.xr, side)]

    def along_z(self):
        z, x, p, c = self.spots
        place = self.place
        return [
            self.wire.copy(
                (self.name, "z", k),
                self.acc.at[place.mirror(z, k), x],
                self.zr.at[k - 1],
                place.device(place.mirror(z, k), x, p, c),
            )
            for k in place.across_z()
        ]

    def along_y(self):
        z, x, p, c = self.spots
        place = self.place
        return [
            self.wire.copy(
                (self.name, "y", k),
                self.total.at[0],
                self.total.at[k],
                place.device(z, x, (p + k) % place.Y, c),
            )
            for k in range(1, place.Y)
        ]

    def to_core(self):
        z, x, p, c = self.spots
        return [
            self.wire.copy(
                (self.name, "core"), self.total, self.far, self.place.device(z, x, p, 1 - c)
            )
        ]

    def go_z(self):
        z, x, p, c = self.spots
        arrive_all(self.along_x())

        def one(i, nothing):
            total = self.acc[i, x].astype(f32) + self.xr[i].astype(f32)
            self.acc[i, x] = total.astype(bf16)
            return nothing

        lax.fori_loop(0, self.place.Z, one, 0)
        start_all(self.along_z())

    def go_y(self):
        z, x, p, c = self.spots
        arrive_all(self.along_z())
        total = self.acc[z, x].astype(f32)
        for k in range(self.place.Z - 1):
            total = total + self.zr[k].astype(f32)
        self.total[0] = total.astype(bf16)
        start_all(self.along_y())

    def go_core(self):
        arrive_all(self.along_y())
        start_all(self.to_core())

    def result(self):
        arrive_all(self.to_core())
        return [
            sum(part[k].astype(f32) for k in range(self.place.Y)) for part in (self.total, self.far)
        ]

    def leave(self):
        for copies in (self.along_x(), self.along_z(), self.along_y(), self.to_core()):
            leave_all(copies)


BACKWARD_PLAN = (
    "U0", "S00", "S01", "O0", "S02", "S03", "U1", "C0x", "S10", "D0", "U2", "S11", "S12",
    "C0z", "S13", "C1x", "S20", "B3", "D1", "S21", "C1z", "B2", "S22", "S23", "D2", "T3",
    "C2x", "B1", "C0y", "O1", "UF", "T2", "B0", "C1y", "T1", "C0c", "T0", "C2z", "C1c",
    "Vc", "Vx", "C2y", "Vz", "O2", "C0r", "Vy", "C1r", "DF", "C2c", "OF", "Vr", "C2r",
)


def backward_kernel(place, n, BQ, *refs):
    (begin, proj, grad_in, oT_in, lt, normedT, w_in, tok, gm, vec, vec_two) = refs[:11]
    parts, others = refs[11 : 11 + n], refs[11 + n : 11 + 2 * n]
    outs = refs[11 + 2 * n :]
    sums, (vec_out, tg_home) = outs[: n + 1], outs[n + 1 : n + 3]
    landing = outs[n + 3 : 2 * n + 3]
    rest = outs[2 * n + 3 :]
    (
        pv, do, oT, wv, kT, dk, dv, nT,
        keep, g_send, g_recv, tok_v, gm_v, grads, v0, v1, v2, v3, vc, vy, vx, vz, whole,
    ) = rest[:23]
    buffers = rest[23 : 23 + 6 * n - 2]
    chunk_buffers = rest[23 + 6 * n - 2 : -3]
    send_sem, recv_sem, local_sem = rest[-3:]
    tg_v = g_recv
    spots = place.here()
    z, x, p, c = spots
    Z, X, Y, C = place.Z, place.X, place.Y, place.C
    L, W3 = pv.shape
    H = W3 // 3
    D = wv.shape[0]
    T = L // (Y * C)
    pairs = H // 128
    nq = L // BQ
    scale = HEAD_DIM ** (-0.5) * LOG2E
    scale_back = HEAD_DIM ** (-0.5)
    wire = Wire(send_sem, recv_sem)
    sibling = place.device(z, x, p, 1 - c)
    beside = place.device(z, 1 - x, p, c)
    adds = [DepthSum(place, wire, 0, spots, *buffers[:4])]
    adds += [
        Summing(place, wire, m, spots, *buffers[6 * m - 2 : 6 * m + 4]) for m in range(1, n)
    ]
    chunks = [
        ChunkSum(place, wire, ("chunk", i), spots, *chunk_buffers[5 * i : 5 * i + 5])
        for i in range(pairs)
    ]

    def local(i, src, dst):
        return pltpu.make_async_copy(src, dst, local_sem.at[i])

    def lane(offset, size):
        return pl.ds(pl.multiple_of(offset, 128), size)

    def line(offset, size):
        return pl.ds(pl.multiple_of(offset, 16), size)

    def out_fetch(pair):
        return local(2, oT_in.at[line(pair * 128, 128), :], oT)

    loads = [local(0, proj, pv), local(1, grad_in, do)]
    columns = local(3, w_in, wv)
    late = local(4 + 2 * n, normedT, nT)
    columns_here = []
    halves = [
        (local(4 + m, parts[m], adds[m].acc), local(4 + n + m, others[m], landing[m]))
        for m in range(n)
    ]
    start_all(halves[1])
    start_all(loads)
    out_fetch(0).start()
    for m in (2, 0):
        start_all(halves[m])
    start_all([late, columns])
    greet(place, partners_of(place))
    row_sem = 5 + 2 * n

    def core_add(m):
        for copy in halves[m]:
            copy.wait()
        acc, other = adds[m].acc, landing[m]

        def one(i, nothing):
            a, b, d = i // (Z * X), (i // X) % Z, i % X
            total = acc[a, b, d].astype(f32) + other[a, b, d].astype(f32)
            acc[a, b, d] = total.astype(bf16)
            return nothing

        lax.fori_loop(0, Y * Z * X, one, 0)

    for copy in loads:
        copy.wait()
    kT[...] = pv[:, H : 2 * H].T
    grads[...] = jnp.zeros_like(grads)

    U = BQ // T
    gain = vec[0:1, :]

    def sub_blocks(qi):
        found = []
        for u in range(U):
            block = qi * U + u
            found.append((u, block // C, block % C))
        return found

    reserved = send_sem.shape[0] - 3 * Y

    def g_wire(q):
        return pltpu.make_async_remote_copy(
            src_ref=g_send.at[q],
            dst_ref=g_recv.at[q],
            send_sem=send_sem.at[reserved + q],
            recv_sem=recv_sem.at[reserved + q],
            device_id=sibling,
            device_id_type=MESH,
        )

    def home_from(k):
        q = (p + k) % Y
        return pltpu.make_async_remote_copy(
            src_ref=tg_v.at[p],
            dst_ref=tg_home.at[q],
            send_sem=send_sem.at[reserved + Y + q],
            recv_sem=recv_sem.at[reserved + 2 * Y + q],
            device_id=place.device(z, x, q, c),
            device_id_type=MESH,
        )

    def home_to(q):
        return pltpu.make_async_remote_copy(
            src_ref=tg_v.at[q],
            dst_ref=tg_home.at[p],
            send_sem=send_sem.at[reserved + Y + q],
            recv_sem=recv_sem.at[reserved + 2 * Y + p],
            device_id=place.device(z, x, q, c),
            device_id_type=MESH,
        )

    def block_done(qi):
        if not columns_here:
            columns.wait()
            columns_here.append(True)
        g = dot(pv[line(qi * BQ, BQ), :], wv[...], 1, 1)
        for u, q, owner in sub_blocks(qi):
            rows = slice(u * T, (u + 1) * T)

            @pl.when(owner == c)
            def _():
                keep[(qi % 2 * U + u) // C] = g[rows, :]

            @pl.when(owner != c)
            def _():
                g_send[q] = g[rows, :].astype(bf16)
                g_wire(q).start()

    def pair_done(i):
        if i == 0:
            late.wait()
        wide = [pv[:, t * H + i * 128 : t * H + (i + 1) * 128] for t in range(3)]
        value = dot(nT[...], jnp.concatenate(wide, axis=1), 1, 0).astype(bf16)
        chunk = chunks[i]
        r = chunk.acc.shape[2]
        for b in range(Z * X):
            chunk.acc[b // X, b % X] = value[b * r : (b + 1) * r, :]
        start_all(chunk.along_x())

    def token_rows(qi):
        for u, q, owner in sub_blocks(qi):

            @pl.when(owner == c)
            def _():
                a = local(row_sem, tok.at[line(q * T, T)], tok_v)
                b = local(row_sem + 1, gm.at[line(q * T, T)], gm_v)
                a.start()
                b.start()
                g_wire(q).wait_recv()
                grad = keep[(qi % 2 * U + u) // C] + g_recv[q].astype(f32)
                a.wait()
                unit, factor = normed(tok_v[...].astype(f32))
                grads[0:1, :] += jnp.sum(grad * unit, axis=0, keepdims=True)
                grads[1:2, :] += jnp.sum(grad, axis=0, keepdims=True)
                b.wait()
                tg_v[q] = (gm_v[...] + norm_back(grad, gain, unit, factor)).astype(bf16)

                @pl.when(q == p)
                def _():
                    local(row_sem + 2, tg_v.at[q], tg_home.at[p]).start()

                @pl.when(q != p)
                def _():
                    home_to(q).start()

    def one_query(pair, qi):
        d0 = qi * BQ
        qs = slice(d0, d0 + BQ)
        cols = lane(pair * 128, 128)
        k_cols, v_cols = lane(H + pair * 128, 128), lane(2 * H + pair * 128, 128)
        q_val, do_val = pv[qs, cols], do[qs, cols]
        qT, doT = q_val.T, do_val.T
        part = BQ // 2
        cuts = []
        if d0 and qi < nq - 1:
            cuts = [(0, part, 1, 0), (part, min(BQ, d0), 0, 0)]
            cuts += [(a, a + BQ, 0, 0) for a in range(BQ, d0, BQ)]
        elif d0:
            cuts = [(a, a + BQ, 1, 0) for a in range(0, d0, BQ)]
        cuts += [(d0, d0 + part, 2, 0), (d0 + part, d0 + BQ, 2, part)]
        dqs = []
        for h in range(2):
            rows = slice(h * HEAD_DIM, (h + 1) * HEAD_DIM)
            kT_rows = pl.ds(pl.multiple_of(pair * 128 + h * HEAD_DIM, HEAD_DIM), HEAD_DIM)
            query, grad = head_masked(qT, h, 0), head_masked(doT, h, 0)
            q_nat, do_nat = head_masked(q_val, h, 1), head_masked(do_val, h, 1)
            delta = jnp.sum(doT[rows, :].astype(f32) * oT[rows, qs], axis=0, keepdims=True)
            log_total = lt[pair, h : h + 1, qs]
            dq = jnp.zeros((HEAD_DIM, BQ), f32)
            for a, b, mode, qa in cuts:
                sc = dot(pv[a:b, k_cols], query[:, qa:], 1, 0) * scale
                prob = jnp.exp2(sc - log_total[:, qa:])
                if mode:
                    shape = (b - a, BQ - qa)
                    key_pos = lax.broadcasted_iota(jnp.int32, shape, 0) + a
                    visible = key_pos >= begin[:, d0 + qa : d0 + BQ]
                    if mode == 2:
                        query_pos = lax.broadcasted_iota(jnp.int32, shape, 1) + d0 + qa
                        visible = jnp.logical_and(visible, key_pos <= query_pos)
                    prob = jnp.where(visible, prob, 0.0)
                dp = dot(pv[a:b, v_cols], grad[:, qa:], 1, 0)
                ds = (prob * (dp - delta[:, qa:])).astype(bf16)
                dv[a:b, :] += dot(prob.astype(bf16), do_nat[qa:], 1, 0)
                dk[a:b, :] += dot(ds, q_nat[qa:], 1, 0)
                more = dot(kT[kT_rows, a:b], ds, 1, 0)
                if qa:
                    more = jnp.concatenate([jnp.zeros((HEAD_DIM, qa), f32), more], axis=1)
                dq = dq + more
            dqs.append(dq)
        pv[qs, cols] = (jnp.concatenate(dqs, axis=0) * scale_back).astype(bf16).T
        pv[qs, k_cols] = (dk[qs, :] * scale_back).astype(bf16)
        pv[qs, v_cols] = dv[qs, :].astype(bf16)

    out_m, up_m, down_m = adds
    v_core = wire.copy("vc", v0, vc, sibling)
    v_x = wire.copy("vx", v1, vx, beside)
    v_z = [
        wire.copy(("vz", k), v2, vz.at[k - 1], place.device(place.mirror(z, k), x, p, c))
        for k in place.across_z()
    ]
    v_y = [
        wire.copy(("vy", k), v3, vy.at[k - 1], place.device(z, x, (p + k) % Y, c))
        for k in range(1, Y)
    ]

    def vector_core():
        grads[2:4, :] = vec_two[...]
        v0[0:4, :] = grads[0:4, 0:H]
        v0[4:8, :] = grads[0:4, H:]
        v_core.start()

    def vector_x():
        v_core.wait_recv()
        v1[...] = v0[...] + vc[...]
        v_x.start()

    def vector_z():
        v_x.wait_recv()
        v2[...] = v1[...] + vx[...]
        start_all(v_z)

    def vector_y():
        arrive_all(v_z)
        v3[...] = v2[...] + sum(vz[k] for k in range(Z - 1))
        start_all(v_y)

    def vector_end():
        arrive_all(v_y)
        vec_out[...] = v3[...] + sum(vy[k] for k in range(Y - 1))

    def chunk_end(i):
        mine, far = chunks[i].result()
        for half in range(C):

            @pl.when(c == half)
            def _():
                for value, core in ((mine, half), (far, 1 - half)):
                    for t in range(3):
                        lo = t * D + core * H + i * 128
                        whole[:, lo : lo + 128] = value[:, t * 128 : (t + 1) * 128]

    def out_start():
        core_add(0)
        start_all(out_m.one())

    def up_start():
        core_add(1)
        start_all(up_m.one())

    def down_start():
        core_add(2)
        start_all(down_m.one())

    acts = {
        "U0": up_start,
        "U1": up_m.add_one,
        "U2": up_m.add_two,
        "UF": lambda: up_m.finish(sums[2]),
        "D0": down_start,
        "D1": down_m.add_one,
        "D2": down_m.add_two,
        "DF": lambda: down_m.finish(sums[3]),
        "O0": out_start,
        "O1": out_m.add_one,
        "O2": out_m.add_two,
        "OF": lambda: out_m.finish(sums[1]),
        "Vc": vector_core,
        "Vx": vector_x,
        "Vz": vector_z,
        "Vy": vector_y,
        "Vr": vector_end,
    }
    for i, chunk in enumerate(chunks):
        acts[f"C{i}x"] = functools.partial(pair_done, i)
        acts[f"C{i}z"] = chunk.go_z
        acts[f"C{i}y"] = chunk.go_y
        acts[f"C{i}c"] = chunk.go_core
        acts[f"C{i}r"] = functools.partial(chunk_end, i)
    for qi in range(nq):
        acts[f"B{qi}"] = functools.partial(block_done, qi)
        acts[f"T{qi}"] = functools.partial(token_rows, qi)
    events, spot = {}, None
    for name in BACKWARD_PLAN:
        if name[0] == "S":
            spot = (int(name[1]), int(name[2]))
        else:
            events.setdefault(spot, []).append(name)

    def one_pair(pair, nothing):
        out_fetch(pair).wait()
        dk[...] = jnp.zeros_like(dk)
        dv[...] = jnp.zeros_like(dv)
        for i in range(nq):
            one_query(pair, nq - 1 - i)
            if i == nq - 1:

                @pl.when(pair < pairs - 1)
                def _():
                    out_fetch(pair + 1).start()

            for number in range(pairs):
                if (number, i) in events and (number, i) != (pairs - 1, nq - 1):

                    @pl.when(pair == number)
                    def _():
                        for name in events[number, i]:
                            acts[name]()

        return nothing

    for name in events.get(None, ()):
        acts[name]()
    lax.fori_loop(0, pairs, one_pair, 0)
    for name in events[pairs - 1, nq - 1]:
        acts[name]()
    w = sums[0].shape[1]
    for d in range(Y * C):

        @pl.when(p * C + c == d)
        def _():
            sums[0][...] = whole[:, d * w : (d + 1) * w]

    for k in range(1, Y):
        home_from(k).wait_recv()
        home_to((p + k) % Y).wait_send()
    local(row_sem + 2, tg_v.at[p], tg_home.at[p]).wait()
    for q in range(Y):
        g_wire(q).wait_send()
    v_core.wait_send()
    leave_all(v_y)
    v_x.wait_send()
    leave_all(v_z)
    for summing in adds + chunks:
        summing.leave()


def backward(place, parts, others, proj_shape, begin, proj, heads, oT, lt, normedT, w_own, tok, gm, vec, vec_two):
    n = len(parts)
    Z, X, Y, C = place.Z, place.X, place.Y, place.C
    L, W3 = proj.shape
    H = W3 // 3
    D = w_own.shape[0]
    T = L // (Y * C)
    BQ = 512
    inside = pl.BlockSpec(memory_space=pltpu.VMEM)
    anywhere = pl.BlockSpec(memory_space=pl.ANY)
    shapes = [proj_shape] + [part.shape[3:] for part in parts]
    sixths = [3, 3]
    out_shape = [jax.ShapeDtypeStruct(shape, f32) for shape in shapes]
    out_shape += [
        jax.ShapeDtypeStruct((8, H), f32),
        jax.ShapeDtypeStruct((Y, T, D), bf16),
    ]
    scratch = [pltpu.VMEM((Y, Z, X) + shape, bf16) for shape in shapes[1:]]
    scratch += [
        pltpu.VMEM((L, W3), bf16),
        pltpu.VMEM((L, H), bf16),
        pltpu.VMEM((128, L), f32),
        pltpu.VMEM((D, W3), bf16),
        pltpu.VMEM((H, L), bf16),
        pltpu.VMEM((L, 128), f32),
        pltpu.VMEM((L, 128), f32),
        pltpu.VMEM((D, L), bf16),
        pltpu.VMEM((max(1, 2 * (BQ // T) // C), T, D), f32),
        pltpu.VMEM((Y, T, D), bf16),
        pltpu.VMEM((Y, T, D), bf16),
        pltpu.VMEM((T, D), bf16),
        pltpu.VMEM((T, D), f32),
    ]
    scratch += [pltpu.VMEM((8, D), f32)] + [pltpu.VMEM((8, H), f32)] * 5
    scratch += [
        pltpu.VMEM((Y - 1, 8, H), f32),
        pltpu.VMEM((8, H), f32),
        pltpu.VMEM((Z - 1, 8, H), f32),
        pltpu.VMEM((proj_shape[0], 3 * D), f32),
    ]
    r, w = shapes[1]
    scratch += [
        pltpu.VMEM((Y, Z, X, r, w), bf16),
        pltpu.VMEM((Z - 1, Y, X, r, w), bf16),
        pltpu.VMEM((Y, r, w), bf16),
        pltpu.VMEM((Y - 1, r, w), bf16),
    ]
    for shape, part in zip(shapes[2:], sixths):
        r, w = shape
        h = first_rows(r, part)
        scratch += [
            pltpu.VMEM((Y, Z, X, r, w), bf16),
            pltpu.VMEM((Y, Z, h, w), bf16),
            pltpu.VMEM((Y - 1, Z, X, r - h, w), bf16),
            pltpu.VMEM((Y - 1, Z, h, w), bf16),
            pltpu.VMEM((Z, r - h, w), bf16),
            pltpu.VMEM((Z - 1, r, w), bf16),
        ]
    r = proj_shape[0]
    for pair in range(H // 128):
        scratch += [
            pltpu.VMEM((Z, X, r, 384), bf16),
            pltpu.VMEM((Z, r, 384), bf16),
            pltpu.VMEM((Z - 1, r, 384), bf16),
            pltpu.VMEM((Y, r, 384), bf16),
            pltpu.VMEM((Y, r, 384), bf16),
        ]
    each = 1 + (Y - 1) + (Y - 1) + 1 + (Z - 1)
    chunk_copies = 1 + (Z - 1) + (Y - 1) + 1
    copies = n * each + (H // 128) * chunk_copies + 2 + (Y - 1) + 1 + (Z - 1) + 3 * Y
    scratch += [
        pltpu.SemaphoreType.DMA((copies,)),
        pltpu.SemaphoreType.DMA((copies,)),
        pltpu.SemaphoreType.DMA((5 + 2 * n + 3,)),
    ]
    return pl.pallas_call(
        functools.partial(backward_kernel, place, n, BQ),
        out_shape=out_shape,
        in_specs=[inside] + [anywhere] * 3 + [inside] + [anywhere] * 4 + [inside] * 2 + [anywhere] * (2 * n),
        out_specs=[inside] * (n + 2) + [anywhere],
        scratch_shapes=scratch,
        compiler_params=pltpu.CompilerParams(
            collective_id=1, has_side_effects=True, vmem_limit_bytes=63 << 20
        ),
        name="backward",
    )(begin, proj, heads, oT, lt, normedT, w_own, tok, gm, vec, vec_two, *parts, *others)


def gelu_both(u):
    k = 0.7978845608028654
    square = u * u
    t = jnp.tanh(k * u * (1.0 + 0.044715 * square))
    half = 0.5 * (1.0 + t)
    slope = half + 0.5 * k * u * (1.0 - t * t) * (1.0 + 3 * 0.044715 * square)
    return u * half, slope


class Task:
    def __init__(self, copy, far):
        self.copy, self.far, self.left, self.here = copy, far, False, False
        copy.start()

    def gone(self):
        if not self.left:
            if self.far:
                self.copy.wait_send()
            else:
                self.copy.wait()
            self.left = True

    def came(self):
        if self.far and not self.here:
            self.copy.wait_recv()
            self.here = True


def dense_kernel(
    place, aligned, att, tok, cot, out_w, up_w, down_w, vec,
    home, gm_out, heads, up_own, down_own, out_own, up_other, down_other, out_other, vec_out,
    att_v, tok_v, cot_v, out_v, up_v, down_v, out_full, mid, n2, act, gh, n2T, cotT, oacc, g2,
    h_buf, g_buf, stage, up_cut, down_cut, load_sem, store_sem, send_sem, recv_sem,
):
    S, nb, Y, C = place.blk, place.batch, place.Y, place.C
    z, x, p, c = place.here()
    M, D = att_v.shape
    J = up_v.shape[1] // D
    T = M // Y
    H = D // C
    half = M // 2
    sibling = place.device(z, x, p, 1 - c)
    others = [place.device(z, x, (p + k) % Y, c) for k in range(1, Y)]
    wire = Wire(send_sem, recv_sem)
    loads, tasks = [], []

    def line(offset, size):
        return pl.ds(pl.multiple_of(offset, 16), size)

    def lane(offset, size):
        return pl.ds(pl.multiple_of(offset, 128), size)

    def load(src, dst):
        task = Task(pltpu.make_async_copy(src, dst, load_sem.at[len(loads)]), False)
        loads.append(task)
        return task

    def store(src, dst):
        count = sum(not task.far for task in tasks)
        tasks.append(Task(pltpu.make_async_copy(src, dst, store_sem.at[count]), False))
        return tasks[-1]

    def send(name, src, dst, device):
        tasks.append(Task(wire.copy(name, src, dst, device), True))
        return tasks[-1]

    per_half = half // T
    near = p // per_half
    halves = [1 - near, near]
    rows_of = [slice(0, half), slice(half, M)]

    def spot_of(q, chip):
        apart = q // per_half - chip // per_half
        return (1 - apart * apart) * half + q % per_half * T

    w_up = up_own.shape[2]
    in_chunk = D // w_up
    chunks = []
    for s in range(J):
        if in_chunk == 1:
            chunks.append((s // C) * C + (1 - c if s % C == 0 else c))
        else:
            chunks.append(s)

    first = [load(out_w, out_v)]
    for t in (0, 1):
        there = line(halves[t] * half, half)
        first += [load(att.at[there], att_v.at[rows_of[t]]), load(tok.at[there], tok_v.at[rows_of[t]])]
    first.append(load(cot.at[p], cot_v.at[line(spot_of(p, p), T), :]))
    if aligned:
        weights = []
        r, w = down_w.shape[2:]
        for s in range(J):
            for i in range(in_chunk):
                at = s * D + i * w_up
                weights.append(load(up_w.at[chunks[s] * in_chunk + i], up_v.at[:, at : at + w_up]))
            for i in range(D // w):
                at = s * D + i * w
                weights += [
                    load(
                        down_w.at[d, chunks[s] * (D // w) + i],
                        down_v.at[d * r : (d + 1) * r, at : at + w],
                    )
                    for d in range(S)
                ]
    else:
        weights = [load(up_w, up_v), load(down_w, down_v)]
    greet(place, others + [sibling])
    cots = []
    for k in range(1, Y):
        to = (p + k) % Y
        dst = cot_v.at[line(spot_of(p, to), T), :]
        cots.append(send(("cot", k), cot.at[to], dst, others[k - 1]))
    for task in first:
        task.gone()
    w = out_v.shape[2]
    for d in range(S):
        out_full[:, d * w : (d + 1) * w] = out_v[d]
    gain, shift = vec[2:3, :], vec[3:4, :]
    for t in (0, 1):
        ts = rows_of[t]
        middle = tok_v[ts, :].astype(f32) + dot(att_v[ts, :], out_full[...], 1, 0)
        unit, factor = normed(middle)
        mid[ts, :] = middle
        low = (unit * gain + shift).astype(bf16)
        n2[ts, :] = low
        n2T[:, ts] = low.T
    for task in weights:
        task.gone()
    def cols(s):
        return slice(s * D, (s + 1) * D)

    busy = {}

    def staged(key, value, width, cut):
        for task in busy.get(key, []):
            task.gone()
        busy[key] = []
        if cut is not None:
            for i in range(value.shape[1] // width):
                cut[i] = value[:, i * width : (i + 1) * width]
            return lambda rows, i: cut.at[i, rows, :]
        stage[key] = value
        if value.shape[1] == width:
            return lambda rows, i: stage.at[key, rows, :]
        return lambda rows, i: stage.at[key, rows, i * width : (i + 1) * width]

    def up_gradient(s):
        value = dot(n2T[...], gh[:, cols(s)], 1, 0).astype(bf16)
        piece = staged(0, value, w_up, None if aligned else up_cut)
        every = slice(0, D)
        if in_chunk == 1:
            q = s // C
            if s % C == 0:
                busy[0].append(send(("up", s), piece(every, 0), up_other.at[q], sibling))
            else:
                busy[0].append(store(piece(every, 0), up_own.at[q]))
            return
        for i in range(in_chunk // C):
            q = s * in_chunk // C + i
            busy[0].append(store(piece(every, C * i + c), up_own.at[q]))
            busy[0].append(send(("up", q), piece(every, C * i + 1 - c), up_other.at[q], sibling))

    def down_gradient(s):
        value = dot(cotT[...], act[:, cols(s)], 1, 0).astype(bf16)
        r, w = down_own.shape[2:]
        piece = staged(1, value, w, None if aligned else down_cut)
        for q in range(Y):
            for i in range(D // w):
                b = chunks[s] * (D // w) + i
                busy[1].append(store(piece(line((C * q + c) * r, r), i), down_own.at[q, b]))
                busy[1].append(
                    send(
                        ("down", s, q, i),
                        piece(line((C * q + 1 - c) * r, r), i),
                        down_other.at[q, b],
                        sibling,
                    )
                )

    units = [(0, "f", s) for s in range(J)] + [(1, "fb", s) for s in range(J)]
    units += [(0, "b", s) for s in range(J)]

    W = D

    def part_of(s, i):
        return slice(s * D + i * W, s * D + (i + 1) * W)

    def enter(number, i):
        t, kind, s = units[number]
        mine = slice(i * W, (i + 1) * W)
        if "f" in kind:
            h_buf[number % 2, :, mine] = dot(n2[rows_of[t], :], up_v[:, part_of(s, i)], 1, 0)
        if "b" in kind:
            g_buf[number % 2, :, mine] = dot(cot_v[rows_of[t], :], down_v[:, part_of(s, i)], 1, 0)

    def activate(number, i):
        t, kind, s = units[number]
        ts, mine, place_here = rows_of[t], slice(i * W, (i + 1) * W), part_of(s, i)
        if "f" in kind:
            a, slope = gelu_both(h_buf[number % 2, :, mine])
            act[ts, place_here] = a.astype(bf16)
            if kind == "f":
                gh[ts, place_here] = slope.astype(bf16)
        else:
            slope = gh[ts, place_here].astype(f32)
        if "b" in kind:
            gh[ts, place_here] = (g_buf[number % 2, :, mine] * slope).astype(bf16)

    def leave(number, i):
        t, kind, s = units[number]
        ts, mine = rows_of[t], slice(i * W, (i + 1) * W)
        wanted = []
        if "f" in kind:
            wanted.append((oacc, act, down_v))
        if "b" in kind:
            wanted.append((g2, gh, up_v))
        for total, left, right in wanted:
            more = dot(left[ts, cols(s)], right[mine, cols(s)], 1, 1)
            if s == 0:
                total[:, mine] = more
            else:
                total[:, mine] += more

    def output_rows(t):
        ts = rows_of[t]
        tok_v[ts, :] = (mid[ts, :] + oacc[...]).astype(bf16)
        if Y == 2 and t == 1:
            store(tok_v.at[ts, :], home.at[near])
        elif Y == 2:
            send("home", tok_v.at[ts, :], home.at[p], others[0])

    sums = [jnp.zeros((1, D), f32), jnp.zeros((1, D), f32)]

    def norm_rows(t):
        ts = rows_of[t]
        unit, factor = normed(mid[ts, :])
        grad = g2[...]
        sums[0] = sums[0] + jnp.sum(grad * unit, axis=0, keepdims=True)
        sums[1] = sums[1] + jnp.sum(grad, axis=0, keepdims=True)
        gm = cot_v[ts, :].astype(f32) + norm_back(grad, gain, unit, factor)
        mid[ts, :] = gm
        low = gm.astype(bf16)
        n2[ts, :] = low
        cot_v[ts, :] = dot(low, out_full[...], 1, 1).astype(bf16)
        store(mid.at[ts, :], gm_out.at[line(halves[t] * half, half), :])
        for i in range(per_half):
            q = halves[t] * per_half + i
            rows = slice(t * half + i * T, t * half + (i + 1) * T)
            spot = line((C * q + c) * T, T)
            store(cot_v.at[rows, lane(c * H, H)], heads.at[spot, :])
            send(("ga", t, i), cot_v.at[rows, lane((1 - c) * H, H)], heads.at[spot, :], sibling)

    count = len(units)
    for number in range(count + 2):
        if number < count:
            t, kind, s = units[number]
            if units[number] == ((0, "b", 0) if Y == 2 else (1, "fb", 0)):
                for task in cots:
                    task.came()
        for i in range(D // W):
            if number < count:
                enter(number, i)
            if 0 <= number - 1 < count:
                activate(number - 1, i)
            if 0 <= number - 2:
                leave(number - 2, i)
        if number < 2:
            continue
        t, kind, s = units[number - 2]
        if s == J - 1:
            if kind == "f":
                output_rows(t)
            elif kind == "fb":
                output_rows(t)
                cotT[:, rows_of[t]] = cot_v[rows_of[t], :].T
                norm_rows(t)
                cotT[:, rows_of[0]] = cot_v[rows_of[0], :].T
            else:
                norm_rows(t)
        if kind == "b":
            up_gradient(s)
            down_gradient(s)
    if Y > 2:
        store(tok_v.at[line(spot_of(p, p), T), :], home.at[p])
        for k in range(1, Y):
            to = (p + k) % Y
            send(("home", k), tok_v.at[line(spot_of(to, p), T), :], home.at[p], others[k - 1])
    vec_out[0:1, :] = sums[0]
    vec_out[1:2, :] = sums[1]
    value = dot(att_v[...], n2[...], 0, 0).astype(bf16)
    w = out_own.shape[2]
    for d in range(S):
        out_v[d] = value[:, d * w : (d + 1) * w]
    for q in range(Y):
        store(out_v.at[C * q + c], out_own.at[q])
        send(("out", q), out_v.at[C * q + 1 - c], out_other.at[q], sibling)
    for task in tasks:
        task.came()
    for task in tasks:
        task.gone()


def dense(place, att, tok, cot, out_g, up_g, down_g, vec):
    M, D = att.shape
    S, nb, Y, C = place.blk, place.batch, place.Y, place.C
    T = M // Y
    H = D // C
    aligned = up_g.shape[-1] % 128 == 0 and down_g.shape[-1] % 128 == 0
    out_w = out_g.reshape(S, D, -1)
    FF = S * up_g.shape[-1]
    if aligned:
        up_w = up_g.reshape(S, D, -1)
        down_w = down_g.reshape((S, nb) + down_g.shape[-2:])
    else:
        up_w, down_w = joined(up_g, 0), joined(down_g, 1)
    anywhere = pl.BlockSpec(memory_space=pl.ANY)
    inside = pl.BlockSpec(memory_space=pltpu.VMEM)
    pieces = [
        jax.ShapeDtypeStruct((Y, D, up_g.shape[-1]), bf16),
        jax.ShapeDtypeStruct((Y, nb) + down_g.shape[-2:], bf16),
        jax.ShapeDtypeStruct((Y, D, out_g.shape[-1]), bf16),
    ]
    none = (1, 16, 128)
    up_cut = none if aligned else (D // up_g.shape[-1], D, up_g.shape[-1])
    down_cut = none if aligned else (D // down_g.shape[-1], D, down_g.shape[-1])
    loads = 8 + S + S * nb
    J = FF // D
    down_count = J * Y * (D // down_g.shape[-1])
    copies = 2 * (Y - 1) + 2 * Y + S + down_count + 4 * Y + 8
    results = pl.pallas_call(
        functools.partial(dense_kernel, place, aligned),
        out_shape=[
            jax.ShapeDtypeStruct((Y, T, D), bf16),
            jax.ShapeDtypeStruct((M, D), f32),
            jax.ShapeDtypeStruct((S * T, H), bf16),
        ]
        + pieces
        + pieces
        + [jax.ShapeDtypeStruct((2, D), f32)],
        in_specs=[anywhere] * 6 + [inside],
        out_specs=[anywhere] * 9 + [inside],
        scratch_shapes=[
            pltpu.VMEM((M, D), bf16),
            pltpu.VMEM((M, D), bf16),
            pltpu.VMEM((M, D), bf16),
            pltpu.VMEM(out_w.shape, bf16),
            pltpu.VMEM((D, FF), bf16),
            pltpu.VMEM((D, FF), bf16),
            pltpu.VMEM((D, D), bf16),
            pltpu.VMEM((M, D), f32),
            pltpu.VMEM((M, D), bf16),
            pltpu.VMEM((M, FF), bf16),
            pltpu.VMEM((M, FF), bf16),
            pltpu.VMEM((D, M), bf16),
            pltpu.VMEM((D, M), bf16),
            pltpu.VMEM((M // 2, D), f32),
            pltpu.VMEM((M // 2, D), f32),
            pltpu.VMEM((2, M // 2, D), f32),
            pltpu.VMEM((2, M // 2, D), f32),
            pltpu.VMEM((2, D, D), bf16) if aligned else pltpu.VMEM((1, 16, 128), bf16),
            pltpu.VMEM(up_cut, bf16),
            pltpu.VMEM(down_cut, bf16),
            pltpu.SemaphoreType.DMA((loads,)),
            pltpu.SemaphoreType.DMA((copies,)),
            pltpu.SemaphoreType.DMA((copies,)),
            pltpu.SemaphoreType.DMA((copies,)),
        ],
        compiler_params=pltpu.CompilerParams(
            collective_id=2, has_side_effects=True, vmem_limit_bytes=62 << 20
        ),
        name="dense",
    )(att, tok, cot, out_w, up_w, down_w, vec)
    home, gm, heads = results[:3]
    shapes = [(Y,) + up_g.shape[2:], (Y,) + down_g.shape[2:], (Y,) + out_g.shape[2:]]
    own = [value.reshape(shape) for value, shape in zip(results[3:6], shapes)]
    other = [value.reshape(shape) for value, shape in zip(results[6:9], shapes)]
    return home, gm, heads, own, other, results[9]


def hand_over_kernel(place, n, *refs):
    given, vec, out, vec_out = refs[:n], refs[n], refs[n + 1 : 2 * n + 1], refs[2 * n + 1 : 2 * n + 5]
    whole, between, sem = refs[2 * n + 5], refs[2 * n + 6 : 3 * n + 6], refs[3 * n + 6]
    pieces = []
    for i in range(n):
        if len(given[i].shape) == 3:
            R, T, _ = given[i].shape
            cut = [(r, slice(h * T // 2, (h + 1) * T // 2)) for r in range(R) for h in range(2)]
        else:
            cut = [slice(None)]
        pieces += [(given[i].at[k], between[i].at[k], out[i].at[k]) for k in cut]
    here = [
        pltpu.make_async_copy(src, mid, sem.at[0, j]) for j, (src, mid, dst) in enumerate(pieces)
    ]
    away = [
        pltpu.make_async_copy(mid, dst, sem.at[1, j]) for j, (src, mid, dst) in enumerate(pieces)
    ]
    start_all(here)
    H = vec.shape[1]
    whole[0:4, 0:H] = vec[0:4, :]
    whole[0:4, H:] = vec[4:8, :]
    me = lax.axis_index("blk")
    w = vec_out[0].shape[1]
    for d in range(place.blk):

        @pl.when(me == d)
        def _():
            for i in range(4):
                vec_out[i][...] = whole[i : i + 1, d * w : (d + 1) * w]

    for come, go in zip(here, away):
        come.wait()
        go.start()
    for copy in away:
        copy.wait()


def hand_over(place, given, vec):
    n = len(given)
    anywhere = pl.BlockSpec(memory_space=pl.ANY)
    inside = pl.BlockSpec(memory_space=pltpu.VMEM)
    H = vec.shape[1]
    count = sum(2 * v.shape[0] if len(v.shape) == 3 else 1 for v in given)
    return pl.pallas_call(
        functools.partial(hand_over_kernel, place, n),
        out_shape=[jax.ShapeDtypeStruct(v.shape, v.dtype) for v in given]
        + [jax.ShapeDtypeStruct((1, 2 * H // place.blk), f32)] * 4,
        in_specs=[anywhere] * n + [inside],
        out_specs=[anywhere] * n + [inside] * 4,
        scratch_shapes=[pltpu.VMEM((8, 2 * H), f32)]
        + [pltpu.VMEM(v.shape, v.dtype) for v in given]
        + [pltpu.SemaphoreType.DMA((2, count))],
        compiler_params=pltpu.CompilerParams(vmem_limit_bytes=62 << 20),
        name="hand_over",
    )(*given, vec)


def normed(values):
    average = jnp.mean(values, axis=-1, keepdims=True)
    centered = values - average
    variance = jnp.mean(centered * centered, axis=-1, keepdims=True)
    factor = lax.rsqrt(variance + epsilon)
    return centered * factor, factor


def norm_back(grad, gain, unit, factor):
    e = grad * gain
    return factor * (
        e - jnp.mean(e, axis=-1, keepdims=True) - unit * jnp.mean(e * unit, axis=-1, keepdims=True)
    )


def joined(gathered, axis):
    Y, C, Z, X, r, w = gathered.shape
    if axis == 0:
        return gathered.reshape(Y * C, Z * X * r, w).transpose(1, 0, 2).reshape(Z * X * r, -1)
    return gathered.reshape(Y * C, Z * X, r, w).transpose(0, 2, 1, 3).reshape(Y * C * r, -1)


def parted(whole, place, axis):
    Y, C, Z, X = place.Y, place.C, place.Z, place.X
    rows, columns = whole.shape
    if axis == 0:
        value = whole.reshape(Z * X, rows // (Z * X), Y * C, columns // (Y * C))
        value = value.transpose(2, 0, 1, 3)
    else:
        value = whole.reshape(Y * C, rows // (Y * C), Z * X, columns // (Z * X))
        value = value.transpose(0, 2, 1, 3)
    return value.reshape((Y, C, Z, X) + value.shape[2:])


def body(
    place,
    tokens,
    proj_weight,
    out_weight,
    up_weight,
    down_weight,
    gain_one,
    bias_one,
    gain_two,
    bias_two,
    segments,
    present,
    cotangent,
):
    rows, block, width = tokens.shape
    Y = place.Y
    row = lax.broadcasted_iota(jnp.int32, (16, width // place.blk), 0)
    vec_in = jnp.zeros(row.shape, bf16)
    for i, vector in enumerate((gain_one, bias_one, gain_two, bias_two)):
        vec_in = jnp.where(row == i, vector[None, :], vec_in)
    (
        out_g, up_g, down_g, tok_mine, vec, begin, projected, proj_own, normed_t,
        attended_low, attended_t, log_total,
    ) = forward(
        place,
        [proj_weight, out_weight, up_weight, down_weight.T],
        tokens,
        segments,
        present,
        vec_in,
    )
    tok_mine = tok_mine.reshape(Y * block, width)
    output, grad_middle, grad_heads, own, other, vec_two = dense(
        place, attended_low, tok_mine, cotangent, out_g, up_g, down_g, vec
    )
    order = (2, 0, 1)
    proj_sum, out_sum, up_sum, down_sum, vec_sum, token_grad = backward(
        place,
        [own[i] for i in order],
        [other[i] for i in order],
        proj_weight.shape,
        begin,
        projected,
        grad_heads,
        attended_t,
        log_total,
        normed_t,
        proj_own,
        tok_mine,
        grad_middle,
        vec,
        vec_two,
    )
    output, token_grad, proj_sum, out_sum, up_sum, down_sum, *vectors = hand_over(
        place, (output, token_grad, proj_sum, out_sum, up_sum, down_sum), vec_sum
    )
    return (
        output,
        token_grad,
        proj_sum,
        out_sum,
        up_sum,
        down_sum.T,
        vectors[0].reshape(-1),
        vectors[1].reshape(-1),
        vectors[2].reshape(-1),
        vectors[3].reshape(-1),
    )


def solution(mesh):
    place = Place((mesh.shape["batch"], mesh.shape["blk"]))
    weight, vector = P("batch", "blk"), P("blk")
    row = P("batch", "blk", None)
    in_specs = (row,) + (weight,) * 4 + (vector,) * 4 + (weight,) * 2 + (row,)
    out_specs = (row, row) + (weight,) * 4 + (vector,) * 4
    return jax.shard_map(
        functools.partial(body, place),
        mesh=mesh,
        in_specs=in_specs,
        out_specs=out_specs,
        check_vma=False,
    )
```

```python
import functools

import jax
import jax.numpy as jnp
from jax import lax
from jax.experimental import pallas as pl
from jax.experimental.pallas import tpu as pltpu
from jax.sharding import PartitionSpec as P

HEADS = 12
HEAD_DIM = 64
CORES = 2
LANE_X = 2
MESH = pl.DeviceIdType.MESH
LOG2E = 1.4426950408889634
epsilon = 1e-05
masked = -1e30
bf16 = jnp.bfloat16
f32 = jnp.float32


def dot(left, right, left_dim, right_dim):
    return lax.dot_general(
        left, right, (((left_dim,), (right_dim,)), ((), ())), preferred_element_type=f32
    )


class Place:
    def __init__(self, sizes):
        self.batch, self.blk = sizes
        self.Z, self.X = self.batch // LANE_X, LANE_X
        self.Y, self.C = self.blk // CORES, CORES

    def here(self):
        b, d = lax.axis_index("batch"), lax.axis_index("blk")
        return b // self.X, b % self.X, d // self.C, d % self.C

    def device(self, z, x, p, c):
        return (z * self.X + x, p * self.C + c)

    def across_z(self):
        return [k for k in range(2, self.Z)] + [1]

    def mirror(self, z, k):
        for bit in range(self.Z.bit_length()):
            if k >> bit & 1:
                z = z + (1 << bit) - (2 << bit) * (z // (1 << bit) % 2)
        return z


class Wire:
    def __init__(self, send_sem, recv_sem):
        self.send_sem, self.recv_sem, self.names = send_sem, recv_sem, {}

    def copy(self, name, src, dst, device):
        i = self.names.setdefault(name, len(self.names))
        return pltpu.make_async_remote_copy(
            src_ref=src,
            dst_ref=dst,
            send_sem=self.send_sem.at[i],
            recv_sem=self.recv_sem.at[i],
            device_id=device,
            device_id_type=MESH,
        )


def start_all(copies):
    for copy in copies:
        copy.start()


def arrive_all(copies):
    for copy in copies:
        copy.wait_recv()


def leave_all(copies):
    for copy in copies:
        copy.wait_send()


def first_rows(rows, sixths):
    return min(rows - 16, 16 * ((rows * sixths // 6) // 16)) if rows > 16 else 0


def greet(place, partners):
    barrier = pltpu.get_barrier_semaphore()
    for partner in partners:
        pl.semaphore_signal(barrier, inc=1, device_id=partner, device_id_type=MESH)
    pl.semaphore_wait(barrier, len(partners))


def partners_of(place):
    z, x, p, c = place.here()
    found = [place.device(place.mirror(z, k), x, p, c) for k in place.across_z()]
    found += [place.device(z, 1 - x, p, c)]
    found += [place.device(z, x, (p + k) % place.Y, c) for k in range(1, place.Y)]
    found += [place.device(z, x, p, 1 - c)]
    return found


def head_masked(value, h, axis):
    index = lax.broadcasted_iota(jnp.int32, value.shape, axis)
    return jnp.where((index // HEAD_DIM) == h, value, jnp.zeros_like(value))


class Spreading:
    def __init__(self, place, wire, name, spots, shard, whole, deep, low):
        self.place, self.wire, self.name, self.spots = place, wire, name, spots
        self.shard, self.whole = shard, whole
        self.r = shard.shape[0]
        self.g = sixths(self.r, deep)
        self.h = self.g + sixths(self.r, low)

    def copy(self, what, src, dst, device):
        return self.wire.copy((self.name, what), src, dst, device)

    def sides(self):
        z, x, p, c = self.spots
        place = self.place
        along_y = [(k, place.device(z, x, (p + k) % place.Y, c)) for k in range(1, place.Y)]
        along_z = [(k, place.device(place.mirror(z, k), x, p, c)) for k in place.across_z()]
        return place.device(z, 1 - x, p, c), along_y, along_z

    def deep_one(self):
        z, x, p, c = self.spots
        src, dst = self.shard.at[0 : self.g], self.whole.at[p, c, z, x, 0 : self.g]
        return [self.copy(("dy", k), src, dst, side) for k, side in self.sides()[1]]

    def deep_two(self):
        z, x, p, c = self.spots
        part = self.whole.at[:, c, z, x, 0 : self.g]
        return [self.copy("dx", part, part, self.sides()[0])]

    def deep_three(self):
        z, x, p, c = self.spots
        part = self.whole.at[:, c, z, :, 0 : self.g]
        return [self.copy(("dz", k), part, part, side) for k, side in self.sides()[2]]

    def along_z(self, what, rows):
        z, x, p, c = self.spots
        src, dst = self.shard.at[rows], self.whole.at[p, c, z, x, rows]
        return [self.copy((what, k), src, dst, side) for k, side in self.sides()[2]]

    def low_zero(self):
        return self.along_z("za", slice(self.g, self.h))

    def high_zero(self):
        return self.along_z("zb", slice(self.h, self.r))

    def low_one(self):
        z, x, p, c = self.spots
        part = self.whole.at[p, c, :, x, self.g : self.h]
        return [self.copy("xa", part, part, self.sides()[0])]

    def high_one(self):
        z, x, p, c = self.spots
        part = self.whole.at[p, c, :, x, self.h : self.r]
        return [self.copy(("yb", k), part, part, side) for k, side in self.sides()[1]]

    def low_two(self):
        z, x, p, c = self.spots
        part = self.whole.at[p, c, :, :, self.g : self.h]
        return [self.copy(("ya", k), part, part, side) for k, side in self.sides()[1]]

    def high_two(self):
        z, x, p, c = self.spots
        part = self.whole.at[:, c, :, x, self.h : self.r]
        return [self.copy("xb", part, part, self.sides()[0])]

    def to_core(self, what, rows):
        z, x, p, c = self.spots
        part = self.whole.at[:, c, :, :, rows]
        return [self.copy(what, part, part, self.place.device(z, x, p, 1 - c))]

    def low_three(self):
        return self.to_core("ca", slice(self.g, self.h))

    def high_three(self):
        return self.to_core("cb", slice(self.h, self.r))

    def deep_four(self):
        return self.to_core("cd", slice(0, self.g))

    def chains(self):
        found = []
        if self.g:
            found.append([self.deep_one, self.deep_two, self.deep_three, self.deep_four])
        if self.g < self.h:
            found.append([self.low_zero, self.low_one, self.low_two, self.low_three])
        if self.h < self.r:
            found.append([self.high_zero, self.high_one, self.high_two, self.high_three])
        return found

    def begin(self):
        for chain in self.chains():
            start_all(chain[0]())

    def step(self, group, number):
        chain = (
            [self.deep_one, self.deep_two, self.deep_three, self.deep_four],
            [self.low_zero, self.low_one, self.low_two, self.low_three],
            [self.high_zero, self.high_one, self.high_two, self.high_three],
        )[group]
        arrive_all(chain[number - 1]())
        start_all(chain[number]())

    def arrive(self):
        for chain in self.chains():
            arrive_all(chain[3]())

    def leave(self):
        for chain in self.chains():
            for stage in chain:
                leave_all(stage())


FORWARD_PLAN = (
    "t1", "O1d", "V", "D1d", "O2d", "t2", "U1d", "N0", "P1a", "P1b", "t3", "P2b", "P2a",
    "U1b", "K", "U1a", "D1b", "P3b", "D1a", "P3a", "N2", "N3", "W", "U2b", "U2a", "D2d",
    "J", "S00", "S01", "D2b", "D2a", "S02", "S10", "O3d", "S11", "S12", "U2d", "S20",
    "S21", "S22", "U3a", "S30", "U3b", "D3b", "U3d", "S31", "D3a", "D3d", "S32",
)
ROW_PARTS = 4


def forward_kernel(place, n, BQ, *refs):
    shards, (tok, segments, present) = refs[: n + 1], refs[n + 1 : n + 4]
    vectors, outs = refs[n + 4 : n + 8], refs[n + 8 :]
    wholes = outs[:n]
    (tok_out, vec_out, begin, proj_out, w_out, normedT_out, att_out, oT_out, lt) = outs[
        n : n + 9
    ]
    (
        vec_in, proj_v, tok_v, tag, tag_v, vec_v, n_v, nT, wv, pv, vT, att, oT,
        send_sem, recv_sem, local_sem,
    ) = outs[n + 9 :]
    spots = place.here()
    z, x, p, c = spots
    Z, X, Y, C = place.Z, place.X, place.Y, place.C
    D, W3 = wv.shape
    H = W3 // 3
    L = pv.shape[0]
    T = L // (Y * C)
    U = BQ // T
    pairs = H // 128
    nq = L // BQ
    wire = Wire(send_sem, recv_sem)
    sibling = place.device(z, x, p, 1 - c)
    flows = [
        Spreading(place, wire, m, spots, shards[m], proj_v if m == 0 else wholes[m - 1], *way)
        for m, way in enumerate(((0, 3), (6, 0), (1, 3), (1, 3)))
    ]

    def local(i, src, dst):
        return pltpu.make_async_copy(src, dst, local_sem.at[i])

    def lane(offset, size):
        return pl.ds(pl.multiple_of(offset, 128), size)

    def line(offset, size):
        return pl.ds(pl.multiple_of(offset, 16), size)

    row_parts = (("vec", vec_in, vec_v), ("tag", tag, tag_v), ("tok", tok, tok_v))

    def along_y(what, src, dst):
        found = []
        for k in range(1, Y):
            to = (p + k) % Y
            device = place.device(z, x, to, c)
            if what == "tok":
                for i in range(ROW_PARTS):
                    rows = slice(i * T // ROW_PARTS, (i + 1) * T // ROW_PARTS)
                    found.append(
                        wire.copy(
                            (what, "y", k, i), src.at[to, rows], dst.at[p, c, rows], device
                        )
                    )
            else:
                piece = src if what == "vec" else src.at[to]
                found.append(wire.copy((what, "y", k), piece, dst.at[p, c], device))
        return found

    def send_tokens(i):
        start_all(along_y(*row_parts[2])[i::ROW_PARTS])

    def to_sibling_own(what, src, dst):
        piece = src if what == "vec" else src.at[p]
        return wire.copy((what, "own"), piece, dst.at[p, c], sibling)

    def to_sibling(what, dst):
        found = []
        for k in range(1, Y):
            q = (p + k) % Y
            found.append(wire.copy((what, "pass", k), dst.at[q, c], dst.at[q, c], sibling))
        return found

    vec_in[...] = jnp.zeros_like(vec_in)
    for i, vector in enumerate(vectors):
        vec_in[i : i + 1, :] = vector[...].astype(f32).reshape(1, -1).astype(bf16)
    position = lax.broadcasted_iota(jnp.int32, (Y, T), 1) + (p * C + c) * T
    tags = jnp.where(present[...] == 1, segments[...], -1 - position)
    for q in range(Y):
        tag[q] = jnp.broadcast_to(tags[q : q + 1, :], tag.shape[1:])
    greet(place, partners_of(place))
    start_all(along_y(*row_parts[0]))
    for part in row_parts:
        to_sibling_own(*part).start()
    for flow in flows:
        flow.begin()
    start_all(along_y(*row_parts[1]))
    send_tokens(0)
    kept = [local(m, shards[m], flows[m].whole.at[p, c, z, x]) for m in range(n + 1)]
    kept += [
        local(n + 1, vec_in, vec_v.at[p, c]),
        local(n + 2, tag.at[p], tag_v.at[p, c]),
        local(n + 3, tok.at[p], tok_v.at[p, c]),
    ]
    start_all(kept)
    saves = [
        local(n + 5, nT, normedT_out),
        local(n + 6, tok_v.at[:, c], tok_out),
        local(n + 7, pv, proj_out),
        local(n + 8, wv, w_out),
    ]

    def norm_block(q, i):
        unit, factor = normed(tok_v[q, i].astype(f32))
        low = (unit * vec_out[0:1, :] + vec_out[1:2, :]).astype(bf16)
        rows = line((q * C + i) * T, T)
        n_v[rows, :] = low
        nT[:, lane((q * C + i) * T, T)] = low.T

    waited = set()

    def own_shard(m):
        if m not in waited:
            kept[m].wait()
            waited.add(m)

    def advance(m, group, number):
        own_shard(m)
        flows[m].step(group, number)

    def vector_pass():
        arrive_all(along_y(*row_parts[0]))
        start_all(to_sibling("vec", vec_v))

    def norm_near():
        for copy in kept[n + 1 :]:
            copy.wait()
        to_sibling_own(*row_parts[0]).wait_recv()
        arrive_all(to_sibling("vec", vec_v))
        share = vec_v.shape[3]
        for q in range(Y):
            for i in range(C):
                lo = (q * C + i) * share
                vec_out[:, lo : lo + share] = vec_v[q, i, 0:8, :].astype(f32)
        norm_block(p, c)
        to_sibling_own(*row_parts[2]).wait_recv()
        norm_block(p, 1 - c)

    def row_pass():
        for what, src, dst in row_parts[1:]:
            arrive_all(along_y(what, src, dst))
            start_all(to_sibling(what, dst))

    def norm_far():
        for k in range(1, Y):
            norm_block((p + k) % Y, c)

    def norm_last():
        arrive_all(to_sibling("tok", tok_v))
        for k in range(1, Y):
            norm_block((p + k) % Y, 1 - c)
        start_all(saves[:2])
        to_sibling_own(*row_parts[1]).wait_recv()
        arrive_all(to_sibling("tag", tag_v))
        tags = [tag_v[q, i, 0:1, :] for q in range(Y) for i in range(C)]
        counts = []
        for s in range(4):
            hits = sum((t == s).astype(f32) for t in tags)
            counts.append(jnp.sum(hits, axis=1, keepdims=True).astype(jnp.int32))
        for b, t in enumerate(tags):
            first = sum(jnp.where(t > s, counts[s], 0) for s in range(4))
            position = lax.broadcasted_iota(jnp.int32, (1, T), 1) + b * T
            begin[:, b * T : (b + 1) * T] = jnp.where(t < 0, position, first)

    def weight_columns():
        flows[0].arrive()
        r, w = proj_v.shape[4:]
        for mine in range(C):

            @pl.when(c == mine)
            def _():
                for third in range(3):
                    base = third * D + mine * H
                    for d in range(Y * C):
                        a, b = max(base, d * w), min(base + H, (d + 1) * w)
                        if a >= b:
                            continue
                        to = third * H + a - base
                        for i in range(Z * X):
                            wv[i * r : (i + 1) * r, to : to + b - a] = proj_v[
                                d // C, d % C, i // X, i % X, :, a - d * w : b - d * w
                            ]

    def project_all():
        def project(i, nothing):
            rows = line(i * BQ, BQ)
            pv[rows, :] = dot(n_v[rows, :], wv[...], 1, 0).astype(bf16)
            return nothing

        lax.fori_loop(0, nq, project, 0)
        values = pv[:, 2 * H :].T
        for h in range(2 * pairs):
            vT[h, 0:HEAD_DIM, :] = values[h * HEAD_DIM : (h + 1) * HEAD_DIM, :]
            vT[h, HEAD_DIM:, :] = jnp.ones((16, L), bf16)
        start_all(saves[2:])

    scale = HEAD_DIM ** (-0.5) * LOG2E

    def block_copies(qi):
        found = []
        for u in range(U):
            b = qi * U + u
            q, owner = b // C, b % C
            src = att.at[b * T : (b + 1) * T, :]
            dst = att_out.at[q * T : (q + 1) * T, lane(c * H, H)]
            found.append(
                (owner, local(n + 9 + q, src, dst), wire.copy(("att", q), src, dst, sibling))
            )
        return found

    acts = {
        "V": vector_pass,
        "N0": norm_near,
        "K": row_pass,
        "N2": norm_far,
        "N3": norm_last,
        "W": weight_columns,
        "J": project_all,
    }
    for m, name in enumerate("POUD"):
        for group, letter in enumerate("dab"):
            for number in (1, 2, 3):
                acts[f"{name}{number}{letter}"] = functools.partial(advance, m, group, number)
    for i in range(1, ROW_PARTS):
        acts[f"t{i}"] = functools.partial(send_tokens, i)
    events, spot = {}, None
    for name in FORWARD_PLAN:
        if name[0] == "S":
            spot = (int(name[1]), int(name[2]))
        else:
            events.setdefault(spot, []).append(name)
    for name in events[None]:
        acts[name]()
    for qi in range(nq):
        qs = slice(qi * BQ, (qi + 1) * BQ)
        d0 = qi * BQ
        part = BQ // 2
        cuts = []
        if d0 and qi < nq - 1:
            cuts = [(0, part, 1, 0), (part, min(BQ, d0), 0, 0)]
            cuts += [(a, a + BQ, 0, 0) for a in range(BQ, d0, BQ)]
        elif d0:
            cuts = [(a, a + BQ, 1, 0) for a in range(0, d0, BQ)]
        cuts += [(d0, d0 + part, 2, 0), (d0 + part, d0 + BQ, 2, part)]

        def widened(value, qa, blank):
            if not qa:
                return value
            return jnp.concatenate([jnp.full((value.shape[0], qa), blank, f32), value], axis=1)

        def one_pair(pair, nothing):
            cols = lane(pair * 128, 128)
            k_cols = lane(H + pair * 128, 128)
            qT = pv[qs, cols].T
            found, scores = [], []
            for h in range(2):
                query = head_masked(qT, h, 0)
                parts = []
                for a, b, mode, qa in cuts:
                    s = dot(pv[a:b, k_cols], query[:, qa:], 1, 0)
                    if mode:
                        shape = (b - a, BQ - qa)
                        key_pos = lax.broadcasted_iota(jnp.int32, shape, 0) + a
                        visible = key_pos >= begin[:, d0 + qa : d0 + BQ]
                        if mode == 2:
                            query_pos = lax.broadcasted_iota(jnp.int32, shape, 1) + d0 + qa
                            visible = jnp.logical_and(visible, key_pos <= query_pos)
                        s = jnp.where(visible, s, masked)
                    parts.append(s)
                scores.append(parts)
            for h in range(2):
                tops = [
                    widened(jnp.max(s, axis=0, keepdims=True), cut[3], masked)
                    for cut, s in zip(cuts, scores[h])
                ]
                top = functools.reduce(jnp.maximum, tops) * scale
                accum = jnp.zeros((vT.shape[1], BQ), f32)
                for (a, b, mode, qa), s in zip(cuts, scores[h]):
                    e = jnp.exp2(s * scale - top[:, qa:]).astype(bf16)
                    accum = accum + widened(dot(vT[pair * 2 + h, :, a:b], e, 1, 0), qa, 0.0)
                total = accum[HEAD_DIM : HEAD_DIM + 1]
                result = accum[:HEAD_DIM] / total
                rows = pl.ds(pl.multiple_of(pair * 128 + h * HEAD_DIM, HEAD_DIM), HEAD_DIM)
                oT[rows, qs] = result
                found.append(result)
                lt[pair, h : h + 1, qs] = top + jnp.log2(total)
            att[qs, cols] = jnp.concatenate(found, axis=0).astype(bf16).T
            for number in range(pairs):
                if (qi, number) in events:

                    @pl.when(pair == number)
                    def _():
                        for name in events[qi, number]:
                            acts[name]()

            return nothing

        lax.fori_loop(0, pairs, one_pair, 0)
        save = local(n + 9 + Y + qi, oT.at[:, qs], oT_out.at[:, qs])
        save.start()
        saves.append(save)
        for owner, keep, send in block_copies(qi):

            @pl.when(owner == c)
            def _():
                keep.start()

            @pl.when(owner != c)
            def _():
                send.start()

    for flow in flows[1:]:
        flow.arrive()
    for qi in range(nq):
        for owner, keep, send in block_copies(qi):

            @pl.when(owner == c)
            def _():
                keep.wait()

            @pl.when(owner != c)
            def _():
                send.wait_send()

            @pl.when(owner == c)
            def _():
                send.wait_recv()

    for what, src, dst in row_parts:
        leave_all(along_y(what, src, dst))
        to_sibling_own(what, src, dst).wait_send()
        leave_all(to_sibling(what, dst))
    for flow in flows:
        flow.leave()
    for copy in saves:
        copy.wait()


def forward(place, shards, tok, segments, present, vectors):
    n = len(shards) - 1
    Z, X, Y, C = place.Z, place.X, place.Y, place.C
    R, T, D = tok.shape
    L = Y * C * T
    H = D // C
    W3 = 3 * H
    BQ = 512
    pairs = H // 128
    inside = pl.BlockSpec(memory_space=pltpu.VMEM)
    anywhere = pl.BlockSpec(memory_space=pl.ANY)
    out_shape = [jax.ShapeDtypeStruct((Y, C, Z, X) + m.shape, bf16) for m in shards[1:]]
    out_shape += [
        jax.ShapeDtypeStruct((Y, T, D), bf16),
        jax.ShapeDtypeStruct((8, D), f32),
        jax.ShapeDtypeStruct((1, L), jnp.int32),
        jax.ShapeDtypeStruct((L, W3), bf16),
        jax.ShapeDtypeStruct((D, W3), bf16),
        jax.ShapeDtypeStruct((D, L), bf16),
        jax.ShapeDtypeStruct((Y * T, D), bf16),
        jax.ShapeDtypeStruct((H, L), f32),
        jax.ShapeDtypeStruct((pairs, 2, L), f32),
    ]
    each = 3 * (Z - 1) + 3 * (Y - 1) + 6
    copies = (n + 1) * each + 3 * (2 * (Y - 1) + 1) + ROW_PARTS * (Y - 1) + Y
    vec_shape = (16, vectors[0].shape[0])
    scratch = [
        pltpu.VMEM(vec_shape, bf16),
        pltpu.VMEM((Y, C, Z, X) + shards[0].shape, bf16),
        pltpu.VMEM((Y, C, T, D), bf16),
        pltpu.VMEM((Y, 8, T), jnp.int32),
        pltpu.VMEM((Y, C, 8, T), jnp.int32),
        pltpu.VMEM((Y, C) + vec_shape, bf16),
        pltpu.VMEM((L, D), bf16),
        pltpu.VMEM((D, L), bf16),
        pltpu.VMEM((D, W3), bf16),
        pltpu.VMEM((L, W3), bf16),
        pltpu.VMEM((H // HEAD_DIM, HEAD_DIM + 16, L), bf16),
        pltpu.VMEM((L, H), bf16),
        pltpu.VMEM((H, L), f32),
        pltpu.SemaphoreType.DMA((copies,)),
        pltpu.SemaphoreType.DMA((copies,)),
        pltpu.SemaphoreType.DMA((n + 9 + Y + L // BQ,)),
    ]
    return pl.pallas_call(
        functools.partial(forward_kernel, place, n, BQ),
        out_shape=out_shape,
        in_specs=[inside] * (n + 1) + [anywhere] + [inside] * 6,
        out_specs=[anywhere] * (n + 1) + [inside] * 2 + [anywhere] * 5 + [inside],
        scratch_shapes=scratch,
        compiler_params=pltpu.CompilerParams(
            collective_id=0, has_side_effects=True, vmem_limit_bytes=60 << 20
        ),
        name="forward",
    )(*shards, tok, segments, present, *vectors)


def sixths(rows, count):
    return rows if count == 6 else 0 if count == 0 else max(16, 16 * (rows * count // 96))


class Summing:
    def __init__(self, place, wire, name, spots, acc, xa, yb, ya, xb, zz):
        self.place, self.wire, self.name, self.spots = place, wire, name, spots
        self.acc, self.xa, self.yb, self.ya, self.xb, self.zz = acc, xa, yb, ya, xb, zz
        self.rows = acc.shape[3]
        self.h = xa.shape[2]

    def one(self):
        z, x, p, c = self.spots
        place, h, r = self.place, self.h, self.rows
        side = place.device(z, 1 - x, p, c)
        found = [
            self.wire.copy((self.name, "xa"), self.acc.at[:, :, 1 - x, 0:h], self.xa, side)
        ]
        for k in range(1, place.Y):
            to = (p + k) % place.Y
            found.append(
                self.wire.copy(
                    (self.name, "yb", k),
                    self.acc.at[to, :, :, h:r],
                    self.yb.at[k - 1],
                    place.device(z, x, to, c),
                )
            )
        return found

    def two(self):
        z, x, p, c = self.spots
        place, h, r = self.place, self.h, self.rows
        found = []
        for k in range(1, place.Y):
            to = (p + k) % place.Y
            found.append(
                self.wire.copy(
                    (self.name, "ya", k),
                    self.acc.at[to, :, x, 0:h],
                    self.ya.at[k - 1],
                    place.device(z, x, to, c),
                )
            )
        side = place.device(z, 1 - x, p, c)
        found.append(
            self.wire.copy((self.name, "xb"), self.acc.at[p, :, 1 - x, h:r], self.xb, side)
        )
        return found

    def three(self):
        z, x, p, c = self.spots
        place = self.place
        found = []
        for k in place.across_z():
            to = place.mirror(z, k)
            found.append(
                self.wire.copy(
                    (self.name, "z", k),
                    self.acc.at[p, to, x],
                    self.zz.at[k - 1],
                    place.device(to, x, p, c),
                )
            )
        return found

    def add_one(self):
        z, x, p, c = self.spots
        place, h, r, acc = self.place, self.h, self.rows, self.acc
        ones = self.one()
        ones[0].wait_recv()

        def low(i, nothing):
            a, b = i // place.Z, i % place.Z
            total = acc[a, b, x, 0:h].astype(f32) + self.xa[a, b].astype(f32)
            acc[a, b, x, 0:h] = total.astype(bf16)
            return nothing

        lax.fori_loop(0, place.Y * place.Z, low, 0)
        twos = self.two()
        start_all(twos[:-1])
        arrive_all(ones[1:])

        def high(i, nothing):
            a, b = i // place.X, i % place.X
            total = acc[p, a, b, h:r].astype(f32)
            for k in range(place.Y - 1):
                total = total + self.yb[k, a, b].astype(f32)
            acc[p, a, b, h:r] = total.astype(bf16)
            return nothing

        lax.fori_loop(0, place.Z * place.X, high, 0)
        twos[-1].start()

    def add_two(self):
        z, x, p, c = self.spots
        place, h, r, acc = self.place, self.h, self.rows, self.acc
        arrive_all(self.two())

        def both(i, nothing):
            total = acc[p, i, x, 0:h].astype(f32)
            for k in range(place.Y - 1):
                total = total + self.ya[k, i].astype(f32)
            acc[p, i, x, 0:h] = total.astype(bf16)
            total = acc[p, i, x, h:r].astype(f32) + self.xb[i].astype(f32)
            acc[p, i, x, h:r] = total.astype(bf16)
            return nothing

        lax.fori_loop(0, place.Z, both, 0)
        start_all(self.three())

    def finish(self, target):
        z, x, p, c = self.spots
        arrive_all(self.three())
        total = self.acc[p, z, x].astype(f32)
        for k in range(self.place.Z - 1):
            total = total + self.zz[k].astype(f32)
        target[...] = total

    def leave(self):
        leave_all(self.one())
        leave_all(self.two())
        leave_all(self.three())


class DepthSum:
    def __init__(self, place, wire, name, spots, acc, zr, xr, yr):
        self.place, self.wire, self.name, self.spots = place, wire, name, spots
        self.acc, self.zr, self.xr, self.yr = acc, zr, xr, yr

    def one(self):
        z, x, p, c = self.spots
        place = self.place
        return [
            self.wire.copy(
                (self.name, "z", k),
                self.acc.at[:, place.mirror(z, k)],
                self.zr.at[k - 1],
                place.device(place.mirror(z, k), x, p, c),
            )
            for k in place.across_z()
        ]

    def two(self):
        z, x, p, c = self.spots
        side = self.place.device(z, 1 - x, p, c)
        return [self.wire.copy((self.name, "x"), self.acc.at[:, z, 1 - x], self.xr, side)]

    def three(self):
        z, x, p, c = self.spots
        place = self.place
        return [
            self.wire.copy(
                (self.name, "y", k),
                self.acc.at[(p + k) % place.Y, z, x],
                self.yr.at[k - 1],
                place.device(z, x, (p + k) % place.Y, c),
            )
            for k in range(1, place.Y)
        ]

    def add_one(self):
        z, x, p, c = self.spots
        place, acc = self.place, self.acc
        arrive_all(self.one())

        def add(i, nothing):
            a, b = i // place.X, i % place.X
            total = acc[a, z, b].astype(f32)
            for k in range(place.Z - 1):
                total = total + self.zr[k, a, b].astype(f32)
            acc[a, z, b] = total.astype(bf16)
            return nothing

        lax.fori_loop(0, place.Y * place.X, add, 0)
        start_all(self.two())

    def add_two(self):
        z, x, p, c = self.spots
        place, acc = self.place, self.acc
        arrive_all(self.two())

        def add(i, nothing):
            total = acc[i, z, x].astype(f32) + self.xr[i].astype(f32)
            acc[i, z, x] = total.astype(bf16)
            return nothing

        lax.fori_loop(0, place.Y, add, 0)
        start_all(self.three())

    def finish(self, target):
        z, x, p, c = self.spots
        arrive_all(self.three())
        total = self.acc[p, z, x].astype(f32)
        for k in range(self.place.Y - 1):
            total = total + self.yr[k].astype(f32)
        target[...] = total

    def leave(self):
        leave_all(self.one())
        leave_all(self.two())
        leave_all(self.three())


class ChunkSum:
    def __init__(self, place, wire, name, spots, acc, xr, zr, total, far):
        self.place, self.wire, self.name, self.spots = place, wire, name, spots
        self.acc, self.xr, self.zr, self.total, self.far = acc, xr, zr, total, far

    def along_x(self):
        z, x, p, c = self.spots
        side = self.place.device(z, 1 - x, p, c)
        return [self.wire.copy((self.name, "x"), self.acc.at[:, 1 - x], self.xr, side)]

    def along_z(self):
        z, x, p, c = self.spots
        place = self.place
        return [
            self.wire.copy(
                (self.name, "z", k),
                self.acc.at[place.mirror(z, k), x],
                self.zr.at[k - 1],
                place.device(place.mirror(z, k), x, p, c),
            )
            for k in place.across_z()
        ]

    def along_y(self):
        z, x, p, c = self.spots
        place = self.place
        return [
            self.wire.copy(
                (self.name, "y", k),
                self.total.at[0],
                self.total.at[k],
                place.device(z, x, (p + k) % place.Y, c),
            )
            for k in range(1, place.Y)
        ]

    def to_core(self):
        z, x, p, c = self.spots
        return [
            self.wire.copy(
                (self.name, "core"), self.total, self.far, self.place.device(z, x, p, 1 - c)
            )
        ]

    def go_z(self):
        z, x, p, c = self.spots
        arrive_all(self.along_x())

        def one(i, nothing):
            total = self.acc[i, x].astype(f32) + self.xr[i].astype(f32)
            self.acc[i, x] = total.astype(bf16)
            return nothing

        lax.fori_loop(0, self.place.Z, one, 0)
        start_all(self.along_z())

    def go_y(self):
        z, x, p, c = self.spots
        arrive_all(self.along_z())
        total = self.acc[z, x].astype(f32)
        for k in range(self.place.Z - 1):
            total = total + self.zr[k].astype(f32)
        self.total[0] = total.astype(bf16)
        start_all(self.along_y())

    def go_core(self):
        arrive_all(self.along_y())
        start_all(self.to_core())

    def result(self):
        arrive_all(self.to_core())
        return [
            sum(part[k].astype(f32) for k in range(self.place.Y)) for part in (self.total, self.far)
        ]

    def leave(self):
        for copies in (self.along_x(), self.along_z(), self.along_y(), self.to_core()):
            leave_all(copies)


BACKWARD_PLAN = (
    "U0", "S00", "S01", "O0", "S02", "S03", "U1", "C0x", "S10", "D0", "U2", "S11", "S12",
    "C0z", "S13", "C1x", "S20", "B3", "D1", "S21", "C1z", "B2", "S22", "S23", "D2", "T3",
    "C2x", "B1", "C0y", "O1", "UF", "T2", "B0", "C1y", "T1", "C0c", "T0", "C2z", "C1c",
    "Vc", "Vx", "C2y", "Vz", "O2", "C0r", "Vy", "C1r", "DF", "C2c", "OF", "Vr", "C2r",
)


def backward_kernel(place, n, BQ, *refs):
    (begin, proj, grad_in, oT_in, lt, normedT, w_in, tok, gm, vec, vec_two) = refs[:11]
    parts, others = refs[11 : 11 + n], refs[11 + n : 11 + 2 * n]
    outs = refs[11 + 2 * n :]
    sums, (vec_out, tg_home) = outs[: n + 1], outs[n + 1 : n + 3]
    landing = outs[n + 3 : 2 * n + 3]
    rest = outs[2 * n + 3 :]
    (
        pv, do, oT, wv, kT, dk, dv, nT,
        keep, g_send, g_recv, tok_v, gm_v, grads, v0, v1, v2, v3, vc, vy, vx, vz, whole,
    ) = rest[:23]
    buffers = rest[23 : 23 + 6 * n - 2]
    chunk_buffers = rest[23 + 6 * n - 2 : -3]
    send_sem, recv_sem, local_sem = rest[-3:]
    tg_v = g_recv
    spots = place.here()
    z, x, p, c = spots
    Z, X, Y, C = place.Z, place.X, place.Y, place.C
    L, W3 = pv.shape
    H = W3 // 3
    D = wv.shape[0]
    T = L // (Y * C)
    pairs = H // 128
    nq = L // BQ
    scale = HEAD_DIM ** (-0.5) * LOG2E
    scale_back = HEAD_DIM ** (-0.5)
    wire = Wire(send_sem, recv_sem)
    sibling = place.device(z, x, p, 1 - c)
    beside = place.device(z, 1 - x, p, c)
    adds = [DepthSum(place, wire, 0, spots, *buffers[:4])]
    adds += [
        Summing(place, wire, m, spots, *buffers[6 * m - 2 : 6 * m + 4]) for m in range(1, n)
    ]
    chunks = [
        ChunkSum(place, wire, ("chunk", i), spots, *chunk_buffers[5 * i : 5 * i + 5])
        for i in range(pairs)
    ]

    def local(i, src, dst):
        return pltpu.make_async_copy(src, dst, local_sem.at[i])

    def lane(offset, size):
        return pl.ds(pl.multiple_of(offset, 128), size)

    def line(offset, size):
        return pl.ds(pl.multiple_of(offset, 16), size)

    def out_fetch(pair):
        return local(2, oT_in.at[line(pair * 128, 128), :], oT)

    loads = [local(0, proj, pv), local(1, grad_in, do)]
    columns = local(3, w_in, wv)
    late = local(4 + 2 * n, normedT, nT)
    columns_here = []
    halves = [
        (local(4 + m, parts[m], adds[m].acc), local(4 + n + m, others[m], landing[m]))
        for m in range(n)
    ]
    start_all(halves[1])
    start_all(loads)
    out_fetch(0).start()
    for m in (2, 0):
        start_all(halves[m])
    start_all([late, columns])
    greet(place, partners_of(place))
    row_sem = 5 + 2 * n

    def core_add(m):
        for copy in halves[m]:
            copy.wait()
        acc, other = adds[m].acc, landing[m]

        def one(i, nothing):
            a, b, d = i // (Z * X), (i // X) % Z, i % X
            total = acc[a, b, d].astype(f32) + other[a, b, d].astype(f32)
            acc[a, b, d] = total.astype(bf16)
            return nothing

        lax.fori_loop(0, Y * Z * X, one, 0)

    for copy in loads:
        copy.wait()
    kT[...] = pv[:, H : 2 * H].T
    grads[...] = jnp.zeros_like(grads)

    U = BQ // T
    gain = vec[0:1, :]

    def sub_blocks(qi):
        found = []
        for u in range(U):
            block = qi * U + u
            found.append((u, block // C, block % C))
        return found

    reserved = send_sem.shape[0] - 3 * Y

    def g_wire(q):
        return pltpu.make_async_remote_copy(
            src_ref=g_send.at[q],
            dst_ref=g_recv.at[q],
            send_sem=send_sem.at[reserved + q],
            recv_sem=recv_sem.at[reserved + q],
            device_id=sibling,
            device_id_type=MESH,
        )

    def home_from(k):
        q = (p + k) % Y
        return pltpu.make_async_remote_copy(
            src_ref=tg_v.at[p],
            dst_ref=tg_home.at[q],
            send_sem=send_sem.at[reserved + Y + q],
            recv_sem=recv_sem.at[reserved + 2 * Y + q],
            device_id=place.device(z, x, q, c),
            device_id_type=MESH,
        )

    def home_to(q):
        return pltpu.make_async_remote_copy(
            src_ref=tg_v.at[q],
            dst_ref=tg_home.at[p],
            send_sem=send_sem.at[reserved + Y + q],
            recv_sem=recv_sem.at[reserved + 2 * Y + p],
            device_id=place.device(z, x, q, c),
            device_id_type=MESH,
        )

    def block_done(qi):
        if not columns_here:
            columns.wait()
            columns_here.append(True)
        g = dot(pv[line(qi * BQ, BQ), :], wv[...], 1, 1)
        for u, q, owner in sub_blocks(qi):
            rows = slice(u * T, (u + 1) * T)

            @pl.when(owner == c)
            def _():
                keep[(qi % 2 * U + u) // C] = g[rows, :]

            @pl.when(owner != c)
            def _():
                g_send[q] = g[rows, :].astype(bf16)
                g_wire(q).start()

    def pair_done(i):
        if i == 0:
            late.wait()
        wide = [pv[:, t * H + i * 128 : t * H + (i + 1) * 128] for t in range(3)]
        value = dot(nT[...], jnp.concatenate(wide, axis=1), 1, 0).astype(bf16)
        chunk = chunks[i]
        r = chunk.acc.shape[2]
        for b in range(Z * X):
            chunk.acc[b // X, b % X] = value[b * r : (b + 1) * r, :]
        start_all(chunk.along_x())

    def token_rows(qi):
        for u, q, owner in sub_blocks(qi):

            @pl.when(owner == c)
            def _():
                a = local(row_sem, tok.at[line(q * T, T)], tok_v)
                b = local(row_sem + 1, gm.at[line(q * T, T)], gm_v)
                a.start()
                b.start()
                g_wire(q).wait_recv()
                grad = keep[(qi % 2 * U + u) // C] + g_recv[q].astype(f32)
                a.wait()
                unit, factor = normed(tok_v[...].astype(f32))
                grads[0:1, :] += jnp.sum(grad * unit, axis=0, keepdims=True)
                grads[1:2, :] += jnp.sum(grad, axis=0, keepdims=True)
                b.wait()
                tg_v[q] = (gm_v[...] + norm_back(grad, gain, unit, factor)).astype(bf16)

                @pl.when(q == p)
                def _():
                    local(row_sem + 2, tg_v.at[q], tg_home.at[p]).start()

                @pl.when(q != p)
                def _():
                    home_to(q).start()

    def one_query(pair, qi):
        d0 = qi * BQ
        qs = slice(d0, d0 + BQ)
        cols = lane(pair * 128, 128)
        k_cols, v_cols = lane(H + pair * 128, 128), lane(2 * H + pair * 128, 128)
        q_val, do_val = pv[qs, cols], do[qs, cols]
        qT, doT = q_val.T, do_val.T
        part = BQ // 2
        cuts = []
        if d0 and qi < nq - 1:
            cuts = [(0, part, 1, 0), (part, min(BQ, d0), 0, 0)]
            cuts += [(a, a + BQ, 0, 0) for a in range(BQ, d0, BQ)]
        elif d0:
            cuts = [(a, a + BQ, 1, 0) for a in range(0, d0, BQ)]
        cuts += [(d0, d0 + part, 2, 0), (d0 + part, d0 + BQ, 2, part)]
        dqs = []
        for h in range(2):
            rows = slice(h * HEAD_DIM, (h + 1) * HEAD_DIM)
            kT_rows = pl.ds(pl.multiple_of(pair * 128 + h * HEAD_DIM, HEAD_DIM), HEAD_DIM)
            query, grad = head_masked(qT, h, 0), head_masked(doT, h, 0)
            q_nat, do_nat = head_masked(q_val, h, 1), head_masked(do_val, h, 1)
            delta = jnp.sum(doT[rows, :].astype(f32) * oT[rows, qs], axis=0, keepdims=True)
            log_total = lt[pair, h : h + 1, qs]
            dq = jnp.zeros((HEAD_DIM, BQ), f32)
            for a, b, mode, qa in cuts:
                sc = dot(pv[a:b, k_cols], query[:, qa:], 1, 0) * scale
                prob = jnp.exp2(sc - log_total[:, qa:])
                if mode:
                    shape = (b - a, BQ - qa)
                    key_pos = lax.broadcasted_iota(jnp.int32, shape, 0) + a
                    visible = key_pos >= begin[:, d0 + qa : d0 + BQ]
                    if mode == 2:
                        query_pos = lax.broadcasted_iota(jnp.int32, shape, 1) + d0 + qa
                        visible = jnp.logical_and(visible, key_pos <= query_pos)
                    prob = jnp.where(visible, prob, 0.0)
                dp = dot(pv[a:b, v_cols], grad[:, qa:], 1, 0)
                ds = (prob * (dp - delta[:, qa:])).astype(bf16)
                dv[a:b, :] += dot(prob.astype(bf16), do_nat[qa:], 1, 0)
                dk[a:b, :] += dot(ds, q_nat[qa:], 1, 0)
                more = dot(kT[kT_rows, a:b], ds, 1, 0)
                if qa:
                    more = jnp.concatenate([jnp.zeros((HEAD_DIM, qa), f32), more], axis=1)
                dq = dq + more
            dqs.append(dq)
        pv[qs, cols] = (jnp.concatenate(dqs, axis=0) * scale_back).astype(bf16).T
        pv[qs, k_cols] = (dk[qs, :] * scale_back).astype(bf16)
        pv[qs, v_cols] = dv[qs, :].astype(bf16)

    out_m, up_m, down_m = adds
    v_core = wire.copy("vc", v0, vc, sibling)
    v_x = wire.copy("vx", v1, vx, beside)
    v_z = [
        wire.copy(("vz", k), v2, vz.at[k - 1], place.device(place.mirror(z, k), x, p, c))
        for k in place.across_z()
    ]
    v_y = [
        wire.copy(("vy", k), v3, vy.at[k - 1], place.device(z, x, (p + k) % Y, c))
        for k in range(1, Y)
    ]

    def vector_core():
        grads[2:4, :] = vec_two[...]
        v0[0:4, :] = grads[0:4, 0:H]
        v0[4:8, :] = grads[0:4, H:]
        v_core.start()

    def vector_x():
        v_core.wait_recv()
        v1[...] = v0[...] + vc[...]
        v_x.start()

    def vector_z():
        v_x.wait_recv()
        v2[...] = v1[...] + vx[...]
        start_all(v_z)

    def vector_y():
        arrive_all(v_z)
        v3[...] = v2[...] + sum(vz[k] for k in range(Z - 1))
        start_all(v_y)

    def vector_end():
        arrive_all(v_y)
        vec_out[...] = v3[...] + sum(vy[k] for k in range(Y - 1))

    def chunk_end(i):
        mine, far = chunks[i].result()
        for half in range(C):

            @pl.when(c == half)
            def _():
                for value, core in ((mine, half), (far, 1 - half)):
                    for t in range(3):
                        lo = t * D + core * H + i * 128
                        whole[:, lo : lo + 128] = value[:, t * 128 : (t + 1) * 128]

    def out_start():
        core_add(0)
        start_all(out_m.one())

    def up_start():
        core_add(1)
        start_all(up_m.one())

    def down_start():
        core_add(2)
        start_all(down_m.one())

    acts = {
        "U0": up_start,
        "U1": up_m.add_one,
        "U2": up_m.add_two,
        "UF": lambda: up_m.finish(sums[2]),
        "D0": down_start,
        "D1": down_m.add_one,
        "D2": down_m.add_two,
        "DF": lambda: down_m.finish(sums[3]),
        "O0": out_start,
        "O1": out_m.add_one,
        "O2": out_m.add_two,
        "OF": lambda: out_m.finish(sums[1]),
        "Vc": vector_core,
        "Vx": vector_x,
        "Vz": vector_z,
        "Vy": vector_y,
        "Vr": vector_end,
    }
    for i, chunk in enumerate(chunks):
        acts[f"C{i}x"] = functools.partial(pair_done, i)
        acts[f"C{i}z"] = chunk.go_z
        acts[f"C{i}y"] = chunk.go_y
        acts[f"C{i}c"] = chunk.go_core
        acts[f"C{i}r"] = functools.partial(chunk_end, i)
    for qi in range(nq):
        acts[f"B{qi}"] = functools.partial(block_done, qi)
        acts[f"T{qi}"] = functools.partial(token_rows, qi)
    events, spot = {}, None
    for name in BACKWARD_PLAN:
        if name[0] == "S":
            spot = (int(name[1]), int(name[2]))
        else:
            events.setdefault(spot, []).append(name)

    def one_pair(pair, nothing):
        out_fetch(pair).wait()
        dk[...] = jnp.zeros_like(dk)
        dv[...] = jnp.zeros_like(dv)
        for i in range(nq):
            one_query(pair, nq - 1 - i)
            if i == nq - 1:

                @pl.when(pair < pairs - 1)
                def _():
                    out_fetch(pair + 1).start()

            for number in range(pairs):
                if (number, i) in events and (number, i) != (pairs - 1, nq - 1):

                    @pl.when(pair == number)
                    def _():
                        for name in events[number, i]:
                            acts[name]()

        return nothing

    for name in events.get(None, ()):
        acts[name]()
    lax.fori_loop(0, pairs, one_pair, 0)
    for name in events[pairs - 1, nq - 1]:
        acts[name]()
    w = sums[0].shape[1]
    for d in range(Y * C):

        @pl.when(p * C + c == d)
        def _():
            sums[0][...] = whole[:, d * w : (d + 1) * w]

    for k in range(1, Y):
        home_from(k).wait_recv()
        home_to((p + k) % Y).wait_send()
    local(row_sem + 2, tg_v.at[p], tg_home.at[p]).wait()
    for q in range(Y):
        g_wire(q).wait_send()
    v_core.wait_send()
    leave_all(v_y)
    v_x.wait_send()
    leave_all(v_z)
    for summing in adds + chunks:
        summing.leave()


def backward(place, parts, others, proj_shape, begin, proj, heads, oT, lt, normedT, w_own, tok, gm, vec, vec_two):
    n = len(parts)
    Z, X, Y, C = place.Z, place.X, place.Y, place.C
    L, W3 = proj.shape
    H = W3 // 3
    D = w_own.shape[0]
    T = L // (Y * C)
    BQ = 512
    inside = pl.BlockSpec(memory_space=pltpu.VMEM)
    anywhere = pl.BlockSpec(memory_space=pl.ANY)
    shapes = [proj_shape] + [part.shape[3:] for part in parts]
    sixths = [3, 3]
    out_shape = [jax.ShapeDtypeStruct(shape, f32) for shape in shapes]
    out_shape += [
        jax.ShapeDtypeStruct((8, H), f32),
        jax.ShapeDtypeStruct((Y, T, D), bf16),
    ]
    scratch = [pltpu.VMEM((Y, Z, X) + shape, bf16) for shape in shapes[1:]]
    scratch += [
        pltpu.VMEM((L, W3), bf16),
        pltpu.VMEM((L, H), bf16),
        pltpu.VMEM((128, L), f32),
        pltpu.VMEM((D, W3), bf16),
        pltpu.VMEM((H, L), bf16),
        pltpu.VMEM((L, 128), f32),
        pltpu.VMEM((L, 128), f32),
        pltpu.VMEM((D, L), bf16),
        pltpu.VMEM((max(1, 2 * (BQ // T) // C), T, D), f32),
        pltpu.VMEM((Y, T, D), bf16),
        pltpu.VMEM((Y, T, D), bf16),
        pltpu.VMEM((T, D), bf16),
        pltpu.VMEM((T, D), f32),
    ]
    scratch += [pltpu.VMEM((8, D), f32)] + [pltpu.VMEM((8, H), f32)] * 5
    scratch += [
        pltpu.VMEM((Y - 1, 8, H), f32),
        pltpu.VMEM((8, H), f32),
        pltpu.VMEM((Z - 1, 8, H), f32),
        pltpu.VMEM((proj_shape[0], 3 * D), f32),
    ]
    r, w = shapes[1]
    scratch += [
        pltpu.VMEM((Y, Z, X, r, w), bf16),
        pltpu.VMEM((Z - 1, Y, X, r, w), bf16),
        pltpu.VMEM((Y, r, w), bf16),
        pltpu.VMEM((Y - 1, r, w), bf16),
    ]
    for shape, part in zip(shapes[2:], sixths):
        r, w = shape
        h = first_rows(r, part)
        scratch += [
            pltpu.VMEM((Y, Z, X, r, w), bf16),
            pltpu.VMEM((Y, Z, h, w), bf16),
            pltpu.VMEM((Y - 1, Z, X, r - h, w), bf16),
            pltpu.VMEM((Y - 1, Z, h, w), bf16),
            pltpu.VMEM((Z, r - h, w), bf16),
            pltpu.VMEM((Z - 1, r, w), bf16),
        ]
    r = proj_shape[0]
    for pair in range(H // 128):
        scratch += [
            pltpu.VMEM((Z, X, r, 384), bf16),
            pltpu.VMEM((Z, r, 384), bf16),
            pltpu.VMEM((Z - 1, r, 384), bf16),
            pltpu.VMEM((Y, r, 384), bf16),
            pltpu.VMEM((Y, r, 384), bf16),
        ]
    each = 1 + (Y - 1) + (Y - 1) + 1 + (Z - 1)
    chunk_copies = 1 + (Z - 1) + (Y - 1) + 1
    copies = n * each + (H // 128) * chunk_copies + 2 + (Y - 1) + 1 + (Z - 1) + 3 * Y
    scratch += [
        pltpu.SemaphoreType.DMA((copies,)),
        pltpu.SemaphoreType.DMA((copies,)),
        pltpu.SemaphoreType.DMA((5 + 2 * n + 3,)),
    ]
    return pl.pallas_call(
        functools.partial(backward_kernel, place, n, BQ),
        out_shape=out_shape,
        in_specs=[inside] + [anywhere] * 3 + [inside] + [anywhere] * 4 + [inside] * 2 + [anywhere] * (2 * n),
        out_specs=[inside] * (n + 2) + [anywhere],
        scratch_shapes=scratch,
        compiler_params=pltpu.CompilerParams(
            collective_id=1, has_side_effects=True, vmem_limit_bytes=63 << 20
        ),
        name="backward",
    )(begin, proj, heads, oT, lt, normedT, w_own, tok, gm, vec, vec_two, *parts, *others)


def gelu_both(u):
    k = 0.7978845608028654
    square = u * u
    t = jnp.tanh(k * u * (1.0 + 0.044715 * square))
    half = 0.5 * (1.0 + t)
    slope = half + 0.5 * k * u * (1.0 - t * t) * (1.0 + 3 * 0.044715 * square)
    return u * half, slope


class Task:
    def __init__(self, copy, far):
        self.copy, self.far, self.left, self.here = copy, far, False, False
        copy.start()

    def gone(self):
        if not self.left:
            if self.far:
                self.copy.wait_send()
            else:
                self.copy.wait()
            self.left = True

    def came(self):
        if self.far and not self.here:
            self.copy.wait_recv()
            self.here = True


def dense_kernel(
    place, aligned, att, tok, cot, out_w, up_w, down_w, vec,
    home, gm_out, heads, up_own, down_own, out_own, up_other, down_other, out_other, vec_out,
    att_v, tok_v, cot_v, out_v, up_v, down_v, out_full, mid, n2, act, gh, n2T, cotT, oacc, g2,
    h_buf, g_buf, stage, up_cut, down_cut, load_sem, store_sem, send_sem, recv_sem,
):
    S, nb, Y, C = place.blk, place.batch, place.Y, place.C
    z, x, p, c = place.here()
    M, D = att_v.shape
    J = up_v.shape[1] // D
    T = M // Y
    H = D // C
    half = M // 2
    sibling = place.device(z, x, p, 1 - c)
    others = [place.device(z, x, (p + k) % Y, c) for k in range(1, Y)]
    wire = Wire(send_sem, recv_sem)
    loads, tasks = [], []

    def line(offset, size):
        return pl.ds(pl.multiple_of(offset, 16), size)

    def lane(offset, size):
        return pl.ds(pl.multiple_of(offset, 128), size)

    def load(src, dst):
        task = Task(pltpu.make_async_copy(src, dst, load_sem.at[len(loads)]), False)
        loads.append(task)
        return task

    def store(src, dst):
        count = sum(not task.far for task in tasks)
        tasks.append(Task(pltpu.make_async_copy(src, dst, store_sem.at[count]), False))
        return tasks[-1]

    def send(name, src, dst, device):
        tasks.append(Task(wire.copy(name, src, dst, device), True))
        return tasks[-1]

    per_half = half // T
    near = p // per_half
    halves = [1 - near, near]
    rows_of = [slice(0, half), slice(half, M)]

    def spot_of(q, chip):
        apart = q // per_half - chip // per_half
        return (1 - apart * apart) * half + q % per_half * T

    w_up = up_own.shape[2]
    in_chunk = D // w_up
    chunks = []
    for s in range(J):
        if in_chunk == 1:
            chunks.append((s // C) * C + (1 - c if s % C == 0 else c))
        else:
            chunks.append(s)

    first = [load(out_w, out_v)]
    for t in (0, 1):
        there = line(halves[t] * half, half)
        first += [load(att.at[there], att_v.at[rows_of[t]]), load(tok.at[there], tok_v.at[rows_of[t]])]
    first.append(load(cot.at[p], cot_v.at[line(spot_of(p, p), T), :]))
    if aligned:
        weights = []
        r, w = down_w.shape[2:]
        for s in range(J):
            for i in range(in_chunk):
                at = s * D + i * w_up
                weights.append(load(up_w.at[chunks[s] * in_chunk + i], up_v.at[:, at : at + w_up]))
            for i in range(D // w):
                at = s * D + i * w
                weights += [
                    load(
                        down_w.at[d, chunks[s] * (D // w) + i],
                        down_v.at[d * r : (d + 1) * r, at : at + w],
                    )
                    for d in range(S)
                ]
    else:
        weights = [load(up_w, up_v), load(down_w, down_v)]
    greet(place, others + [sibling])
    cots = []
    for k in range(1, Y):
        to = (p + k) % Y
        dst = cot_v.at[line(spot_of(p, to), T), :]
        cots.append(send(("cot", k), cot.at[to], dst, others[k - 1]))
    for task in first:
        task.gone()
    w = out_v.shape[2]
    for d in range(S):
        out_full[:, d * w : (d + 1) * w] = out_v[d]
    gain, shift = vec[2:3, :], vec[3:4, :]
    for t in (0, 1):
        ts = rows_of[t]
        middle = tok_v[ts, :].astype(f32) + dot(att_v[ts, :], out_full[...], 1, 0)
        unit, factor = normed(middle)
        mid[ts, :] = middle
        low = (unit * gain + shift).astype(bf16)
        n2[ts, :] = low
        n2T[:, ts] = low.T
    for task in weights:
        task.gone()
    def cols(s):
        return slice(s * D, (s + 1) * D)

    busy = {}

    def staged(key, value, width, cut):
        for task in busy.get(key, []):
            task.gone()
        busy[key] = []
        if cut is not None:
            for i in range(value.shape[1] // width):
                cut[i] = value[:, i * width : (i + 1) * width]
            return lambda rows, i: cut.at[i, rows, :]
        stage[key] = value
        if value.shape[1] == width:
            return lambda rows, i: stage.at[key, rows, :]
        return lambda rows, i: stage.at[key, rows, i * width : (i + 1) * width]

    def up_gradient(s):
        value = dot(n2T[...], gh[:, cols(s)], 1, 0).astype(bf16)
        piece = staged(0, value, w_up, None if aligned else up_cut)
        every = slice(0, D)
        if in_chunk == 1:
            q = s // C
            if s % C == 0:
                busy[0].append(send(("up", s), piece(every, 0), up_other.at[q], sibling))
            else:
                busy[0].append(store(piece(every, 0), up_own.at[q]))
            return
        for i in range(in_chunk // C):
            q = s * in_chunk // C + i
            busy[0].append(store(piece(every, C * i + c), up_own.at[q]))
            busy[0].append(send(("up", q), piece(every, C * i + 1 - c), up_other.at[q], sibling))

    def down_gradient(s):
        value = dot(cotT[...], act[:, cols(s)], 1, 0).astype(bf16)
        r, w = down_own.shape[2:]
        piece = staged(1, value, w, None if aligned else down_cut)
        for q in range(Y):
            for i in range(D // w):
                b = chunks[s] * (D // w) + i
                busy[1].append(store(piece(line((C * q + c) * r, r), i), down_own.at[q, b]))
                busy[1].append(
                    send(
                        ("down", s, q, i),
                        piece(line((C * q + 1 - c) * r, r), i),
                        down_other.at[q, b],
                        sibling,
                    )
                )

    units = [(0, "f", s) for s in range(J)] + [(1, "fb", s) for s in range(J)]
    units += [(0, "b", s) for s in range(J)]

    W = D

    def part_of(s, i):
        return slice(s * D + i * W, s * D + (i + 1) * W)

    def enter(number, i):
        t, kind, s = units[number]
        mine = slice(i * W, (i + 1) * W)
        if "f" in kind:
            h_buf[number % 2, :, mine] = dot(n2[rows_of[t], :], up_v[:, part_of(s, i)], 1, 0)
        if "b" in kind:
            g_buf[number % 2, :, mine] = dot(cot_v[rows_of[t], :], down_v[:, part_of(s, i)], 1, 0)

    def activate(number, i):
        t, kind, s = units[number]
        ts, mine, place_here = rows_of[t], slice(i * W, (i + 1) * W), part_of(s, i)
        if "f" in kind:
            a, slope = gelu_both(h_buf[number % 2, :, mine])
            act[ts, place_here] = a.astype(bf16)
            if kind == "f":
                gh[ts, place_here] = slope.astype(bf16)
        else:
            slope = gh[ts, place_here].astype(f32)
        if "b" in kind:
            gh[ts, place_here] = (g_buf[number % 2, :, mine] * slope).astype(bf16)

    def leave(number, i):
        t, kind, s = units[number]
        ts, mine = rows_of[t], slice(i * W, (i + 1) * W)
        wanted = []
        if "f" in kind:
            wanted.append((oacc, act, down_v))
        if "b" in kind:
            wanted.append((g2, gh, up_v))
        for total, left, right in wanted:
            more = dot(left[ts, cols(s)], right[mine, cols(s)], 1, 1)
            if s == 0:
                total[:, mine] = more
            else:
                total[:, mine] += more

    def output_rows(t):
        ts = rows_of[t]
        tok_v[ts, :] = (mid[ts, :] + oacc[...]).astype(bf16)
        if Y == 2 and t == 1:
            store(tok_v.at[ts, :], home.at[near])
        elif Y == 2:
            send("home", tok_v.at[ts, :], home.at[p], others[0])

    sums = [jnp.zeros((1, D), f32), jnp.zeros((1, D), f32)]

    def norm_rows(t):
        ts = rows_of[t]
        unit, factor = normed(mid[ts, :])
        grad = g2[...]
        sums[0] = sums[0] + jnp.sum(grad * unit, axis=0, keepdims=True)
        sums[1] = sums[1] + jnp.sum(grad, axis=0, keepdims=True)
        gm = cot_v[ts, :].astype(f32) + norm_back(grad, gain, unit, factor)
        mid[ts, :] = gm
        low = gm.astype(bf16)
        n2[ts, :] = low
        cot_v[ts, :] = dot(low, out_full[...], 1, 1).astype(bf16)
        store(mid.at[ts, :], gm_out.at[line(halves[t] * half, half), :])
        for i in range(per_half):
            q = halves[t] * per_half + i
            rows = slice(t * half + i * T, t * half + (i + 1) * T)
            spot = line((C * q + c) * T, T)
            store(cot_v.at[rows, lane(c * H, H)], heads.at[spot, :])
            send(("ga", t, i), cot_v.at[rows, lane((1 - c) * H, H)], heads.at[spot, :], sibling)

    count = len(units)
    for number in range(count + 2):
        if number < count:
            t, kind, s = units[number]
            if units[number] == ((0, "b", 0) if Y == 2 else (1, "fb", 0)):
                for task in cots:
                    task.came()
        for i in range(D // W):
            if number < count:
                enter(number, i)
            if 0 <= number - 1 < count:
                activate(number - 1, i)
            if 0 <= number - 2:
                leave(number - 2, i)
        if number < 2:
            continue
        t, kind, s = units[number - 2]
        if s == J - 1:
            if kind == "f":
                output_rows(t)
            elif kind == "fb":
                output_rows(t)
                cotT[:, rows_of[t]] = cot_v[rows_of[t], :].T
                norm_rows(t)
                cotT[:, rows_of[0]] = cot_v[rows_of[0], :].T
            else:
                norm_rows(t)
        if kind == "b":
            up_gradient(s)
            down_gradient(s)
    if Y > 2:
        store(tok_v.at[line(spot_of(p, p), T), :], home.at[p])
        for k in range(1, Y):
            to = (p + k) % Y
            send(("home", k), tok_v.at[line(spot_of(to, p), T), :], home.at[p], others[k - 1])
    vec_out[0:1, :] = sums[0]
    vec_out[1:2, :] = sums[1]
    value = dot(att_v[...], n2[...], 0, 0).astype(bf16)
    w = out_own.shape[2]
    for d in range(S):
        out_v[d] = value[:, d * w : (d + 1) * w]
    for q in range(Y):
        store(out_v.at[C * q + c], out_own.at[q])
        send(("out", q), out_v.at[C * q + 1 - c], out_other.at[q], sibling)
    for task in tasks:
        task.came()
    for task in tasks:
        task.gone()


def dense(place, att, tok, cot, out_g, up_g, down_g, vec):
    M, D = att.shape
    S, nb, Y, C = place.blk, place.batch, place.Y, place.C
    T = M // Y
    H = D // C
    aligned = up_g.shape[-1] % 128 == 0 and down_g.shape[-1] % 128 == 0
    out_w = out_g.reshape(S, D, -1)
    FF = S * up_g.shape[-1]
    if aligned:
        up_w = up_g.reshape(S, D, -1)
        down_w = down_g.reshape((S, nb) + down_g.shape[-2:])
    else:
        up_w, down_w = joined(up_g, 0), joined(down_g, 1)
    anywhere = pl.BlockSpec(memory_space=pl.ANY)
    inside = pl.BlockSpec(memory_space=pltpu.VMEM)
    pieces = [
        jax.ShapeDtypeStruct((Y, D, up_g.shape[-1]), bf16),
        jax.ShapeDtypeStruct((Y, nb) + down_g.shape[-2:], bf16),
        jax.ShapeDtypeStruct((Y, D, out_g.shape[-1]), bf16),
    ]
    none = (1, 16, 128)
    up_cut = none if aligned else (D // up_g.shape[-1], D, up_g.shape[-1])
    down_cut = none if aligned else (D // down_g.shape[-1], D, down_g.shape[-1])
    loads = 8 + S + S * nb
    J = FF // D
    down_count = J * Y * (D // down_g.shape[-1])
    copies = 2 * (Y - 1) + 2 * Y + S + down_count + 4 * Y + 8
    results = pl.pallas_call(
        functools.partial(dense_kernel, place, aligned),
        out_shape=[
            jax.ShapeDtypeStruct((Y, T, D), bf16),
            jax.ShapeDtypeStruct((M, D), f32),
            jax.ShapeDtypeStruct((S * T, H), bf16),
        ]
        + pieces
        + pieces
        + [jax.ShapeDtypeStruct((2, D), f32)],
        in_specs=[anywhere] * 6 + [inside],
        out_specs=[anywhere] * 9 + [inside],
        scratch_shapes=[
            pltpu.VMEM((M, D), bf16),
            pltpu.VMEM((M, D), bf16),
            pltpu.VMEM((M, D), bf16),
            pltpu.VMEM(out_w.shape, bf16),
            pltpu.VMEM((D, FF), bf16),
            pltpu.VMEM((D, FF), bf16),
            pltpu.VMEM((D, D), bf16),
            pltpu.VMEM((M, D), f32),
            pltpu.VMEM((M, D), bf16),
            pltpu.VMEM((M, FF), bf16),
            pltpu.VMEM((M, FF), bf16),
            pltpu.VMEM((D, M), bf16),
            pltpu.VMEM((D, M), bf16),
            pltpu.VMEM((M // 2, D), f32),
            pltpu.VMEM((M // 2, D), f32),
            pltpu.VMEM((2, M // 2, D), f32),
            pltpu.VMEM((2, M // 2, D), f32),
            pltpu.VMEM((2, D, D), bf16) if aligned else pltpu.VMEM((1, 16, 128), bf16),
            pltpu.VMEM(up_cut, bf16),
            pltpu.VMEM(down_cut, bf16),
            pltpu.SemaphoreType.DMA((loads,)),
            pltpu.SemaphoreType.DMA((copies,)),
            pltpu.SemaphoreType.DMA((copies,)),
            pltpu.SemaphoreType.DMA((copies,)),
        ],
        compiler_params=pltpu.CompilerParams(
            collective_id=2, has_side_effects=True, vmem_limit_bytes=62 << 20
        ),
        name="dense",
    )(att, tok, cot, out_w, up_w, down_w, vec)
    home, gm, heads = results[:3]
    shapes = [(Y,) + up_g.shape[2:], (Y,) + down_g.shape[2:], (Y,) + out_g.shape[2:]]
    own = [value.reshape(shape) for value, shape in zip(results[3:6], shapes)]
    other = [value.reshape(shape) for value, shape in zip(results[6:9], shapes)]
    return home, gm, heads, own, other, results[9]


def hand_over_kernel(place, n, *refs):
    given, vec, out, vec_out = refs[:n], refs[n], refs[n + 1 : 2 * n + 1], refs[2 * n + 1 : 2 * n + 5]
    whole, between, sem = refs[2 * n + 5], refs[2 * n + 6 : 3 * n + 6], refs[3 * n + 6]
    pieces = []
    for i in range(n):
        if len(given[i].shape) == 3:
            R, T, _ = given[i].shape
            cut = [(r, slice(h * T // 2, (h + 1) * T // 2)) for r in range(R) for h in range(2)]
        else:
            cut = [slice(None)]
        pieces += [(given[i].at[k], between[i].at[k], out[i].at[k]) for k in cut]
    here = [
        pltpu.make_async_copy(src, mid, sem.at[0, j]) for j, (src, mid, dst) in enumerate(pieces)
    ]
    away = [
        pltpu.make_async_copy(mid, dst, sem.at[1, j]) for j, (src, mid, dst) in enumerate(pieces)
    ]
    start_all(here)
    H = vec.shape[1]
    whole[0:4, 0:H] = vec[0:4, :]
    whole[0:4, H:] = vec[4:8, :]
    me = lax.axis_index("blk")
    w = vec_out[0].shape[1]
    for d in range(place.blk):

        @pl.when(me == d)
        def _():
            for i in range(4):
                vec_out[i][...] = whole[i : i + 1, d * w : (d + 1) * w]

    for come, go in zip(here, away):
        come.wait()
        go.start()
    for copy in away:
        copy.wait()


def hand_over(place, given, vec):
    n = len(given)
    anywhere = pl.BlockSpec(memory_space=pl.ANY)
    inside = pl.BlockSpec(memory_space=pltpu.VMEM)
    H = vec.shape[1]
    count = sum(2 * v.shape[0] if len(v.shape) == 3 else 1 for v in given)
    return pl.pallas_call(
        functools.partial(hand_over_kernel, place, n),
        out_shape=[jax.ShapeDtypeStruct(v.shape, v.dtype) for v in given]
        + [jax.ShapeDtypeStruct((1, 2 * H // place.blk), f32)] * 4,
        in_specs=[anywhere] * n + [inside],
        out_specs=[anywhere] * n + [inside] * 4,
        scratch_shapes=[pltpu.VMEM((8, 2 * H), f32)]
        + [pltpu.VMEM(v.shape, v.dtype) for v in given]
        + [pltpu.SemaphoreType.DMA((2, count))],
        compiler_params=pltpu.CompilerParams(vmem_limit_bytes=62 << 20),
        name="hand_over",
    )(*given, vec)


def normed(values):
    average = jnp.mean(values, axis=-1, keepdims=True)
    centered = values - average
    variance = jnp.mean(centered * centered, axis=-1, keepdims=True)
    factor = lax.rsqrt(variance + epsilon)
    return centered * factor, factor


def norm_back(grad, gain, unit, factor):
    e = grad * gain
    return factor * (
        e - jnp.mean(e, axis=-1, keepdims=True) - unit * jnp.mean(e * unit, axis=-1, keepdims=True)
    )


def joined(gathered, axis):
    Y, C, Z, X, r, w = gathered.shape
    if axis == 0:
        return gathered.reshape(Y * C, Z * X * r, w).transpose(1, 0, 2).reshape(Z * X * r, -1)
    return gathered.reshape(Y * C, Z * X, r, w).transpose(0, 2, 1, 3).reshape(Y * C * r, -1)


def parted(whole, place, axis):
    Y, C, Z, X = place.Y, place.C, place.Z, place.X
    rows, columns = whole.shape
    if axis == 0:
        value = whole.reshape(Z * X, rows // (Z * X), Y * C, columns // (Y * C))
        value = value.transpose(2, 0, 1, 3)
    else:
        value = whole.reshape(Y * C, rows // (Y * C), Z * X, columns // (Z * X))
        value = value.transpose(0, 2, 1, 3)
    return value.reshape((Y, C, Z, X) + value.shape[2:])


def body(
    place,
    tokens,
    proj_weight,
    out_weight,
    up_weight,
    down_weight,
    gain_one,
    bias_one,
    gain_two,
    bias_two,
    segments,
    present,
    cotangent,
):
    rows, block, width = tokens.shape
    Y = place.Y
    (
        out_g, up_g, down_g, tok_mine, vec, begin, projected, proj_own, normed_t,
        attended_low, attended_t, log_total,
    ) = forward(
        place,
        [proj_weight, out_weight, up_weight, down_weight.T],
        tokens,
        segments,
        present,
        (gain_one, bias_one, gain_two, bias_two),
    )
    tok_mine = tok_mine.reshape(Y * block, width)
    output, grad_middle, grad_heads, own, other, vec_two = dense(
        place, attended_low, tok_mine, cotangent, out_g, up_g, down_g, vec
    )
    order = (2, 0, 1)
    proj_sum, out_sum, up_sum, down_sum, vec_sum, token_grad = backward(
        place,
        [own[i] for i in order],
        [other[i] for i in order],
        proj_weight.shape,
        begin,
        projected,
        grad_heads,
        attended_t,
        log_total,
        normed_t,
        proj_own,
        tok_mine,
        grad_middle,
        vec,
        vec_two,
    )
    output, token_grad, proj_sum, out_sum, up_sum, down_sum, *vectors = hand_over(
        place, (output, token_grad, proj_sum, out_sum, up_sum, down_sum), vec_sum
    )
    return (
        output,
        token_grad,
        proj_sum,
        out_sum,
        up_sum,
        down_sum.T,
        vectors[0].reshape(-1),
        vectors[1].reshape(-1),
        vectors[2].reshape(-1),
        vectors[3].reshape(-1),
    )


def solution(mesh):
    place = Place((mesh.shape["batch"], mesh.shape["blk"]))
    weight, vector = P("batch", "blk"), P("blk")
    row = P("batch", "blk", None)
    in_specs = (row,) + (weight,) * 4 + (vector,) * 4 + (weight,) * 2 + (row,)
    out_specs = (row, row) + (weight,) * 4 + (vector,) * 4
    return jax.shard_map(
        functools.partial(body, place),
        mesh=mesh,
        in_specs=in_specs,
        out_specs=out_specs,
        check_vma=False,
    )
```
